32 devices in a mesh: segment: 4 (over y, x), dp: 8 (over z, core).
Axes of the slice: x: 2, y: 2, z: 4, core: 2. Of those that a mesh axis runs over, the one named last changes fastest.
Arguments:
- layer_input: bfloat16 [4, 48, 49, 2048], P(None, 'dp'), may hold values from -12 to 12
- output_grad: bfloat16 [4, 48, 49, 2048], P(None, 'dp'), may hold values from -12 to 12
- resolution: int32 [4, 48], P(None, 'dp'), may hold values from 0 to 2
- tile_order: int32 [4, 48, 9], P(None, 'dp'), may hold values from 0 to 8, each once within a row
- proj_weight: bfloat16 [4, 2048, 512], P('segment'), may hold values from -0.125 to 0.125
- spatial_weight: bfloat16 [4, 4608, 512], P('segment'), may hold values from -0.09375 to 0.09375
- shortcut_weight: bfloat16 [4, 2048, 2048], P('segment'), may hold values from -0.125 to 0.125
- bn_gain: float32 [4, 2048], P('segment'), may hold values from 0.1 to 1.9
- bn_bias: float32 [4, 2048], P('segment'), may hold values from -2.5 to 2.5
Outputs:
- section_maps: bfloat16 [4, 4, 48, 49, 2048], P('segment', None, 'dp')
- proj_grad: float32 [4, 2048, 512], P('segment')
- spatial_grad: float32 [4, 4608, 512], P('segment')
- shortcut_grad: float32 [4, 2048, 2048], P('segment')
- gain_grad: float32 [4, 2048], P('segment')
- bias_grad: float32 [4, 2048], P('segment')
The draws below stay inside these ranges and needn't reach their ends.
All inputs are finite; a program needn't handle non-finite values.
Results may differ from the reference program's by a relative error of at most 0.018.
Values may be sent and summed in bfloat16 or wider, within the bound.
A program may use at most 320 MiB of HBM per device.

```python
import jax
import jax.numpy as jnp
from jax import lax

D = 2048
MID = 512
MAP = 7
MICRO = 4
SECTIONS = 4
IMAGES = 48


def rising_scales(power):
    fraction = jnp.arange(IMAGES, dtype=jnp.float32) / max(IMAGES - 1, 1)
    return (1.0 + 2.0 * fraction) ** power


def draw_layer_input(key, part):
    key = jax.random.fold_in(key, 11)
    values = jnp.clip(jax.random.normal(key, (MICRO, IMAGES, MAP * MAP, D), jnp.float32), -4.0, 4.0)
    values = values * rising_scales(1.0)[None, :, None, None]
    return values.astype(jnp.bfloat16)


def draw_output_grad(key, part):
    key = jax.random.fold_in(key, 13)
    values = jnp.clip(jax.random.normal(key, (MICRO, IMAGES, MAP * MAP, D), jnp.float32), -4.0, 4.0)
    values = values * rising_scales(1.0)[None, :, None, None]
    return values.astype(jnp.bfloat16)


def touch_ends(drawn, stream_key, low, high):
    index_at = [jax.random.randint(jax.random.fold_in(stream_key, axis), (), 0, length) for axis, length in enumerate(drawn.shape)]
    longest = drawn.shape.index(max(drawn.shape))
    neighbour = index_at[:longest] + [(index_at[longest] + 1) % drawn.shape[longest]] + index_at[longest + 1:]
    return drawn.at[tuple(index_at)].set(low).at[tuple(neighbour)].set(high)


def block_levels(own_key, dims, cuts, least, largest):
    level, own = 1.0, jax.random.fold_in(own_key, 6)
    for axis_at, parts in cuts:
        draws = jnp.exp(jax.random.uniform(jax.random.fold_in(own, axis_at), (parts,), jnp.float32, least / len(cuts), largest / len(cuts)))
        level = level * jnp.repeat(draws, dims[axis_at] // parts).reshape([-1 if axis == axis_at else 1 for axis in range(len(dims))])
    return level


def scatter_about(key, dims, spread, most, split=(), held_as=jnp.bfloat16):
    loudness = block_levels(key, dims, split, -0.22, 0.18) if split else 1.0
    values = jax.random.normal(key, dims, jnp.float32) * spread * loudness
    return jnp.minimum(jnp.maximum(values, -most), most).astype(held_as)


def setup_inputs(seed: int = 0) -> dict:
    streams_of = jax.random.split(jax.random.key(seed), 10)
    return {
        "layer_input": draw_layer_input(jax.random.fold_in(streams_of[9], 71), 0),
        "output_grad": draw_output_grad(jax.random.fold_in(streams_of[9], 71), 0),
        "resolution": touch_ends(jax.random.randint(streams_of[2], (MICRO, IMAGES), 0, 3), jax.random.fold_in(streams_of[2], 1), 0, 2).astype(jnp.int32),
        "tile_order": jax.vmap(lambda own: jax.random.permutation(own, 9))(jax.random.split(streams_of[3], MICRO * IMAGES)).reshape((MICRO, IMAGES, 9)).astype(jnp.int32),
        "proj_weight": scatter_about(streams_of[4], (SECTIONS, D, MID), D ** -0.5, 0.125, ((0, 4),)),
        "spatial_weight": scatter_about(streams_of[5], (SECTIONS, 9 * MID, MID), (9 * MID) ** -0.5, 0.09375, ((0, 4),)),
        "shortcut_weight": scatter_about(streams_of[6], (SECTIONS, D, D), D ** -0.5, 0.125, ((0, 4),)),
        "bn_gain": jnp.clip(1.0 + 0.18 * jax.random.normal(streams_of[7], (SECTIONS, D), jnp.float32), 0.1, 1.9),
        "bn_bias": scatter_about(streams_of[8], (SECTIONS, D), 0.5, 2.5, ((0, 4),), jnp.float32),
    }


EPSILON = 1e-05
OFFSETS = ((-1, -1), (-1, 0), (-1, 1), (0, -1), (0, 0), (0, 1), (1, -1), (1, 0), (1, 1))

@jax.custom_vjp
def low(v):
    return lax.optimization_barrier(v.astype(jnp.bfloat16)).astype(jnp.float32)

@jax.custom_vjp
def low_back(v):
    return v

def low_keep(v):
    return (low(v), None)

def low_pass(kept, grad):
    return (grad,)

def back_keep(v):
    return (v, None)

def back_low(kept, grad):
    return (low(grad),)
low.defvjp(low_keep, low_pass)
low_back.defvjp(back_keep, back_low)

def matmul(left, right):
    return jnp.dot(left, right, precision=lax.Precision.HIGHEST)

def layout(resolution_ids, order_ids):
    pixels = jnp.arange(MAP * MAP, dtype=jnp.int32)
    row_of = pixels // MAP
    column_of = pixels % MAP
    extent = 5 + resolution_ids.astype(jnp.int32)[:, None]
    image_mask = ((row_of[None, :] < extent) & (column_of[None, :] < extent)).astype(jnp.float32)
    inside = (row_of < 6) & (column_of < 6)
    position = jnp.where(inside, row_of // 2 * 3 + column_of // 2, 0).astype(jnp.int32)
    picked = order_ids.astype(jnp.int32)[:, position]
    target = (2 * (picked // 3) + row_of % 2) * MAP + 2 * (picked % 3) + column_of % 2
    source = jnp.where(inside[None, :], target, pixels[None, :]).astype(jnp.int32)
    tile_mask = inside.astype(jnp.float32)[None, :] * jnp.take_along_axis(image_mask, source, axis=1)
    return (image_mask, tile_mask, source, inside)

def tap_masks(tiled):
    lattice = jnp.arange(MAP, dtype=jnp.int32)
    tables = []
    for vertical, lateral in OFFSETS:
        same_row = (lattice + vertical) // 2 == lattice // 2
        same_column = (lattice + lateral) // 2 == lattice // 2
        within = same_row[:, None] & same_column[None, :]
        if tiled:
            tables.append(within)
        else:
            tables.append(jnp.ones_like(within))
    return jnp.stack(tables)

def columns(activation, taps):
    images = activation.shape[0]
    narrow = activation.shape[-1]
    lattice = activation.reshape(images, MAP, MAP, narrow)
    padded = jnp.pad(lattice, ((0, 0), (1, 1), (1, 1), (0, 0)))
    pieces = []
    for number, (vertical, lateral) in enumerate(OFFSETS):
        window = padded[:, 1 + vertical:1 + vertical + MAP, 1 + lateral:1 + lateral + MAP, :]
        pieces.append(jnp.where(taps[number][None, :, :, None], window, jnp.zeros_like(window)))
    return jnp.concatenate(pieces, axis=-1).reshape(images * MAP * MAP, 9 * narrow)

def normalize(hidden, weight_mask, gamma_part, beta_part):
    counts = jnp.sum(weight_mask)
    average = lax.optimization_barrier(jnp.sum(weight_mask[:, None] * hidden, axis=0)) / counts
    variance = lax.optimization_barrier(jnp.sum(weight_mask[:, None] * hidden * hidden, axis=0)) / counts - average * average
    return gamma_part * (hidden - average) * lax.rsqrt(variance + EPSILON) + beta_part

def bottleneck(inputs, resolution_ids, order_ids, tiled, projection, spatial, shortcut, gamma, beta, first, second):
    images = inputs.shape[0]
    narrow = projection.shape[2]
    image_mask, tile_mask, source, inside = layout(resolution_ids, order_ids)
    taps = tap_masks(tiled)
    entering = low_back(inputs)
    if tiled:
        gathered = jnp.take_along_axis(entering, source[:, :, None], axis=1)
        moved = jnp.where(inside[None, :, None], gathered, jnp.zeros_like(gathered))
        weight_mask = tile_mask.reshape(-1)
    else:
        moved = entering
        weight_mask = image_mask.reshape(-1)
    flat = moved.reshape(images * MAP * MAP, -1)
    hidden_one = low_back(matmul(flat, projection[first]))
    normed_one = normalize(hidden_one, weight_mask, gamma[first, :narrow], beta[first, :narrow])
    act_one = low(weight_mask[:, None] * jax.nn.silu(normed_one))
    hidden_two = low_back(matmul(columns(act_one.reshape(images, MAP * MAP, narrow), taps), spatial[first]))
    normed_two = normalize(hidden_two, weight_mask, gamma[first, narrow:2 * narrow], beta[first, narrow:2 * narrow])
    act_two = low_back(low(weight_mask[:, None] * jax.nn.silu(normed_two)))
    if tiled:
        residual = flat
    else:
        residual = low(matmul(flat, shortcut[first]))
    hidden_three = low_back(matmul(act_two, projection[second].T))
    summed = low_back(normalize(hidden_three, weight_mask, gamma[second], beta[second]) + residual)
    result = low(weight_mask[:, None] * jax.nn.silu(summed))
    return result.reshape(images, MAP * MAP, -1)

def reference(layer_input, output_grad, resolution, tile_order, proj_weight, spatial_weight, shortcut_weight, bn_gain, bn_bias):
    inputs = layer_input.astype(jnp.float32)
    probe = jnp.zeros_like(inputs)

    def forward(inputs, probe, projection, spatial, shortcut, gamma, beta):

        def one_batch(carried, slices):
            batch_inputs, batch_probe, resolution_ids, order_ids = slices
            first_out = bottleneck(batch_inputs, resolution_ids, order_ids, False, projection, spatial, shortcut, gamma, beta, 0, 1)
            second_out = bottleneck(first_out + batch_probe, resolution_ids, order_ids, True, projection, spatial, shortcut, gamma, beta, 2, 3)
            return (carried, (first_out, second_out))
        unused, outputs = lax.scan(jax.checkpoint(one_batch), jnp.zeros((), jnp.float32), (inputs, probe, resolution, tile_order))
        return outputs
    outputs, pullback = jax.vjp(forward, inputs, probe, proj_weight.astype(jnp.float32), spatial_weight.astype(jnp.float32), shortcut_weight.astype(jnp.float32), bn_gain.astype(jnp.float32), bn_bias.astype(jnp.float32))
    first_all, second_all = outputs
    grads = pullback((jnp.zeros_like(first_all), output_grad.astype(jnp.float32)))
    grad_inputs, grad_probe, grad_projection, grad_spatial, grad_shortcut, grad_gamma, grad_beta = grads
    section_maps = jnp.stack([grad_inputs, first_all, grad_probe, second_all]).astype(jnp.bfloat16)
    return (section_maps, grad_projection, grad_spatial, grad_shortcut, grad_gamma, grad_beta)
```

```python
import functools

import jax
import jax.numpy as jnp
import numpy as np
from jax import lax
from jax.experimental import pallas as pl
from jax.experimental.pallas import tpu as pltpu
from jax.sharding import PartitionSpec as P

MAP = 7
EPSILON = 1e-05
OFFSETS = ((-1, -1), (-1, 0), (-1, 1), (0, -1), (0, 0), (0, 1), (1, -1), (1, 0), (1, 1))
MESH = pl.DeviceIdType.MESH
F32 = jnp.float32
BF16 = jnp.bfloat16


def dp_sum_kernel(count, x_ref, o_ref, slots, own_sem, send_sem, recv_sem):
    segment = lax.axis_index("segment")
    me = lax.axis_index("dp")
    barrier = pltpu.get_barrier_semaphore()

    def greet(k, carry):
        pl.semaphore_signal(
            barrier, inc=1, device_id=(segment, lax.rem(me + k, count)), device_id_type=MESH
        )
        return carry

    lax.fori_loop(1, count, greet, 0)
    pl.semaphore_wait(barrier, count - 1)

    def copy(k):
        return pltpu.make_async_remote_copy(
            src_ref=x_ref,
            dst_ref=slots.at[me],
            send_sem=send_sem.at[k],
            recv_sem=recv_sem.at[k],
            device_id=(segment, lax.rem(me + k, count)),
            device_id_type=MESH,
        )

    def start(k, carry):
        copy(k).start()
        return carry

    lax.fori_loop(1, count, start, 0)
    own = pltpu.make_async_copy(x_ref, slots.at[me], own_sem)
    own.start()
    own.wait()

    def finish(k, carry):
        copy(k).wait_recv()
        copy(k).wait_send()
        return carry

    lax.fori_loop(1, count, finish, 0)
    total = slots[0]
    for k in range(1, count):
        total = total + slots[k]
    o_ref[...] = total


def dp_sum(values, ident):
    count = lax.axis_size("dp")
    return pl.pallas_call(
        functools.partial(dp_sum_kernel, count),
        out_shape=jax.ShapeDtypeStruct(values.shape, values.dtype),
        in_specs=[pl.BlockSpec(memory_space=pltpu.VMEM)],
        out_specs=pl.BlockSpec(memory_space=pltpu.VMEM),
        scratch_shapes=[
            pltpu.VMEM((count,) + values.shape, values.dtype),
            pltpu.SemaphoreType.DMA,
            pltpu.SemaphoreType.DMA((count,)),
            pltpu.SemaphoreType.DMA((count,)),
        ],
        compiler_params=pltpu.CompilerParams(collective_id=ident, has_side_effects=True),
    )(values)


def silu_slope(values):
    sigmoid = jax.nn.sigmoid(values)
    return sigmoid * (1.0 + values * (1.0 - sigmoid))


def layouts(resolution_ids, order_ids):
    pixels = jnp.arange(MAP * MAP, dtype=jnp.int32)
    row_of = pixels // MAP
    column_of = pixels % MAP
    extent = 5 + resolution_ids[:, None]
    image_mask = ((row_of[None, :] < extent) & (column_of[None, :] < extent)).astype(F32)
    inside = (row_of < 6) & (column_of < 6)
    position = jnp.where(inside, row_of // 2 * 3 + column_of // 2, 0)
    onehot_tile = (position[:, None] == jnp.arange(9)[None, :]).astype(jnp.int32)
    picked = jnp.sum(onehot_tile[None] * order_ids[:, None, :], axis=2)
    target = (2 * (picked // 3) + row_of % 2) * MAP + 2 * (picked % 3) + column_of % 2
    moves = (inside[None, :, None] & (target[:, :, None] == pixels[None, None, :])).astype(BF16)
    tile_mask = jnp.einsum("ipq,iq->ip", moves.astype(F32), image_mask)
    return image_mask, tile_mask, moves


def tap_tables(tiled):
    lattice = np.arange(MAP)
    tables = []
    for vertical, lateral in OFFSETS:
        same_row = (lattice + vertical) // 2 == lattice // 2
        same_column = (lattice + lateral) // 2 == lattice // 2
        within = same_row[:, None] & same_column[None, :]
        tables.append(within if tiled else np.ones_like(within))
    return np.stack(tables)


def columns(activation, tiled):
    images, pixels, narrow = activation.shape
    taps = tap_tables(tiled)
    padded = jnp.pad(
        activation.reshape(images, MAP, MAP, narrow), ((0, 0), (1, 1), (1, 1), (0, 0))
    )
    pieces = []
    for number, (vertical, lateral) in enumerate(OFFSETS):
        window = padded[:, 1 + vertical : 1 + vertical + MAP, 1 + lateral : 1 + lateral + MAP, :]
        pieces.append(jnp.where(taps[number][None, :, :, None], window, jnp.zeros_like(window)))
    return jnp.concatenate(pieces, axis=-1).reshape(images * pixels, 9 * narrow)


def uncolumns(gradient, images, tiled):
    narrow = gradient.shape[-1] // 9
    taps = tap_tables(tiled)
    pieces = gradient.reshape(images, MAP, MAP, 9, narrow)
    padded = jnp.zeros((images, MAP + 2, MAP + 2, narrow), F32)
    for number, (vertical, lateral) in enumerate(OFFSETS):
        window = jnp.where(taps[number][None, :, :, None], pieces[:, :, :, number, :], 0.0)
        padded = padded + jnp.pad(
            window, ((0, 0), (1 + vertical, 1 - vertical), (1 + lateral, 1 - lateral), (0, 0))
        )
    return padded[:, 1 : 1 + MAP, 1 : 1 + MAP, :].reshape(images * MAP * MAP, narrow)


def batched(values, batches):
    return values.reshape((batches, values.shape[0] // batches) + values.shape[1:])


def norm_stats(hidden, mask, batches, ident):
    h = batched(hidden, batches)
    m = batched(mask, batches)
    width = hidden.shape[1]
    sums = jnp.concatenate(
        [
            jnp.sum(m * h, axis=1),
            jnp.sum(m * h * h, axis=1),
            jnp.broadcast_to(jnp.sum(m, axis=1), (batches, width)),
        ]
    )
    sums = dp_sum(sums, ident)
    counts = sums[2 * batches :]
    average = sums[:batches] / counts
    inverse = lax.rsqrt(sums[batches : 2 * batches] / counts - average * average + EPSILON)
    return average[:, None, :], inverse[:, None, :], counts[:, None, :]


def norm_apply(hidden, stats, gain, bias, batches):
    average, inverse, _ = stats
    out = gain * (batched(hidden, batches) - average) * inverse + bias
    return out.reshape(hidden.shape)


def norm_back(grad_out, hidden, stats, mask, gain, batches, ident):
    average, inverse, counts = stats
    g = batched(grad_out, batches)
    normed = (batched(hidden, batches) - average) * inverse
    sums = dp_sum(jnp.concatenate([jnp.sum(g, axis=1), jnp.sum(g * normed, axis=1)]), ident)
    offset, scale = sums[:batches, None, :], sums[batches:, None, :]
    out = batched(mask, batches) * gain * inverse * (g - (offset + normed * scale) / counts)
    return (
        out.reshape(hidden.shape).astype(BF16),
        jnp.sum(scale, axis=(0, 1)),
        jnp.sum(offset, axis=(0, 1)),
    )


def mm(a, b, dims="rk,kn->rn"):
    return jnp.einsum(dims, a, b, preferred_element_type=F32)


def to_section_zero(value):
    sections = lax.axis_size("segment")
    parts = [value] + [lax.ppermute(value, "segment", [(t, 0)]) for t in range(1, sections)]
    return jnp.stack(parts)


def core_swap(value):
    count = lax.axis_size("dp")
    return lax.ppermute(value, "dp", [(d, d ^ 1) for d in range(count)])


def body(
    layer_input,
    output_grad,
    resolution,
    tile_order,
    proj_weight,
    spatial_weight,
    shortcut_weight,
    bn_gain,
    bn_bias,
):
    micro, images, pixels, wide = layer_input.shape
    narrow = proj_weight.shape[2]
    rows = images * pixels
    sections = lax.axis_size("segment")
    count = lax.axis_size("dp")
    section = lax.axis_index("segment")
    place = lax.axis_index("dp")
    core = place % 2
    first = section == 0
    proj, spatial, shortcut = proj_weight[0], spatial_weight[0], shortcut_weight[0]

    slice_rows = wide // count
    tap_rows = spatial.shape[0] // count
    own_proj = lax.dynamic_slice_in_dim(proj, place * slice_rows, slice_rows)
    own_taps = lax.dynamic_slice_in_dim(spatial, place * tap_rows, tap_rows)
    fine = tap_rows // sections
    taps_piece = lax.dynamic_slice_in_dim(own_taps, 2 * fine, fine)
    for t in range(sections):
        if t != 2:
            got = lax.ppermute(own_taps[t * fine : (t + 1) * fine], "segment", [(2, t)])
            taps_piece = jnp.where(section == t, got, taps_piece)
    packed = jnp.concatenate([own_proj, taps_piece])
    everyone = lax.all_gather(packed, ("segment", "dp"), axis=0, tiled=True)
    everyone = everyone.reshape(sections, count, slice_rows + fine, narrow)
    proj_of = [everyone[k, :, :slice_rows].reshape(wide, narrow) for k in range(sections)]
    taps_two = jnp.swapaxes(everyone[:, :, slice_rows:], 0, 1).reshape(9 * narrow, narrow)

    quarter = wide // sections
    half = wide // 2
    own_half = lax.dynamic_slice_in_dim(shortcut, core * half, half)
    short_half = own_half[:, :quarter]
    for t in range(1, sections):
        got = lax.ppermute(own_half[:, t * quarter : (t + 1) * quarter], "segment", [(0, t)])
        short_half = jnp.where(section == t, got, short_half)
    short_other = core_swap(short_half)
    short_quarter = jnp.where(
        core == 0,
        jnp.concatenate([short_half, short_other]),
        jnp.concatenate([short_other, short_half]),
    )

    stats_gain = jnp.concatenate([bn_gain[0], bn_bias[0]])
    gains = lax.all_gather(stats_gain, "segment", axis=0)
    gain, bias = gains[:, :wide], gains[:, wide:]

    image_mask_all, tile_mask_all, moves_all = layouts(
        resolution.reshape(-1), tile_order.reshape(micro * images, -1)
    )
    mask_all = image_mask_all.reshape(micro * rows, 1)
    pick = lambda a: lax.dynamic_index_in_dim(a, section, 0, keepdims=False)
    image_mask = pick(image_mask_all.reshape(micro, rows, 1))
    tile_mask = pick(tile_mask_all.reshape(micro, rows, 1))
    moves = pick(moves_all.reshape(micro, images, pixels, pixels))

    flat_all = layer_input.reshape(micro * rows, wide)
    gain_a, bias_a = bn_gain[0, :narrow], bn_bias[0, :narrow]
    gain_b, bias_b = bn_gain[0, narrow : 2 * narrow], bn_bias[0, narrow : 2 * narrow]
    hidden_one = mm(flat_all, proj)
    stats_one = norm_stats(hidden_one, mask_all, micro, 0)
    normed_one = norm_apply(hidden_one, stats_one, gain_a, bias_a, micro)
    act_one = (mask_all * jax.nn.silu(normed_one)).astype(BF16)
    hidden_two = mm(columns(act_one.reshape(micro * images, pixels, narrow), False), spatial)
    stats_two = norm_stats(hidden_two, mask_all, micro, 1)
    normed_two = norm_apply(hidden_two, stats_two, gain_b, bias_b, micro)
    act_two_all = (mask_all * jax.nn.silu(normed_two)).astype(BF16)
    act_two_parts = act_two_all.reshape(micro, rows, narrow)
    act_two = act_two_parts[0]
    for t in range(1, sections):
        got = lax.ppermute(act_two_parts[t], "segment", [(0, t)])
        act_two = jnp.where(section == t, got, act_two)

    residual_quarter = mm(flat_all, short_quarter).astype(BF16).reshape(micro, rows, quarter)
    residual = lax.all_to_all(residual_quarter, "segment", 0, 2, tiled=True).reshape(rows, wide)

    hidden_three = mm(act_two, proj_of[1], "rk,dk->rd")
    stats_three = norm_stats(hidden_three, image_mask, 1, 2)
    summed = norm_apply(hidden_three, stats_three, gain[1], bias[1], 1) + residual.astype(F32)
    first_out = (image_mask * jax.nn.silu(summed)).astype(BF16)

    moved = mm(moves, first_out.reshape(images, pixels, wide), "ipq,iqd->ipd").astype(BF16)
    moved = moved.reshape(rows, wide)
    tile_gain_a, tile_bias_a = gain[2, :narrow], bias[2, :narrow]
    tile_gain_b, tile_bias_b = gain[2, narrow : 2 * narrow], bias[2, narrow : 2 * narrow]
    tile_one = mm(moved, proj_of[2])
    tile_stats_one = norm_stats(tile_one, tile_mask, 1, 3)
    tile_normed_one = norm_apply(tile_one, tile_stats_one, tile_gain_a, tile_bias_a, 1)
    tile_act_one = (tile_mask * jax.nn.silu(tile_normed_one)).astype(BF16)
    tile_columns = columns(tile_act_one.reshape(images, pixels, narrow), True)
    tile_two = mm(tile_columns, taps_two)
    tile_stats_two = norm_stats(tile_two, tile_mask, 1, 4)
    tile_normed_two = norm_apply(tile_two, tile_stats_two, tile_gain_b, tile_bias_b, 1)
    tile_act_two = (tile_mask * jax.nn.silu(tile_normed_two)).astype(BF16)
    tile_three = mm(tile_act_two, proj_of[3], "rk,dk->rd")
    tile_stats_three = norm_stats(tile_three, tile_mask, 1, 5)
    tile_summed = norm_apply(tile_three, tile_stats_three, gain[3], bias[3], 1) + moved.astype(F32)
    second_out = (tile_mask * jax.nn.silu(tile_summed)).astype(BF16)

    grad = pick(output_grad).reshape(rows, wide)
    grad_summed = (grad.astype(F32) * tile_mask * silu_slope(tile_summed)).astype(BF16)
    grad_three, scale_3, offset_3 = norm_back(
        grad_summed.astype(F32), tile_three, tile_stats_three, tile_mask, gain[3], 1, 6
    )
    proj_term_3 = mm(grad_three, tile_act_two, "rd,rk->dk")
    grad_act_two = mm(grad_three, proj_of[3]).astype(BF16)
    grad_normed = grad_act_two.astype(F32) * tile_mask * silu_slope(tile_normed_two)
    grad_two, scale_2b, offset_2b = norm_back(
        grad_normed, tile_two, tile_stats_two, tile_mask, tile_gain_b, 1, 7
    )
    taps_term_2 = mm(tile_columns, grad_two, "rk,rn->kn")
    grad_act_one = uncolumns(mm(grad_two, taps_two, "rn,kn->rk"), images, True)
    grad_normed = grad_act_one * tile_mask * silu_slope(tile_normed_one)
    grad_one, scale_2a, offset_2a = norm_back(
        grad_normed, tile_one, tile_stats_one, tile_mask, tile_gain_a, 1, 8
    )
    proj_term_2 = mm(moved, grad_one, "rc,rn->cn")
    grad_moved = (mm(grad_one, proj_of[2], "rn,cn->rc") + grad_summed.astype(F32)).astype(BF16)
    grad_first = mm(moves, grad_moved.reshape(images, pixels, wide), "ipq,ipd->iqd").astype(BF16)
    grad_first = grad_first.reshape(rows, wide)

    grad_sum_one = (grad_first.astype(F32) * image_mask * silu_slope(summed)).astype(BF16)
    grad_sum_all = to_section_zero(grad_sum_one).reshape(micro * rows, wide)
    grad_sum_quarter = lax.all_to_all(
        grad_sum_one.reshape(rows, sections, quarter), "segment", 1, 0, tiled=True
    ).reshape(micro * rows, quarter)
    short_term = mm(flat_all, grad_sum_quarter, "rc,rd->cd")
    grad_hidden_three, scale_1, offset_1 = norm_back(
        grad_sum_one.astype(F32), hidden_three, stats_three, image_mask, gain[1], 1, 9
    )
    proj_term_1 = mm(grad_hidden_three, act_two, "rd,rk->dk")
    grad_act_two = to_section_zero(mm(grad_hidden_three, proj_of[1]).astype(BF16))
    grad_act_two = grad_act_two.reshape(micro * rows, narrow)

    grad_normed = grad_act_two.astype(F32) * mask_all * silu_slope(normed_two)
    grad_hidden_two, scale_0b, offset_0b = norm_back(
        grad_normed, hidden_two, stats_two, mask_all, gain_b, micro, 10
    )
    taps_term_0 = mm(
        columns(act_one.reshape(micro * images, pixels, narrow), False),
        grad_hidden_two,
        "rk,rn->kn",
    )
    grad_act_one = uncolumns(mm(grad_hidden_two, spatial, "rn,kn->rk"), micro * images, False)
    grad_normed = grad_act_one * mask_all * silu_slope(normed_one)
    grad_hidden_one, scale_0a, offset_0a = norm_back(
        grad_normed, hidden_one, stats_one, mask_all, gain_a, micro, 11
    )
    proj_term_0 = mm(flat_all, grad_hidden_one, "rc,rn->cn")
    grad_input = (
        mm(grad_hidden_one, proj, "rn,cn->rc") + mm(grad_sum_all, shortcut, "rd,cd->rc")
    ).astype(BF16)

    as_map = lambda a: a.reshape(images, pixels, wide)
    exchanged = lax.all_to_all(
        jnp.stack([as_map(first_out), as_map(first_out), as_map(grad_first), as_map(second_out)]),
        "segment",
        0,
        0,
        tiled=True,
    )
    maps = jnp.where(first, grad_input.reshape(micro, images, pixels, wide), exchanged)

    blank = jnp.zeros((wide,), F32)
    pad = jnp.zeros((wide - 2 * narrow,), F32)
    zero_gain = jnp.where(first, jnp.concatenate([scale_0a, scale_0b, pad]), blank)
    zero_bias = jnp.where(first, jnp.concatenate([offset_0a, offset_0b, pad]), blank)
    vectors = jnp.stack(
        [
            zero_gain,
            zero_bias,
            scale_1,
            offset_1,
            jnp.concatenate([scale_2a, scale_2b, pad]),
            jnp.concatenate([offset_2a, offset_2b, pad]),
            scale_3,
            offset_3,
        ]
    )
    vectors = pick(lax.psum(vectors, "segment").reshape(sections, 2, wide))

    def halved(term):
        rows_half = term.shape[0] // 2
        mine = lax.dynamic_slice_in_dim(term, core * rows_half, rows_half)
        theirs = lax.dynamic_slice_in_dim(term, (1 - core) * rows_half, rows_half)
        return mine + core_swap(theirs.astype(BF16)).astype(F32)

    def planar(term):
        part = halved(term).astype(BF16)
        part = lax.all_to_all(
            part.reshape((sections, part.shape[0] // sections) + part.shape[1:]),
            "segment",
            0,
            0,
        )
        return jnp.sum(part.astype(F32), axis=0)

    keep = lambda term: jnp.where(first, term, jnp.zeros_like(term))
    stacked = [
        planar(keep(proj_term_0)),
        planar(keep(taps_term_0)),
        planar(proj_term_1),
        planar(proj_term_2),
        planar(taps_term_2),
        planar(proj_term_3),
        halved(short_term),
    ]
    heights = [a.shape[0] for a in stacked]
    groups = [[d for d in range(count) if d % 2 == c] for c in range(2)]
    depth = count // 2
    joined = jnp.concatenate(
        [a.astype(BF16).reshape(depth, a.shape[0] // depth, narrow) for a in stacked], axis=1
    )
    summed_up = lax.psum_scatter(
        joined, "dp", scatter_dimension=0, tiled=False, axis_index_groups=groups
    )
    whole = lax.all_gather(summed_up.astype(BF16), "dp", axis=0, axis_index_groups=groups)
    pieces, at = [], 0
    for h in heights:
        pieces.append(whole[:, at : at + h // depth].reshape(h, narrow))
        at += h // depth
    none_taps, none_short = jnp.zeros_like(pieces[1]), jnp.zeros_like(pieces[6])
    parcels = jnp.stack(
        [
            jnp.concatenate([pieces[0], pieces[1], pieces[6]]),
            jnp.concatenate([pieces[2], none_taps, none_short]),
            jnp.concatenate([pieces[3], pieces[4], none_short]),
            jnp.concatenate([pieces[5], none_taps, none_short]),
        ]
    )
    parcels = lax.all_to_all(parcels, "segment", 0, 0)
    other = core_swap(parcels)
    both = jnp.where(core == 0, jnp.stack([parcels, other]), jnp.stack([other, parcels]))
    hp, ht = heights[0], heights[1]
    proj_grad = both[:, :, :hp].reshape(wide, narrow).astype(F32)
    spatial_grad = both[:, :, hp : hp + ht].reshape(9 * narrow, narrow).astype(F32)
    short_grad = jnp.swapaxes(both[:, :, hp + ht :], 1, 2).reshape(wide, wide).astype(F32)
    return (
        maps[None],
        proj_grad[None],
        spatial_grad[None],
        short_grad[None],
        vectors[:1],
        vectors[1:],
    )


def solution(mesh):
    return jax.shard_map(
        body,
        mesh=mesh,
        in_specs=(
            P(None, "dp", None, None),
            P(None, "dp", None, None),
            P(None, "dp"),
            P(None, "dp", None),
            P("segment", None, None),
            P("segment", None, None),
            P("segment", None, None),
            P("segment", None),
            P("segment", None),
        ),
        out_specs=(
            P("segment", None, "dp", None, None),
            P("segment", None, None),
            P("segment", None, None),
            P("segment", None, None),
            P("segment", None),
            P("segment", None),
        ),
        check_vma=False,
    )
```

```python
import functools

import jax
import jax.numpy as jnp
import numpy as np
from jax import lax
from jax.experimental import pallas as pl
from jax.experimental.pallas import tpu as pltpu
from jax.sharding import PartitionSpec as P

MAP = 7
EPSILON = 1e-05
OFFSETS = ((-1, -1), (-1, 0), (-1, 1), (0, -1), (0, 0), (0, 1), (1, -1), (1, 0), (1, 1))
MESH = pl.DeviceIdType.MESH
F32 = jnp.float32
BF16 = jnp.bfloat16
VMEM_BYTES = 58 * 2**20
TILE = 256


def greet(count):
    segment, me = lax.axis_index("segment"), lax.axis_index("dp")
    barrier = pltpu.get_barrier_semaphore()

    def one(k, carry):
        pl.semaphore_signal(
            barrier, inc=1, device_id=(segment, lax.rem(me + k, count)), device_id_type=MESH
        )
        return carry

    lax.fori_loop(1, count, one, 0)


def greeted(count):
    pl.semaphore_wait(pltpu.get_barrier_semaphore(), count - 1)


def exchange(count, slots, send_sem, recv_sem):
    segment, me = lax.axis_index("segment"), lax.axis_index("dp")

    def copy(k):
        return pltpu.make_async_remote_copy(
            src_ref=slots.at[me],
            dst_ref=slots.at[me],
            send_sem=send_sem.at[k],
            recv_sem=recv_sem.at[k],
            device_id=(segment, lax.rem(me + k, count)),
            device_id_type=MESH,
        )

    def start(k, carry):
        copy(k).start()
        return carry

    def finish(k, carry):
        copy(k).wait_recv()
        copy(k).wait_send()
        return carry

    lax.fori_loop(1, count, start, 0)
    lax.fori_loop(1, count, finish, 0)
    total = slots[0]
    for k in range(1, count):
        total = total + slots[k]
    return total


def sync_scratch(count, shapes):
    out = []
    for shape in shapes:
        out += [
            pltpu.VMEM((count,) + shape, F32),
            pltpu.SemaphoreType.DMA((count,)),
            pltpu.SemaphoreType.DMA((count,)),
        ]
    return out


def kernel_call(kernel, outs, args, scratch, ident, flops, moved, spaces=None):
    params = dict(has_side_effects=True, vmem_limit_bytes=VMEM_BYTES)
    if ident is not None:
        params["collective_id"] = ident
    return pl.pallas_call(
        kernel,
        out_shape=outs,
        in_specs=[pl.BlockSpec(memory_space=pltpu.VMEM) for _ in args],
        out_specs=[pl.BlockSpec(memory_space=pltpu.VMEM) for _ in outs],
        scratch_shapes=scratch,
        compiler_params=pltpu.CompilerParams(**params),
        cost_estimate=pl.CostEstimate(flops=flops, bytes_accessed=moved, transcendentals=0),
    )(*args)


def shape_of(shape, dtype):
    return jax.ShapeDtypeStruct(shape, dtype)


def dot(a, b):
    return jnp.dot(a, b, preferred_element_type=F32)


def dot_t(a, b):
    return lax.dot_general(a, b, (((1,), (1,)), ((), ())), preferred_element_type=F32)


def sigmoid(v):
    return 1.0 / (1.0 + jnp.exp(-v))


def slope(v):
    s = sigmoid(v)
    return s * (1.0 + v * (1.0 - s))


def over(width, step, body):
    def one(j, carry):
        body(pl.ds(pl.multiple_of(j * step, step), step))
        return carry

    lax.fori_loop(0, width // step, one, 0)


def lane(at):
    return lax.div(at.start, 128)


def unrolled_shift(ref_value, shift):
    rows = ref_value.shape[0]
    return ref_value if shift % rows == 0 else pltpu.roll(ref_value, (-shift) % rows, 0)


def by_batch(values):
    rows, width = values.shape
    part = jnp.sum(values.reshape(rows // 8, 8, width), axis=0)
    return part[:4] + part[4:]


def spread8(values):
    return jnp.concatenate([values, values], axis=0)[None]


def first_kernel(
    count, x, w, k, gb, pack, tiles, a2_out, cols, h1n, h2n, stats_out, count_out, act, *sync
):
    s1, send1, recv1, s2, send2, recv2 = sync
    rows, narrow = h1n.shape
    me = lax.axis_index("dp")
    greet(count)
    full = act.shape[1]

    def tile8(v):
        return v.reshape(rows // 8, 8, v.shape[1])

    def project(at):
        h = dot(x[...], w[:, at])
        h1n[:, at] = h
        m = pack[:, 0:1] * h
        s1[me, 0:4, at] = by_batch(m)
        s1[me, 4:8, at] = by_batch(m * h)

    over(narrow, TILE, project)
    s1[me, 0:4, narrow:] = jnp.broadcast_to(by_batch(pack[:, 0:1]), (4, 128))
    s1[me, 4:8, narrow:] = jnp.broadcast_to(by_batch(tiles[:, 0:1]), (4, 128))
    greeted(count)
    total = exchange(count, s1, send1, recv1)
    counts = total[:, narrow:]
    count_out[...] = counts
    valid = counts[0:4, 0:1]
    average = total[0:4, :narrow] / valid
    inverse = lax.rsqrt(total[4:8, :narrow] / valid - average * average + EPSILON)
    stats_out[0:4, :] = average
    stats_out[4:8, :] = inverse

    def activate(stat_at, gain_at, source):
        def body(at):
            mean = spread8(stats_out[stat_at : stat_at + 4, at])
            inv = spread8(stats_out[stat_at + 4 : stat_at + 8, at])
            hn = (tile8(source[:, at]) - mean) * inv
            source[:, at] = hn.reshape(rows, hn.shape[2])
            n = gb[gain_at : gain_at + 1, at][None] * hn + gb[gain_at + 1 : gain_at + 2, at][None]
            n = n.reshape(rows, n.shape[2])
            act[lane(at), 0:rows, :] = pack[:, 0:1] * (n * sigmoid(n))

        return body

    over(narrow, 128, activate(0, 0, h1n))

    for t, (vertical, lateral) in enumerate(OFFSETS):
        shift = 4 * (7 * vertical + lateral)

        def place(j, carry, t=t, shift=shift):
            at = pl.ds(pl.multiple_of(j * 128, 128), 128)
            to = pl.ds(pl.multiple_of(t * narrow + j * 128, 128), 128)
            moved = unrolled_shift(act[j, 0:rows, :], shift)
            cols[:, to] = (pack[:, 1 + t : 2 + t] * moved).astype(BF16)
            return carry

        lax.fori_loop(0, narrow // 128, place, 0)

    def convolve(at):
        h = dot(cols[...], k[:, at])
        h2n[:, at] = h
        m = pack[:, 0:1] * h
        s2[me, 0:4, at] = by_batch(m)
        s2[me, 4:8, at] = by_batch(m * h)

    over(narrow, TILE, convolve)
    total = exchange(count, s2, send2, recv2)
    average = total[0:4] / valid
    stats_out[8:12, :] = average
    stats_out[12:16, :] = lax.rsqrt(total[4:8] / valid - average * average + EPSILON)
    over(narrow, 128, activate(8, 2, h2n))
    act[:, rows:, :] = jnp.zeros((narrow // 128, full - rows, 128), F32)
    for m in range(4):

        def pick(j, carry, m=m):
            at = pl.ds(pl.multiple_of(j * 128, 128), 128)
            a2_out[m, :, at] = act[j, pl.ds(m, full // 4, stride=4), :].astype(BF16)
            return carry

        lax.fori_loop(0, narrow // 128, pick, 0)


def residual_kernel(x, wa, wb, out, hold):
    rows, depth = x.shape[0], wa.shape[0]
    full, quarter = hold.shape[1], out.shape[2]
    core = lax.rem(lax.axis_index("dp"), 2)
    first = pl.ds(pl.multiple_of(core * depth, depth), depth)
    second = pl.ds(pl.multiple_of((1 - core) * depth, depth), depth)
    hold[:, rows:, :] = jnp.zeros((quarter // 128, full - rows, 128), F32)

    def body(at):
        value = dot(x[:, first], wa[:, at]) + dot(x[:, second], wb[:, at])
        for part in range(TILE // 128):
            hold[lane(at) + part, 0:rows, :] = value[:, part * 128 : part * 128 + 128]

    over(quarter, TILE, body)
    for m in range(4):

        def pick(j, carry, m=m):
            at = pl.ds(pl.multiple_of(j * 128, 128), 128)
            out[m, :, at] = hold[j, pl.ds(m, full // 4, stride=4), :].astype(BF16)
            return carry

        lax.fori_loop(0, quarter // 128, pick, 0)


def norm_sums(slots, me, at, masked, h):
    slots[me, 0:1, at] = jnp.sum(masked, axis=0, keepdims=True)
    slots[me, 1:2, at] = jnp.sum(masked * h, axis=0, keepdims=True)


def finish_stats(total, valid, stats_out, at_row):
    average = total[0:1] / valid
    width = average.shape[1]
    stats_out[at_row : at_row + 1, 0:width] = average
    stats_out[at_row + 1 : at_row + 2, 0:width] = lax.rsqrt(
        total[1:2] / valid - average * average + EPSILON
    )


def second_kernel(
    count, a2, w1, res, pack, gb, valid_in, moves, y_out, u_out, h3n, stats_out, s1, send1, recv1
):
    wide = h3n.shape[1]
    quarter = res.shape[2]
    me = lax.axis_index("dp")
    greet(count)

    def project(at):
        h = dot_t(a2[...], w1[at, :])
        h3n[:, at] = h
        norm_sums(s1, me, at, pack[:, 0:1] * h, h)

    over(wide, TILE, project)
    greeted(count)
    valid = valid_in[0:1, 0:1]
    finish_stats(exchange(count, s1, send1, recv1), valid, stats_out, 0)
    for q in range(wide // quarter):

        def body(j, carry, q=q):
            at = pl.ds(pl.multiple_of(q * quarter + j * 128, 128), 128)
            own = pl.ds(pl.multiple_of(j * 128, 128), 128)
            hn = (h3n[:, at] - stats_out[0:1, at]) * stats_out[1:2, at]
            h3n[:, at] = hn
            z = gb[0:1, at] * hn + gb[1:2, at] + res[q, :, own].astype(F32)
            y_out[:, at] = (pack[:, 0:1] * (z * sigmoid(z))).astype(BF16)
            return carry

        lax.fori_loop(0, quarter // 128, body, 0)

    def permute(at):
        u_out[:, at] = dot(moves[...], y_out[:, at]).astype(BF16)

    over(wide, TILE, permute)


def back_sums(slots, me, at, grad, hn):
    slots[me, 0:1, at] = jnp.sum(grad, axis=0, keepdims=True)
    slots[me, 1:2, at] = jnp.sum(grad * hn, axis=0, keepdims=True)


def tile_kernel(
    count,
    u,
    w2,
    k2,
    w3,
    og,
    pack,
    gb2,
    gb3,
    valid_in,
    back,
    y_out,
    a2,
    cols,
    dh3,
    dh2,
    dh1,
    dy,
    sums_out,
    h1n,
    h2n,
    h3n,
    act,
    dz,
    stats,
    *sync,
):
    s1, send1, recv1, s2, send2, recv2, s3, send3, recv3 = sync[:9]
    b3, bsend3, brecv3, b2, bsend2, brecv2, b1, bsend1, brecv1 = sync[9:]
    rows, wide = u.shape
    narrow = h1n.shape[1]
    me = lax.axis_index("dp")
    valid = valid_in[0:1, 0:1]
    greet(count)

    def project(at):
        h = dot(u[...], w2[:, at])
        h1n[:, at] = h
        norm_sums(s1, me, at, pack[:, 0:1] * h, h)

    over(narrow, TILE, project)
    greeted(count)
    finish_stats(exchange(count, s1, send1, recv1), valid, stats, 0)

    def activate(row, gain, source, store):
        def body(at):
            hn = (source[:, at] - stats[row : row + 1, at]) * stats[row + 1 : row + 2, at]
            source[:, at] = hn
            n = gb2[gain : gain + 1, at] * hn + gb2[gain + 1 : gain + 2, at]
            store(at, pack[:, 0:1] * (n * sigmoid(n)))

        return body

    def to_act(at, value):
        act[:, at] = value

    def to_a2(at, value):
        a2[:, at] = value.astype(BF16)

    over(narrow, 128, activate(0, 0, h1n, to_act))
    for t, (vertical, lateral) in enumerate(OFFSETS):
        shift = 7 * vertical + lateral

        def place(j, carry, t=t, shift=shift):
            at = pl.ds(pl.multiple_of(j * 128, 128), 128)
            to = pl.ds(pl.multiple_of(t * narrow + j * 128, 128), 128)
            moved = unrolled_shift(act[:, at], shift)
            cols[:, to] = (pack[:, 1 + t : 2 + t] * moved).astype(BF16)
            return carry

        lax.fori_loop(0, narrow // 128, place, 0)

    def convolve(at):
        h = dot(cols[...], k2[:, at])
        h2n[:, at] = h
        norm_sums(s2, me, at, pack[:, 0:1] * h, h)

    over(narrow, TILE, convolve)
    finish_stats(exchange(count, s2, send2, recv2), valid, stats, 2)
    over(narrow, 128, activate(2, 2, h2n, to_a2))

    def expand(at):
        h = dot_t(a2[...], w3[at, :])
        h3n[:, at] = h
        norm_sums(s3, me, at, pack[:, 0:1] * h, h)

    over(wide, TILE, expand)
    finish_stats(exchange(count, s3, send3, recv3), valid, stats, 4)

    def result(at):
        hn = (h3n[:, at] - stats[4:5, at]) * stats[5:6, at]
        h3n[:, at] = hn
        z = gb3[0:1, at] * hn + gb3[1:2, at] + u[:, at].astype(F32)
        s = sigmoid(z)
        m = pack[:, 0:1]
        y_out[:, at] = (m * (z * s)).astype(BF16)
        grad = (og[:, at].astype(F32) * m * (s * (1.0 + z * (1.0 - s)))).astype(BF16)
        dz[:, at] = grad
        grad = grad.astype(F32)
        back_sums(b3, me, at, grad, hn)

    over(wide, 128, result)
    total = exchange(count, b3, bsend3, brecv3)
    sums_out[0:2, :] = total

    def through(at):
        offset, scale = sums_out[0:1, at], sums_out[1:2, at]
        dh3[:, at] = (
            pack[:, 0:1]
            * gb3[0:1, at]
            * stats[5:6, at]
            * (dz[:, at].astype(F32) - (offset + h3n[:, at] * scale) / valid)
        ).astype(BF16)

    over(wide, 128, through)

    def into_two(at):
        grad = dot(dh3[...], w3[:, at]).astype(BF16).astype(F32)
        hn = h2n[:, at]
        n = gb2[2:3, at] * hn + gb2[3:4, at]
        grad = grad * pack[:, 0:1] * slope(n)
        act[:, at] = grad
        back_sums(b2, me, at, grad, hn)

    over(narrow, TILE, into_two)
    total = exchange(count, b2, bsend2, brecv2)
    sums_out[2:4, 0:narrow] = total

    def through_two(at):
        offset, scale = sums_out[2:3, at], sums_out[3:4, at]
        grad = (
            pack[:, 0:1]
            * gb2[2:3, at]
            * stats[3:4, at]
            * (act[:, at] - (offset + h2n[:, at] * scale) / valid)
        )
        dh2[:, at] = grad.astype(BF16)
        act[:, at] = dh2[:, at].astype(F32)

    over(narrow, 128, through_two)
    h2n[...] = jnp.zeros((rows, narrow), F32)
    for t, (vertical, lateral) in enumerate(OFFSETS):
        shift = -(7 * vertical + lateral)
        other = 8 - t

        def place_back(j, carry, t=t, shift=shift, other=other):
            at = pl.ds(pl.multiple_of(j * 128, 128), 128)
            moved = unrolled_shift(act[:, at], shift)
            dy[:, at] = (pack[:, 1 + other : 2 + other] * moved).astype(BF16)
            return carry

        lax.fori_loop(0, narrow // 128, place_back, 0)

        def gather(at, t=t):
            row = pl.ds(pl.multiple_of(t * narrow + at.start, TILE), TILE)
            h2n[:, at] += dot_t(dy[:, 0:narrow], k2[row, :])

        over(narrow, TILE, gather)

    def into_one(at):
        hn = h1n[:, at]
        n = gb2[0:1, at] * hn + gb2[1:2, at]
        grad = h2n[:, at] * pack[:, 0:1] * slope(n)
        act[:, at] = grad
        back_sums(b1, me, at, grad, hn)

    over(narrow, 128, into_one)
    total = exchange(count, b1, bsend1, brecv1)
    sums_out[4:6, 0:narrow] = total

    def through_one(at):
        offset, scale = sums_out[4:5, at], sums_out[5:6, at]
        dh1[:, at] = (
            pack[:, 0:1]
            * gb2[0:1, at]
            * stats[1:2, at]
            * (act[:, at] - (offset + h1n[:, at] * scale) / valid)
        ).astype(BF16)

    over(narrow, 128, through_one)

    def into_input(at):
        grad = dot_t(dh1[...], w2[at, :]) + dz[:, at].astype(F32)
        dy[:, at] = dot(back[...], grad.astype(BF16)).astype(BF16)

    over(wide, TILE, into_input)


def image_back_kernel(
    count, dy, res, h3n, pack, gb, stats, valid_in, w1, dz, dh3, da2, sums_out, b3, send3, recv3
):
    wide = dy.shape[1]
    quarter = res.shape[2]
    narrow = da2.shape[1]
    me = lax.axis_index("dp")
    valid = valid_in[0:1, 0:1]
    greet(count)
    for q in range(wide // quarter):

        def body(j, carry, q=q):
            at = pl.ds(pl.multiple_of(q * quarter + j * 128, 128), 128)
            own = pl.ds(pl.multiple_of(j * 128, 128), 128)
            hn = h3n[:, at]
            z = gb[0:1, at] * hn + gb[1:2, at] + res[q, :, own].astype(F32)
            grad = (dy[:, at].astype(F32) * pack[:, 0:1] * slope(z)).astype(BF16)
            dz[:, at] = grad
            back_sums(b3, me, at, grad.astype(F32), hn)
            return carry

        lax.fori_loop(0, quarter // 128, body, 0)
    greeted(count)
    total = exchange(count, b3, send3, recv3)
    sums_out[...] = total

    def through(at):
        offset, scale = sums_out[0:1, at], sums_out[1:2, at]
        dh3[:, at] = (
            pack[:, 0:1]
            * gb[0:1, at]
            * stats[1:2, at]
            * (dz[:, at].astype(F32) - (offset + h3n[:, at] * scale) / valid)
        ).astype(BF16)

    over(wide, 128, through)

    def into(at):
        da2[:, at] = dot(dh3[...], w1[:, at]).astype(BF16)

    over(narrow, TILE, into)


def last_kernel(
    count, da2, k, gb, pack, h1n, h2n, stats, counts, dh2, dh1, sums_out, act, acc, hold, *sync
):
    b2, send2, recv2, b1, send1, recv1 = sync
    rows, narrow = h1n.shape
    full = act.shape[1]
    me = lax.axis_index("dp")
    greet(count)
    valid = counts[0:4, 0:1]

    def tile8(v):
        return v.reshape(rows // 8, 8, v.shape[1])

    for m in range(4):

        def put(j, carry, m=m):
            at = pl.ds(pl.multiple_of(j * 128, 128), 128)
            act[j, pl.ds(m, full // 4, stride=4), :] = da2[m, :, at].astype(F32)
            return carry

        lax.fori_loop(0, narrow // 128, put, 0)

    def into(gain, source, hidden, slots):
        def body(at):
            hn = hidden[:, at]
            n = gb[gain : gain + 1, at] * hn + gb[gain + 1 : gain + 2, at]
            grad = source(at) * pack[:, 0:1] * slope(n)
            act[lane(at), 0:rows, :] = grad
            slots[me, 0:4, at] = by_batch(grad)
            slots[me, 4:8, at] = by_batch(grad * hn)

        return body

    def through(gain, stat_at, row, hidden, out):
        def body(at):
            offset = spread8(sums_out[row : row + 4, at] / valid)
            scale = spread8(sums_out[row + 4 : row + 8, at] / valid)
            inv = spread8(stats[stat_at : stat_at + 4, at])
            g = tile8(act[lane(at), 0:rows, :])
            value = inv * gb[gain : gain + 1, at][None] * (g - (offset + tile8(hidden[:, at]) * scale))
            value = (pack[:, 0:1] * value.reshape(rows, value.shape[2])).astype(BF16)
            out[:, at] = value
            act[lane(at), 0:rows, :] = value.astype(F32)

        return body

    over(narrow, 128, into(2, lambda at: act[lane(at), 0:rows, :], h2n, b2))
    greeted(count)
    sums_out[0:8, :] = exchange(count, b2, send2, recv2)
    over(narrow, 128, through(2, 12, 0, h2n, dh2))
    acc[...] = jnp.zeros((rows, narrow), F32)
    for t, (vertical, lateral) in enumerate(OFFSETS):
        shift = -4 * (7 * vertical + lateral)
        other = 8 - t

        def place_back(j, carry, t=t, shift=shift, other=other):
            at = pl.ds(pl.multiple_of(j * 128, 128), 128)
            moved = unrolled_shift(act[j, 0:rows, :], shift)
            hold[:, at] = (pack[:, 1 + other : 2 + other] * moved).astype(BF16)
            return carry

        lax.fori_loop(0, narrow // 128, place_back, 0)

        def gather(at, t=t):
            row = pl.ds(pl.multiple_of(t * narrow + at.start, TILE), TILE)
            acc[:, at] += dot_t(hold[...], k[row, :])

        over(narrow, TILE, gather)
    over(narrow, 128, into(0, lambda at: acc[:, at], h1n, b1))
    sums_out[8:16, :] = exchange(count, b1, send1, recv1)
    over(narrow, 128, through(0, 4, 8, h1n, dh1))


def input_kernel(dh1, dz, w, short, out):
    def body(at):
        out[:, at] = (dot_t(dh1[...], w[at, :]) + dot_t(dz[...], short[at, :])).astype(BF16)

    over(out.shape[1], TILE, body)


def layouts(resolution_ids, order_ids):
    pixels = jnp.arange(MAP * MAP, dtype=jnp.int32)
    row_of = pixels // MAP
    column_of = pixels % MAP
    extent = 5 + resolution_ids[:, None]
    image_mask = ((row_of[None, :] < extent) & (column_of[None, :] < extent)).astype(F32)
    inside = (row_of < 6) & (column_of < 6)
    position = jnp.where(inside, row_of // 2 * 3 + column_of // 2, 0)
    onehot_tile = (position[:, None] == jnp.arange(9)[None, :]).astype(jnp.int32)
    picked = jnp.sum(onehot_tile[None] * order_ids[:, None, :], axis=2)
    row_to = 2 * (picked // 3) + row_of % 2
    column_to = 2 * (picked % 3) + column_of % 2
    target = row_to * MAP + column_to
    tile_mask = (inside & (row_to < extent) & (column_to < extent)).astype(F32)
    return image_mask, tile_mask, jnp.where(inside, target, -1)


def tap_tables(tiled):
    lattice = np.arange(MAP)
    tables = []
    for vertical, lateral in OFFSETS:
        row, column = lattice + vertical, lattice + lateral
        in_row = (row >= 0) & (row < MAP)
        in_column = (column >= 0) & (column < MAP)
        if tiled:
            in_row &= row // 2 == lattice // 2
            in_column &= column // 2 == lattice // 2
        tables.append((in_row[:, None] & in_column[None, :]).reshape(-1))
    return np.stack(tables, axis=1).astype(np.float32)


def mm(a, b, dims="rk,kn->rn"):
    return jnp.einsum(dims, a, b, preferred_element_type=F32)


def core_swap(value):
    count = lax.axis_size("dp")
    return lax.ppermute(value, "dp", [(d, d ^ 1) for d in range(count)])


def from_section(value, source, section):
    out = value[source]
    for t in range(value.shape[0]):
        if t != source:
            got = lax.ppermute(value[t], "segment", [(source, t)])
            out = jnp.where(section == t, got, out)
    return out


def to_section_zero(value):
    sections = lax.axis_size("segment")
    parts = [value] + [lax.ppermute(value, "segment", [(t, 0)]) for t in range(1, sections)]
    return jnp.stack(parts)


def body(
    layer_input,
    output_grad,
    resolution,
    tile_order,
    proj_weight,
    spatial_weight,
    shortcut_weight,
    bn_gain,
    bn_bias,
):
    micro, images, pixels, wide = layer_input.shape
    narrow = proj_weight.shape[2]
    rows = images * pixels
    padded = -(-rows // 16) * 16
    sections = lax.axis_size("segment")
    count = lax.axis_size("dp")
    section = lax.axis_index("segment")
    place = lax.axis_index("dp")
    core = place % 2
    first = section == 0
    proj, spatial, shortcut = proj_weight[0], spatial_weight[0], shortcut_weight[0]
    pick = lambda a: lax.dynamic_index_in_dim(a, section, 0, keepdims=False)

    half_rows = wide // 2
    w1_half = lax.dynamic_slice_in_dim(proj, core * half_rows, half_rows)
    w1_half = from_section(jnp.broadcast_to(w1_half, (sections,) + w1_half.shape), 1, section)
    w1_other = core_swap(w1_half)
    w1 = jnp.where(
        core == 0,
        jnp.concatenate([w1_half, w1_other]),
        jnp.concatenate([w1_other, w1_half]),
    )

    quarter = wide // sections
    own_half = lax.dynamic_slice_in_dim(shortcut, core * half_rows, half_rows)
    short_half = from_section(
        jnp.stack([own_half[:, t * quarter : (t + 1) * quarter] for t in range(sections)]),
        0,
        section,
    )
    short_other = core_swap(short_half)

    slice_rows = wide // count
    tap_rows = spatial.shape[0] // count
    own_proj = lax.dynamic_slice_in_dim(proj, place * slice_rows, slice_rows)
    own_taps = lax.dynamic_slice_in_dim(spatial, place * tap_rows, tap_rows)
    fine = tap_rows // sections
    taps_piece = from_section(own_taps.reshape(sections, fine, narrow), 2, section)
    packed = jnp.concatenate([own_proj, taps_piece])
    everyone = lax.all_gather(packed, ("segment", "dp"), axis=0, tiled=True)
    everyone = everyone.reshape(sections, count, slice_rows + fine, narrow)
    w2 = everyone[2, :, :slice_rows].reshape(wide, narrow)
    w3 = everyone[3, :, :slice_rows].reshape(wide, narrow)
    k2 = jnp.swapaxes(everyone[:, :, slice_rows:], 0, 1).reshape(9 * narrow, narrow)

    gains = lax.all_gather(jnp.concatenate([bn_gain[0], bn_bias[0]]), "segment", axis=0)
    gain, bias = gains[:, :wide], gains[:, wide:]

    image_masks, tile_masks, targets = layouts(
        resolution.reshape(-1), tile_order.reshape(micro * images, -1)
    )
    interleave = lambda a: jnp.transpose(a.reshape(micro, rows), (1, 0)).reshape(rows * micro, 1)
    taps_image = np.tile(np.repeat(tap_tables(False), micro, axis=0), (images, 1))
    pack_all = jnp.concatenate(
        [interleave(image_masks), jnp.asarray(taps_image), jnp.zeros((rows * micro, 6), F32)], axis=1
    )
    tiles_all = interleave(tile_masks)
    pad_rows = lambda a: jnp.pad(a, ((0, padded - rows), (0, 0)))
    image_mask = pad_rows(pick(image_masks.reshape(micro, rows, 1)))
    tile_mask = pad_rows(pick(tile_masks.reshape(micro, rows, 1)))
    taps_tile = np.pad(np.tile(tap_tables(True), (images, 1)), ((0, padded - rows), (0, 6)))
    pack_tile = jnp.concatenate([tile_mask, jnp.asarray(taps_tile)], axis=1)
    target = pick(targets.reshape(micro, images, pixels))
    base = (jnp.arange(images) * pixels)[:, None]
    target = jnp.where(target >= 0, target + base, -1).reshape(rows)
    target = jnp.pad(target, (0, padded - rows), constant_values=-1)
    index = jnp.arange(padded)
    moves = (target[:, None] == index[None, :]).astype(BF16)
    moves_back = (target[None, :] == index[:, None]).astype(BF16)

    x_all = jnp.transpose(layer_input, (1, 2, 0, 3)).reshape(rows * micro, wide)
    gb_first = jnp.stack(
        [bn_gain[0, :narrow], bn_bias[0, :narrow]]
        + [bn_gain[0, narrow : 2 * narrow], bn_bias[0, narrow : 2 * narrow]]
    )
    total = rows * micro
    a2_all, cols_all, h1n_all, h2n_all, stats_all, counts = kernel_call(
        functools.partial(first_kernel, count),
        [
            shape_of((micro, padded, narrow), BF16),
            shape_of((total, 9 * narrow), BF16),
            shape_of((total, narrow), F32),
            shape_of((total, narrow), F32),
            shape_of((16, narrow), F32),
            shape_of((8, 128), F32),
        ],
        [x_all, proj, spatial, gb_first, pack_all, tiles_all],
        [pltpu.VMEM((narrow // 128, 4 * padded, 128), F32)]
        + sync_scratch(count, [(8, narrow + 128), (8, narrow)]),
        0,
        2 * total * narrow * (wide + 9 * narrow),
        40 * 2**20,
    )
    a2 = from_section(a2_all, 0, section)
    [res_quarter] = kernel_call(
        residual_kernel,
        [shape_of((micro, padded, quarter), BF16)],
        [x_all, short_half, short_other],
        [pltpu.VMEM((quarter // 128, 4 * padded, 128), F32)],
        None,
        2 * total * wide * quarter,
        10 * 2**20,
    )
    residual = lax.all_to_all(res_quarter, "segment", 0, 0, tiled=True)

    valid_image = pick(counts[:4])[None]
    valid_tile = pick(counts[4:])[None]
    gb_one = jnp.stack([gain[1], bias[1]])
    y1, u, h3n, stats_three = kernel_call(
        functools.partial(second_kernel, count),
        [
            shape_of((padded, wide), BF16),
            shape_of((padded, wide), BF16),
            shape_of((padded, wide), F32),
            shape_of((2, wide), F32),
        ],
        [a2, w1, residual, image_mask, gb_one, valid_image, moves],
        sync_scratch(count, [(2, wide)]),
        1,
        2 * padded * wide * (narrow + padded),
        10 * 2**20,
    )
    gb_two = jnp.stack(
        [gain[2, :narrow], bias[2, :narrow]]
        + [gain[2, narrow : 2 * narrow], bias[2, narrow : 2 * narrow]]
    )
    gb_three = jnp.stack([gain[3], bias[3]])
    og = jnp.transpose(output_grad, (1, 2, 0, 3)).reshape(rows, micro, wide)
    og = pad_rows(lax.dynamic_index_in_dim(og, section, 1, keepdims=False))
    y2, t_a2, t_cols, t_dh3, t_dh2, t_dh1, dy1, t_sums = kernel_call(
        functools.partial(tile_kernel, count),
        [
            shape_of((padded, wide), BF16),
            shape_of((padded, narrow), BF16),
            shape_of((padded, 9 * narrow), BF16),
            shape_of((padded, wide), BF16),
            shape_of((padded, narrow), BF16),
            shape_of((padded, narrow), BF16),
            shape_of((padded, wide), BF16),
            shape_of((6, wide), F32),
        ],
        [u, w2, k2, w3, og, pack_tile, gb_two, gb_three, valid_tile, moves_back],
        [
            pltpu.VMEM((padded, narrow), F32),
            pltpu.VMEM((padded, narrow), F32),
            pltpu.VMEM((padded, wide), F32),
            pltpu.VMEM((padded, narrow), F32),
            pltpu.VMEM((padded, wide), BF16),
            pltpu.VMEM((6, wide), F32),
        ]
        + sync_scratch(
            count, [(2, narrow), (2, narrow), (2, wide), (2, wide), (2, narrow), (2, narrow)]
        ),
        2,
        4 * padded * narrow * (2 * wide + 9 * narrow),
        30 * 2**20,
    )
    dz, dh3, da2, i_sums = kernel_call(
        functools.partial(image_back_kernel, count),
        [
            shape_of((padded, wide), BF16),
            shape_of((padded, wide), BF16),
            shape_of((padded, narrow), BF16),
            shape_of((2, wide), F32),
        ],
        [dy1, residual, h3n, image_mask, gb_one, stats_three, valid_image, w1],
        sync_scratch(count, [(2, wide)]),
        3,
        2 * padded * narrow * wide,
        12 * 2**20,
    )
    da2_all = to_section_zero(da2)
    dh2_all, dh1_all, f_sums = kernel_call(
        functools.partial(last_kernel, count),
        [
            shape_of((total, narrow), BF16),
            shape_of((total, narrow), BF16),
            shape_of((16, narrow), F32),
        ],
        [da2_all, spatial, gb_first, pack_all, h1n_all, h2n_all, stats_all, counts],
        [
            pltpu.VMEM((narrow // 128, 4 * padded, 128), F32),
            pltpu.VMEM((total, narrow), F32),
            pltpu.VMEM((total, narrow), BF16),
        ]
        + sync_scratch(count, [(8, narrow), (8, narrow)]),
        4,
        2 * total * narrow * 9 * narrow,
        20 * 2**20,
    )
    weave = lambda a: jnp.swapaxes(a[:, :rows], 0, 1).reshape(total, a.shape[2])
    dz_all = weave(to_section_zero(dz))
    dz_quarter = weave(
        lax.all_to_all(dz.reshape(padded, sections, quarter), "segment", 1, 0, tiled=True).reshape(
            micro, padded, quarter
        )
    )
    [grad_input] = kernel_call(
        input_kernel,
        [shape_of((total, wide), BF16)],
        [dh1_all, dz_all, proj, shortcut],
        [],
        None,
        2 * total * wide * (wide + narrow),
        30 * 2**20,
    )

    proj_term_3 = mm(t_dh3, t_a2, "rd,rk->dk")
    taps_term_2 = mm(t_cols, t_dh2, "rk,rn->kn")
    proj_term_2 = mm(u, t_dh1, "rc,rn->cn")
    proj_term_1 = mm(dh3, a2, "rd,rk->dk")
    short_term = mm(x_all, dz_quarter, "rc,rd->cd")
    taps_term_0 = mm(cols_all, dh2_all, "rk,rn->kn")
    proj_term_0 = mm(x_all, dh1_all, "rc,rn->cn")

    exchanged = lax.all_to_all(jnp.stack([y1, y1, dy1, y2]), "segment", 0, 0)
    exchanged = jnp.swapaxes(exchanged[:, :rows], 0, 1)
    maps = jnp.where(first, grad_input.reshape(rows, micro, wide), exchanged)
    maps = jnp.transpose(maps.reshape(images, pixels, micro, wide), (2, 0, 1, 3))

    blank = jnp.zeros((wide,), F32)
    pad = jnp.zeros((wide - 2 * narrow,), F32)
    of_batches = lambda at: jnp.sum(f_sums[at : at + 4], axis=0)
    zero_gain = jnp.where(first, jnp.concatenate([of_batches(12), of_batches(4), pad]), blank)
    zero_bias = jnp.where(first, jnp.concatenate([of_batches(8), of_batches(0), pad]), blank)
    vectors = jnp.stack(
        [
            zero_gain,
            zero_bias,
            i_sums[1],
            i_sums[0],
            jnp.concatenate([t_sums[5, :narrow], t_sums[3, :narrow], pad]),
            jnp.concatenate([t_sums[4, :narrow], t_sums[2, :narrow], pad]),
            t_sums[1],
            t_sums[0],
        ]
    )
    vectors = pick(lax.psum(vectors, "segment").reshape(sections, 2, wide))

    groups = [[d for d in range(count) if d % 2 == c] for c in range(2)]
    depth = count // 2

    def halved(term):
        rows_half = term.shape[0] // 2
        mine = lax.dynamic_slice_in_dim(term, core * rows_half, rows_half)
        theirs = lax.dynamic_slice_in_dim(term, (1 - core) * rows_half, rows_half)
        return (mine + core_swap(theirs.astype(BF16)).astype(F32)).astype(BF16)

    def planar(terms):
        part = jnp.concatenate(
            [a.reshape(sections, a.shape[0] // sections, narrow) for a in terms], axis=1
        )
        part = lax.all_to_all(part, "segment", 0, 0)
        return jnp.sum(part.astype(F32), axis=0).astype(BF16)

    def over_z(joined):
        shape = joined.shape
        part = joined.reshape(depth, shape[0] // depth, narrow)
        part = lax.psum_scatter(
            part, "dp", scatter_dimension=0, tiled=False, axis_index_groups=groups
        )
        return lax.all_gather(part, "dp", axis=0, axis_index_groups=groups, tiled=True).reshape(shape)

    hp, ht = wide // 8, 9 * narrow // 8
    early = over_z(
        planar([halved(proj_term_1), halved(proj_term_2), halved(taps_term_2), halved(proj_term_3)])
    )
    early_of = {
        1: jnp.pad(early[:hp], ((0, ht), (0, 0))),
        2: early[hp : 2 * hp + ht],
        3: jnp.pad(early[2 * hp + ht :], ((0, ht), (0, 0))),
    }
    keep = jnp.stack([early_of[1], early_of[1], early_of[2], early_of[3]])
    early_parts = lax.all_to_all(keep, "segment", 0, 0)

    scattered = from_section(
        jnp.concatenate(
            [
                halved(a).reshape(sections, a.shape[0] // 2 // sections, narrow)
                for a in (proj_term_0, taps_term_0)
            ],
            axis=1,
        ),
        0,
        section,
    )
    late = over_z(jnp.concatenate([scattered, halved(short_term)]))
    late_parts = to_section_zero(late)

    parts = jnp.where(first, late_parts[:, : hp + ht], early_parts)
    other = core_swap(parts)
    both = jnp.where(core == 0, jnp.stack([parts, other]), jnp.stack([other, parts]))
    short_parts = late_parts[:, hp + ht :]
    short_swap = core_swap(short_parts)
    short_both = jnp.where(
        core == 0, jnp.stack([short_parts, short_swap]), jnp.stack([short_swap, short_parts])
    )
    short_both = jnp.where(first, short_both, jnp.zeros_like(short_both))
    proj_grad = both[:, :, :hp].reshape(wide, narrow).astype(F32)
    spatial_grad = both[:, :, hp:].reshape(9 * narrow, narrow).astype(F32)
    has_taps = (section % 2) == 0
    spatial_grad = jnp.where(has_taps, spatial_grad, jnp.zeros_like(spatial_grad))
    short_grad = jnp.swapaxes(short_both, 1, 2).reshape(wide, wide).astype(F32)
    return (
        maps[None],
        proj_grad[None],
        spatial_grad[None],
        short_grad[None],
        vectors[:1],
        vectors[1:],
    )


def solution(mesh):
    return jax.shard_map(
        body,
        mesh=mesh,
        in_specs=(
            P(None, "dp", None, None),
            P(None, "dp", None, None),
            P(None, "dp"),
            P(None, "dp", None),
            P("segment", None, None),
            P("segment", None, None),
            P("segment", None, None),
            P("segment", None),
            P("segment", None),
        ),
        out_specs=(
            P("segment", None, "dp", None, None),
            P("segment", None, None),
            P("segment", None, None),
            P("segment", None, None),
            P("segment", None),
            P("segment", None),
        ),
        check_vma=False,
    )
```

```python
import functools

import jax
import jax.numpy as jnp
import numpy as np
from jax import lax
from jax.experimental import pallas as pl
from jax.experimental.pallas import tpu as pltpu
from jax.sharding import PartitionSpec as P

MAP = 7
EPSILON = 1e-05
OFFSETS = ((-1, -1), (-1, 0), (-1, 1), (0, -1), (0, 0), (0, 1), (1, -1), (1, 0), (1, 1))
MESH = pl.DeviceIdType.MESH
F32 = jnp.float32
BF16 = jnp.bfloat16
VMEM_BYTES = 58 * 2**20
TILE = 256


def greet(count):
    segment, me = lax.axis_index("segment"), lax.axis_index("dp")
    barrier = pltpu.get_barrier_semaphore()

    def one(k, carry):
        pl.semaphore_signal(
            barrier, inc=1, device_id=(segment, lax.rem(me + k, count)), device_id_type=MESH
        )
        return carry

    lax.fori_loop(1, count, one, 0)


def greeted(count):
    pl.semaphore_wait(pltpu.get_barrier_semaphore(), count - 1)


def exchange(count, slots, send_sem, recv_sem):
    segment, me = lax.axis_index("segment"), lax.axis_index("dp")

    def copy(k):
        return pltpu.make_async_remote_copy(
            src_ref=slots.at[me],
            dst_ref=slots.at[me],
            send_sem=send_sem.at[k],
            recv_sem=recv_sem.at[k],
            device_id=(segment, lax.rem(me + k, count)),
            device_id_type=MESH,
        )

    def start(k, carry):
        copy(k).start()
        return carry

    def finish(k, carry):
        copy(k).wait_recv()
        copy(k).wait_send()
        return carry

    lax.fori_loop(1, count, start, 0)
    lax.fori_loop(1, count, finish, 0)
    total = slots[0]
    for k in range(1, count):
        total = total + slots[k]
    return total


def sync_scratch(count, shapes):
    out = []
    for shape in shapes:
        out += [
            pltpu.VMEM((count,) + shape, F32),
            pltpu.SemaphoreType.DMA((count,)),
            pltpu.SemaphoreType.DMA((count,)),
        ]
    return out


def kernel_call(kernel, outs, args, scratch, ident, flops, moved, spaces=None):
    params = dict(has_side_effects=True, vmem_limit_bytes=VMEM_BYTES)
    if ident is not None:
        params["collective_id"] = ident
    return pl.pallas_call(
        kernel,
        out_shape=outs,
        in_specs=[pl.BlockSpec(memory_space=pltpu.VMEM) for _ in args],
        out_specs=[pl.BlockSpec(memory_space=pltpu.VMEM) for _ in outs],
        scratch_shapes=scratch,
        compiler_params=pltpu.CompilerParams(**params),
        cost_estimate=pl.CostEstimate(flops=flops, bytes_accessed=moved, transcendentals=0),
    )(*args)


def shape_of(shape, dtype):
    return jax.ShapeDtypeStruct(shape, dtype)


def dot(a, b):
    return jnp.dot(a, b, preferred_element_type=F32)


def dot_t(a, b):
    return lax.dot_general(a, b, (((1,), (1,)), ((), ())), preferred_element_type=F32)


def sigmoid(v):
    return 1.0 / (1.0 + jnp.exp(-v))


def slope(v):
    s = sigmoid(v)
    return s * (1.0 + v * (1.0 - s))


def over(width, step, body):
    def one(j, carry):
        body(pl.ds(pl.multiple_of(j * step, step), step))
        return carry

    lax.fori_loop(0, width // step, one, 0)


def lane(at):
    return lax.div(at.start, 128)


def unrolled_shift(ref_value, shift):
    rows = ref_value.shape[0]
    return ref_value if shift % rows == 0 else pltpu.roll(ref_value, (-shift) % rows, 0)


def by_batch(values):
    rows, width = values.shape
    part = jnp.sum(values.reshape(rows // 8, 8, width), axis=0)
    return part[:4] + part[4:]


def spread8(values):
    return jnp.concatenate([values, values], axis=0)[None]


def first_kernel(
    count, x, w, k, gb, pack, tiles, a2_out, cols, h1n, h2n, stats_out, count_out, act, *sync
):
    s1, send1, recv1, s2, send2, recv2 = sync
    rows, narrow = h1n.shape
    me = lax.axis_index("dp")
    greet(count)
    full = act.shape[1]

    def tile8(v):
        return v.reshape(rows // 8, 8, v.shape[1])

    def project(at):
        h = dot(x[...], w[:, at])
        h1n[:, at] = h
        m = pack[:, 0:1] * h
        s1[me, 0:4, at] = by_batch(m)
        s1[me, 4:8, at] = by_batch(m * h)

    over(narrow, TILE, project)
    s1[me, 0:4, narrow:] = jnp.broadcast_to(by_batch(pack[:, 0:1]), (4, 128))
    s1[me, 4:8, narrow:] = jnp.broadcast_to(by_batch(tiles[:, 0:1]), (4, 128))
    greeted(count)
    total = exchange(count, s1, send1, recv1)
    counts = total[:, narrow:]
    count_out[...] = counts
    valid = counts[0:4, 0:1]
    average = total[0:4, :narrow] / valid
    inverse = lax.rsqrt(total[4:8, :narrow] / valid - average * average + EPSILON)
    stats_out[0:4, :] = average
    stats_out[4:8, :] = inverse

    def activate(stat_at, gain_at, source):
        def body(at):
            mean = spread8(stats_out[stat_at : stat_at + 4, at])
            inv = spread8(stats_out[stat_at + 4 : stat_at + 8, at])
            hn = (tile8(source[:, at]) - mean) * inv
            source[:, at] = hn.reshape(rows, hn.shape[2])
            n = gb[gain_at : gain_at + 1, at][None] * hn + gb[gain_at + 1 : gain_at + 2, at][None]
            n = n.reshape(rows, n.shape[2])
            act[lane(at), 0:rows, :] = pack[:, 0:1] * (n * sigmoid(n))

        return body

    over(narrow, 128, activate(0, 0, h1n))

    for t, (vertical, lateral) in enumerate(OFFSETS):
        shift = 4 * (7 * vertical + lateral)

        def place(j, carry, t=t, shift=shift):
            at = pl.ds(pl.multiple_of(j * 128, 128), 128)
            to = pl.ds(pl.multiple_of(t * narrow + j * 128, 128), 128)
            moved = unrolled_shift(act[j, 0:rows, :], shift)
            cols[:, to] = (pack[:, 1 + t : 2 + t] * moved).astype(BF16)
            return carry

        lax.fori_loop(0, narrow // 128, place, 0)

    def convolve(at):
        h = dot(cols[...], k[:, at])
        h2n[:, at] = h
        m = pack[:, 0:1] * h
        s2[me, 0:4, at] = by_batch(m)
        s2[me, 4:8, at] = by_batch(m * h)

    over(narrow, TILE, convolve)
    total = exchange(count, s2, send2, recv2)
    average = total[0:4] / valid
    stats_out[8:12, :] = average
    stats_out[12:16, :] = lax.rsqrt(total[4:8] / valid - average * average + EPSILON)
    over(narrow, 128, activate(8, 2, h2n))
    act[:, rows:, :] = jnp.zeros((narrow // 128, full - rows, 128), F32)
    for m in range(4):

        def pick(j, carry, m=m):
            at = pl.ds(pl.multiple_of(j * 128, 128), 128)
            a2_out[m, :, at] = act[j, pl.ds(m, full // 4, stride=4), :].astype(BF16)
            return carry

        lax.fori_loop(0, narrow // 128, pick, 0)


def residual_kernel(x, wa, wb, out, hold):
    rows, depth = x.shape[0], wa.shape[0]
    full, quarter = hold.shape[1], out.shape[2]
    core = lax.rem(lax.axis_index("dp"), 2)
    first = pl.ds(pl.multiple_of(core * depth, depth), depth)
    second = pl.ds(pl.multiple_of((1 - core) * depth, depth), depth)
    hold[:, rows:, :] = jnp.zeros((quarter // 128, full - rows, 128), F32)

    def body(at):
        value = dot(x[:, first], wa[:, at]) + dot(x[:, second], wb[:, at])
        for part in range(TILE // 128):
            hold[lane(at) + part, 0:rows, :] = value[:, part * 128 : part * 128 + 128]

    over(quarter, TILE, body)
    for m in range(4):

        def pick(j, carry, m=m):
            at = pl.ds(pl.multiple_of(j * 128, 128), 128)
            out[m, :, at] = hold[j, pl.ds(m, full // 4, stride=4), :].astype(BF16)
            return carry

        lax.fori_loop(0, quarter // 128, pick, 0)


def norm_sums(slots, me, at, masked, h):
    slots[me, 0:1, at] = jnp.sum(masked, axis=0, keepdims=True)
    slots[me, 1:2, at] = jnp.sum(masked * h, axis=0, keepdims=True)


def finish_stats(total, valid, stats_out, at_row):
    average = total[0:1] / valid
    width = average.shape[1]
    stats_out[at_row : at_row + 1, 0:width] = average
    stats_out[at_row + 1 : at_row + 2, 0:width] = lax.rsqrt(
        total[1:2] / valid - average * average + EPSILON
    )


def second_kernel(
    count, a2, w1, res, pack, gb, valid_in, moves, y_out, u_out, h3n, stats_out, s1, send1, recv1
):
    wide = h3n.shape[1]
    quarter = res.shape[2]
    me = lax.axis_index("dp")
    greet(count)

    def project(at):
        h = dot_t(a2[...], w1[at, :])
        h3n[:, at] = h
        norm_sums(s1, me, at, pack[:, 0:1] * h, h)

    over(wide, TILE, project)
    greeted(count)
    valid = valid_in[0:1, 0:1]
    finish_stats(exchange(count, s1, send1, recv1), valid, stats_out, 0)
    for q in range(wide // quarter):

        def body(j, carry, q=q):
            at = pl.ds(pl.multiple_of(q * quarter + j * 128, 128), 128)
            own = pl.ds(pl.multiple_of(j * 128, 128), 128)
            hn = (h3n[:, at] - stats_out[0:1, at]) * stats_out[1:2, at]
            h3n[:, at] = hn
            z = gb[0:1, at] * hn + gb[1:2, at] + res[q, :, own].astype(F32)
            y_out[:, at] = (pack[:, 0:1] * (z * sigmoid(z))).astype(BF16)
            return carry

        lax.fori_loop(0, quarter // 128, body, 0)

    def permute(at):
        u_out[:, at] = dot(moves[...], y_out[:, at]).astype(BF16)

    over(wide, TILE, permute)


def back_sums(slots, me, at, grad, hn):
    slots[me, 0:1, at] = jnp.sum(grad, axis=0, keepdims=True)
    slots[me, 1:2, at] = jnp.sum(grad * hn, axis=0, keepdims=True)


def tile_kernel(
    count,
    u,
    w2,
    k2,
    w3,
    og,
    pack,
    gb2,
    gb3,
    valid_in,
    back,
    y_out,
    a2,
    cols,
    dh3,
    dh2,
    dh1,
    dy,
    sums_out,
    h1n,
    h2n,
    h3n,
    act,
    dz,
    stats,
    *sync,
):
    s1, send1, recv1, s2, send2, recv2, s3, send3, recv3 = sync[:9]
    b3, bsend3, brecv3, b2, bsend2, brecv2, b1, bsend1, brecv1 = sync[9:]
    rows, wide = u.shape
    narrow = h1n.shape[1]
    me = lax.axis_index("dp")
    valid = valid_in[0:1, 0:1]
    greet(count)

    def project(at):
        h = dot(u[...], w2[:, at])
        h1n[:, at] = h
        norm_sums(s1, me, at, pack[:, 0:1] * h, h)

    over(narrow, TILE, project)
    greeted(count)
    finish_stats(exchange(count, s1, send1, recv1), valid, stats, 0)

    def activate(row, gain, source, store):
        def body(at):
            hn = (source[:, at] - stats[row : row + 1, at]) * stats[row + 1 : row + 2, at]
            source[:, at] = hn
            n = gb2[gain : gain + 1, at] * hn + gb2[gain + 1 : gain + 2, at]
            store(at, pack[:, 0:1] * (n * sigmoid(n)))

        return body

    def to_act(at, value):
        act[:, at] = value

    def to_a2(at, value):
        a2[:, at] = value.astype(BF16)

    over(narrow, 128, activate(0, 0, h1n, to_act))
    for t, (vertical, lateral) in enumerate(OFFSETS):
        shift = 7 * vertical + lateral

        def place(j, carry, t=t, shift=shift):
            at = pl.ds(pl.multiple_of(j * 128, 128), 128)
            to = pl.ds(pl.multiple_of(t * narrow + j * 128, 128), 128)
            moved = unrolled_shift(act[:, at], shift)
            cols[:, to] = (pack[:, 1 + t : 2 + t] * moved).astype(BF16)
            return carry

        lax.fori_loop(0, narrow // 128, place, 0)

    def convolve(at):
        h = dot(cols[...], k2[:, at])
        h2n[:, at] = h
        norm_sums(s2, me, at, pack[:, 0:1] * h, h)

    over(narrow, TILE, convolve)
    finish_stats(exchange(count, s2, send2, recv2), valid, stats, 2)
    over(narrow, 128, activate(2, 2, h2n, to_a2))

    def expand(at):
        h = dot_t(a2[...], w3[at, :])
        h3n[:, at] = h
        norm_sums(s3, me, at, pack[:, 0:1] * h, h)

    over(wide, TILE, expand)
    finish_stats(exchange(count, s3, send3, recv3), valid, stats, 4)

    def result(at):
        hn = (h3n[:, at] - stats[4:5, at]) * stats[5:6, at]
        h3n[:, at] = hn
        z = gb3[0:1, at] * hn + gb3[1:2, at] + u[:, at].astype(F32)
        s = sigmoid(z)
        m = pack[:, 0:1]
        y_out[:, at] = (m * (z * s)).astype(BF16)
        grad = (og[:, at].astype(F32) * m * (s * (1.0 + z * (1.0 - s)))).astype(BF16)
        dz[:, at] = grad
        grad = grad.astype(F32)
        back_sums(b3, me, at, grad, hn)

    over(wide, 128, result)
    total = exchange(count, b3, bsend3, brecv3)
    sums_out[0:2, :] = total

    def through(at):
        offset, scale = sums_out[0:1, at], sums_out[1:2, at]
        dh3[:, at] = (
            pack[:, 0:1]
            * gb3[0:1, at]
            * stats[5:6, at]
            * (dz[:, at].astype(F32) - (offset + h3n[:, at] * scale) / valid)
        ).astype(BF16)

    over(wide, 128, through)

    def into_two(at):
        grad = dot(dh3[...], w3[:, at]).astype(BF16).astype(F32)
        hn = h2n[:, at]
        n = gb2[2:3, at] * hn + gb2[3:4, at]
        grad = grad * pack[:, 0:1] * slope(n)
        act[:, at] = grad
        back_sums(b2, me, at, grad, hn)

    over(narrow, TILE, into_two)
    total = exchange(count, b2, bsend2, brecv2)
    sums_out[2:4, 0:narrow] = total

    def through_two(at):
        offset, scale = sums_out[2:3, at], sums_out[3:4, at]
        grad = (
            pack[:, 0:1]
            * gb2[2:3, at]
            * stats[3:4, at]
            * (act[:, at] - (offset + h2n[:, at] * scale) / valid)
        )
        dh2[:, at] = grad.astype(BF16)
        act[:, at] = dh2[:, at].astype(F32)

    over(narrow, 128, through_two)
    h2n[...] = jnp.zeros((rows, narrow), F32)
    for t, (vertical, lateral) in enumerate(OFFSETS):
        shift = -(7 * vertical + lateral)
        other = 8 - t

        def place_back(j, carry, t=t, shift=shift, other=other):
            at = pl.ds(pl.multiple_of(j * 128, 128), 128)
            moved = unrolled_shift(act[:, at], shift)
            dy[:, at] = (pack[:, 1 + other : 2 + other] * moved).astype(BF16)
            return carry

        lax.fori_loop(0, narrow // 128, place_back, 0)

        def gather(at, t=t):
            row = pl.ds(pl.multiple_of(t * narrow + at.start, TILE), TILE)
            h2n[:, at] += dot_t(dy[:, 0:narrow], k2[row, :])

        over(narrow, TILE, gather)

    def into_one(at):
        hn = h1n[:, at]
        n = gb2[0:1, at] * hn + gb2[1:2, at]
        grad = h2n[:, at] * pack[:, 0:1] * slope(n)
        act[:, at] = grad
        back_sums(b1, me, at, grad, hn)

    over(narrow, 128, into_one)
    total = exchange(count, b1, bsend1, brecv1)
    sums_out[4:6, 0:narrow] = total

    def through_one(at):
        offset, scale = sums_out[4:5, at], sums_out[5:6, at]
        dh1[:, at] = (
            pack[:, 0:1]
            * gb2[0:1, at]
            * stats[1:2, at]
            * (act[:, at] - (offset + h1n[:, at] * scale) / valid)
        ).astype(BF16)

    over(narrow, 128, through_one)

    def into_input(at):
        grad = dot_t(dh1[...], w2[at, :]) + dz[:, at].astype(F32)
        dy[:, at] = dot(back[...], grad.astype(BF16)).astype(BF16)

    over(wide, TILE, into_input)


def image_back_kernel(
    count, dy, res, h3n, pack, gb, stats, valid_in, w1, dz, dh3, da2, sums_out, b3, send3, recv3
):
    wide = dy.shape[1]
    quarter = res.shape[2]
    narrow = da2.shape[1]
    me = lax.axis_index("dp")
    valid = valid_in[0:1, 0:1]
    greet(count)
    for q in range(wide // quarter):

        def body(j, carry, q=q):
            at = pl.ds(pl.multiple_of(q * quarter + j * 128, 128), 128)
            own = pl.ds(pl.multiple_of(j * 128, 128), 128)
            hn = h3n[:, at]
            z = gb[0:1, at] * hn + gb[1:2, at] + res[q, :, own].astype(F32)
            grad = (dy[:, at].astype(F32) * pack[:, 0:1] * slope(z)).astype(BF16)
            dz[:, at] = grad
            back_sums(b3, me, at, grad.astype(F32), hn)
            return carry

        lax.fori_loop(0, quarter // 128, body, 0)
    greeted(count)
    total = exchange(count, b3, send3, recv3)
    sums_out[...] = total

    def through(at):
        offset, scale = sums_out[0:1, at], sums_out[1:2, at]
        dh3[:, at] = (
            pack[:, 0:1]
            * gb[0:1, at]
            * stats[1:2, at]
            * (dz[:, at].astype(F32) - (offset + h3n[:, at] * scale) / valid)
        ).astype(BF16)

    over(wide, 128, through)

    def into(at):
        da2[:, at] = dot(dh3[...], w1[:, at]).astype(BF16)

    over(narrow, TILE, into)


def last_kernel(
    count, da2, k, gb, pack, h1n, h2n, stats, counts, dh2, dh1, sums_out, act, acc, hold, *sync
):
    b2, send2, recv2, b1, send1, recv1 = sync
    rows, narrow = h1n.shape
    full = act.shape[1]
    me = lax.axis_index("dp")
    greet(count)
    valid = counts[0:4, 0:1]

    def tile8(v):
        return v.reshape(rows // 8, 8, v.shape[1])

    for m in range(4):

        def put(j, carry, m=m):
            at = pl.ds(pl.multiple_of(j * 128, 128), 128)
            act[j, pl.ds(m, full // 4, stride=4), :] = da2[m, :, at].astype(F32)
            return carry

        lax.fori_loop(0, narrow // 128, put, 0)

    def into(gain, source, hidden, slots):
        def body(at):
            hn = hidden[:, at]
            n = gb[gain : gain + 1, at] * hn + gb[gain + 1 : gain + 2, at]
            grad = source(at) * pack[:, 0:1] * slope(n)
            act[lane(at), 0:rows, :] = grad
            slots[me, 0:4, at] = by_batch(grad)
            slots[me, 4:8, at] = by_batch(grad * hn)

        return body

    def through(gain, stat_at, row, hidden, out):
        def body(at):
            offset = spread8(sums_out[row : row + 4, at] / valid)
            scale = spread8(sums_out[row + 4 : row + 8, at] / valid)
            inv = spread8(stats[stat_at : stat_at + 4, at])
            g = tile8(act[lane(at), 0:rows, :])
            value = inv * gb[gain : gain + 1, at][None] * (g - (offset + tile8(hidden[:, at]) * scale))
            value = (pack[:, 0:1] * value.reshape(rows, value.shape[2])).astype(BF16)
            out[:, at] = value
            act[lane(at), 0:rows, :] = value.astype(F32)

        return body

    over(narrow, 128, into(2, lambda at: act[lane(at), 0:rows, :], h2n, b2))
    greeted(count)
    sums_out[0:8, :] = exchange(count, b2, send2, recv2)
    over(narrow, 128, through(2, 12, 0, h2n, dh2))
    acc[...] = jnp.zeros((rows, narrow), F32)
    for t, (vertical, lateral) in enumerate(OFFSETS):
        shift = -4 * (7 * vertical + lateral)
        other = 8 - t

        def place_back(j, carry, t=t, shift=shift, other=other):
            at = pl.ds(pl.multiple_of(j * 128, 128), 128)
            moved = unrolled_shift(act[j, 0:rows, :], shift)
            hold[:, at] = (pack[:, 1 + other : 2 + other] * moved).astype(BF16)
            return carry

        lax.fori_loop(0, narrow // 128, place_back, 0)

        def gather(at, t=t):
            row = pl.ds(pl.multiple_of(t * narrow + at.start, TILE), TILE)
            acc[:, at] += dot_t(hold[...], k[row, :])

        over(narrow, TILE, gather)
    over(narrow, 128, into(0, lambda at: acc[:, at], h1n, b1))
    sums_out[8:16, :] = exchange(count, b1, send1, recv1)
    over(narrow, 128, through(0, 4, 8, h1n, dh1))


def input_kernel(dh1, dz, w, short, out):
    def body(at):
        out[:, at] = (dot_t(dh1[...], w[at, :]) + dot_t(dz[...], short[at, :])).astype(BF16)

    over(out.shape[1], TILE, body)


def mesh_copy(src, dst, send_sem, recv_sem, segment, place):
    return pltpu.make_async_remote_copy(
        src_ref=src,
        dst_ref=dst,
        send_sem=send_sem,
        recv_sem=recv_sem,
        device_id=(segment, place),
        device_id_type=MESH,
    )


def loop(low, high, body):
    def one(k, carry):
        body(k)
        return carry

    lax.fori_loop(low, high, one, 0)


SUMS = (("k2", 2, True), ("p3", 3, True), ("p2", 2, True), ("p1", 1, True), ("k0", 0, False), ("p0", 0, False))


def gradient_kernel(
    sections, count, sh, k2, p3, p2, p1, k0, p0, vec, sh_out, p_out, k_out, vec_out, *scratch
):
    names = [name for name, _, _ in SUMS]
    terms = dict(zip(names, (k2, p3, p2, p1, k0, p0)))
    owner = {name: section for name, section, _ in SUMS}
    spread = {name: part for name, _, part in SUMS}
    depth = count // 2
    me, place = lax.axis_index("segment"), lax.axis_index("dp")
    core, z = lax.rem(place, 2), lax.div(place, 2)
    sibling = place + 1 - 2 * core
    scratch = list(scratch)
    take = lambda: scratch.pop(0)
    half, theirs, planes, total, others, whole = {}, {}, {}, {}, {}, {}
    for name in names:
        half[name], theirs[name] = take(), take()
        if spread[name]:
            planes[name] = take()
        total[name], others[name], whole[name] = take(), take(), take()
    sh_half, sh_theirs, sh_others, sh_whole, vec_slots = take(), take(), take(), take(), take()
    load_sem, a_send, a_recv, b_send, b_recv, c_send, c_recv, d_send, d_recv = (take() for _ in range(9))
    e_send, e_recv, e_own, f_send, f_recv, v_send, v_recv = (take() for _ in range(7))
    slot = {name: i for i, name in enumerate(names)}
    last = len(names)

    def chip(k):
        return 2 * lax.rem(z + k, depth) + core

    barrier = pltpu.get_barrier_semaphore()
    pl.semaphore_signal(barrier, inc=1, device_id=(me, sibling), device_id_type=MESH)
    for k in range(1, sections):
        pl.semaphore_signal(
            barrier, inc=1, device_id=(jnp.bitwise_xor(me, k), place), device_id_type=MESH
        )
    loop(
        1,
        depth,
        lambda k: pl.semaphore_signal(
            barrier, inc=1, device_id=(me, chip(k)), device_id_type=MESH
        ),
    )
    pl.semaphore_wait(barrier, 1 + sections - 1 + depth - 1)

    def swap(name):
        return mesh_copy(
            terms[name].at[1 - core],
            theirs[name],
            a_send.at[slot[name]],
            a_recv.at[slot[name]],
            me,
            sibling,
        )

    def load(name):
        return pltpu.make_async_copy(terms[name].at[core], half[name], load_sem.at[slot[name]])

    def when_held(name, body):
        if spread[name]:
            body()
        else:
            pl.when(me == owner[name])(body)

    sh_rows = sh_half.shape[0]
    sh_swap = mesh_copy(
        sh.at[1 - core], sh_theirs, a_send.at[last], a_recv.at[last], me, sibling
    )
    sh_load = pltpu.make_async_copy(sh.at[core], sh_half, load_sem.at[last])
    sh_swap.start()
    sh_load.start()

    def vec_copy(k):
        other = jnp.bitwise_xor(me, k)
        return mesh_copy(
            vec.at[other], vec_slots.at[k], v_send.at[k], v_recv.at[k], other, place
        )

    for k in range(1, sections):
        vec_copy(k).start()
    for name in names:

        def begin(name=name):
            swap(name).start()
            load(name).start()

        when_held(name, begin)

    piece = sh_rows // depth
    step = 32

    def sh_at(i):
        return pl.ds(pl.multiple_of(i * piece, 16), piece)

    def sh_send(k):
        to = lax.rem(z + k, depth)
        return mesh_copy(
            sh_half.at[sh_at(to)],
            sh_others.at[k],
            c_send.at[last, k],
            c_recv.at[last, k],
            me,
            2 * to + core,
        )

    sh_load.wait()
    sh_swap.wait_recv()

    def sh_add(i):
        at = pl.ds(pl.multiple_of(i * step, step), step)
        sh_half[at, :] = (sh_half[at, :].astype(F32) + sh_theirs[at, :].astype(F32)).astype(BF16)

    loop(0, sh_rows // step, sh_add)
    loop(1, depth, lambda k: sh_send(k).start())

    def to_section(name, k):
        other = jnp.bitwise_xor(me, k)
        target = planes[name].at[k] if spread[name] else total[name]
        return mesh_copy(
            half[name].at[other],
            target,
            b_send.at[slot[name], k],
            b_recv.at[slot[name], k],
            other,
            place,
        )

    for name in names:

        def combine(name=name):
            load(name).wait()
            swap(name).wait_recv()

            def add(i):
                q, y = lax.div(i, depth), lax.rem(i, depth)
                half[name][q, y] = (
                    half[name][q, y].astype(F32) + theirs[name][q, y].astype(F32)
                ).astype(BF16)

            loop(0, sections * depth, add)
            for k in range(1, sections):
                to_section(name, k).start()

        when_held(name, combine)

    loop(1, depth, lambda k: sh_send(k).wait_recv())
    mine = sh_at(z)
    acc = sh_half[mine, :].astype(F32)
    for k in range(1, depth):
        acc = acc + sh_others[k].astype(F32)
    sh_whole[mine, :] = acc.astype(BF16)

    def sh_share(k):
        return mesh_copy(
            sh_whole.at[mine],
            sh_whole.at[mine],
            d_send.at[last, k],
            d_recv.at[last, k],
            me,
            chip(k),
        )

    loop(1, depth, lambda k: sh_share(k).start())

    def to_chip(name, k):
        to = lax.rem(z + k, depth)
        return mesh_copy(
            total[name].at[to],
            others[name].at[k],
            c_send.at[slot[name], k],
            c_recv.at[slot[name], k],
            me,
            2 * to + core,
        )

    for name in names:
        if spread[name]:
            for k in range(1, sections):
                to_section(name, k).wait_recv()

            def plane_add(y, name=name):
                acc = half[name][me, y].astype(F32)
                for k in range(1, sections):
                    acc = acc + planes[name][k, y].astype(F32)
                total[name][y] = acc.astype(BF16)

            loop(0, depth, plane_add)
        else:

            @pl.when(me == owner[name])
            def _(name=name):
                def keep(y):
                    total[name][y] = half[name][owner[name], y]

                loop(0, depth, keep)

            for k in range(1, sections):

                @pl.when(me == owner[name] ^ k)
                def _(name=name, k=k):
                    to_section(name, k).wait_recv()

        loop(1, depth, lambda k, name=name: to_chip(name, k).start())

    def sh_deliver(k):
        at = pl.ds(pl.multiple_of(me * sh_whole.shape[1], 128), sh_whole.shape[1])
        return mesh_copy(
            sh_whole,
            sh_out.at[core, :, at],
            e_send.at[last],
            e_recv.at[last, k],
            0,
            place,
        )

    loop(1, depth, lambda k: sh_share(k).wait_recv())
    at_zero = pl.ds(0, sh_whole.shape[1])
    sh_keep = pltpu.make_async_copy(sh_whole, sh_out.at[core, :, at_zero], e_own.at[last])

    @pl.when(me == 0)
    def _():
        sh_keep.start()

    for k in range(1, sections):

        @pl.when(me == k)
        def _(k=k):
            sh_deliver(k).start()

    def share(name, k):
        return mesh_copy(
            whole[name].at[z],
            whole[name].at[z],
            d_send.at[slot[name], k],
            d_recv.at[slot[name], k],
            me,
            chip(k),
        )

    for name in names:
        loop(1, depth, lambda k, name=name: to_chip(name, k).wait_recv())
        acc = total[name][z].astype(F32)
        for k in range(1, depth):
            acc = acc + others[name][k].astype(F32)
        whole[name][z] = acc.astype(BF16)
        loop(1, depth, lambda k, name=name: share(name, k).start())

    def final(name):
        return k_out if name[0] == "k" else p_out

    def deliver(name, k):
        return mesh_copy(
            whole[name],
            final(name).at[core, me],
            e_send.at[slot[name]],
            e_recv.at[slot[name], k],
            owner[name],
            place,
        )

    def keep_own(name):
        return pltpu.make_async_copy(whole[name], final(name).at[core, me], e_own.at[slot[name]])

    for name in names:
        loop(1, depth, lambda k, name=name: share(name, k).wait_recv())

        @pl.when(me == owner[name])
        def _(name=name):
            keep_own(name).start()

        for k in range(1, sections):

            @pl.when(me == owner[name] ^ k)
            def _(name=name, k=k):
                deliver(name, k).start()

    def cross(name):
        return mesh_copy(
            final(name).at[core],
            final(name).at[core],
            f_send.at[slot[name]],
            f_recv.at[slot[name]],
            me,
            sibling,
        )

    sh_cross = mesh_copy(
        sh_out.at[core], sh_out.at[core], f_send.at[last], f_recv.at[last], me, sibling
    )

    @pl.when(me == 0)
    def _():
        sh_keep.wait()
        for k in range(1, sections):
            sh_deliver(k).wait_recv()
        sh_cross.start()

    for name in names:

        @pl.when(me == owner[name])
        def _(name=name):
            keep_own(name).wait()
            for k in range(1, sections):
                deliver(name, k).wait_recv()
            cross(name).start()

    for k in range(1, sections):
        vec_copy(k).wait_recv()
    sums = vec[me]
    for k in range(1, sections):
        sums = sums + vec_slots[k]
    vec_out[...] = sums

    for k in range(1, sections):
        vec_copy(k).wait_send()
    sh_swap.wait_send()
    loop(1, depth, lambda k: sh_send(k).wait_send())
    loop(1, depth, lambda k: sh_share(k).wait_send())

    @pl.when(me == 0)
    def _():
        sh_cross.wait()

    @pl.when(me != 0)
    def _():
        sh_deliver(0).wait_send()

    for name in names:

        def sent(name=name):
            swap(name).wait_send()
            for k in range(1, sections):
                to_section(name, k).wait_send()

        when_held(name, sent)
        loop(1, depth, lambda k, name=name: to_chip(name, k).wait_send())
        loop(1, depth, lambda k, name=name: share(name, k).wait_send())

        @pl.when(me == owner[name])
        def _(name=name):
            cross(name).wait()

        @pl.when(me != owner[name])
        def _(name=name):
            deliver(name, 0).wait_send()


def sum_gradients(sections, count, short, terms, vectors):
    narrow = short.shape[1]
    depth = count // 2
    args, scratch = [], []
    for name, _, part in SUMS:
        rows = terms[name].shape[0]
        fine = rows // (2 * sections * depth)
        args.append(terms[name].reshape(2, sections, depth, fine, narrow))
        shapes = [(sections, depth, fine, narrow)] * 2
        if part:
            shapes.append((sections, depth, fine, narrow))
        shapes += [(depth, fine, narrow)] * 3
        scratch += [pltpu.VMEM(a, BF16) for a in shapes]
    sh_rows = short.shape[0] // 2
    scratch += [
        pltpu.VMEM((sh_rows, narrow), BF16),
        pltpu.VMEM((sh_rows, narrow), BF16),
        pltpu.VMEM((depth, sh_rows // depth, narrow), BF16),
        pltpu.VMEM((sh_rows, narrow), BF16),
        pltpu.VMEM((sections,) + vectors.shape[1:], F32),
    ]
    kinds = len(SUMS) + 1
    for shape in [(kinds,)] * 3 + [(kinds, sections)] * 2 + [(kinds, depth)] * 4:
        scratch.append(pltpu.SemaphoreType.DMA(shape))
    for shape in [(kinds,), (kinds, sections), (kinds,), (kinds,), (kinds,), (sections,), (sections,)]:
        scratch.append(pltpu.SemaphoreType.DMA(shape))
    hbm = pl.BlockSpec(memory_space=pl.ANY)
    vmem = pl.BlockSpec(memory_space=pltpu.VMEM)
    proj_shape = args[1].shape
    taps_shape = args[0].shape
    return pl.pallas_call(
        functools.partial(gradient_kernel, sections, count),
        out_shape=[
            shape_of((2, sh_rows, narrow * sections), BF16),
            shape_of(proj_shape, BF16),
            shape_of(taps_shape, BF16),
            shape_of(vectors.shape[1:], F32),
        ],
        in_specs=[hbm] * 7 + [vmem],
        out_specs=[hbm, hbm, hbm, vmem],
        scratch_shapes=scratch,
        compiler_params=pltpu.CompilerParams(
            has_side_effects=True, vmem_limit_bytes=VMEM_BYTES, collective_id=5
        ),
        cost_estimate=pl.CostEstimate(flops=0, bytes_accessed=400 * 2**20, transcendentals=0),
    )(short.reshape(2, sh_rows, narrow), *args, vectors)


def layouts(resolution_ids, order_ids):
    pixels = jnp.arange(MAP * MAP, dtype=jnp.int32)
    row_of = pixels // MAP
    column_of = pixels % MAP
    extent = 5 + resolution_ids[:, None]
    image_mask = ((row_of[None, :] < extent) & (column_of[None, :] < extent)).astype(F32)
    inside = (row_of < 6) & (column_of < 6)
    position = jnp.where(inside, row_of // 2 * 3 + column_of // 2, 0)
    onehot_tile = (position[:, None] == jnp.arange(9)[None, :]).astype(jnp.int32)
    picked = jnp.sum(onehot_tile[None] * order_ids[:, None, :], axis=2)
    row_to = 2 * (picked // 3) + row_of % 2
    column_to = 2 * (picked % 3) + column_of % 2
    target = row_to * MAP + column_to
    tile_mask = (inside & (row_to < extent) & (column_to < extent)).astype(F32)
    return image_mask, tile_mask, jnp.where(inside, target, -1)


def tap_tables(tiled):
    lattice = np.arange(MAP)
    tables = []
    for vertical, lateral in OFFSETS:
        row, column = lattice + vertical, lattice + lateral
        in_row = (row >= 0) & (row < MAP)
        in_column = (column >= 0) & (column < MAP)
        if tiled:
            in_row &= row // 2 == lattice // 2
            in_column &= column // 2 == lattice // 2
        tables.append((in_row[:, None] & in_column[None, :]).reshape(-1))
    return np.stack(tables, axis=1).astype(np.float32)


def mm(a, b, dims="rk,kn->rn"):
    return jnp.einsum(dims, a, b, preferred_element_type=F32)


def core_swap(value):
    count = lax.axis_size("dp")
    return lax.ppermute(value, "dp", [(d, d ^ 1) for d in range(count)])


def from_section(value, source, section):
    out = value[source]
    for t in range(value.shape[0]):
        if t != source:
            got = lax.ppermute(value[t], "segment", [(source, t)])
            out = jnp.where(section == t, got, out)
    return out


def to_section_zero(value):
    sections = lax.axis_size("segment")
    parts = [value] + [lax.ppermute(value, "segment", [(t, 0)]) for t in range(1, sections)]
    return jnp.stack(parts)


def body(
    layer_input,
    output_grad,
    resolution,
    tile_order,
    proj_weight,
    spatial_weight,
    shortcut_weight,
    bn_gain,
    bn_bias,
):
    micro, images, pixels, wide = layer_input.shape
    narrow = proj_weight.shape[2]
    rows = images * pixels
    padded = -(-rows // 16) * 16
    sections = lax.axis_size("segment")
    count = lax.axis_size("dp")
    section = lax.axis_index("segment")
    place = lax.axis_index("dp")
    core = place % 2
    first = section == 0
    proj, spatial, shortcut = proj_weight[0], spatial_weight[0], shortcut_weight[0]
    pick = lambda a: lax.dynamic_index_in_dim(a, section, 0, keepdims=False)

    half_rows = wide // 2
    w1_half = lax.dynamic_slice_in_dim(proj, core * half_rows, half_rows)
    w1_half = from_section(jnp.broadcast_to(w1_half, (sections,) + w1_half.shape), 1, section)
    w1_other = core_swap(w1_half)
    w1 = jnp.where(
        core == 0,
        jnp.concatenate([w1_half, w1_other]),
        jnp.concatenate([w1_other, w1_half]),
    )

    quarter = wide // sections
    own_half = lax.dynamic_slice_in_dim(shortcut, core * half_rows, half_rows)
    short_half = from_section(
        jnp.stack([own_half[:, t * quarter : (t + 1) * quarter] for t in range(sections)]),
        0,
        section,
    )
    short_other = core_swap(short_half)

    slice_rows = wide // count
    tap_rows = spatial.shape[0] // count
    own_proj = lax.dynamic_slice_in_dim(proj, place * slice_rows, slice_rows)
    own_taps = lax.dynamic_slice_in_dim(spatial, place * tap_rows, tap_rows)
    fine = tap_rows // sections
    taps_piece = from_section(own_taps.reshape(sections, fine, narrow), 2, section)
    packed = jnp.concatenate([own_proj, taps_piece])
    everyone = lax.all_gather(packed, ("segment", "dp"), axis=0, tiled=True)
    everyone = everyone.reshape(sections, count, slice_rows + fine, narrow)
    w2 = everyone[2, :, :slice_rows].reshape(wide, narrow)
    w3 = everyone[3, :, :slice_rows].reshape(wide, narrow)
    k2 = jnp.swapaxes(everyone[:, :, slice_rows:], 0, 1).reshape(9 * narrow, narrow)

    gains = lax.all_gather(jnp.concatenate([bn_gain[0], bn_bias[0]]), "segment", axis=0)
    gain, bias = gains[:, :wide], gains[:, wide:]

    image_masks, tile_masks, targets = layouts(
        resolution.reshape(-1), tile_order.reshape(micro * images, -1)
    )
    interleave = lambda a: jnp.transpose(a.reshape(micro, rows), (1, 0)).reshape(rows * micro, 1)
    taps_image = np.tile(np.repeat(tap_tables(False), micro, axis=0), (images, 1))
    pack_all = jnp.concatenate(
        [interleave(image_masks), jnp.asarray(taps_image), jnp.zeros((rows * micro, 6), F32)], axis=1
    )
    tiles_all = interleave(tile_masks)
    pad_rows = lambda a: jnp.pad(a, ((0, padded - rows), (0, 0)))
    image_mask = pad_rows(pick(image_masks.reshape(micro, rows, 1)))
    tile_mask = pad_rows(pick(tile_masks.reshape(micro, rows, 1)))
    taps_tile = np.pad(np.tile(tap_tables(True), (images, 1)), ((0, padded - rows), (0, 6)))
    pack_tile = jnp.concatenate([tile_mask, jnp.asarray(taps_tile)], axis=1)
    target = pick(targets.reshape(micro, images, pixels))
    base = (jnp.arange(images) * pixels)[:, None]
    target = jnp.where(target >= 0, target + base, -1).reshape(rows)
    target = jnp.pad(target, (0, padded - rows), constant_values=-1)
    index = jnp.arange(padded)
    moves = (target[:, None] == index[None, :]).astype(BF16)
    moves_back = (target[None, :] == index[:, None]).astype(BF16)

    x_all = jnp.transpose(layer_input, (1, 2, 0, 3)).reshape(rows * micro, wide)
    gb_first = jnp.stack(
        [bn_gain[0, :narrow], bn_bias[0, :narrow]]
        + [bn_gain[0, narrow : 2 * narrow], bn_bias[0, narrow : 2 * narrow]]
    )
    total = rows * micro
    a2_all, cols_all, h1n_all, h2n_all, stats_all, counts = kernel_call(
        functools.partial(first_kernel, count),
        [
            shape_of((micro, padded, narrow), BF16),
            shape_of((total, 9 * narrow), BF16),
            shape_of((total, narrow), F32),
            shape_of((total, narrow), F32),
            shape_of((16, narrow), F32),
            shape_of((8, 128), F32),
        ],
        [x_all, proj, spatial, gb_first, pack_all, tiles_all],
        [pltpu.VMEM((narrow // 128, 4 * padded, 128), F32)]
        + sync_scratch(count, [(8, narrow + 128), (8, narrow)]),
        0,
        2 * total * narrow * (wide + 9 * narrow),
        40 * 2**20,
    )
    a2 = from_section(a2_all, 0, section)
    [res_quarter] = kernel_call(
        residual_kernel,
        [shape_of((micro, padded, quarter), BF16)],
        [x_all, short_half, short_other],
        [pltpu.VMEM((quarter // 128, 4 * padded, 128), F32)],
        None,
        2 * total * wide * quarter,
        10 * 2**20,
    )
    residual = lax.all_to_all(res_quarter, "segment", 0, 0, tiled=True)

    valid_image = pick(counts[:4])[None]
    valid_tile = pick(counts[4:])[None]
    gb_one = jnp.stack([gain[1], bias[1]])
    y1, u, h3n, stats_three = kernel_call(
        functools.partial(second_kernel, count),
        [
            shape_of((padded, wide), BF16),
            shape_of((padded, wide), BF16),
            shape_of((padded, wide), F32),
            shape_of((2, wide), F32),
        ],
        [a2, w1, residual, image_mask, gb_one, valid_image, moves],
        sync_scratch(count, [(2, wide)]),
        1,
        2 * padded * wide * (narrow + padded),
        10 * 2**20,
    )
    gb_two = jnp.stack(
        [gain[2, :narrow], bias[2, :narrow]]
        + [gain[2, narrow : 2 * narrow], bias[2, narrow : 2 * narrow]]
    )
    gb_three = jnp.stack([gain[3], bias[3]])
    og = jnp.transpose(output_grad, (1, 2, 0, 3)).reshape(rows, micro, wide)
    og = pad_rows(lax.dynamic_index_in_dim(og, section, 1, keepdims=False))
    y2, t_a2, t_cols, t_dh3, t_dh2, t_dh1, dy1, t_sums = kernel_call(
        functools.partial(tile_kernel, count),
        [
            shape_of((padded, wide), BF16),
            shape_of((padded, narrow), BF16),
            shape_of((padded, 9 * narrow), BF16),
            shape_of((padded, wide), BF16),
            shape_of((padded, narrow), BF16),
            shape_of((padded, narrow), BF16),
            shape_of((padded, wide), BF16),
            shape_of((6, wide), F32),
        ],
        [u, w2, k2, w3, og, pack_tile, gb_two, gb_three, valid_tile, moves_back],
        [
            pltpu.VMEM((padded, narrow), F32),
            pltpu.VMEM((padded, narrow), F32),
            pltpu.VMEM((padded, wide), F32),
            pltpu.VMEM((padded, narrow), F32),
            pltpu.VMEM((padded, wide), BF16),
            pltpu.VMEM((6, wide), F32),
        ]
        + sync_scratch(
            count, [(2, narrow), (2, narrow), (2, wide), (2, wide), (2, narrow), (2, narrow)]
        ),
        2,
        4 * padded * narrow * (2 * wide + 9 * narrow),
        30 * 2**20,
    )
    dz, dh3, da2, i_sums = kernel_call(
        functools.partial(image_back_kernel, count),
        [
            shape_of((padded, wide), BF16),
            shape_of((padded, wide), BF16),
            shape_of((padded, narrow), BF16),
            shape_of((2, wide), F32),
        ],
        [dy1, residual, h3n, image_mask, gb_one, stats_three, valid_image, w1],
        sync_scratch(count, [(2, wide)]),
        3,
        2 * padded * narrow * wide,
        12 * 2**20,
    )
    da2_all = to_section_zero(da2)
    dh2_all, dh1_all, f_sums = kernel_call(
        functools.partial(last_kernel, count),
        [
            shape_of((total, narrow), BF16),
            shape_of((total, narrow), BF16),
            shape_of((16, narrow), F32),
        ],
        [da2_all, spatial, gb_first, pack_all, h1n_all, h2n_all, stats_all, counts],
        [
            pltpu.VMEM((narrow // 128, 4 * padded, 128), F32),
            pltpu.VMEM((total, narrow), F32),
            pltpu.VMEM((total, narrow), BF16),
        ]
        + sync_scratch(count, [(8, narrow), (8, narrow)]),
        4,
        2 * total * narrow * 9 * narrow,
        20 * 2**20,
    )
    weave = lambda a: jnp.swapaxes(a[:, :rows], 0, 1).reshape(total, a.shape[2])
    dz_all = weave(to_section_zero(dz))
    dz_quarter = weave(
        lax.all_to_all(dz.reshape(padded, sections, quarter), "segment", 1, 0, tiled=True).reshape(
            micro, padded, quarter
        )
    )
    [grad_input] = kernel_call(
        input_kernel,
        [shape_of((total, wide), BF16)],
        [dh1_all, dz_all, proj, shortcut],
        [],
        None,
        2 * total * wide * (wide + narrow),
        30 * 2**20,
    )

    terms = {
        "p3": mm(t_dh3, t_a2, "rd,rk->dk").astype(BF16),
        "k2": mm(t_cols, t_dh2, "rk,rn->kn").astype(BF16),
        "p2": mm(u, t_dh1, "rc,rn->cn").astype(BF16),
        "p1": mm(dh3, a2, "rd,rk->dk").astype(BF16),
        "k0": mm(cols_all, dh2_all, "rk,rn->kn").astype(BF16),
        "p0": mm(x_all, dh1_all, "rc,rn->cn").astype(BF16),
    }
    short_term = mm(x_all, dz_quarter, "rc,rd->cd").astype(BF16)

    exchanged = lax.all_to_all(jnp.stack([y1, y1, dy1, y2]), "segment", 0, 0)
    exchanged = jnp.swapaxes(exchanged[:, :rows], 0, 1)
    maps = jnp.where(first, grad_input.reshape(rows, micro, wide), exchanged)
    maps = jnp.transpose(maps.reshape(images, pixels, micro, wide), (2, 0, 1, 3))

    blank = jnp.zeros((wide,), F32)
    pad = jnp.zeros((wide - 2 * narrow,), F32)
    of_batches = lambda at: jnp.sum(f_sums[at : at + 4], axis=0)
    zero_gain = jnp.where(first, jnp.concatenate([of_batches(12), of_batches(4), pad]), blank)
    zero_bias = jnp.where(first, jnp.concatenate([of_batches(8), of_batches(0), pad]), blank)
    vectors = jnp.stack(
        [
            zero_gain,
            zero_bias,
            i_sums[1],
            i_sums[0],
            jnp.concatenate([t_sums[5, :narrow], t_sums[3, :narrow], pad]),
            jnp.concatenate([t_sums[4, :narrow], t_sums[2, :narrow], pad]),
            t_sums[1],
            t_sums[0],
        ]
    )
    short_sum, proj_sum, taps_sum, vectors = sum_gradients(
        sections, count, short_term, terms, vectors.reshape(sections, 2, wide)
    )
    proj_grad = proj_sum.reshape(wide, narrow).astype(F32)
    spatial_grad = taps_sum.reshape(9 * narrow, narrow).astype(F32)
    spatial_grad = jnp.where((section % 2) == 0, spatial_grad, jnp.zeros_like(spatial_grad))
    short_grad = short_sum.reshape(wide, wide).astype(F32)
    short_grad = jnp.where(first, short_grad, jnp.zeros_like(short_grad))
    return (
        maps[None],
        proj_grad[None],
        spatial_grad[None],
        short_grad[None],
        vectors[:1],
        vectors[1:],
    )


def solution(mesh):
    return jax.shard_map(
        body,
        mesh=mesh,
        in_specs=(
            P(None, "dp", None, None),
            P(None, "dp", None, None),
            P(None, "dp"),
            P(None, "dp", None),
            P("segment", None, None),
            P("segment", None, None),
            P("segment", None, None),
            P("segment", None),
            P("segment", None),
        ),
        out_specs=(
            P("segment", None, "dp", None, None),
            P("segment", None, None),
            P("segment", None, None),
            P("segment", None, None),
            P("segment", None),
            P("segment", None),
        ),
        check_vma=False,
    )
```

```python
import functools

import jax
import jax.numpy as jnp
import numpy as np
from jax import lax
from jax.experimental import pallas as pl
from jax.experimental.pallas import tpu as pltpu
from jax.sharding import PartitionSpec as P

MAP = 7
EPSILON = 1e-05
OFFSETS = ((-1, -1), (-1, 0), (-1, 1), (0, -1), (0, 0), (0, 1), (1, -1), (1, 0), (1, 1))
MESH = pl.DeviceIdType.MESH
F32 = jnp.float32
BF16 = jnp.bfloat16
VMEM_BYTES = 58 * 2**20
TILE = 256


def greet(count, sections=0):
    segment, me = lax.axis_index("segment"), lax.axis_index("dp")
    barrier = pltpu.get_barrier_semaphore()

    def one(k, carry):
        pl.semaphore_signal(
            barrier, inc=1, device_id=(segment, lax.rem(me + k, count)), device_id_type=MESH
        )
        return carry

    lax.fori_loop(1, count, one, 0)
    for k in range(1, sections):
        pl.semaphore_signal(
            barrier, inc=1, device_id=(jnp.bitwise_xor(segment, k), me), device_id_type=MESH
        )


def greeted(count, sections=1):
    pl.semaphore_wait(pltpu.get_barrier_semaphore(), count - 1 + sections - 1)


def exchange(count, slots, send_sem, recv_sem):
    segment, me = lax.axis_index("segment"), lax.axis_index("dp")

    def copy(k):
        return pltpu.make_async_remote_copy(
            src_ref=slots.at[me],
            dst_ref=slots.at[me],
            send_sem=send_sem.at[k],
            recv_sem=recv_sem.at[k],
            device_id=(segment, lax.rem(me + k, count)),
            device_id_type=MESH,
        )

    def start(k, carry):
        copy(k).start()
        return carry

    def finish(k, carry):
        copy(k).wait_recv()
        copy(k).wait_send()
        return carry

    lax.fori_loop(1, count, start, 0)
    lax.fori_loop(1, count, finish, 0)
    total = slots[0]
    for k in range(1, count):
        total = total + slots[k]
    return total


def mesh_copy(src, dst, send_sem, recv_sem, segment, place):
    return pltpu.make_async_remote_copy(
        src_ref=src,
        dst_ref=dst,
        send_sem=send_sem,
        recv_sem=recv_sem,
        device_id=(segment, place),
        device_id_type=MESH,
    )


def loop(low, high, body):
    def one(k, carry):
        body(k)
        return carry

    lax.fori_loop(low, high, one, 0)


def sync_scratch(count, shapes):
    out = []
    for shape in shapes:
        out += [
            pltpu.VMEM((count,) + shape, F32),
            pltpu.SemaphoreType.DMA((count,)),
            pltpu.SemaphoreType.DMA((count,)),
        ]
    return out


def kernel_call(kernel, outs, args, scratch, ident, flops, moved, far_in=(), far_out=()):
    params = dict(has_side_effects=True, vmem_limit_bytes=VMEM_BYTES)
    if ident is not None:
        params["collective_id"] = ident
    return pl.pallas_call(
        kernel,
        out_shape=outs,
        in_specs=[
            pl.BlockSpec(memory_space=pl.ANY if i in far_in else pltpu.VMEM) for i in range(len(args))
        ],
        out_specs=[
            pl.BlockSpec(memory_space=pl.ANY if i in far_out else pltpu.VMEM) for i in range(len(outs))
        ],
        scratch_shapes=scratch,
        compiler_params=pltpu.CompilerParams(**params),
        cost_estimate=pl.CostEstimate(flops=flops, bytes_accessed=moved, transcendentals=0),
    )(*args)


def shape_of(shape, dtype):
    return jax.ShapeDtypeStruct(shape, dtype)


def dot(a, b):
    return jnp.dot(a, b, preferred_element_type=F32)


def dot_t(a, b):
    return lax.dot_general(a, b, (((1,), (1,)), ((), ())), preferred_element_type=F32)


def sigmoid(v):
    return 1.0 / (1.0 + jnp.exp(-v))


def slope(v):
    s = sigmoid(v)
    return s * (1.0 + v * (1.0 - s))


def over(width, step, body):
    def one(j, carry):
        body(pl.ds(pl.multiple_of(j * step, step), step))
        return carry

    lax.fori_loop(0, width // step, one, 0)


def lane(at):
    return lax.div(at.start, 128)


def unrolled_shift(ref_value, shift):
    rows = ref_value.shape[0]
    return ref_value if shift % rows == 0 else pltpu.roll(ref_value, (-shift) % rows, 0)


def by_batch(values):
    rows, width = values.shape
    part = jnp.sum(values.reshape(rows // 8, 8, width), axis=0)
    return part[:4] + part[4:]


def spread8(values):
    return jnp.concatenate([values, values], axis=0)[None]


def first_part(
    count, ready, x, w, k, gb, pack, tiles, a2_out, cols, h1n, h2n, stats_out, count_out, act, *sync
):
    s1, send1, recv1, s2, send2, recv2 = sync
    rows, narrow = h1n.shape
    me = lax.axis_index("dp")
    full = act.shape[1]

    def tile8(v):
        return v.reshape(rows // 8, 8, v.shape[1])

    def project(at):
        h = dot(x[...], w[:, at])
        h1n[:, at] = h
        m = pack[:, 0:1] * h
        s1[me, 0:4, at] = by_batch(m)
        s1[me, 4:8, at] = by_batch(m * h)

    over(narrow, TILE, project)
    s1[me, 0:4, narrow:] = jnp.broadcast_to(by_batch(pack[:, 0:1]), (4, 128))
    s1[me, 4:8, narrow:] = jnp.broadcast_to(by_batch(tiles[:, 0:1]), (4, 128))
    ready()
    total = exchange(count, s1, send1, recv1)
    counts = total[:, narrow:]
    count_out[...] = counts
    valid = counts[0:4, 0:1]
    average = total[0:4, :narrow] / valid
    inverse = lax.rsqrt(total[4:8, :narrow] / valid - average * average + EPSILON)
    stats_out[0:4, :] = average
    stats_out[4:8, :] = inverse

    def activate(stat_at, gain_at, source):
        def body(at):
            mean = spread8(stats_out[stat_at : stat_at + 4, at])
            inv = spread8(stats_out[stat_at + 4 : stat_at + 8, at])
            hn = (tile8(source[:, at]) - mean) * inv
            source[:, at] = hn.reshape(rows, hn.shape[2])
            n = gb[gain_at : gain_at + 1, at][None] * hn + gb[gain_at + 1 : gain_at + 2, at][None]
            n = n.reshape(rows, n.shape[2])
            act[lane(at), 0:rows, :] = pack[:, 0:1] * (n * sigmoid(n))

        return body

    over(narrow, 128, activate(0, 0, h1n))

    for t, (vertical, lateral) in enumerate(OFFSETS):
        shift = 4 * (7 * vertical + lateral)

        def place(j, carry, t=t, shift=shift):
            at = pl.ds(pl.multiple_of(j * 128, 128), 128)
            to = pl.ds(pl.multiple_of(t * narrow + j * 128, 128), 128)
            moved = unrolled_shift(act[j, 0:rows, :], shift)
            cols[:, to] = (pack[:, 1 + t : 2 + t] * moved).astype(BF16)
            return carry

        lax.fori_loop(0, narrow // 128, place, 0)

    def convolve(at):
        h = dot(cols[...], k[:, at])
        h2n[:, at] = h
        m = pack[:, 0:1] * h
        s2[me, 0:4, at] = by_batch(m)
        s2[me, 4:8, at] = by_batch(m * h)

    over(narrow, TILE, convolve)
    total = exchange(count, s2, send2, recv2)
    average = total[0:4] / valid
    stats_out[8:12, :] = average
    stats_out[12:16, :] = lax.rsqrt(total[4:8] / valid - average * average + EPSILON)
    over(narrow, 128, activate(8, 2, h2n))
    act[:, rows:, :] = jnp.zeros((narrow // 128, full - rows, 128), F32)
    for m in range(4):

        def pick(j, carry, m=m):
            at = pl.ds(pl.multiple_of(j * 128, 128), 128)
            a2_out[m, :, at] = act[j, pl.ds(m, full // 4, stride=4), :].astype(BF16)
            return carry

        lax.fori_loop(0, narrow // 128, pick, 0)


def residual_part(x, w, out, hold):
    rows, full, quarter = x.shape[0], hold.shape[1], out.shape[2]
    hold[:, rows:, :] = jnp.zeros((quarter // 128, full - rows, 128), F32)

    def body(at):
        value = dot(x[...], w[:, at])
        for part in range(TILE // 128):
            hold[lane(at) + part, 0:rows, :] = value[:, part * 128 : part * 128 + 128]

    over(quarter, TILE, body)
    for m in range(4):

        def pick(j, carry, m=m):
            at = pl.ds(pl.multiple_of(j * 128, 128), 128)
            out[m, :, at] = hold[j, pl.ds(m, full // 4, stride=4), :].astype(BF16)
            return carry

        lax.fori_loop(0, quarter // 128, pick, 0)


def norm_sums(slots, me, at, masked, h):
    slots[me, 0:1, at] = jnp.sum(masked, axis=0, keepdims=True)
    slots[me, 1:2, at] = jnp.sum(masked * h, axis=0, keepdims=True)


def finish_stats(total, valid, stats_out, at_row):
    average = total[0:1] / valid
    width = average.shape[1]
    stats_out[at_row : at_row + 1, 0:width] = average
    stats_out[at_row + 1 : at_row + 2, 0:width] = lax.rsqrt(
        total[1:2] / valid - average * average + EPSILON
    )


def second_part(
    count, before, a2, w1, res, mask, gb, valid, moves, y_out, u_out, h3n, stats_out, s1, send1, recv1
):
    wide = h3n.shape[1]
    quarter = res.shape[2]
    me = lax.axis_index("dp")

    def project(at):
        h = dot_t(a2[...], w1[at, :])
        h3n[:, at] = h
        norm_sums(s1, me, at, mask[:, 0:1] * h, h)

    over(wide, TILE, project)
    finish_stats(exchange(count, s1, send1, recv1), valid, stats_out, 0)
    before()
    for q in range(wide // quarter):

        def body(j, carry, q=q):
            at = pl.ds(pl.multiple_of(q * quarter + j * 128, 128), 128)
            own = pl.ds(pl.multiple_of(j * 128, 128), 128)
            hn = (h3n[:, at] - stats_out[0:1, at]) * stats_out[1:2, at]
            h3n[:, at] = hn
            z = gb[1, 0:1, at] * hn + gb[1, 1:2, at] + res[q, :, own].astype(F32)
            y_out[:, at] = (mask[:, 0:1] * (z * sigmoid(z))).astype(BF16)
            return carry

        lax.fori_loop(0, quarter // 128, body, 0)

    def permute(at):
        u_out[:, at] = dot(moves[...], y_out[:, at]).astype(BF16)

    over(wide, TILE, permute)


def batch_valid(counts, row):
    me = lax.axis_index("segment")
    value = counts[row : row + 1, 0:1]
    for m in range(1, 4):
        value = jnp.where(me == m, counts[row + m : row + m + 1, 0:1], value)
    return value


def head_kernel(
    sections,
    count,
    x3,
    w,
    short,
    k,
    gb,
    vec,
    pack,
    tiles,
    mask,
    moves,
    x,
    cols,
    h1n,
    h2n,
    stats_out,
    count_out,
    g_out,
    y_out,
    u_out,
    h3n,
    stats3,
    a2_out,
    w1_out,
    res_out,
    act,
    a2_all,
    a2,
    wsc,
    w1,
    rq,
    res,
    gslots,
    *rest,
):
    sync, rest = rest[:9], list(rest[9:])
    short_send, short_recv, short_relay_send, short_relay_recv = rest[:4]
    w1_send, w1_recv, w1_relay_send, w1_relay_recv = rest[4:8]
    g_send, g_recv, a2_send, a2_recv, res_send, res_recv, own_sem, out_sem = rest[8:]
    me, place = lax.axis_index("segment"), lax.axis_index("dp")
    core = lax.rem(place, 2)
    sibling = place + 1 - 2 * core
    wide = x.shape[1]
    quarter = wide // sections
    half_rows = wide // 2
    mine = pl.ds(pl.multiple_of(core * half_rows, 16), half_rows)
    greet(count, sections)

    def short_copy(t):
        src = short.at[mine, pl.ds(t * quarter, quarter)]
        return mesh_copy(src, wsc.at[mine], short_send.at[t], short_recv, t, place)

    def w1_copy(t):
        return mesh_copy(w.at[mine], w1.at[mine], w1_send.at[t], w1_recv, t, place)

    short_own = pltpu.make_async_copy(short.at[:, pl.ds(0, quarter)], wsc, own_sem.at[0])
    w1_own = pltpu.make_async_copy(w, w1, own_sem.at[1])
    short_relay = mesh_copy(
        wsc.at[mine], wsc.at[mine], short_relay_send, short_relay_recv, me, sibling
    )
    w1_relay = mesh_copy(w1.at[mine], w1.at[mine], w1_relay_send, w1_relay_recv, me, sibling)

    def g_copy(k_):
        return mesh_copy(
            gslots.at[me],
            gslots.at[me],
            g_send.at[k_],
            g_recv.at[k_],
            jnp.bitwise_xor(me, k_),
            place,
        )

    gslots[me] = vec[...]
    greeted(count, sections)

    @pl.when(me == 0)
    def _():
        for t in (3, 1, 2):
            short_copy(t).start()
        short_own.start()

    @pl.when(me == 1)
    def _():
        for t in (2, 0, 3):
            w1_copy(t).start()
        w1_own.start()

    for k_ in range(1, sections):
        g_copy(k_).start()

    def relayout(j, carry):
        at = pl.ds(pl.multiple_of(j * 128, 128), 128)
        x[:, at] = x3[:, :, at].reshape(x.shape[0], 128)
        return carry

    lax.fori_loop(0, wide // 128, relayout, 0)
    first_part(
        count,
        lambda: None,
        x,
        w,
        k,
        gb,
        pack,
        tiles,
        a2_all,
        cols,
        h1n,
        h2n,
        stats_out,
        count_out,
        act,
        *sync[:6],
    )

    def a2_copy(t):
        return mesh_copy(a2_all.at[t], a2, a2_send.at[t], a2_recv, t, place)

    @pl.when(me == 0)
    def _():
        for t in range(1, sections):
            a2_copy(t).start()
        a2[...] = a2_all[0]
        short_own.wait()

    @pl.when(me != 0)
    def _():
        short_copy(0).wait_recv()
        short_relay.start()

    @pl.when(me == 1)
    def _():
        w1_own.wait()

    @pl.when(me != 1)
    def _():
        w1_copy(0).wait_recv()
        w1_relay.start()

    @pl.when(me != 0)
    def _():
        short_relay.wait_recv()

    residual_part(x, wsc, rq, act)

    def res_copy(k_):
        other = jnp.bitwise_xor(me, k_)
        return mesh_copy(
            rq.at[other], res.at[me], res_send.at[k_], res_recv.at[k_], other, place
        )

    for k_ in range(1, sections):
        res_copy(k_).start()
    res[me] = rq[me]

    @pl.when(me != 0)
    def _():
        a2_copy(0).wait_recv()

    @pl.when(me != 1)
    def _():
        w1_relay.wait_recv()

    for k_ in range(1, sections):
        g_copy(k_).wait_recv()
    g_out[...] = gslots[...]

    def before():
        for k_ in range(1, sections):
            res_copy(k_).wait_recv()

    second_part(
        count,
        before,
        a2,
        w1,
        res,
        mask,
        gslots,
        batch_valid(count_out, 0),
        moves,
        y_out,
        u_out,
        h3n,
        stats3,
        *sync[6:],
    )
    outs = [
        pltpu.make_async_copy(src, dst, out_sem.at[i])
        for i, (src, dst) in enumerate(((a2, a2_out), (w1, w1_out), (res, res_out)))
    ]
    for copy in outs:
        copy.start()
    for k_ in range(1, sections):
        g_copy(k_).wait_send()
        res_copy(k_).wait_send()

    @pl.when(me == 0)
    def _():
        for t in range(1, sections):
            short_copy(t).wait_send()
            a2_copy(t).wait_send()

    @pl.when(me != 0)
    def _():
        short_relay.wait_send()

    @pl.when(me == 1)
    def _():
        for t in (0, 2, 3):
            w1_copy(t).wait_send()

    @pl.when(me != 1)
    def _():
        w1_relay.wait_send()

    for copy in outs:
        copy.wait()


def back_sums(slots, me, at, grad, hn):
    slots[me, 0:1, at] = jnp.sum(grad, axis=0, keepdims=True)
    slots[me, 1:2, at] = jnp.sum(grad * hn, axis=0, keepdims=True)


def map_sender(sections, src, dst, owner, send_sem, recv_sem, own_sem):
    me, place = lax.axis_index("segment"), lax.axis_index("dp")
    own = pltpu.make_async_copy(src, dst.at[me], own_sem)

    def copy(k):
        return mesh_copy(src, dst.at[me], send_sem, recv_sem.at[k], owner, place)

    def start():
        @pl.when(me == owner)
        def _():
            own.start()

        for k in range(1, sections):

            @pl.when(me == owner ^ k)
            def _(k=k):
                copy(k).start()

    def finish():
        @pl.when(me == owner)
        def _():
            own.wait()
            for k in range(1, sections):
                copy(k).wait_recv()

        @pl.when(me != owner)
        def _():
            copy(0).wait_send()

    return start, finish


def tile_kernel(
    sections,
    count,
    u,
    w2,
    k2,
    w3,
    og3,
    pack,
    gains,
    counts,
    back,
    y1,
    y_out,
    a2,
    cols,
    dh3,
    dh2,
    dh1,
    dy,
    sums_out,
    map_one,
    h1n,
    h2n,
    h3n,
    act,
    dz,
    stats,
    og,
    map_send,
    map_recv,
    map_own,
    *sync,
):
    s1, send1, recv1, s2, send2, recv2, s3, send3, recv3 = sync[:9]
    b3, bsend3, brecv3, b2, bsend2, brecv2, b1, bsend1, brecv1 = sync[9:]
    rows, wide = u.shape
    narrow = h1n.shape[1]
    me = lax.axis_index("dp")
    section = lax.axis_index("segment")
    valid = batch_valid(counts, 4)
    gb3 = gains.at[3]

    def gb2(row, at):
        return gains[2, row % 2 : row % 2 + 1, pl.ds(at.start + row // 2 * narrow, at.size)]

    greet(count, sections)

    def project(at):
        h = dot(u[...], w2[:, at])
        h1n[:, at] = h
        norm_sums(s1, me, at, pack[:, 0:1] * h, h)

    over(narrow, TILE, project)
    greeted(count, sections)
    send_map, wait_map = map_sender(sections, y1, map_one, 1, map_send, map_recv, map_own)
    send_map()
    real = og3.shape[0]
    for m in range(sections):

        @pl.when(section == m)
        def _(m=m):
            def one(j, carry):
                at = pl.ds(pl.multiple_of(j * 128, 128), 128)
                og[0:real, at] = og3[:, m, at].astype(F32)
                return carry

            lax.fori_loop(0, wide // 128, one, 0)

    og[real:, :] = jnp.zeros((rows - real, wide), F32)
    finish_stats(exchange(count, s1, send1, recv1), valid, stats, 0)

    def activate(row, gain, source, store):
        def body(at):
            hn = (source[:, at] - stats[row : row + 1, at]) * stats[row + 1 : row + 2, at]
            source[:, at] = hn
            n = gb2(gain, at) * hn + gb2(gain + 1, at)
            store(at, pack[:, 0:1] * (n * sigmoid(n)))

        return body

    def to_act(at, value):
        act[:, at] = value

    def to_a2(at, value):
        a2[:, at] = value.astype(BF16)

    over(narrow, 128, activate(0, 0, h1n, to_act))
    for t, (vertical, lateral) in enumerate(OFFSETS):
        shift = 7 * vertical + lateral

        def place(j, carry, t=t, shift=shift):
            at = pl.ds(pl.multiple_of(j * 128, 128), 128)
            to = pl.ds(pl.multiple_of(t * narrow + j * 128, 128), 128)
            moved = unrolled_shift(act[:, at], shift)
            cols[:, to] = (pack[:, 1 + t : 2 + t] * moved).astype(BF16)
            return carry

        lax.fori_loop(0, narrow // 128, place, 0)

    def convolve(at):
        h = dot(cols[...], k2[:, at])
        h2n[:, at] = h
        norm_sums(s2, me, at, pack[:, 0:1] * h, h)

    over(narrow, TILE, convolve)
    finish_stats(exchange(count, s2, send2, recv2), valid, stats, 2)
    over(narrow, 128, activate(2, 2, h2n, to_a2))

    def expand(at):
        h = dot_t(a2[...], w3[at, :])
        h3n[:, at] = h
        norm_sums(s3, me, at, pack[:, 0:1] * h, h)

    over(wide, TILE, expand)
    finish_stats(exchange(count, s3, send3, recv3), valid, stats, 4)

    def result(at):
        hn = (h3n[:, at] - stats[4:5, at]) * stats[5:6, at]
        h3n[:, at] = hn
        z = gb3[0:1, at] * hn + gb3[1:2, at] + u[:, at].astype(F32)
        s = sigmoid(z)
        m = pack[:, 0:1]
        y_out[:, at] = (m * (z * s)).astype(BF16)
        grad = (og[:, at] * m * (s * (1.0 + z * (1.0 - s)))).astype(BF16)
        dz[:, at] = grad
        grad = grad.astype(F32)
        back_sums(b3, me, at, grad, hn)

    over(wide, 128, result)
    total = exchange(count, b3, bsend3, brecv3)
    sums_out[0:2, :] = total

    def through(at):
        offset, scale = sums_out[0:1, at], sums_out[1:2, at]
        dh3[:, at] = (
            pack[:, 0:1]
            * gb3[0:1, at]
            * stats[5:6, at]
            * (dz[:, at].astype(F32) - (offset + h3n[:, at] * scale) / valid)
        ).astype(BF16)

    over(wide, 128, through)

    def into_two(at):
        grad = dot(dh3[...], w3[:, at]).astype(BF16).astype(F32)
        hn = h2n[:, at]
        n = gb2(2, at) * hn + gb2(3, at)
        grad = grad * pack[:, 0:1] * slope(n)
        act[:, at] = grad
        back_sums(b2, me, at, grad, hn)

    over(narrow, TILE, into_two)
    total = exchange(count, b2, bsend2, brecv2)
    sums_out[2:4, 0:narrow] = total

    def through_two(at):
        offset, scale = sums_out[2:3, at], sums_out[3:4, at]
        grad = (
            pack[:, 0:1]
            * gb2(2, at)
            * stats[3:4, at]
            * (act[:, at] - (offset + h2n[:, at] * scale) / valid)
        )
        dh2[:, at] = grad.astype(BF16)
        act[:, at] = dh2[:, at].astype(F32)

    over(narrow, 128, through_two)
    h2n[...] = jnp.zeros((rows, narrow), F32)
    for t, (vertical, lateral) in enumerate(OFFSETS):
        shift = -(7 * vertical + lateral)
        other = 8 - t

        def place_back(j, carry, t=t, shift=shift, other=other):
            at = pl.ds(pl.multiple_of(j * 128, 128), 128)
            moved = unrolled_shift(act[:, at], shift)
            dy[:, at] = (pack[:, 1 + other : 2 + other] * moved).astype(BF16)
            return carry

        lax.fori_loop(0, narrow // 128, place_back, 0)

        def gather(at, t=t):
            row = pl.ds(pl.multiple_of(t * narrow + at.start, TILE), TILE)
            h2n[:, at] += dot_t(dy[:, 0:narrow], k2[row, :])

        over(narrow, TILE, gather)

    def into_one(at):
        hn = h1n[:, at]
        n = gb2(0, at) * hn + gb2(1, at)
        grad = h2n[:, at] * pack[:, 0:1] * slope(n)
        act[:, at] = grad
        back_sums(b1, me, at, grad, hn)

    over(narrow, 128, into_one)
    total = exchange(count, b1, bsend1, brecv1)
    sums_out[4:6, 0:narrow] = total

    def through_one(at):
        offset, scale = sums_out[4:5, at], sums_out[5:6, at]
        dh1[:, at] = (
            pack[:, 0:1]
            * gb2(0, at)
            * stats[1:2, at]
            * (act[:, at] - (offset + h1n[:, at] * scale) / valid)
        ).astype(BF16)

    over(narrow, 128, through_one)

    def into_input(at):
        grad = dot_t(dh1[...], w2[at, :]) + dz[:, at].astype(F32)
        dy[:, at] = dot(back[...], grad.astype(BF16)).astype(BF16)

    over(wide, TILE, into_input)
    wait_map()


def image_back_part(
    count, after, dy, res, h3n, mask, gb, stats, valid, w1, dz, dh3, da2, sums_out, b3, send3, recv3
):
    wide = dy.shape[1]
    quarter = res.shape[2]
    narrow = da2.shape[1]
    me = lax.axis_index("dp")
    for q in range(wide // quarter):

        def body(j, carry, q=q):
            at = pl.ds(pl.multiple_of(q * quarter + j * 128, 128), 128)
            own = pl.ds(pl.multiple_of(j * 128, 128), 128)
            hn = h3n[:, at]
            z = gb[0:1, at] * hn + gb[1:2, at] + res[q, :, own].astype(F32)
            grad = (dy[:, at].astype(F32) * mask[:, 0:1] * slope(z)).astype(BF16)
            dz[:, at] = grad
            back_sums(b3, me, at, grad.astype(F32), hn)
            return carry

        lax.fori_loop(0, quarter // 128, body, 0)
    after()
    total = exchange(count, b3, send3, recv3)
    sums_out[...] = total

    def through(at):
        offset, scale = sums_out[0:1, at], sums_out[1:2, at]
        dh3[:, at] = (
            mask[:, 0:1]
            * gb[0:1, at]
            * stats[1:2, at]
            * (dz[:, at].astype(F32) - (offset + h3n[:, at] * scale) / valid)
        ).astype(BF16)

    over(wide, 128, through)

    def into(at):
        da2[:, at] = dot(dh3[...], w1[:, at]).astype(BF16)

    over(narrow, TILE, into)


def last_part(
    count, da2, k, gb, pack, h1n, h2n, stats, counts, dh2, dh1, sums_out, act, acc, hold, *sync
):
    b2, send2, recv2, b1, send1, recv1 = sync
    rows, narrow = h1n.shape
    full = act.shape[1]
    me = lax.axis_index("dp")
    valid = counts[0:4, 0:1]

    def tile8(v):
        return v.reshape(rows // 8, 8, v.shape[1])

    for m in range(4):

        def put(j, carry, m=m):
            at = pl.ds(pl.multiple_of(j * 128, 128), 128)
            act[j, pl.ds(m, full // 4, stride=4), :] = da2[m, :, at].astype(F32)
            return carry

        lax.fori_loop(0, narrow // 128, put, 0)

    def into(gain, source, hidden, slots):
        def body(at):
            hn = hidden[:, at]
            n = gb[gain : gain + 1, at] * hn + gb[gain + 1 : gain + 2, at]
            grad = source(at) * pack[:, 0:1] * slope(n)
            act[lane(at), 0:rows, :] = grad
            slots[me, 0:4, at] = by_batch(grad)
            slots[me, 4:8, at] = by_batch(grad * hn)

        return body

    def through(gain, stat_at, row, hidden, out):
        def body(at):
            offset = spread8(sums_out[row : row + 4, at] / valid)
            scale = spread8(sums_out[row + 4 : row + 8, at] / valid)
            inv = spread8(stats[stat_at : stat_at + 4, at])
            g = tile8(act[lane(at), 0:rows, :])
            value = inv * gb[gain : gain + 1, at][None] * (g - (offset + tile8(hidden[:, at]) * scale))
            value = (pack[:, 0:1] * value.reshape(rows, value.shape[2])).astype(BF16)
            out[:, at] = value
            act[lane(at), 0:rows, :] = value.astype(F32)

        return body

    over(narrow, 128, into(2, lambda at: act[lane(at), 0:rows, :], h2n, b2))
    sums_out[0:8, :] = exchange(count, b2, send2, recv2)
    over(narrow, 128, through(2, 12, 0, h2n, dh2))
    acc[...] = jnp.zeros((rows, narrow), F32)
    for t, (vertical, lateral) in enumerate(OFFSETS):
        shift = -4 * (7 * vertical + lateral)
        other = 8 - t

        def place_back(j, carry, t=t, shift=shift, other=other):
            at = pl.ds(pl.multiple_of(j * 128, 128), 128)
            moved = unrolled_shift(act[j, 0:rows, :], shift)
            hold[:, at] = (pack[:, 1 + other : 2 + other] * moved).astype(BF16)
            return carry

        lax.fori_loop(0, narrow // 128, place_back, 0)

        def gather(at, t=t):
            row = pl.ds(pl.multiple_of(t * narrow + at.start, TILE), TILE)
            acc[:, at] += dot_t(hold[...], k[row, :])

        over(narrow, TILE, gather)
    over(narrow, 128, into(0, lambda at: acc[:, at], h1n, b1))
    sums_out[8:16, :] = exchange(count, b1, send1, recv1)
    over(narrow, 128, through(0, 4, 8, h1n, dh1))


def back_kernel(
    sections,
    count,
    dy,
    res,
    h3n,
    mask,
    gains,
    stats3,
    w1,
    k,
    gb,
    pack,
    h1n,
    h2n,
    stats,
    counts,
    y2,
    dz,
    dh3,
    dh2,
    dh1,
    sums3,
    sums12,
    dzq_out,
    dz_all,
    map_two,
    map_three,
    da2,
    da2_all,
    dzq,
    act,
    acc,
    hold,
    *rest,
):
    sync, rest = rest[:9], list(rest[9:])
    a_send, a_recv, q_send, q_recv = rest[:4]
    maps = [rest[4:7], rest[7:10], rest[10:13]]
    me, place = lax.axis_index("segment"), lax.axis_index("dp")
    quarter = dzq.shape[2]
    greet(count, sections)
    send_dz, wait_dz = map_sender(sections, dz, dz_all, 0, *maps[0])
    send_two, wait_two = map_sender(sections, dy, map_two, 2, *maps[1])
    send_three, wait_three = map_sender(sections, y2, map_three, 3, *maps[2])

    def q_copy(k_):
        other = jnp.bitwise_xor(me, k_)
        at = pl.ds(pl.multiple_of(other * quarter, 128), quarter)
        return mesh_copy(dz.at[:, at], dzq.at[me], q_send.at[k_], q_recv.at[k_], other, place)

    def after():
        greeted(count, sections)
        for k_ in range(1, sections):
            q_copy(k_).start()

    image_back_part(
        count,
        after,
        dy,
        res,
        h3n,
        mask,
        gains.at[1],
        stats3,
        batch_valid(counts, 0),
        w1,
        dz,
        dh3,
        da2,
        sums3,
        *sync[:3],
    )

    def a_copy(k_):
        return mesh_copy(da2, da2_all.at[me], a_send, a_recv.at[k_], 0, place)

    for k_ in range(1, sections):

        @pl.when(me == k_)
        def _(k_=k_):
            a_copy(k_).start()

    for k_ in range(1, sections):
        q_copy(k_).wait_recv()
    dzq[me] = dz[:, pl.ds(pl.multiple_of(me * quarter, 128), quarter)]
    rows, full = dzq_out.shape[0], act.shape[1]
    for m in range(4):

        def put(j, carry, m=m):
            at = pl.ds(pl.multiple_of(j * 128, 128), 128)
            act[j, pl.ds(m, full // 4, stride=4), :] = dzq[m, :, at].astype(F32)
            return carry

        lax.fori_loop(0, quarter // 128, put, 0)

    def weave(j, carry):
        at = pl.ds(pl.multiple_of(j * 128, 128), 128)
        dzq_out[:, at] = act[j, 0:rows, :].astype(BF16)
        return carry

    lax.fori_loop(0, quarter // 128, weave, 0)

    @pl.when(me == 0)
    def _():
        for k_ in range(1, sections):
            a_copy(k_).wait_recv()
        da2_all[0] = da2[...]

    @pl.when(me != 0)
    def _():
        da2_all[...] = jnp.zeros(da2_all.shape, BF16)

    send_dz()
    send_two()
    send_three()
    last_part(
        count, da2_all, k, gb, pack, h1n, h2n, stats, counts, dh2, dh1, sums12, act, acc, hold, *sync[3:]
    )
    for k_ in range(1, sections):
        q_copy(k_).wait_send()

    @pl.when(me != 0)
    def _():
        a_copy(0).wait_send()

    wait_dz()
    wait_two()
    wait_three()


SUMS = (("k2", 2, True), ("p3", 3, True), ("p2", 2, True), ("p1", 1, True), ("k0", 0, False), ("p0", 0, False))


def gradient_kernel(
    sections,
    count,
    sh,
    k2,
    p3,
    p2,
    p1,
    k0,
    p0,
    vec,
    dh1,
    w,
    short,
    map_zero,
    map_one,
    map_two,
    map_three,
    sh_out,
    p_out,
    k_out,
    vec_out,
    maps,
    *scratch,
):
    names = [name for name, _, _ in SUMS]
    terms = dict(zip(names, (k2, p3, p2, p1, k0, p0)))
    owner = {name: section for name, section, _ in SUMS}
    spread = {name: part for name, _, part in SUMS}
    depth = count // 2
    me, place = lax.axis_index("segment"), lax.axis_index("dp")
    core, z = lax.rem(place, 2), lax.div(place, 2)
    sibling = place + 1 - 2 * core
    scratch = list(scratch)
    take = lambda: scratch.pop(0)
    half, theirs, planes, total, others, whole = {}, {}, {}, {}, {}, {}
    for name in names:
        half[name], theirs[name] = take(), take()
        if spread[name]:
            planes[name] = take()
        total[name], others[name], whole[name] = take(), take(), take()
    sh_half, sh_theirs, sh_others, sh_whole, vec_slots = take(), take(), take(), take(), take()
    load_sem, a_send, a_recv, b_send, b_recv, c_send, c_recv, d_send, d_recv = (take() for _ in range(9))
    e_send, e_recv, e_own, f_send, f_recv, v_send, v_recv = (take() for _ in range(7))
    pages, s_rows, w_rows, hold, stage, page_sem, s_sem, w_sem, stage_sem = (take() for _ in range(9))
    slot = {name: i for i, name in enumerate(names)}
    last = len(names)

    page_loads = [
        pltpu.make_async_copy(source, pages, page_sem)
        for source in (map_zero, map_one, map_two, map_three)
    ]
    for i, copy in enumerate(page_loads):
        pl.when(me == i)(copy.start)
    wide = pages.shape[2]
    full_rows, map_rows = hold.shape[1], maps.shape[0] * maps.shape[1]

    def tile_loads(j):
        at = pl.ds(pl.multiple_of(j * TILE, TILE), TILE)
        at_slot = lax.rem(j, 2)
        return (
            pltpu.make_async_copy(short.at[at], s_rows.at[at_slot], s_sem.at[at_slot]),
            pltpu.make_async_copy(w.at[at], w_rows.at[at_slot], w_sem.at[at_slot]),
        )

    def tile_store(j):
        at = pl.ds(pl.multiple_of(j * TILE, TILE), TILE)
        at_slot = lax.rem(j, 2)
        return pltpu.make_async_copy(stage.at[at_slot], maps.at[:, :, at], stage_sem.at[at_slot])

    @pl.when(me == 0)
    def _():
        for copy in tile_loads(0):
            copy.start()

    def map_tile(j):
        at = pl.ds(pl.multiple_of(j * TILE, TILE), TILE)
        at_slot = lax.rem(j, 2)

        def weave(m, value):
            for part in range(TILE // 128):
                hold[part, pl.ds(m, full_rows // 4, stride=4), :] = value[
                    :, part * 128 : part * 128 + 128
                ]

        @pl.when(j >= 2)
        def _():
            tile_store(j - 2).wait()

        @pl.when(me == 0)
        def _():
            @pl.when(j + 1 < wide // TILE)
            def _():
                for copy in tile_loads(j + 1):
                    copy.start()

            for copy in tile_loads(j):
                copy.wait()
            for m in range(4):
                weave(m, dot_t(pages[m], s_rows[at_slot]))
            extra = dot_t(dh1[...], w_rows[at_slot])
            for part in range(TILE // 128):
                cols = slice(part * 128, part * 128 + 128)
                value = (hold[part, 0:map_rows, :] + extra[:, cols]).astype(BF16)
                stage[at_slot, :, :, cols] = value.reshape(map_rows // 4, 4, 128)

        @pl.when(me != 0)
        def _():
            for m in range(4):
                weave(m, pages[m, :, at].astype(F32))
            for part in range(TILE // 128):
                cols = slice(part * 128, part * 128 + 128)
                value = hold[part, 0:map_rows, :].astype(BF16)
                stage[at_slot, :, :, cols] = value.reshape(map_rows // 4, 4, 128)

        tile_store(j).start()

    def chip(k):
        return 2 * lax.rem(z + k, depth) + core

    barrier = pltpu.get_barrier_semaphore()
    pl.semaphore_signal(barrier, inc=1, device_id=(me, sibling), device_id_type=MESH)
    for k in range(1, sections):
        pl.semaphore_signal(
            barrier, inc=1, device_id=(jnp.bitwise_xor(me, k), place), device_id_type=MESH
        )
    loop(
        1,
        depth,
        lambda k: pl.semaphore_signal(
            barrier, inc=1, device_id=(me, chip(k)), device_id_type=MESH
        ),
    )
    pl.semaphore_wait(barrier, 1 + sections - 1 + depth - 1)

    def swap(name):
        return mesh_copy(
            terms[name].at[1 - core],
            theirs[name],
            a_send.at[slot[name]],
            a_recv.at[slot[name]],
            me,
            sibling,
        )

    def load(name):
        return pltpu.make_async_copy(terms[name].at[core], half[name], load_sem.at[slot[name]])

    def when_held(name, body):
        if spread[name]:
            body()
        else:
            pl.when(me == owner[name])(body)

    sh_rows = sh_half.shape[0]
    sh_swap = mesh_copy(
        sh.at[1 - core], sh_theirs, a_send.at[last], a_recv.at[last], me, sibling
    )
    sh_load = pltpu.make_async_copy(sh.at[core], sh_half, load_sem.at[last])
    sh_swap.start()
    sh_load.start()

    def vec_copy(k):
        other = jnp.bitwise_xor(me, k)
        return mesh_copy(
            vec.at[other], vec_slots.at[k], v_send.at[k], v_recv.at[k], other, place
        )

    for k in range(1, sections):
        vec_copy(k).start()
    for name in names:

        def begin(name=name):
            swap(name).start()
            load(name).start()

        when_held(name, begin)

    piece = sh_rows // depth
    step = 32

    def sh_at(i):
        return pl.ds(pl.multiple_of(i * piece, 16), piece)

    def sh_send(k):
        to = lax.rem(z + k, depth)
        return mesh_copy(
            sh_half.at[sh_at(to)],
            sh_others.at[k],
            c_send.at[last, k],
            c_recv.at[last, k],
            me,
            2 * to + core,
        )

    sh_load.wait()
    sh_swap.wait_recv()

    def sh_add(i):
        at = pl.ds(pl.multiple_of(i * step, step), step)
        sh_half[at, :] = (sh_half[at, :].astype(F32) + sh_theirs[at, :].astype(F32)).astype(BF16)

    loop(0, sh_rows // step, sh_add)
    loop(1, depth, lambda k: sh_send(k).start())

    def to_section(name, k):
        other = jnp.bitwise_xor(me, k)
        target = planes[name].at[k] if spread[name] else total[name]
        return mesh_copy(
            half[name].at[other],
            target,
            b_send.at[slot[name], k],
            b_recv.at[slot[name], k],
            other,
            place,
        )

    for name in names:

        def combine(name=name):
            load(name).wait()
            swap(name).wait_recv()

            def add(i):
                q, y = lax.div(i, depth), lax.rem(i, depth)
                half[name][q, y] = (
                    half[name][q, y].astype(F32) + theirs[name][q, y].astype(F32)
                ).astype(BF16)

            loop(0, sections * depth, add)
            for k in range(1, sections):
                to_section(name, k).start()

        when_held(name, combine)

    for i, copy in enumerate(page_loads):
        pl.when(me == i)(copy.wait)
    loop(0, 2, map_tile)

    loop(1, depth, lambda k: sh_send(k).wait_recv())
    mine = sh_at(z)
    acc = sh_half[mine, :].astype(F32)
    for k in range(1, depth):
        acc = acc + sh_others[k].astype(F32)
    sh_whole[mine, :] = acc.astype(BF16)

    def sh_share(k):
        return mesh_copy(
            sh_whole.at[mine],
            sh_whole.at[mine],
            d_send.at[last, k],
            d_recv.at[last, k],
            me,
            chip(k),
        )

    loop(1, depth, lambda k: sh_share(k).start())
    loop(2, wide // TILE, map_tile)

    def to_chip(name, k):
        to = lax.rem(z + k, depth)
        return mesh_copy(
            total[name].at[to],
            others[name].at[k],
            c_send.at[slot[name], k],
            c_recv.at[slot[name], k],
            me,
            2 * to + core,
        )

    for name in names:
        if spread[name]:
            for k in range(1, sections):
                to_section(name, k).wait_recv()

            def plane_add(y, name=name):
                acc = half[name][me, y].astype(F32)
                for k in range(1, sections):
                    acc = acc + planes[name][k, y].astype(F32)
                total[name][y] = acc.astype(BF16)

            loop(0, depth, plane_add)
        else:

            @pl.when(me == owner[name])
            def _(name=name):
                def keep(y):
                    total[name][y] = half[name][owner[name], y]

                loop(0, depth, keep)

            for k in range(1, sections):

                @pl.when(me == owner[name] ^ k)
                def _(name=name, k=k):
                    to_section(name, k).wait_recv()

        loop(1, depth, lambda k, name=name: to_chip(name, k).start())

    def sh_deliver(k):
        at = pl.ds(pl.multiple_of(me * sh_whole.shape[1], 128), sh_whole.shape[1])
        return mesh_copy(
            sh_whole,
            sh_out.at[core, :, at],
            e_send.at[last],
            e_recv.at[last, k],
            0,
            place,
        )

    loop(1, depth, lambda k: sh_share(k).wait_recv())
    at_zero = pl.ds(0, sh_whole.shape[1])
    sh_keep = pltpu.make_async_copy(sh_whole, sh_out.at[core, :, at_zero], e_own.at[last])

    @pl.when(me == 0)
    def _():
        sh_keep.start()

    for k in range(1, sections):

        @pl.when(me == k)
        def _(k=k):
            sh_deliver(k).start()

    def share(name, k):
        return mesh_copy(
            whole[name].at[z],
            whole[name].at[z],
            d_send.at[slot[name], k],
            d_recv.at[slot[name], k],
            me,
            chip(k),
        )

    for name in names:
        loop(1, depth, lambda k, name=name: to_chip(name, k).wait_recv())
        acc = total[name][z].astype(F32)
        for k in range(1, depth):
            acc = acc + others[name][k].astype(F32)
        whole[name][z] = acc.astype(BF16)
        loop(1, depth, lambda k, name=name: share(name, k).start())

    def final(name):
        return k_out if name[0] == "k" else p_out

    def deliver(name, k):
        return mesh_copy(
            whole[name],
            final(name).at[core, me],
            e_send.at[slot[name]],
            e_recv.at[slot[name], k],
            owner[name],
            place,
        )

    def keep_own(name):
        return pltpu.make_async_copy(whole[name], final(name).at[core, me], e_own.at[slot[name]])

    for name in names:
        loop(1, depth, lambda k, name=name: share(name, k).wait_recv())

        @pl.when(me == owner[name])
        def _(name=name):
            keep_own(name).start()

        for k in range(1, sections):

            @pl.when(me == owner[name] ^ k)
            def _(name=name, k=k):
                deliver(name, k).start()

    def cross(name):
        return mesh_copy(
            final(name).at[core],
            final(name).at[core],
            f_send.at[slot[name]],
            f_recv.at[slot[name]],
            me,
            sibling,
        )

    sh_cross = mesh_copy(
        sh_out.at[core], sh_out.at[core], f_send.at[last], f_recv.at[last], me, sibling
    )

    @pl.when(me == 0)
    def _():
        sh_keep.wait()
        for k in range(1, sections):
            sh_deliver(k).wait_recv()
        sh_cross.start()

    for name in names:

        @pl.when(me == owner[name])
        def _(name=name):
            keep_own(name).wait()
            for k in range(1, sections):
                deliver(name, k).wait_recv()
            cross(name).start()

    for k in range(1, sections):
        vec_copy(k).wait_recv()
    sums = vec[me]
    for k in range(1, sections):
        sums = sums + vec_slots[k]
    vec_out[...] = sums

    tile_store(wide // TILE - 2).wait()
    tile_store(wide // TILE - 1).wait()
    for k in range(1, sections):
        vec_copy(k).wait_send()
    sh_swap.wait_send()
    loop(1, depth, lambda k: sh_send(k).wait_send())
    loop(1, depth, lambda k: sh_share(k).wait_send())

    @pl.when(me == 0)
    def _():
        sh_cross.wait()

    @pl.when(me != 0)
    def _():
        sh_deliver(0).wait_send()

    for name in names:

        def sent(name=name):
            swap(name).wait_send()
            for k in range(1, sections):
                to_section(name, k).wait_send()

        when_held(name, sent)
        loop(1, depth, lambda k, name=name: to_chip(name, k).wait_send())
        loop(1, depth, lambda k, name=name: share(name, k).wait_send())

        @pl.when(me == owner[name])
        def _(name=name):
            cross(name).wait()

        @pl.when(me != owner[name])
        def _(name=name):
            deliver(name, 0).wait_send()


def sum_gradients(sections, count, short, terms, vectors, dh1, w, weights, map_sources, real):
    narrow = short.shape[1]
    depth = count // 2
    args, scratch = [], []
    for name, _, part in SUMS:
        rows = terms[name].shape[0]
        fine = rows // (2 * sections * depth)
        args.append(terms[name].reshape(2, sections, depth, fine, narrow))
        shapes = [(sections, depth, fine, narrow)] * 2
        if part:
            shapes.append((sections, depth, fine, narrow))
        shapes += [(depth, fine, narrow)] * 3
        scratch += [pltpu.VMEM(a, BF16) for a in shapes]
    sh_rows = short.shape[0] // 2
    scratch += [
        pltpu.VMEM((sh_rows, narrow), BF16),
        pltpu.VMEM((sh_rows, narrow), BF16),
        pltpu.VMEM((depth, sh_rows // depth, narrow), BF16),
        pltpu.VMEM((sh_rows, narrow), BF16),
        pltpu.VMEM((sections,) + vectors.shape[1:], F32),
    ]
    kinds = len(SUMS) + 1
    for shape in [(kinds,)] * 3 + [(kinds, sections)] * 2 + [(kinds, depth)] * 4:
        scratch.append(pltpu.SemaphoreType.DMA(shape))
    for shape in [(kinds,), (kinds, sections), (kinds,), (kinds,), (kinds,), (sections,), (sections,)]:
        scratch.append(pltpu.SemaphoreType.DMA(shape))
    wide = w.shape[0]
    padded = map_sources[0].shape[1]
    scratch += [
        pltpu.VMEM(map_sources[0].shape, BF16),
        pltpu.VMEM((2, TILE, wide), BF16),
        pltpu.VMEM((2, TILE, narrow), BF16),
        pltpu.VMEM((TILE // 128, 4 * padded, 128), F32),
        pltpu.VMEM((2, real, 4, TILE), BF16),
        pltpu.SemaphoreType.DMA,
        pltpu.SemaphoreType.DMA((2,)),
        pltpu.SemaphoreType.DMA((2,)),
        pltpu.SemaphoreType.DMA((2,)),
    ]
    hbm = pl.BlockSpec(memory_space=pl.ANY)
    vmem = pl.BlockSpec(memory_space=pltpu.VMEM)
    proj_shape = args[1].shape
    taps_shape = args[0].shape
    return pl.pallas_call(
        functools.partial(gradient_kernel, sections, count),
        out_shape=[
            shape_of((2, sh_rows, narrow * sections), BF16),
            shape_of(proj_shape, BF16),
            shape_of(taps_shape, BF16),
            shape_of(vectors.shape[1:], F32),
            shape_of((real, 4, wide), BF16),
        ],
        in_specs=[hbm] * 7 + [vmem, vmem] + [hbm] * 6,
        out_specs=[hbm, hbm, hbm, vmem, hbm],
        scratch_shapes=scratch,
        compiler_params=pltpu.CompilerParams(
            has_side_effects=True, vmem_limit_bytes=VMEM_BYTES, collective_id=5
        ),
        cost_estimate=pl.CostEstimate(flops=0, bytes_accessed=400 * 2**20, transcendentals=0),
    )(short.reshape(2, sh_rows, narrow), *args, vectors, dh1, w, weights, *map_sources)


def layouts(resolution_ids, order_ids):
    pixels = jnp.arange(MAP * MAP, dtype=jnp.int32)
    row_of = pixels // MAP
    column_of = pixels % MAP
    extent = 5 + resolution_ids[:, None]
    image_mask = ((row_of[None, :] < extent) & (column_of[None, :] < extent)).astype(F32)
    inside = (row_of < 6) & (column_of < 6)
    position = jnp.where(inside, row_of // 2 * 3 + column_of // 2, 0)
    onehot_tile = (position[:, None] == jnp.arange(9)[None, :]).astype(jnp.int32)
    picked = jnp.sum(onehot_tile[None] * order_ids[:, None, :], axis=2)
    row_to = 2 * (picked // 3) + row_of % 2
    column_to = 2 * (picked % 3) + column_of % 2
    target = row_to * MAP + column_to
    tile_mask = (inside & (row_to < extent) & (column_to < extent)).astype(F32)
    return image_mask, tile_mask, jnp.where(inside, target, -1)


def tap_tables(tiled):
    lattice = np.arange(MAP)
    tables = []
    for vertical, lateral in OFFSETS:
        row, column = lattice + vertical, lattice + lateral
        in_row = (row >= 0) & (row < MAP)
        in_column = (column >= 0) & (column < MAP)
        if tiled:
            in_row &= row // 2 == lattice // 2
            in_column &= column // 2 == lattice // 2
        tables.append((in_row[:, None] & in_column[None, :]).reshape(-1))
    return np.stack(tables, axis=1).astype(np.float32)


def mm(a, b, dims="rk,kn->rn"):
    return jnp.einsum(dims, a, b, preferred_element_type=F32)


def from_section(value, source, section):
    out = value[source]
    for t in range(value.shape[0]):
        if t != source:
            got = lax.ppermute(value[t], "segment", [(source, t)])
            out = jnp.where(section == t, got, out)
    return out


def by_share(weights, sections, count, place):
    rows, width = weights.shape
    blocks = weights.reshape(sections, count, rows // (sections * count), width)
    return lax.dynamic_index_in_dim(blocks, place, 1, keepdims=False)


def body(
    layer_input,
    output_grad,
    resolution,
    tile_order,
    proj_weight,
    spatial_weight,
    shortcut_weight,
    bn_gain,
    bn_bias,
):
    micro, images, pixels, wide = layer_input.shape
    narrow = proj_weight.shape[2]
    rows = images * pixels
    padded = -(-rows // 16) * 16
    sections = lax.axis_size("segment")
    count = lax.axis_size("dp")
    section = lax.axis_index("segment")
    place = lax.axis_index("dp")
    first = section == 0
    proj, spatial, shortcut = proj_weight[0], spatial_weight[0], shortcut_weight[0]
    pick = lambda a: lax.dynamic_index_in_dim(a, section, 0, keepdims=False)

    taps_share = from_section(by_share(spatial, sections, count, place), 2, section)
    two_share = from_section(by_share(proj, sections, count, place), 2, section)
    three_share = from_section(by_share(proj, sections, count, place), 3, section)
    k2 = lax.all_gather(taps_share, ("segment", "dp"), axis=0, tiled=True)
    w2 = lax.all_gather(two_share, ("segment", "dp"), axis=0, tiled=True)
    w3 = lax.all_gather(three_share, ("segment", "dp"), axis=0, tiled=True)

    image_masks, tile_masks, targets = layouts(
        resolution.reshape(-1), tile_order.reshape(micro * images, -1)
    )
    interleave = lambda a: jnp.transpose(a.reshape(micro, rows), (1, 0)).reshape(rows * micro, 1)
    taps_image = np.tile(np.repeat(tap_tables(False), micro, axis=0), (images, 1))
    pack_all = jnp.concatenate(
        [interleave(image_masks), jnp.asarray(taps_image), jnp.zeros((rows * micro, 6), F32)], axis=1
    )
    tiles_all = interleave(tile_masks)
    pad_rows = lambda a: jnp.pad(a, ((0, padded - rows), (0, 0)))
    image_mask = pad_rows(pick(image_masks.reshape(micro, rows, 1)))
    tile_mask = pad_rows(pick(tile_masks.reshape(micro, rows, 1)))
    taps_tile = np.pad(np.tile(tap_tables(True), (images, 1)), ((0, padded - rows), (0, 6)))
    pack_tile = jnp.concatenate([tile_mask, jnp.asarray(taps_tile)], axis=1)
    target = pick(targets.reshape(micro, images, pixels))
    base = (jnp.arange(images) * pixels)[:, None]
    target = jnp.where(target >= 0, target + base, -1).reshape(rows)
    target = jnp.pad(target, (0, padded - rows), constant_values=-1)
    index = jnp.arange(padded)
    moves = (target[:, None] == index[None, :]).astype(BF16)
    moves_back = (target[None, :] == index[:, None]).astype(BF16)

    x_in = jnp.transpose(layer_input, (1, 2, 0, 3)).reshape(rows, micro, wide)
    og_in = jnp.transpose(output_grad, (1, 2, 0, 3)).reshape(rows, micro, wide)
    gb_first = jnp.stack(
        [bn_gain[0, :narrow], bn_bias[0, :narrow]]
        + [bn_gain[0, narrow : 2 * narrow], bn_bias[0, narrow : 2 * narrow]]
    )
    gains_here = jnp.concatenate([bn_gain, bn_bias])
    total = rows * micro
    quarter = wide // sections
    dma = pltpu.SemaphoreType.DMA
    x_all, cols_all, h1n_all, h2n_all, stats_all, counts, gains, y1, u, h3n, stats3, a2, w1, res = (
        kernel_call(
            functools.partial(head_kernel, sections, count),
            [
                shape_of((total, wide), BF16),
                shape_of((total, 9 * narrow), BF16),
                shape_of((total, narrow), F32),
                shape_of((total, narrow), F32),
                shape_of((16, narrow), F32),
                shape_of((8, 128), F32),
                shape_of((sections, 2, wide), F32),
                shape_of((padded, wide), BF16),
                shape_of((padded, wide), BF16),
                shape_of((padded, wide), F32),
                shape_of((2, wide), F32),
                shape_of((padded, narrow), BF16),
                shape_of((wide, narrow), BF16),
                shape_of((sections, padded, quarter), BF16),
            ],
            [x_in, proj, shortcut, spatial, gb_first, gains_here, pack_all, tiles_all, image_mask, moves],
            [
                pltpu.VMEM((narrow // 128, 4 * padded, 128), F32),
                pltpu.VMEM((micro, padded, narrow), BF16),
                pltpu.VMEM((padded, narrow), BF16),
                pltpu.VMEM((wide, quarter), BF16),
                pltpu.VMEM((wide, narrow), BF16),
                pltpu.VMEM((micro, padded, quarter), BF16),
                pltpu.VMEM((sections, padded, quarter), BF16),
                pltpu.VMEM((sections, 2, wide), F32),
            ]
            + sync_scratch(count, [(8, narrow + 128), (8, narrow), (2, wide)])
            + [dma((sections,)), dma, dma, dma]
            + [dma((sections,)), dma, dma, dma]
            + [dma((sections,)), dma((sections,)), dma((sections,)), dma]
            + [dma((sections,)), dma((sections,)), dma((2,)), dma((3,))],
            0,
            2 * total * (narrow * (wide + 9 * narrow) + wide * quarter),
            60 * 2**20,
            far_in=(2,),
            far_out=(11, 12, 13),
        )
    )
    paged = shape_of((sections, padded, wide), BF16)
    y2, t_a2, t_cols, t_dh3, t_dh2, t_dh1, dy1, t_sums, map_one = kernel_call(
        functools.partial(tile_kernel, sections, count),
        [
            shape_of((padded, wide), BF16),
            shape_of((padded, narrow), BF16),
            shape_of((padded, 9 * narrow), BF16),
            shape_of((padded, wide), BF16),
            shape_of((padded, narrow), BF16),
            shape_of((padded, narrow), BF16),
            shape_of((padded, wide), BF16),
            shape_of((6, wide), F32),
            paged,
        ],
        [u, w2, k2, w3, og_in, pack_tile, gains, counts, moves_back, y1],
        [
            pltpu.VMEM((padded, narrow), F32),
            pltpu.VMEM((padded, narrow), F32),
            pltpu.VMEM((padded, wide), F32),
            pltpu.VMEM((padded, narrow), F32),
            pltpu.VMEM((padded, wide), BF16),
            pltpu.VMEM((6, wide), F32),
            pltpu.VMEM((padded, wide), F32),
            dma,
            dma((sections,)),
            dma,
        ]
        + sync_scratch(
            count, [(2, narrow), (2, narrow), (2, wide), (2, wide), (2, narrow), (2, narrow)]
        ),
        1,
        4 * padded * narrow * (2 * wide + 9 * narrow),
        30 * 2**20,
        far_in=(9,),
        far_out=(8,),
    )
    dz, dh3, dh2_all, dh1_all, i_sums, f_sums, dz_quarter, map_zero, map_two, map_three = kernel_call(
        functools.partial(back_kernel, sections, count),
        [
            shape_of((padded, wide), BF16),
            shape_of((padded, wide), BF16),
            shape_of((total, narrow), BF16),
            shape_of((total, narrow), BF16),
            shape_of((2, wide), F32),
            shape_of((16, narrow), F32),
            shape_of((total, quarter), BF16),
            paged,
            paged,
            paged,
        ],
        [dy1, res, h3n, image_mask, gains, stats3, w1, spatial, gb_first, pack_all]
        + [h1n_all, h2n_all, stats_all, counts, y2],
        [
            pltpu.VMEM((padded, narrow), BF16),
            pltpu.VMEM((micro, padded, narrow), BF16),
            pltpu.VMEM((micro, padded, quarter), BF16),
            pltpu.VMEM((narrow // 128, 4 * padded, 128), F32),
            pltpu.VMEM((total, narrow), F32),
            pltpu.VMEM((total, narrow), BF16),
        ]
        + sync_scratch(count, [(2, wide), (8, narrow), (8, narrow)])
        + [dma, dma((sections,)), dma((sections,)), dma((sections,))]
        + [dma, dma((sections,)), dma] * 3,
        2,
        2 * total * narrow * 9 * narrow,
        40 * 2**20,
        far_in=(14,),
        far_out=(7, 8, 9),
    )

    terms = {
        "p3": mm(t_dh3, t_a2, "rd,rk->dk").astype(BF16),
        "k2": mm(t_cols, t_dh2, "rk,rn->kn").astype(BF16),
        "p2": mm(u, t_dh1, "rc,rn->cn").astype(BF16),
        "p1": mm(dh3, a2, "rd,rk->dk").astype(BF16),
        "k0": mm(cols_all, dh2_all, "rk,rn->kn").astype(BF16),
        "p0": mm(x_all, dh1_all, "rc,rn->cn").astype(BF16),
    }
    short_term = mm(x_all, dz_quarter, "rc,rd->cd").astype(BF16)

    blank = jnp.zeros((wide,), F32)
    pad = jnp.zeros((wide - 2 * narrow,), F32)
    of_batches = lambda at: jnp.sum(f_sums[at : at + 4], axis=0)
    zero_gain = jnp.where(first, jnp.concatenate([of_batches(12), of_batches(4), pad]), blank)
    zero_bias = jnp.where(first, jnp.concatenate([of_batches(8), of_batches(0), pad]), blank)
    vectors = jnp.stack(
        [
            zero_gain,
            zero_bias,
            i_sums[1],
            i_sums[0],
            jnp.concatenate([t_sums[5, :narrow], t_sums[3, :narrow], pad]),
            jnp.concatenate([t_sums[4, :narrow], t_sums[2, :narrow], pad]),
            t_sums[1],
            t_sums[0],
        ]
    )
    short_sum, proj_sum, taps_sum, vectors, maps = sum_gradients(
        sections,
        count,
        short_term,
        terms,
        vectors.reshape(sections, 2, wide),
        dh1_all,
        proj,
        shortcut,
        (map_zero, map_one, map_two, map_three),
        rows,
    )
    maps = jnp.transpose(maps.reshape(images, pixels, micro, wide), (2, 0, 1, 3))
    proj_grad = proj_sum.reshape(wide, narrow).astype(F32)
    spatial_grad = taps_sum.reshape(9 * narrow, narrow).astype(F32)
    spatial_grad = jnp.where((section % 2) == 0, spatial_grad, jnp.zeros_like(spatial_grad))
    short_grad = short_sum.reshape(wide, wide).astype(F32)
    short_grad = jnp.where(first, short_grad, jnp.zeros_like(short_grad))
    return (
        maps[None],
        proj_grad[None],
        spatial_grad[None],
        short_grad[None],
        vectors[:1],
        vectors[1:],
    )


def solution(mesh):
    return jax.shard_map(
        body,
        mesh=mesh,
        in_specs=(
            P(None, "dp", None, None),
            P(None, "dp", None, None),
            P(None, "dp"),
            P(None, "dp", None),
            P("segment", None, None),
            P("segment", None, None),
            P("segment", None, None),
            P("segment", None),
            P("segment", None),
        ),
        out_specs=(
            P("segment", None, "dp", None, None),
            P("segment", None, None),
            P("segment", None, None),
            P("segment", None, None),
            P("segment", None),
            P("segment", None),
        ),
        check_vma=False,
    )
```

```python
import functools

import jax
import jax.numpy as jnp
import numpy as np
from jax import lax
from jax.experimental import pallas as pl
from jax.experimental.pallas import tpu as pltpu
from jax.sharding import PartitionSpec as P

MAP = 7
EPSILON = 1e-05
OFFSETS = ((-1, -1), (-1, 0), (-1, 1), (0, -1), (0, 0), (0, 1), (1, -1), (1, 0), (1, 1))
MESH = pl.DeviceIdType.MESH
F32 = jnp.float32
BF16 = jnp.bfloat16
VMEM_BYTES = 58 * 2**20
TILE = 256


def greet(count, sections=0):
    segment, me = lax.axis_index("segment"), lax.axis_index("dp")
    barrier = pltpu.get_barrier_semaphore()

    def one(k, carry):
        pl.semaphore_signal(
            barrier, inc=1, device_id=(segment, lax.rem(me + k, count)), device_id_type=MESH
        )
        return carry

    lax.fori_loop(1, count, one, 0)
    for k in range(1, sections):
        pl.semaphore_signal(
            barrier, inc=1, device_id=(jnp.bitwise_xor(segment, k), me), device_id_type=MESH
        )


def greeted(count, sections=1):
    pl.semaphore_wait(pltpu.get_barrier_semaphore(), count - 1 + sections - 1)


def exchange(count, slots, send_sem, recv_sem):
    segment, me = lax.axis_index("segment"), lax.axis_index("dp")

    def copy(k):
        return pltpu.make_async_remote_copy(
            src_ref=slots.at[me],
            dst_ref=slots.at[me],
            send_sem=send_sem.at[k],
            recv_sem=recv_sem.at[k],
            device_id=(segment, lax.rem(me + k, count)),
            device_id_type=MESH,
        )

    def start(k, carry):
        copy(k).start()
        return carry

    def finish(k, carry):
        copy(k).wait_recv()
        copy(k).wait_send()
        return carry

    lax.fori_loop(1, count, start, 0)
    lax.fori_loop(1, count, finish, 0)
    total = slots[0]
    for k in range(1, count):
        total = total + slots[k]
    return total


def mesh_copy(src, dst, send_sem, recv_sem, segment, place):
    return pltpu.make_async_remote_copy(
        src_ref=src,
        dst_ref=dst,
        send_sem=send_sem,
        recv_sem=recv_sem,
        device_id=(segment, place),
        device_id_type=MESH,
    )


def loop(low, high, body):
    def one(k, carry):
        body(k)
        return carry

    lax.fori_loop(low, high, one, 0)


def sync_scratch(count, shapes):
    out = []
    for shape in shapes:
        out += [
            pltpu.VMEM((count,) + shape, F32),
            pltpu.SemaphoreType.DMA((count,)),
            pltpu.SemaphoreType.DMA((count,)),
        ]
    return out


def kernel_call(kernel, outs, args, scratch, ident, flops, moved, far_in=(), far_out=()):
    params = dict(has_side_effects=True, vmem_limit_bytes=VMEM_BYTES)
    if ident is not None:
        params["collective_id"] = ident
    return pl.pallas_call(
        kernel,
        out_shape=outs,
        in_specs=[
            pl.BlockSpec(memory_space=pl.ANY if i in far_in else pltpu.VMEM) for i in range(len(args))
        ],
        out_specs=[
            pl.BlockSpec(memory_space=pl.ANY if i in far_out else pltpu.VMEM) for i in range(len(outs))
        ],
        scratch_shapes=scratch,
        compiler_params=pltpu.CompilerParams(**params),
        cost_estimate=pl.CostEstimate(flops=flops, bytes_accessed=moved, transcendentals=0),
    )(*args)


def shape_of(shape, dtype):
    return jax.ShapeDtypeStruct(shape, dtype)


def dot(a, b):
    return jnp.dot(a, b, preferred_element_type=F32)


def dot_t(a, b):
    return lax.dot_general(a, b, (((1,), (1,)), ((), ())), preferred_element_type=F32)


def sigmoid(v):
    return 1.0 / (1.0 + jnp.exp(-v))


def slope(v):
    s = sigmoid(v)
    return s * (1.0 + v * (1.0 - s))


def over(width, step, body):
    def one(j, carry):
        body(pl.ds(pl.multiple_of(j * step, step), step))
        return carry

    lax.fori_loop(0, width // step, one, 0)


def lane(at):
    return lax.div(at.start, 128)


def unrolled_shift(ref_value, shift):
    rows = ref_value.shape[0]
    return ref_value if shift % rows == 0 else pltpu.roll(ref_value, (-shift) % rows, 0)


def by_batch(values):
    rows, width = values.shape
    part = jnp.sum(values.reshape(rows // 8, 8, width), axis=0)
    return part[:4] + part[4:]


def spread8(values):
    return jnp.concatenate([values, values], axis=0)[None]


def first_part(
    count, ready, writes, x, w, k, gb, pack, tiles, a2_out, cols, h1n, h2n, stats_out, count_out, act, *sync
):
    s1, send1, recv1, s2, send2, recv2 = sync
    rows, narrow = h1n.shape
    me = lax.axis_index("dp")
    full = act.shape[1]

    def tile8(v):
        return v.reshape(rows // 8, 8, v.shape[1])

    def project(at):
        h = dot(x[...], w[:, at])
        h1n[:, at] = h
        m = pack[:, 0:1] * h
        s1[me, 0:4, at] = by_batch(m)
        s1[me, 4:8, at] = by_batch(m * h)

    over(narrow, TILE, project)
    s1[me, 0:4, narrow:] = jnp.broadcast_to(by_batch(pack[:, 0:1]), (4, 128))
    s1[me, 4:8, narrow:] = jnp.broadcast_to(by_batch(tiles[:, 0:1]), (4, 128))
    ready[0]()
    total = exchange(count, s1, send1, recv1)
    counts = total[:, narrow:]
    count_out[...] = counts
    valid = counts[0:4, 0:1]
    average = total[0:4, :narrow] / valid
    inverse = lax.rsqrt(total[4:8, :narrow] / valid - average * average + EPSILON)
    stats_out[0:4, :] = average
    stats_out[4:8, :] = inverse

    def activate(stat_at, gain_at, source):
        def body(at):
            mean = spread8(stats_out[stat_at : stat_at + 4, at])
            inv = spread8(stats_out[stat_at + 4 : stat_at + 8, at])
            hn = (tile8(source[:, at]) - mean) * inv
            source[:, at] = hn.reshape(rows, hn.shape[2])
            n = gb[gain_at : gain_at + 1, at][None] * hn + gb[gain_at + 1 : gain_at + 2, at][None]
            n = n.reshape(rows, n.shape[2])
            act[lane(at), 0:rows, :] = pack[:, 0:1] * (n * sigmoid(n))

        return body

    over(narrow, 128, activate(0, 0, h1n))

    for t, (vertical, lateral) in enumerate(OFFSETS):
        shift = 4 * (7 * vertical + lateral)

        def place(j, carry, t=t, shift=shift):
            at = pl.ds(pl.multiple_of(j * 128, 128), 128)
            to = pl.ds(pl.multiple_of(t * narrow + j * 128, 128), 128)
            moved = unrolled_shift(act[j, 0:rows, :], shift)
            cols[:, to] = (pack[:, 1 + t : 2 + t] * moved).astype(BF16)
            return carry

        lax.fori_loop(0, narrow // 128, place, 0)

    def convolve(at):
        h = dot(cols[...], k[:, at])
        h2n[:, at] = h
        m = pack[:, 0:1] * h
        s2[me, 0:4, at] = by_batch(m)
        s2[me, 4:8, at] = by_batch(m * h)

    for write in writes:
        write.start()
    over(narrow, TILE, convolve)
    ready[1]()
    total = exchange(count, s2, send2, recv2)
    average = total[0:4] / valid
    stats_out[8:12, :] = average
    stats_out[12:16, :] = lax.rsqrt(total[4:8] / valid - average * average + EPSILON)
    over(narrow, 128, activate(8, 2, h2n))
    act[:, rows:, :] = jnp.zeros((narrow // 128, full - rows, 128), F32)
    for m in range(4):

        def pick(j, carry, m=m):
            at = pl.ds(pl.multiple_of(j * 128, 128), 128)
            a2_out[m, :, at] = act[j, pl.ds(m, full // 4, stride=4), :].astype(BF16)
            return carry

        lax.fori_loop(0, narrow // 128, pick, 0)


def residual_part(x, w, out, hold):
    rows, full, quarter = x.shape[0], hold.shape[1], out.shape[2]
    hold[:, rows:, :] = jnp.zeros((quarter // 128, full - rows, 128), F32)

    def body(at):
        value = dot(x[...], w[:, at])
        for part in range(TILE // 128):
            hold[lane(at) + part, 0:rows, :] = value[:, part * 128 : part * 128 + 128]

    over(quarter, TILE, body)
    for m in range(4):

        def pick(j, carry, m=m):
            at = pl.ds(pl.multiple_of(j * 128, 128), 128)
            out[m, :, at] = hold[j, pl.ds(m, full // 4, stride=4), :].astype(BF16)
            return carry

        lax.fori_loop(0, quarter // 128, pick, 0)


def norm_sums(slots, me, at, masked, h):
    slots[me, 0:1, at] = jnp.sum(masked, axis=0, keepdims=True)
    slots[me, 1:2, at] = jnp.sum(masked * h, axis=0, keepdims=True)


def finish_stats(total, valid, stats_out, at_row):
    average = total[0:1] / valid
    width = average.shape[1]
    stats_out[at_row : at_row + 1, 0:width] = average
    stats_out[at_row + 1 : at_row + 2, 0:width] = lax.rsqrt(
        total[1:2] / valid - average * average + EPSILON
    )


def second_part(
    count, before, a2, w1, res, mask, gb, valid, moves, y_out, u_out, h3n, stats_out, s1, send1, recv1
):
    wide = h3n.shape[1]
    quarter = res.shape[2]
    me = lax.axis_index("dp")

    def project(at):
        h = dot_t(a2[...], w1[at, :])
        h3n[:, at] = h
        norm_sums(s1, me, at, mask[:, 0:1] * h, h)

    over(wide, TILE, project)
    finish_stats(exchange(count, s1, send1, recv1), valid, stats_out, 0)
    before()
    for q in range(wide // quarter):

        def body(j, carry, q=q):
            at = pl.ds(pl.multiple_of(q * quarter + j * 128, 128), 128)
            own = pl.ds(pl.multiple_of(j * 128, 128), 128)
            hn = (h3n[:, at] - stats_out[0:1, at]) * stats_out[1:2, at]
            h3n[:, at] = hn
            z = gb[1, 0:1, at] * hn + gb[1, 1:2, at] + res[q, :, own].astype(F32)
            y_out[:, at] = (mask[:, 0:1] * (z * sigmoid(z))).astype(BF16)
            return carry

        lax.fori_loop(0, quarter // 128, body, 0)

    def permute(at):
        u_out[:, at] = dot(moves[...], y_out[:, at]).astype(BF16)

    over(wide, TILE, permute)


def batch_valid(counts, row):
    me = lax.axis_index("segment")
    value = counts[row : row + 1, 0:1]
    for m in range(1, 4):
        value = jnp.where(me == m, counts[row + m : row + m + 1, 0:1], value)
    return value


def head_kernel(
    sections,
    count,
    x3,
    w,
    short,
    k,
    gb,
    vec,
    pack,
    tiles,
    mask,
    moves,
    stats_out,
    count_out,
    g_out,
    y_out,
    u_out,
    h3n,
    stats3,
    a2_out,
    w1_out,
    res_out,
    x_out,
    cols_out,
    h1n_out,
    h2n_out,
    w3_out,
    w2_out,
    k2_out,
    x,
    cols,
    h1n,
    h2n,
    act,
    a2_all,
    a2,
    wsc,
    w1,
    rq,
    res,
    gslots,
    *rest,
):
    sync, rest = rest[:9], list(rest[9:])
    short_send, short_recv, short_relay_send, short_relay_recv = rest[:4]
    w1_send, w1_recv, w1_relay_send, w1_relay_recv = rest[4:8]
    g_send, g_recv, a2_send, a2_recv, res_send, res_recv, own_sem, out_sem = rest[8:16]
    spread_send, spread_recv, far_send, far_recv, near_send, near_recv, keep_sem = rest[16:]
    me, place = lax.axis_index("segment"), lax.axis_index("dp")
    core = lax.rem(place, 2)
    sibling = place + 1 - 2 * core
    wide = x.shape[1]
    quarter = wide // sections
    half_rows = wide // 2
    mine = pl.ds(pl.multiple_of(core * half_rows, 16), half_rows)
    greet(count, sections)

    odd = lax.rem(lax.div(place, 2), 2)
    beside = place + 2 - 4 * odd
    parts = [("w3", w, w3_out, 3, 0, 1), ("w2", w, w2_out, 2, 0, 1)]
    parts += [("k2", k, k2_out, 2, i, 3) for i in range(3)]

    def part_rows(i, at_odd):
        _, src, _, _, piece, pieces = parts[i]
        fine = src.shape[0] // (4 * pieces)
        start = ((2 * at_odd + core) * pieces + piece) * fine
        return pl.ds(pl.multiple_of(start, 16), fine)

    def spread_copy(i, t):
        _, src, dst, _, _, _ = parts[i]
        at = part_rows(i, odd)
        return mesh_copy(src.at[at], dst.at[at], spread_send.at[i, t], spread_recv.at[i], t, place)

    def far_copy(i):
        dst, at = parts[i][2], part_rows(i, odd)
        return mesh_copy(dst.at[at], dst.at[at], far_send.at[i], far_recv.at[i], me, beside)

    def near_copy(i, second):
        dst = parts[i][2]
        at = part_rows(i, 1 - odd if second else odd)
        sems = near_send.at[i, second], near_recv.at[i, second]
        return mesh_copy(dst.at[at], dst.at[at], *sems, me, sibling)

    keeps = [
        (3, pltpu.make_async_copy(w, w3_out, keep_sem.at[0])),
        (2, pltpu.make_async_copy(w, w2_out, keep_sem.at[1])),
        (2, pltpu.make_async_copy(k, k2_out, keep_sem.at[2])),
    ]

    def spread_start(i):
        owner = parts[i][3]

        @pl.when(me == owner)
        def _():
            for d in (3, 1, 2):
                spread_copy(i, owner ^ d).start()

    def spread_on(i):
        @pl.when(me != parts[i][3])
        def _():
            spread_copy(i, 0).wait_recv()
            far_copy(i).start()
            near_copy(i, 0).start()

    def far_on(i):
        @pl.when(me != parts[i][3])
        def _():
            far_copy(i).wait_recv()
            near_copy(i, 1).start()

    def short_copy(t):
        src = short.at[mine, pl.ds(t * quarter, quarter)]
        return mesh_copy(src, wsc.at[mine], short_send.at[t], short_recv, t, place)

    def w1_copy(t):
        return mesh_copy(w.at[mine], w1.at[mine], w1_send.at[t], w1_recv, t, place)

    short_own = pltpu.make_async_copy(short.at[:, pl.ds(0, quarter)], wsc, own_sem.at[0])
    w1_own = pltpu.make_async_copy(w, w1, own_sem.at[1])
    short_relay = mesh_copy(
        wsc.at[mine], wsc.at[mine], short_relay_send, short_relay_recv, me, sibling
    )
    w1_relay = mesh_copy(w1.at[mine], w1.at[mine], w1_relay_send, w1_relay_recv, me, sibling)

    def g_copy(k_):
        return mesh_copy(
            gslots.at[me],
            gslots.at[me],
            g_send.at[k_],
            g_recv.at[k_],
            jnp.bitwise_xor(me, k_),
            place,
        )

    gslots[me] = vec[...]
    greeted(count, sections)

    @pl.when(me == 0)
    def _():
        for t in (3, 1, 2):
            short_copy(t).start()
        short_own.start()

    @pl.when(me == 1)
    def _():
        for t in (2, 0, 3):
            w1_copy(t).start()
        w1_own.start()

    for k_ in range(1, sections):
        g_copy(k_).start()
    spread_start(0)
    spread_start(1)

    def relayout(j, carry):
        at = pl.ds(pl.multiple_of(j * 128, 128), 128)
        x[:, at] = x3[:, :, at].reshape(x.shape[0], 128)
        return carry

    lax.fori_loop(0, wide // 128, relayout, 0)
    writes = [
        pltpu.make_async_copy(src, dst, out_sem.at[i])
        for i, (src, dst) in enumerate(
            ((x, x_out), (h1n, h1n_out), (cols, cols_out), (h2n, h2n_out))
            + ((a2, a2_out), (w1, w1_out), (res, res_out))
        )
    ]
    writes[0].start()
    first_part(
        count,
        (lambda: spread_start(2), lambda: spread_start(3)),
        writes[1:3],
        x,
        w,
        k,
        gb,
        pack,
        tiles,
        a2_all,
        cols,
        h1n,
        h2n,
        stats_out,
        count_out,
        act,
        *sync[:6],
    )

    writes[3].start()
    spread_start(4)

    def a2_copy(t):
        return mesh_copy(a2_all.at[t], a2, a2_send.at[t], a2_recv, t, place)

    @pl.when(me == 0)
    def _():
        for t in range(1, sections):
            a2_copy(t).start()
        a2[...] = a2_all[0]
        short_own.wait()

    @pl.when(me != 0)
    def _():
        short_copy(0).wait_recv()
        short_relay.start()

    @pl.when(me == 1)
    def _():
        w1_own.wait()

    @pl.when(me != 1)
    def _():
        w1_copy(0).wait_recv()
        w1_relay.start()

    spread_on(0)
    spread_on(1)

    @pl.when(me != 0)
    def _():
        short_relay.wait_recv()

    residual_part(x, wsc, rq, act)

    def res_copy(k_):
        other = jnp.bitwise_xor(me, k_)
        return mesh_copy(
            rq.at[other], res.at[me], res_send.at[k_], res_recv.at[k_], other, place
        )

    for k_ in range(1, sections):
        res_copy(k_).start()
    res[me] = rq[me]
    spread_on(2)

    @pl.when(me != 0)
    def _():
        a2_copy(0).wait_recv()

    @pl.when(me != 1)
    def _():
        w1_relay.wait_recv()

    for k_ in range(1, sections):
        g_copy(k_).wait_recv()
    g_out[...] = gslots[...]

    def before():
        spread_on(3)
        far_on(0)
        far_on(1)
        for k_ in range(1, sections):
            res_copy(k_).wait_recv()

    second_part(
        count,
        before,
        a2,
        w1,
        res,
        mask,
        gslots,
        batch_valid(count_out, 0),
        moves,
        y_out,
        u_out,
        h3n,
        stats3,
        *sync[6:],
    )
    spread_on(4)
    for copy in writes[4:]:
        copy.start()
    for owner, copy in keeps:
        pl.when(me == owner)(copy.start)
    for i in range(2, len(parts)):
        far_on(i)
    for k_ in range(1, sections):
        g_copy(k_).wait_send()
        res_copy(k_).wait_send()

    @pl.when(me == 0)
    def _():
        for t in range(1, sections):
            short_copy(t).wait_send()
            a2_copy(t).wait_send()

    @pl.when(me != 0)
    def _():
        short_relay.wait_send()

    @pl.when(me == 1)
    def _():
        for t in (0, 2, 3):
            w1_copy(t).wait_send()

    @pl.when(me != 1)
    def _():
        w1_relay.wait_send()

    for i in range(len(parts)):
        owner = parts[i][3]

        @pl.when(me == owner)
        def _(i=i, owner=owner):
            for d in (1, 2, 3):
                spread_copy(i, owner ^ d).wait_send()

        @pl.when(me != owner)
        def _(i=i):
            far_copy(i).wait_send()
            near_copy(i, 0).wait()
            near_copy(i, 1).wait()

    for owner, copy in keeps:
        pl.when(me == owner)(copy.wait)
    for copy in writes:
        copy.wait()


def back_sums(slots, me, at, grad, hn):
    slots[me, 0:1, at] = jnp.sum(grad, axis=0, keepdims=True)
    slots[me, 1:2, at] = jnp.sum(grad * hn, axis=0, keepdims=True)


def map_sender(sections, src, dst, owner, send_sem, recv_sem, own_sem):
    me, place = lax.axis_index("segment"), lax.axis_index("dp")
    own = pltpu.make_async_copy(src, dst.at[me], own_sem)

    def copy(k):
        return mesh_copy(src, dst.at[me], send_sem, recv_sem.at[k], owner, place)

    def start():
        @pl.when(me == owner)
        def _():
            own.start()

        for k in range(1, sections):

            @pl.when(me == owner ^ k)
            def _(k=k):
                copy(k).start()

    def finish():
        @pl.when(me == owner)
        def _():
            own.wait()
            for k in range(1, sections):
                copy(k).wait_recv()

        @pl.when(me != owner)
        def _():
            copy(0).wait_send()

    return start, finish


def tile_kernel(
    sections,
    count,
    u,
    w2,
    k2,
    w3,
    og3,
    pack,
    gains,
    counts,
    back,
    y1,
    y_out,
    a2,
    cols,
    dh3,
    dh2,
    dh1,
    dy,
    sums_out,
    map_one,
    map_three,
    h1n,
    h2n,
    h3n,
    act,
    dz,
    stats,
    og,
    map_send,
    map_recv,
    map_own,
    three_send,
    three_recv,
    three_own,
    *sync,
):
    s1, send1, recv1, s2, send2, recv2, s3, send3, recv3 = sync[:9]
    b3, bsend3, brecv3, b2, bsend2, brecv2, b1, bsend1, brecv1 = sync[9:]
    rows, wide = u.shape
    narrow = h1n.shape[1]
    me = lax.axis_index("dp")
    section = lax.axis_index("segment")
    valid = batch_valid(counts, 4)
    gb3 = gains.at[3]

    def gb2(row, at):
        return gains[2, row % 2 : row % 2 + 1, pl.ds(at.start + row // 2 * narrow, at.size)]

    greet(count, sections)

    def project(at):
        h = dot(u[...], w2[:, at])
        h1n[:, at] = h
        norm_sums(s1, me, at, pack[:, 0:1] * h, h)

    over(narrow, TILE, project)
    greeted(count, sections)
    send_map, wait_map = map_sender(sections, y1, map_one, 1, map_send, map_recv, map_own)
    send_map()
    real = og3.shape[0]
    for m in range(sections):

        @pl.when(section == m)
        def _(m=m):
            def one(j, carry):
                at = pl.ds(pl.multiple_of(j * 128, 128), 128)
                og[0:real, at] = og3[:, m, at].astype(F32)
                return carry

            lax.fori_loop(0, wide // 128, one, 0)

    og[real:, :] = jnp.zeros((rows - real, wide), F32)
    finish_stats(exchange(count, s1, send1, recv1), valid, stats, 0)

    def activate(row, gain, source, store):
        def body(at):
            hn = (source[:, at] - stats[row : row + 1, at]) * stats[row + 1 : row + 2, at]
            source[:, at] = hn
            n = gb2(gain, at) * hn + gb2(gain + 1, at)
            store(at, pack[:, 0:1] * (n * sigmoid(n)))

        return body

    def to_act(at, value):
        act[:, at] = value

    def to_a2(at, value):
        a2[:, at] = value.astype(BF16)

    over(narrow, 128, activate(0, 0, h1n, to_act))
    for t, (vertical, lateral) in enumerate(OFFSETS):
        shift = 7 * vertical + lateral

        def place(j, carry, t=t, shift=shift):
            at = pl.ds(pl.multiple_of(j * 128, 128), 128)
            to = pl.ds(pl.multiple_of(t * narrow + j * 128, 128), 128)
            moved = unrolled_shift(act[:, at], shift)
            cols[:, to] = (pack[:, 1 + t : 2 + t] * moved).astype(BF16)
            return carry

        lax.fori_loop(0, narrow // 128, place, 0)

    def convolve(at):
        h = dot(cols[...], k2[:, at])
        h2n[:, at] = h
        norm_sums(s2, me, at, pack[:, 0:1] * h, h)

    over(narrow, TILE, convolve)
    finish_stats(exchange(count, s2, send2, recv2), valid, stats, 2)
    over(narrow, 128, activate(2, 2, h2n, to_a2))

    def expand(at):
        h = dot_t(a2[...], w3[at, :])
        h3n[:, at] = h
        norm_sums(s3, me, at, pack[:, 0:1] * h, h)

    over(wide, TILE, expand)
    finish_stats(exchange(count, s3, send3, recv3), valid, stats, 4)

    def result(at):
        hn = (h3n[:, at] - stats[4:5, at]) * stats[5:6, at]
        h3n[:, at] = hn
        z = gb3[0:1, at] * hn + gb3[1:2, at] + u[:, at].astype(F32)
        s = sigmoid(z)
        m = pack[:, 0:1]
        y_out[:, at] = (m * (z * s)).astype(BF16)
        grad = (og[:, at] * m * (s * (1.0 + z * (1.0 - s)))).astype(BF16)
        dz[:, at] = grad
        grad = grad.astype(F32)
        back_sums(b3, me, at, grad, hn)

    over(wide, 128, result)
    send_three, wait_three = map_sender(
        sections, y_out, map_three, 3, three_send, three_recv, three_own
    )
    send_three()
    total = exchange(count, b3, bsend3, brecv3)
    sums_out[0:2, :] = total

    def through(at):
        offset, scale = sums_out[0:1, at], sums_out[1:2, at]
        dh3[:, at] = (
            pack[:, 0:1]
            * gb3[0:1, at]
            * stats[5:6, at]
            * (dz[:, at].astype(F32) - (offset + h3n[:, at] * scale) / valid)
        ).astype(BF16)

    over(wide, 128, through)

    def into_two(at):
        grad = dot(dh3[...], w3[:, at]).astype(BF16).astype(F32)
        hn = h2n[:, at]
        n = gb2(2, at) * hn + gb2(3, at)
        grad = grad * pack[:, 0:1] * slope(n)
        act[:, at] = grad
        back_sums(b2, me, at, grad, hn)

    over(narrow, TILE, into_two)
    total = exchange(count, b2, bsend2, brecv2)
    sums_out[2:4, 0:narrow] = total

    def through_two(at):
        offset, scale = sums_out[2:3, at], sums_out[3:4, at]
        grad = (
            pack[:, 0:1]
            * gb2(2, at)
            * stats[3:4, at]
            * (act[:, at] - (offset + h2n[:, at] * scale) / valid)
        )
        dh2[:, at] = grad.astype(BF16)
        act[:, at] = dh2[:, at].astype(F32)

    over(narrow, 128, through_two)
    h2n[...] = jnp.zeros((rows, narrow), F32)
    for t, (vertical, lateral) in enumerate(OFFSETS):
        shift = -(7 * vertical + lateral)
        other = 8 - t

        def place_back(j, carry, t=t, shift=shift, other=other):
            at = pl.ds(pl.multiple_of(j * 128, 128), 128)
            moved = unrolled_shift(act[:, at], shift)
            dy[:, at] = (pack[:, 1 + other : 2 + other] * moved).astype(BF16)
            return carry

        lax.fori_loop(0, narrow // 128, place_back, 0)

        def gather(at, t=t):
            row = pl.ds(pl.multiple_of(t * narrow + at.start, TILE), TILE)
            h2n[:, at] += dot_t(dy[:, 0:narrow], k2[row, :])

        over(narrow, TILE, gather)

    def into_one(at):
        hn = h1n[:, at]
        n = gb2(0, at) * hn + gb2(1, at)
        grad = h2n[:, at] * pack[:, 0:1] * slope(n)
        act[:, at] = grad
        back_sums(b1, me, at, grad, hn)

    over(narrow, 128, into_one)
    total = exchange(count, b1, bsend1, brecv1)
    sums_out[4:6, 0:narrow] = total

    def through_one(at):
        offset, scale = sums_out[4:5, at], sums_out[5:6, at]
        dh1[:, at] = (
            pack[:, 0:1]
            * gb2(0, at)
            * stats[1:2, at]
            * (act[:, at] - (offset + h1n[:, at] * scale) / valid)
        ).astype(BF16)

    over(narrow, 128, through_one)

    def into_input(at):
        grad = dot_t(dh1[...], w2[at, :]) + dz[:, at].astype(F32)
        dy[:, at] = dot(back[...], grad.astype(BF16)).astype(BF16)

    over(wide, TILE, into_input)
    wait_map()
    wait_three()


def image_back_part(
    count, after, dy, res, h3n, mask, gb, stats, valid, w1, dz, dh3, da2, sums_out, b3, send3, recv3
):
    wide = dy.shape[1]
    quarter = res.shape[2]
    narrow = da2.shape[1]
    me = lax.axis_index("dp")
    for q in range(wide // quarter):

        def body(j, carry, q=q):
            at = pl.ds(pl.multiple_of(q * quarter + j * 128, 128), 128)
            own = pl.ds(pl.multiple_of(j * 128, 128), 128)
            hn = h3n[:, at]
            z = gb[0:1, at] * hn + gb[1:2, at] + res[q, :, own].astype(F32)
            grad = (dy[:, at].astype(F32) * mask[:, 0:1] * slope(z)).astype(BF16)
            dz[:, at] = grad
            back_sums(b3, me, at, grad.astype(F32), hn)
            return carry

        lax.fori_loop(0, quarter // 128, body, 0)
    after()
    total = exchange(count, b3, send3, recv3)
    sums_out[...] = total

    def through(at):
        offset, scale = sums_out[0:1, at], sums_out[1:2, at]
        dh3[:, at] = (
            mask[:, 0:1]
            * gb[0:1, at]
            * stats[1:2, at]
            * (dz[:, at].astype(F32) - (offset + h3n[:, at] * scale) / valid)
        ).astype(BF16)

    over(wide, 128, through)

    def into(at):
        da2[:, at] = dot(dh3[...], w1[:, at]).astype(BF16)

    over(narrow, TILE, into)


def last_part(
    count, da2, k, gb, pack, h1n, h2n, stats, counts, dh2, dh1, sums_out, act, acc, hold, *sync
):
    b2, send2, recv2, b1, send1, recv1 = sync
    rows, narrow = h1n.shape
    full = act.shape[1]
    me = lax.axis_index("dp")
    valid = counts[0:4, 0:1]

    def tile8(v):
        return v.reshape(rows // 8, 8, v.shape[1])

    for m in range(4):

        def put(j, carry, m=m):
            at = pl.ds(pl.multiple_of(j * 128, 128), 128)
            act[j, pl.ds(m, full // 4, stride=4), :] = da2[m, :, at].astype(F32)
            return carry

        lax.fori_loop(0, narrow // 128, put, 0)

    def into(gain, source, hidden, slots):
        def body(at):
            hn = hidden[:, at]
            n = gb[gain : gain + 1, at] * hn + gb[gain + 1 : gain + 2, at]
            grad = source(at) * pack[:, 0:1] * slope(n)
            act[lane(at), 0:rows, :] = grad
            slots[me, 0:4, at] = by_batch(grad)
            slots[me, 4:8, at] = by_batch(grad * hn)

        return body

    def through(gain, stat_at, row, hidden, out):
        def body(at):
            offset = spread8(sums_out[row : row + 4, at] / valid)
            scale = spread8(sums_out[row + 4 : row + 8, at] / valid)
            inv = spread8(stats[stat_at : stat_at + 4, at])
            g = tile8(act[lane(at), 0:rows, :])
            value = inv * gb[gain : gain + 1, at][None] * (g - (offset + tile8(hidden[:, at]) * scale))
            value = (pack[:, 0:1] * value.reshape(rows, value.shape[2])).astype(BF16)
            out[:, at] = value
            act[lane(at), 0:rows, :] = value.astype(F32)

        return body

    over(narrow, 128, into(2, lambda at: act[lane(at), 0:rows, :], h2n, b2))
    sums_out[0:8, :] = exchange(count, b2, send2, recv2)
    over(narrow, 128, through(2, 12, 0, h2n, dh2))
    acc[...] = jnp.zeros((rows, narrow), F32)
    for t, (vertical, lateral) in enumerate(OFFSETS):
        shift = -4 * (7 * vertical + lateral)
        other = 8 - t

        def place_back(j, carry, t=t, shift=shift, other=other):
            at = pl.ds(pl.multiple_of(j * 128, 128), 128)
            moved = unrolled_shift(act[j, 0:rows, :], shift)
            hold[:, at] = (pack[:, 1 + other : 2 + other] * moved).astype(BF16)
            return carry

        lax.fori_loop(0, narrow // 128, place_back, 0)

        def gather(at, t=t):
            row = pl.ds(pl.multiple_of(t * narrow + at.start, TILE), TILE)
            acc[:, at] += dot_t(hold[...], k[row, :])

        over(narrow, TILE, gather)
    over(narrow, 128, into(0, lambda at: acc[:, at], h1n, b1))
    sums_out[8:16, :] = exchange(count, b1, send1, recv1)
    over(narrow, 128, through(0, 4, 8, h1n, dh1))


def back_kernel(
    sections,
    count,
    dy,
    res,
    h3n,
    mask,
    gains,
    stats3,
    w1,
    k,
    gb,
    pack,
    h1n,
    h2n,
    stats,
    counts,
    dz,
    dh3,
    dh2,
    dh1,
    sums3,
    sums12,
    dzq_out,
    dz_all,
    map_two,
    da2,
    da2_all,
    dzq,
    act,
    acc,
    hold,
    *rest,
):
    sync, rest = rest[:9], list(rest[9:])
    a_send, a_recv, q_send, q_recv = rest[:4]
    maps = [rest[4:7], rest[7:10]]
    me, place = lax.axis_index("segment"), lax.axis_index("dp")
    quarter = dzq.shape[2]
    greet(count, sections)
    send_dz, wait_dz = map_sender(sections, dz, dz_all, 0, *maps[0])
    send_two, wait_two = map_sender(sections, dy, map_two, 2, *maps[1])

    def q_copy(k_):
        other = jnp.bitwise_xor(me, k_)
        at = pl.ds(pl.multiple_of(other * quarter, 128), quarter)
        return mesh_copy(dz.at[:, at], dzq.at[me], q_send.at[k_], q_recv.at[k_], other, place)

    greeted(count, sections)
    send_two()

    def after():
        for k_ in range(1, sections):
            q_copy(k_).start()

    image_back_part(
        count,
        after,
        dy,
        res,
        h3n,
        mask,
        gains.at[1],
        stats3,
        batch_valid(counts, 0),
        w1,
        dz,
        dh3,
        da2,
        sums3,
        *sync[:3],
    )

    def a_copy(k_):
        return mesh_copy(da2, da2_all.at[me], a_send, a_recv.at[k_], 0, place)

    for k_ in range(1, sections):

        @pl.when(me == k_)
        def _(k_=k_):
            a_copy(k_).start()

    send_dz()
    for k_ in range(1, sections):
        q_copy(k_).wait_recv()
    dzq[me] = dz[:, pl.ds(pl.multiple_of(me * quarter, 128), quarter)]
    rows, full = dzq_out.shape[0], act.shape[1]
    for m in range(4):

        def put(j, carry, m=m):
            at = pl.ds(pl.multiple_of(j * 128, 128), 128)
            act[j, pl.ds(m, full // 4, stride=4), :] = dzq[m, :, at].astype(F32)
            return carry

        lax.fori_loop(0, quarter // 128, put, 0)

    def weave(j, carry):
        at = pl.ds(pl.multiple_of(j * 128, 128), 128)
        dzq_out[:, at] = act[j, 0:rows, :].astype(BF16)
        return carry

    lax.fori_loop(0, quarter // 128, weave, 0)

    @pl.when(me == 0)
    def _():
        for k_ in range(1, sections):
            a_copy(k_).wait_recv()
        da2_all[0] = da2[...]

    @pl.when(me != 0)
    def _():
        da2_all[...] = jnp.zeros(da2_all.shape, BF16)

    last_part(
        count, da2_all, k, gb, pack, h1n, h2n, stats, counts, dh2, dh1, sums12, act, acc, hold, *sync[3:]
    )
    for k_ in range(1, sections):
        q_copy(k_).wait_send()

    @pl.when(me != 0)
    def _():
        a_copy(0).wait_send()

    wait_dz()
    wait_two()


SUMS = (("k2", 2, True), ("p3", 3, True), ("p2", 2, True), ("p1", 1, True), ("k0", 0, False), ("p0", 0, False))


def gradient_kernel(
    sections,
    count,
    sh,
    k2,
    p3,
    p2,
    p1,
    k0,
    p0,
    vec,
    dh1,
    w,
    short,
    map_zero,
    map_one,
    map_two,
    map_three,
    sh_out,
    p_out,
    k_out,
    vec_out,
    maps,
    *scratch,
):
    names = [name for name, _, _ in SUMS]
    terms = dict(zip(names, (k2, p3, p2, p1, k0, p0)))
    owner = {name: section for name, section, _ in SUMS}
    spread = {name: part for name, _, part in SUMS}
    depth = count // 2
    me, place = lax.axis_index("segment"), lax.axis_index("dp")
    core, z = lax.rem(place, 2), lax.div(place, 2)
    sibling = place + 1 - 2 * core
    scratch = list(scratch)
    take = lambda: scratch.pop(0)
    half, theirs, planes, total, others, whole = {}, {}, {}, {}, {}, {}
    for name in names:
        half[name], theirs[name] = take(), take()
        if spread[name]:
            planes[name] = take()
        total[name], others[name], whole[name] = take(), take(), take()
    sh_half, sh_theirs, sh_others, sh_whole, vec_slots = take(), take(), take(), take(), take()
    load_sem, a_send, a_recv, b_send, b_recv, c_send, c_recv, d_send, d_recv = (take() for _ in range(9))
    e_send, e_recv, e_own, f_send, f_recv, v_send, v_recv = (take() for _ in range(7))
    pages, s_rows, w_rows, hold, stage, page_sem, s_sem, w_sem, stage_sem = (take() for _ in range(9))
    slot = {name: i for i, name in enumerate(names)}
    last = len(names)

    page_loads = [
        pltpu.make_async_copy(source, pages, page_sem)
        for source in (map_zero, map_one, map_two, map_three)
    ]
    for i, copy in enumerate(page_loads):
        pl.when(me == i)(copy.start)
    wide = pages.shape[2]
    full_rows, map_rows = hold.shape[1], maps.shape[0] * maps.shape[1]

    def tile_loads(j):
        at = pl.ds(pl.multiple_of(j * TILE, TILE), TILE)
        at_slot = lax.rem(j, 2)
        return (
            pltpu.make_async_copy(short.at[at], s_rows.at[at_slot], s_sem.at[at_slot]),
            pltpu.make_async_copy(w.at[at], w_rows.at[at_slot], w_sem.at[at_slot]),
        )

    def tile_store(j):
        at = pl.ds(pl.multiple_of(j * TILE, TILE), TILE)
        at_slot = lax.rem(j, 2)
        return pltpu.make_async_copy(stage.at[at_slot], maps.at[:, :, at], stage_sem.at[at_slot])

    @pl.when(me == 0)
    def _():
        for copy in tile_loads(0):
            copy.start()

    def map_tile(j):
        at = pl.ds(pl.multiple_of(j * TILE, TILE), TILE)
        at_slot = lax.rem(j, 2)

        def weave(m, value):
            for part in range(TILE // 128):
                hold[part, pl.ds(m, full_rows // 4, stride=4), :] = value[
                    :, part * 128 : part * 128 + 128
                ]

        @pl.when(j >= 2)
        def _():
            tile_store(j - 2).wait()

        @pl.when(me == 0)
        def _():
            @pl.when(j + 1 < wide // TILE)
            def _():
                for copy in tile_loads(j + 1):
                    copy.start()

            for copy in tile_loads(j):
                copy.wait()
            for m in range(4):
                weave(m, dot_t(pages[m], s_rows[at_slot]))
            extra = dot_t(dh1[...], w_rows[at_slot])
            for part in range(TILE // 128):
                cols = slice(part * 128, part * 128 + 128)
                value = (hold[part, 0:map_rows, :] + extra[:, cols]).astype(BF16)
                stage[at_slot, :, :, cols] = value.reshape(map_rows // 4, 4, 128)

        @pl.when(me != 0)
        def _():
            for m in range(4):
                weave(m, pages[m, :, at].astype(F32))
            for part in range(TILE // 128):
                cols = slice(part * 128, part * 128 + 128)
                value = hold[part, 0:map_rows, :].astype(BF16)
                stage[at_slot, :, :, cols] = value.reshape(map_rows // 4, 4, 128)

        tile_store(j).start()

    def chip(k):
        return 2 * lax.rem(z + k, depth) + core

    barrier = pltpu.get_barrier_semaphore()
    pl.semaphore_signal(barrier, inc=1, device_id=(me, sibling), device_id_type=MESH)
    for k in range(1, sections):
        pl.semaphore_signal(
            barrier, inc=1, device_id=(jnp.bitwise_xor(me, k), place), device_id_type=MESH
        )
    loop(
        1,
        depth,
        lambda k: pl.semaphore_signal(
            barrier, inc=1, device_id=(me, chip(k)), device_id_type=MESH
        ),
    )
    pl.semaphore_wait(barrier, 1 + sections - 1 + depth - 1)

    def swap(name):
        return mesh_copy(
            terms[name].at[1 - core],
            theirs[name],
            a_send.at[slot[name]],
            a_recv.at[slot[name]],
            me,
            sibling,
        )

    def load(name):
        return pltpu.make_async_copy(terms[name].at[core], half[name], load_sem.at[slot[name]])

    def when_held(name, body):
        if spread[name]:
            body()
        else:
            pl.when(me == owner[name])(body)

    sh_rows = sh_half.shape[0]
    sh_swap = mesh_copy(
        sh.at[1 - core], sh_theirs, a_send.at[last], a_recv.at[last], me, sibling
    )
    sh_load = pltpu.make_async_copy(sh.at[core], sh_half, load_sem.at[last])
    sh_swap.start()
    sh_load.start()

    def vec_copy(k):
        other = jnp.bitwise_xor(me, k)
        return mesh_copy(
            vec.at[other], vec_slots.at[k], v_send.at[k], v_recv.at[k], other, place
        )

    for k in range(1, sections):
        vec_copy(k).start()
    for name in names:

        def begin(name=name):
            swap(name).start()
            load(name).start()

        when_held(name, begin)

    piece = sh_rows // depth
    step = 32

    def sh_at(i):
        return pl.ds(pl.multiple_of(i * piece, 16), piece)

    def sh_send(k):
        to = lax.rem(z + k, depth)
        return mesh_copy(
            sh_half.at[sh_at(to)],
            sh_others.at[k],
            c_send.at[last, k],
            c_recv.at[last, k],
            me,
            2 * to + core,
        )

    sh_load.wait()
    sh_swap.wait_recv()

    def sh_add(i):
        at = pl.ds(pl.multiple_of(i * step, step), step)
        sh_half[at, :] = (sh_half[at, :].astype(F32) + sh_theirs[at, :].astype(F32)).astype(BF16)

    loop(0, sh_rows // step, sh_add)
    loop(1, depth, lambda k: sh_send(k).start())

    def to_section(name, k):
        other = jnp.bitwise_xor(me, k)
        target = planes[name].at[k] if spread[name] else total[name]
        return mesh_copy(
            half[name].at[other],
            target,
            b_send.at[slot[name], k],
            b_recv.at[slot[name], k],
            other,
            place,
        )

    for name in names:

        def combine(name=name):
            load(name).wait()
            swap(name).wait_recv()

            def add(i):
                q, y = lax.div(i, depth), lax.rem(i, depth)
                half[name][q, y] = (
                    half[name][q, y].astype(F32) + theirs[name][q, y].astype(F32)
                ).astype(BF16)

            loop(0, sections * depth, add)
            for k in range(1, sections):
                to_section(name, k).start()

        when_held(name, combine)

    for i, copy in enumerate(page_loads):
        pl.when(me == i)(copy.wait)
    loop(0, 2, map_tile)

    loop(1, depth, lambda k: sh_send(k).wait_recv())
    mine = sh_at(z)
    acc = sh_half[mine, :].astype(F32)
    for k in range(1, depth):
        acc = acc + sh_others[k].astype(F32)
    sh_whole[mine, :] = acc.astype(BF16)

    def sh_share(k):
        return mesh_copy(
            sh_whole.at[mine],
            sh_whole.at[mine],
            d_send.at[last, k],
            d_recv.at[last, k],
            me,
            chip(k),
        )

    loop(1, depth, lambda k: sh_share(k).start())
    loop(2, wide // TILE, map_tile)

    def to_chip(name, k):
        to = lax.rem(z + k, depth)
        return mesh_copy(
            total[name].at[to],
            others[name].at[k],
            c_send.at[slot[name], k],
            c_recv.at[slot[name], k],
            me,
            2 * to + core,
        )

    for name in names:
        if spread[name]:
            for k in range(1, sections):
                to_section(name, k).wait_recv()

            def plane_add(y, name=name):
                acc = half[name][me, y].astype(F32)
                for k in range(1, sections):
                    acc = acc + planes[name][k, y].astype(F32)
                total[name][y] = acc.astype(BF16)

            loop(0, depth, plane_add)
        else:

            @pl.when(me == owner[name])
            def _(name=name):
                def keep(y):
                    total[name][y] = half[name][owner[name], y]

                loop(0, depth, keep)

            for k in range(1, sections):

                @pl.when(me == owner[name] ^ k)
                def _(name=name, k=k):
                    to_section(name, k).wait_recv()

        loop(1, depth, lambda k, name=name: to_chip(name, k).start())

    def sh_deliver(k):
        at = pl.ds(pl.multiple_of(me * sh_whole.shape[1], 128), sh_whole.shape[1])
        return mesh_copy(
            sh_whole,
            sh_out.at[core, :, at],
            e_send.at[last],
            e_recv.at[last, k],
            0,
            place,
        )

    loop(1, depth, lambda k: sh_share(k).wait_recv())
    at_zero = pl.ds(0, sh_whole.shape[1])
    sh_keep = pltpu.make_async_copy(sh_whole, sh_out.at[core, :, at_zero], e_own.at[last])

    @pl.when(me == 0)
    def _():
        sh_keep.start()

    for k in range(1, sections):

        @pl.when(me == k)
        def _(k=k):
            sh_deliver(k).start()

    def share(name, k):
        return mesh_copy(
            whole[name].at[z],
            whole[name].at[z],
            d_send.at[slot[name], k],
            d_recv.at[slot[name], k],
            me,
            chip(k),
        )

    for name in names:
        loop(1, depth, lambda k, name=name: to_chip(name, k).wait_recv())
        acc = total[name][z].astype(F32)
        for k in range(1, depth):
            acc = acc + others[name][k].astype(F32)
        whole[name][z] = acc.astype(BF16)
        loop(1, depth, lambda k, name=name: share(name, k).start())

    def final(name):
        return k_out if name[0] == "k" else p_out

    def deliver(name, k):
        return mesh_copy(
            whole[name],
            final(name).at[core, me],
            e_send.at[slot[name]],
            e_recv.at[slot[name], k],
            owner[name],
            place,
        )

    def keep_own(name):
        return pltpu.make_async_copy(whole[name], final(name).at[core, me], e_own.at[slot[name]])

    for name in names:
        loop(1, depth, lambda k, name=name: share(name, k).wait_recv())

        @pl.when(me == owner[name])
        def _(name=name):
            keep_own(name).start()

        for k in range(1, sections):

            @pl.when(me == owner[name] ^ k)
            def _(name=name, k=k):
                deliver(name, k).start()

    def cross(name):
        return mesh_copy(
            final(name).at[core],
            final(name).at[core],
            f_send.at[slot[name]],
            f_recv.at[slot[name]],
            me,
            sibling,
        )

    sh_cross = mesh_copy(
        sh_out.at[core], sh_out.at[core], f_send.at[last], f_recv.at[last], me, sibling
    )

    @pl.when(me == 0)
    def _():
        sh_keep.wait()
        for k in range(1, sections):
            sh_deliver(k).wait_recv()
        sh_cross.start()

    for name in names:

        @pl.when(me == owner[name])
        def _(name=name):
            keep_own(name).wait()
            for k in range(1, sections):
                deliver(name, k).wait_recv()
            cross(name).start()

    for k in range(1, sections):
        vec_copy(k).wait_recv()
    sums = vec[me]
    for k in range(1, sections):
        sums = sums + vec_slots[k]
    vec_out[...] = sums

    tile_store(wide // TILE - 2).wait()
    tile_store(wide // TILE - 1).wait()
    for k in range(1, sections):
        vec_copy(k).wait_send()
    sh_swap.wait_send()
    loop(1, depth, lambda k: sh_send(k).wait_send())
    loop(1, depth, lambda k: sh_share(k).wait_send())

    @pl.when(me == 0)
    def _():
        sh_cross.wait()

    @pl.when(me != 0)
    def _():
        sh_deliver(0).wait_send()

    for name in names:

        def sent(name=name):
            swap(name).wait_send()
            for k in range(1, sections):
                to_section(name, k).wait_send()

        when_held(name, sent)
        loop(1, depth, lambda k, name=name: to_chip(name, k).wait_send())
        loop(1, depth, lambda k, name=name: share(name, k).wait_send())

        @pl.when(me == owner[name])
        def _(name=name):
            cross(name).wait()

        @pl.when(me != owner[name])
        def _(name=name):
            deliver(name, 0).wait_send()


def sum_gradients(sections, count, short, terms, vectors, dh1, w, weights, map_sources, real):
    narrow = short.shape[1]
    depth = count // 2
    args, scratch = [], []
    for name, _, part in SUMS:
        rows = terms[name].shape[0]
        fine = rows // (2 * sections * depth)
        args.append(terms[name].reshape(2, sections, depth, fine, narrow))
        shapes = [(sections, depth, fine, narrow)] * 2
        if part:
            shapes.append((sections, depth, fine, narrow))
        shapes += [(depth, fine, narrow)] * 3
        scratch += [pltpu.VMEM(a, BF16) for a in shapes]
    sh_rows = short.shape[0] // 2
    scratch += [
        pltpu.VMEM((sh_rows, narrow), BF16),
        pltpu.VMEM((sh_rows, narrow), BF16),
        pltpu.VMEM((depth, sh_rows // depth, narrow), BF16),
        pltpu.VMEM((sh_rows, narrow), BF16),
        pltpu.VMEM((sections,) + vectors.shape[1:], F32),
    ]
    kinds = len(SUMS) + 1
    for shape in [(kinds,)] * 3 + [(kinds, sections)] * 2 + [(kinds, depth)] * 4:
        scratch.append(pltpu.SemaphoreType.DMA(shape))
    for shape in [(kinds,), (kinds, sections), (kinds,), (kinds,), (kinds,), (sections,), (sections,)]:
        scratch.append(pltpu.SemaphoreType.DMA(shape))
    wide = w.shape[0]
    padded = map_sources[0].shape[1]
    scratch += [
        pltpu.VMEM(map_sources[0].shape, BF16),
        pltpu.VMEM((2, TILE, wide), BF16),
        pltpu.VMEM((2, TILE, narrow), BF16),
        pltpu.VMEM((TILE // 128, 4 * padded, 128), F32),
        pltpu.VMEM((2, real, 4, TILE), BF16),
        pltpu.SemaphoreType.DMA,
        pltpu.SemaphoreType.DMA((2,)),
        pltpu.SemaphoreType.DMA((2,)),
        pltpu.SemaphoreType.DMA((2,)),
    ]
    hbm = pl.BlockSpec(memory_space=pl.ANY)
    vmem = pl.BlockSpec(memory_space=pltpu.VMEM)
    proj_shape = args[1].shape
    taps_shape = args[0].shape
    return pl.pallas_call(
        functools.partial(gradient_kernel, sections, count),
        out_shape=[
            shape_of((2, sh_rows, narrow * sections), BF16),
            shape_of(proj_shape, BF16),
            shape_of(taps_shape, BF16),
            shape_of(vectors.shape[1:], F32),
            shape_of((real, 4, wide), BF16),
        ],
        in_specs=[hbm] * 7 + [vmem, vmem] + [hbm] * 6,
        out_specs=[hbm, hbm, hbm, vmem, hbm],
        scratch_shapes=scratch,
        compiler_params=pltpu.CompilerParams(
            has_side_effects=True, vmem_limit_bytes=VMEM_BYTES, collective_id=5
        ),
        cost_estimate=pl.CostEstimate(flops=0, bytes_accessed=400 * 2**20, transcendentals=0),
    )(short.reshape(2, sh_rows, narrow), *args, vectors, dh1, w, weights, *map_sources)


def layouts(resolution_ids, order_ids):
    pixels = jnp.arange(MAP * MAP, dtype=jnp.int32)
    row_of = pixels // MAP
    column_of = pixels % MAP
    extent = 5 + resolution_ids[:, None]
    image_mask = ((row_of[None, :] < extent) & (column_of[None, :] < extent)).astype(F32)
    inside = (row_of < 6) & (column_of < 6)
    position = jnp.where(inside, row_of // 2 * 3 + column_of // 2, 0)
    onehot_tile = (position[:, None] == jnp.arange(9)[None, :]).astype(jnp.int32)
    picked = jnp.sum(onehot_tile[None] * order_ids[:, None, :], axis=2)
    row_to = 2 * (picked // 3) + row_of % 2
    column_to = 2 * (picked % 3) + column_of % 2
    target = row_to * MAP + column_to
    tile_mask = (inside & (row_to < extent) & (column_to < extent)).astype(F32)
    return image_mask, tile_mask, jnp.where(inside, target, -1)


def tap_tables(tiled):
    lattice = np.arange(MAP)
    tables = []
    for vertical, lateral in OFFSETS:
        row, column = lattice + vertical, lattice + lateral
        in_row = (row >= 0) & (row < MAP)
        in_column = (column >= 0) & (column < MAP)
        if tiled:
            in_row &= row // 2 == lattice // 2
            in_column &= column // 2 == lattice // 2
        tables.append((in_row[:, None] & in_column[None, :]).reshape(-1))
    return np.stack(tables, axis=1).astype(np.float32)


def mm(a, b, dims="rk,kn->rn"):
    return jnp.einsum(dims, a, b, preferred_element_type=F32)


def body(
    layer_input,
    output_grad,
    resolution,
    tile_order,
    proj_weight,
    spatial_weight,
    shortcut_weight,
    bn_gain,
    bn_bias,
):
    micro, images, pixels, wide = layer_input.shape
    narrow = proj_weight.shape[2]
    rows = images * pixels
    padded = -(-rows // 16) * 16
    sections = lax.axis_size("segment")
    count = lax.axis_size("dp")
    section = lax.axis_index("segment")
    first = section == 0
    proj, spatial, shortcut = proj_weight[0], spatial_weight[0], shortcut_weight[0]
    pick = lambda a: lax.dynamic_index_in_dim(a, section, 0, keepdims=False)

    image_masks, tile_masks, targets = layouts(
        resolution.reshape(-1), tile_order.reshape(micro * images, -1)
    )
    interleave = lambda a: jnp.transpose(a.reshape(micro, rows), (1, 0)).reshape(rows * micro, 1)
    taps_image = np.tile(np.repeat(tap_tables(False), micro, axis=0), (images, 1))
    pack_all = jnp.concatenate(
        [interleave(image_masks), jnp.asarray(taps_image), jnp.zeros((rows * micro, 6), F32)], axis=1
    )
    tiles_all = interleave(tile_masks)
    pad_rows = lambda a: jnp.pad(a, ((0, padded - rows), (0, 0)))
    image_mask = pad_rows(pick(image_masks.reshape(micro, rows, 1)))
    tile_mask = pad_rows(pick(tile_masks.reshape(micro, rows, 1)))
    taps_tile = np.pad(np.tile(tap_tables(True), (images, 1)), ((0, padded - rows), (0, 6)))
    pack_tile = jnp.concatenate([tile_mask, jnp.asarray(taps_tile)], axis=1)
    target = pick(targets.reshape(micro, images, pixels))
    base = (jnp.arange(images) * pixels)[:, None]
    target = jnp.where(target >= 0, target + base, -1).reshape(rows)
    target = jnp.pad(target, (0, padded - rows), constant_values=-1)
    index = jnp.arange(padded)
    moves = (target[:, None] == index[None, :]).astype(BF16)
    moves_back = (target[None, :] == index[:, None]).astype(BF16)

    x_in = jnp.transpose(layer_input, (1, 2, 0, 3)).reshape(rows, micro, wide)
    og_in = jnp.transpose(output_grad, (1, 2, 0, 3)).reshape(rows, micro, wide)
    gb_first = jnp.stack(
        [bn_gain[0, :narrow], bn_bias[0, :narrow]]
        + [bn_gain[0, narrow : 2 * narrow], bn_bias[0, narrow : 2 * narrow]]
    )
    gains_here = jnp.concatenate([bn_gain, bn_bias])
    total = rows * micro
    quarter = wide // sections
    dma = pltpu.SemaphoreType.DMA
    stats_all, counts, gains, y1, u, h3n, stats3, *far = kernel_call(
        functools.partial(head_kernel, sections, count),
        [
            shape_of((16, narrow), F32),
            shape_of((8, 128), F32),
            shape_of((sections, 2, wide), F32),
            shape_of((padded, wide), BF16),
            shape_of((padded, wide), BF16),
            shape_of((padded, wide), F32),
            shape_of((2, wide), F32),
            shape_of((padded, narrow), BF16),
            shape_of((wide, narrow), BF16),
            shape_of((sections, padded, quarter), BF16),
            shape_of((total, wide), BF16),
            shape_of((total, 9 * narrow), BF16),
            shape_of((total, narrow), F32),
            shape_of((total, narrow), F32),
            shape_of((wide, narrow), BF16),
            shape_of((wide, narrow), BF16),
            shape_of((9 * narrow, narrow), BF16),
        ],
        [x_in, proj, shortcut, spatial, gb_first, gains_here, pack_all, tiles_all, image_mask, moves],
        [
            pltpu.VMEM((total, wide), BF16),
            pltpu.VMEM((total, 9 * narrow), BF16),
            pltpu.VMEM((total, narrow), F32),
            pltpu.VMEM((total, narrow), F32),
            pltpu.VMEM((narrow // 128, 4 * padded, 128), F32),
            pltpu.VMEM((micro, padded, narrow), BF16),
            pltpu.VMEM((padded, narrow), BF16),
            pltpu.VMEM((wide, quarter), BF16),
            pltpu.VMEM((wide, narrow), BF16),
            pltpu.VMEM((micro, padded, quarter), BF16),
            pltpu.VMEM((sections, padded, quarter), BF16),
            pltpu.VMEM((sections, 2, wide), F32),
        ]
        + sync_scratch(count, [(8, narrow + 128), (8, narrow), (2, wide)])
        + [dma((sections,)), dma, dma, dma]
        + [dma((sections,)), dma, dma, dma]
        + [dma((sections,)), dma((sections,)), dma((sections,)), dma]
        + [dma((sections,)), dma((sections,)), dma((2,)), dma((7,))]
        + [dma((5, sections)), dma((5,)), dma((5,)), dma((5,))]
        + [dma((5, 2)), dma((5, 2)), dma((3,))],
        0,
        2 * total * (narrow * (wide + 9 * narrow) + wide * quarter),
        60 * 2**20,
        far_in=(2,),
        far_out=tuple(range(7, 17)),
    )
    a2, w1, res, x_all, cols_all, h1n_all, h2n_all, w3, w2, k2 = far
    paged = shape_of((sections, padded, wide), BF16)
    _, t_a2, t_cols, t_dh3, t_dh2, t_dh1, dy1, t_sums, map_one, map_three = kernel_call(
        functools.partial(tile_kernel, sections, count),
        [
            shape_of((padded, wide), BF16),
            shape_of((padded, narrow), BF16),
            shape_of((padded, 9 * narrow), BF16),
            shape_of((padded, wide), BF16),
            shape_of((padded, narrow), BF16),
            shape_of((padded, narrow), BF16),
            shape_of((padded, wide), BF16),
            shape_of((6, wide), F32),
            paged,
            paged,
        ],
        [u, w2, k2, w3, og_in, pack_tile, gains, counts, moves_back, y1],
        [
            pltpu.VMEM((padded, narrow), F32),
            pltpu.VMEM((padded, narrow), F32),
            pltpu.VMEM((padded, wide), F32),
            pltpu.VMEM((padded, narrow), F32),
            pltpu.VMEM((padded, wide), BF16),
            pltpu.VMEM((6, wide), F32),
            pltpu.VMEM((padded, wide), F32),
        ]
        + [dma, dma((sections,)), dma] * 2
        + sync_scratch(
            count, [(2, narrow), (2, narrow), (2, wide), (2, wide), (2, narrow), (2, narrow)]
        ),
        1,
        4 * padded * narrow * (2 * wide + 9 * narrow),
        30 * 2**20,
        far_in=(9,),
        far_out=(8, 9),
    )
    dz, dh3, dh2_all, dh1_all, i_sums, f_sums, dz_quarter, map_zero, map_two = kernel_call(
        functools.partial(back_kernel, sections, count),
        [
            shape_of((padded, wide), BF16),
            shape_of((padded, wide), BF16),
            shape_of((total, narrow), BF16),
            shape_of((total, narrow), BF16),
            shape_of((2, wide), F32),
            shape_of((16, narrow), F32),
            shape_of((total, quarter), BF16),
            paged,
            paged,
        ],
        [dy1, res, h3n, image_mask, gains, stats3, w1, spatial, gb_first, pack_all]
        + [h1n_all, h2n_all, stats_all, counts],
        [
            pltpu.VMEM((padded, narrow), BF16),
            pltpu.VMEM((micro, padded, narrow), BF16),
            pltpu.VMEM((micro, padded, quarter), BF16),
            pltpu.VMEM((narrow // 128, 4 * padded, 128), F32),
            pltpu.VMEM((total, narrow), F32),
            pltpu.VMEM((total, narrow), BF16),
        ]
        + sync_scratch(count, [(2, wide), (8, narrow), (8, narrow)])
        + [dma, dma((sections,)), dma((sections,)), dma((sections,))]
        + [dma, dma((sections,)), dma] * 2,
        2,
        2 * total * narrow * 9 * narrow,
        40 * 2**20,
        far_out=(7, 8),
    )

    terms = {
        "p3": mm(t_dh3, t_a2, "rd,rk->dk").astype(BF16),
        "k2": mm(t_cols, t_dh2, "rk,rn->kn").astype(BF16),
        "p2": mm(u, t_dh1, "rc,rn->cn").astype(BF16),
        "p1": mm(dh3, a2, "rd,rk->dk").astype(BF16),
        "k0": mm(cols_all, dh2_all, "rk,rn->kn").astype(BF16),
        "p0": mm(x_all, dh1_all, "rc,rn->cn").astype(BF16),
    }
    short_term = mm(x_all, dz_quarter, "rc,rd->cd").astype(BF16)

    blank = jnp.zeros((wide,), F32)
    pad = jnp.zeros((wide - 2 * narrow,), F32)
    of_batches = lambda at: jnp.sum(f_sums[at : at + 4], axis=0)
    zero_gain = jnp.where(first, jnp.concatenate([of_batches(12), of_batches(4), pad]), blank)
    zero_bias = jnp.where(first, jnp.concatenate([of_batches(8), of_batches(0), pad]), blank)
    vectors = jnp.stack(
        [
            zero_gain,
            zero_bias,
            i_sums[1],
            i_sums[0],
            jnp.concatenate([t_sums[5, :narrow], t_sums[3, :narrow], pad]),
            jnp.concatenate([t_sums[4, :narrow], t_sums[2, :narrow], pad]),
            t_sums[1],
            t_sums[0],
        ]
    )
    short_sum, proj_sum, taps_sum, vectors, maps = sum_gradients(
        sections,
        count,
        short_term,
        terms,
        vectors.reshape(sections, 2, wide),
        dh1_all,
        proj,
        shortcut,
        (map_zero, map_one, map_two, map_three),
        rows,
    )
    maps = jnp.transpose(maps.reshape(images, pixels, micro, wide), (2, 0, 1, 3))
    proj_grad = proj_sum.reshape(wide, narrow).astype(F32)
    spatial_grad = taps_sum.reshape(9 * narrow, narrow).astype(F32)
    spatial_grad = jnp.where((section % 2) == 0, spatial_grad, jnp.zeros_like(spatial_grad))
    short_grad = short_sum.reshape(wide, wide).astype(F32)
    short_grad = jnp.where(first, short_grad, jnp.zeros_like(short_grad))
    return (
        maps[None],
        proj_grad[None],
        spatial_grad[None],
        short_grad[None],
        vectors[:1],
        vectors[1:],
    )


def solution(mesh):
    return jax.shard_map(
        body,
        mesh=mesh,
        in_specs=(
            P(None, "dp", None, None),
            P(None, "dp", None, None),
            P(None, "dp"),
            P(None, "dp", None),
            P("segment", None, None),
            P("segment", None, None),
            P("segment", None, None),
            P("segment", None),
            P("segment", None),
        ),
        out_specs=(
            P("segment", None, "dp", None, None),
            P("segment", None, None),
            P("segment", None, None),
            P("segment", None, None),
            P("segment", None),
            P("segment", None),
        ),
        check_vma=False,
    )
```

```python
import functools

import jax
import jax.numpy as jnp
import numpy as np
from jax import lax
from jax.experimental import pallas as pl
from jax.experimental.pallas import tpu as pltpu
from jax.sharding import PartitionSpec as P

MAP = 7
EPSILON = 1e-05
OFFSETS = ((-1, -1), (-1, 0), (-1, 1), (0, -1), (0, 0), (0, 1), (1, -1), (1, 0), (1, 1))
MESH = pl.DeviceIdType.MESH
F32 = jnp.float32
BF16 = jnp.bfloat16
VMEM_BYTES = 58 * 2**20
TILE = 256


def greet(count, sections=0):
    segment, me = lax.axis_index("segment"), lax.axis_index("dp")
    barrier = pltpu.get_barrier_semaphore()

    def one(k, carry):
        pl.semaphore_signal(
            barrier, inc=1, device_id=(segment, lax.rem(me + k, count)), device_id_type=MESH
        )
        return carry

    lax.fori_loop(1, count, one, 0)
    for k in range(1, sections):
        pl.semaphore_signal(
            barrier, inc=1, device_id=(jnp.bitwise_xor(segment, k), me), device_id_type=MESH
        )


def greeted(count, sections=1):
    pl.semaphore_wait(pltpu.get_barrier_semaphore(), count - 1 + sections - 1)


def exchange(count, slots, send_sem, recv_sem):
    segment, me = lax.axis_index("segment"), lax.axis_index("dp")

    def copy(k):
        return pltpu.make_async_remote_copy(
            src_ref=slots.at[me],
            dst_ref=slots.at[me],
            send_sem=send_sem.at[k],
            recv_sem=recv_sem.at[k],
            device_id=(segment, lax.rem(me + k, count)),
            device_id_type=MESH,
        )

    def start(k, carry):
        copy(k).start()
        return carry

    def finish(k, carry):
        copy(k).wait_recv()
        copy(k).wait_send()
        return carry

    lax.fori_loop(1, count, start, 0)
    lax.fori_loop(1, count, finish, 0)
    total = slots[0]
    for k in range(1, count):
        total = total + slots[k]
    return total


def mesh_copy(src, dst, send_sem, recv_sem, segment, place):
    return pltpu.make_async_remote_copy(
        src_ref=src,
        dst_ref=dst,
        send_sem=send_sem,
        recv_sem=recv_sem,
        device_id=(segment, place),
        device_id_type=MESH,
    )


def loop(low, high, body):
    def one(k, carry):
        body(k)
        return carry

    lax.fori_loop(low, high, one, 0)


def sync_scratch(count, shapes):
    out = []
    for shape in shapes:
        out += [
            pltpu.VMEM((count,) + shape, F32),
            pltpu.SemaphoreType.DMA((count,)),
            pltpu.SemaphoreType.DMA((count,)),
        ]
    return out


def kernel_call(kernel, outs, args, scratch, ident, flops, moved, far_in=(), far_out=()):
    params = dict(has_side_effects=True, vmem_limit_bytes=VMEM_BYTES)
    if ident is not None:
        params["collective_id"] = ident
    return pl.pallas_call(
        kernel,
        out_shape=outs,
        in_specs=[
            pl.BlockSpec(memory_space=pl.ANY if i in far_in else pltpu.VMEM) for i in range(len(args))
        ],
        out_specs=[
            pl.BlockSpec(memory_space=pl.ANY if i in far_out else pltpu.VMEM) for i in range(len(outs))
        ],
        scratch_shapes=scratch,
        compiler_params=pltpu.CompilerParams(**params),
        cost_estimate=pl.CostEstimate(flops=flops, bytes_accessed=moved, transcendentals=0),
    )(*args)


def shape_of(shape, dtype):
    return jax.ShapeDtypeStruct(shape, dtype)


def dot(a, b):
    return jnp.dot(a, b, preferred_element_type=F32)


def dot_t(a, b):
    return lax.dot_general(a, b, (((1,), (1,)), ((), ())), preferred_element_type=F32)


def sigmoid(v):
    return 1.0 / (1.0 + jnp.exp(-v))


def slope(v):
    s = sigmoid(v)
    return s * (1.0 + v * (1.0 - s))


def over(width, step, body):
    def one(j, carry):
        body(pl.ds(pl.multiple_of(j * step, step), step))
        return carry

    lax.fori_loop(0, width // step, one, 0)


def lane(at):
    return lax.div(at.start, 128)


def unrolled_shift(ref_value, shift):
    rows = ref_value.shape[0]
    return ref_value if shift % rows == 0 else pltpu.roll(ref_value, (-shift) % rows, 0)


def by_batch(values):
    rows, width = values.shape
    part = jnp.sum(values.reshape(rows // 8, 8, width), axis=0)
    return part[:4] + part[4:]


def spread8(values):
    return jnp.concatenate([values, values], axis=0)[None]


def first_part(
    count, writes, x, w, k, gb, pack, tiles, a2_out, cols, h1n, h2n, stats_out, count_out, act, *sync
):
    s1, send1, recv1, s2, send2, recv2 = sync
    rows, narrow = h1n.shape
    me = lax.axis_index("dp")
    full = act.shape[1]

    def tile8(v):
        return v.reshape(rows // 8, 8, v.shape[1])

    def project(at):
        h = dot(x[...], w[:, at])
        h1n[:, at] = h
        m = pack[:, 0:1] * h
        s1[me, 0:4, at] = by_batch(m)
        s1[me, 4:8, at] = by_batch(m * h)

    over(narrow, TILE, project)
    s1[me, 0:4, narrow:] = jnp.broadcast_to(by_batch(pack[:, 0:1]), (4, 128))
    s1[me, 4:8, narrow:] = jnp.broadcast_to(by_batch(tiles[:, 0:1]), (4, 128))
    total = exchange(count, s1, send1, recv1)
    counts = total[:, narrow:]
    count_out[...] = counts
    valid = counts[0:4, 0:1]
    average = total[0:4, :narrow] / valid
    inverse = lax.rsqrt(total[4:8, :narrow] / valid - average * average + EPSILON)
    stats_out[0:4, :] = average
    stats_out[4:8, :] = inverse

    def activate(stat_at, gain_at, source):
        def body(at):
            mean = spread8(stats_out[stat_at : stat_at + 4, at])
            inv = spread8(stats_out[stat_at + 4 : stat_at + 8, at])
            hn = (tile8(source[:, at]) - mean) * inv
            source[:, at] = hn.reshape(rows, hn.shape[2])
            n = gb[gain_at : gain_at + 1, at][None] * hn + gb[gain_at + 1 : gain_at + 2, at][None]
            n = n.reshape(rows, n.shape[2])
            act[lane(at), 0:rows, :] = pack[:, 0:1] * (n * sigmoid(n))

        return body

    over(narrow, 128, activate(0, 0, h1n))

    for t, (vertical, lateral) in enumerate(OFFSETS):
        shift = 4 * (7 * vertical + lateral)

        def place(j, carry, t=t, shift=shift):
            at = pl.ds(pl.multiple_of(j * 128, 128), 128)
            to = pl.ds(pl.multiple_of(t * narrow + j * 128, 128), 128)
            moved = unrolled_shift(act[j, 0:rows, :], shift)
            cols[:, to] = (pack[:, 1 + t : 2 + t] * moved).astype(BF16)
            return carry

        lax.fori_loop(0, narrow // 128, place, 0)

    def convolve(at):
        h = dot(cols[...], k[:, at])
        h2n[:, at] = h
        m = pack[:, 0:1] * h
        s2[me, 0:4, at] = by_batch(m)
        s2[me, 4:8, at] = by_batch(m * h)

    for write in writes:
        write.start()
    over(narrow, TILE, convolve)
    total = exchange(count, s2, send2, recv2)
    average = total[0:4] / valid
    stats_out[8:12, :] = average
    stats_out[12:16, :] = lax.rsqrt(total[4:8] / valid - average * average + EPSILON)
    over(narrow, 128, activate(8, 2, h2n))
    act[:, rows:, :] = jnp.zeros((narrow // 128, full - rows, 128), F32)
    for m in range(4):

        def pick(j, carry, m=m):
            at = pl.ds(pl.multiple_of(j * 128, 128), 128)
            a2_out[m, :, at] = act[j, pl.ds(m, full // 4, stride=4), :].astype(BF16)
            return carry

        lax.fori_loop(0, narrow // 128, pick, 0)


def residual_part(x, w, out, hold):
    rows, full, quarter = x.shape[0], hold.shape[1], out.shape[2]
    hold[:, rows:, :] = jnp.zeros((quarter // 128, full - rows, 128), F32)

    def body(at):
        value = dot(x[...], w[:, at])
        for part in range(TILE // 128):
            hold[lane(at) + part, 0:rows, :] = value[:, part * 128 : part * 128 + 128]

    over(quarter, TILE, body)
    for m in range(4):

        def pick(j, carry, m=m):
            at = pl.ds(pl.multiple_of(j * 128, 128), 128)
            out[m, :, at] = hold[j, pl.ds(m, full // 4, stride=4), :].astype(BF16)
            return carry

        lax.fori_loop(0, quarter // 128, pick, 0)


def norm_sums(slots, me, at, masked, h):
    slots[me, 0:1, at] = jnp.sum(masked, axis=0, keepdims=True)
    slots[me, 1:2, at] = jnp.sum(masked * h, axis=0, keepdims=True)


def finish_stats(total, valid, stats_out, at_row):
    average = total[0:1] / valid
    width = average.shape[1]
    stats_out[at_row : at_row + 1, 0:width] = average
    stats_out[at_row + 1 : at_row + 2, 0:width] = lax.rsqrt(
        total[1:2] / valid - average * average + EPSILON
    )


def second_part(
    count, before, a2, w1, res, mask, gb, valid, moves, y_out, u_out, h3n, stats_out, s1, send1, recv1
):
    wide = h3n.shape[1]
    quarter = res.shape[2]
    me = lax.axis_index("dp")

    def project(at):
        h = dot_t(a2[...], w1[at, :])
        h3n[:, at] = h
        norm_sums(s1, me, at, mask[:, 0:1] * h, h)

    over(wide, TILE, project)
    finish_stats(exchange(count, s1, send1, recv1), valid, stats_out, 0)
    before()
    for q in range(wide // quarter):

        def body(j, carry, q=q):
            at = pl.ds(pl.multiple_of(q * quarter + j * 128, 128), 128)
            own = pl.ds(pl.multiple_of(j * 128, 128), 128)
            hn = (h3n[:, at] - stats_out[0:1, at]) * stats_out[1:2, at]
            h3n[:, at] = hn
            z = gb[1, 0:1, at] * hn + gb[1, 1:2, at] + res[q, :, own].astype(F32)
            y_out[:, at] = (mask[:, 0:1] * (z * sigmoid(z))).astype(BF16)
            return carry

        lax.fori_loop(0, quarter // 128, body, 0)

    def permute(at):
        u_out[:, at] = dot(moves[...], y_out[:, at]).astype(BF16)

    over(wide, TILE, permute)


def batch_valid(counts, row):
    me = lax.axis_index("segment")
    value = counts[row : row + 1, 0:1]
    for m in range(1, 4):
        value = jnp.where(me == m, counts[row + m : row + m + 1, 0:1], value)
    return value


def head_kernel(
    sections,
    count,
    x3,
    w,
    short,
    k,
    gb,
    vec,
    pack,
    tiles,
    mask,
    moves,
    stats_out,
    count_out,
    g_out,
    y_out,
    u_out,
    h3n,
    stats3,
    a2_out,
    w1_out,
    res_out,
    x_out,
    cols_out,
    h1n_out,
    h2n_out,
    w3_out,
    w2_out,
    k2_out,
    x,
    cols,
    h1n,
    h2n,
    act,
    a2_all,
    a2,
    wsc,
    w1,
    rq,
    res,
    gslots,
    *rest,
):
    sync, rest = rest[:9], list(rest[9:])
    short_send, short_recv, short_relay_send, short_relay_recv = rest[:4]
    w1_send, w1_recv, w1_relay_send, w1_relay_recv = rest[4:8]
    g_send, g_recv, a2_send, a2_recv, res_send, res_recv, own_sem, out_sem = rest[8:16]
    spread_send, spread_recv, far_send, far_recv, near_send, near_recv, keep_sem = rest[16:]
    me, place = lax.axis_index("segment"), lax.axis_index("dp")
    core = lax.rem(place, 2)
    sibling = place + 1 - 2 * core
    wide = x.shape[1]
    quarter = wide // sections
    half_rows = wide // 2
    mine = pl.ds(pl.multiple_of(core * half_rows, 16), half_rows)
    greet(count, sections)

    odd = lax.rem(lax.div(place, 2), 2)
    beside = place + 2 - 4 * odd
    parts = [("w3", w, w3_out, 3, 0, 1), ("w2", w, w2_out, 2, 0, 1)]
    parts += [("k2", k, k2_out, 2, i, 3) for i in range(3)]

    def part_rows(i, at_odd):
        _, src, _, _, piece, pieces = parts[i]
        fine = src.shape[0] // (4 * pieces)
        start = ((2 * at_odd + core) * pieces + piece) * fine
        return pl.ds(pl.multiple_of(start, 16), fine)

    def spread_copy(i, t):
        _, src, dst, _, _, _ = parts[i]
        at = part_rows(i, odd)
        return mesh_copy(src.at[at], dst.at[at], spread_send.at[i, t], spread_recv.at[i], t, place)

    def far_copy(i):
        dst, at = parts[i][2], part_rows(i, odd)
        return mesh_copy(dst.at[at], dst.at[at], far_send.at[i], far_recv.at[i], me, beside)

    def near_copy(i, second):
        dst = parts[i][2]
        at = part_rows(i, 1 - odd if second else odd)
        sems = near_send.at[i, second], near_recv.at[i, second]
        return mesh_copy(dst.at[at], dst.at[at], *sems, me, sibling)

    keeps = [
        (3, pltpu.make_async_copy(w, w3_out, keep_sem.at[0])),
        (2, pltpu.make_async_copy(w, w2_out, keep_sem.at[1])),
        (2, pltpu.make_async_copy(k, k2_out, keep_sem.at[2])),
    ]

    def spread_start(i):
        owner = parts[i][3]

        @pl.when(me == owner)
        def _():
            for d in (3, 1, 2):
                spread_copy(i, owner ^ d).start()

    def spread_sent(i):
        for d in (1, 2, 3):
            spread_copy(i, parts[i][3] ^ d).wait_send()

    def spread_on(i):
        @pl.when(me != parts[i][3])
        def _():
            spread_copy(i, 0).wait_recv()
            far_copy(i).start()
            near_copy(i, 0).start()

    def far_on(i):
        @pl.when(me != parts[i][3])
        def _():
            far_copy(i).wait_recv()
            near_copy(i, 1).start()

    def short_copy(t):
        src = short.at[mine, pl.ds(t * quarter, quarter)]
        return mesh_copy(src, wsc.at[mine], short_send.at[t], short_recv, t, place)

    def w1_copy(t):
        return mesh_copy(w.at[mine], w1.at[mine], w1_send.at[t], w1_recv, t, place)

    short_own = pltpu.make_async_copy(short.at[:, pl.ds(0, quarter)], wsc, own_sem.at[0])
    w1_own = pltpu.make_async_copy(w, w1, own_sem.at[1])
    short_relay = mesh_copy(
        wsc.at[mine], wsc.at[mine], short_relay_send, short_relay_recv, me, sibling
    )
    w1_relay = mesh_copy(w1.at[mine], w1.at[mine], w1_relay_send, w1_relay_recv, me, sibling)

    def g_copy(k_):
        return mesh_copy(
            gslots.at[me],
            gslots.at[me],
            g_send.at[k_],
            g_recv.at[k_],
            jnp.bitwise_xor(me, k_),
            place,
        )

    gslots[me] = vec[...]
    greeted(count, sections)

    @pl.when(me == 0)
    def _():
        for t in (3, 1, 2):
            short_copy(t).start()
        short_own.start()

    @pl.when(me == 1)
    def _():
        for t in (2, 0, 3):
            w1_copy(t).start()
        w1_own.start()

    for k_ in range(1, sections):
        g_copy(k_).start()
    for i in range(3):
        spread_start(i)
    for owner, copy in keeps:
        pl.when(me == owner)(copy.start)

    def relayout(j, carry):
        at = pl.ds(pl.multiple_of(j * 128, 128), 128)
        x[:, at] = x3[:, :, at].reshape(x.shape[0], 128)
        return carry

    lax.fori_loop(0, wide // 128, relayout, 0)
    writes = [
        pltpu.make_async_copy(src, dst, out_sem.at[i])
        for i, (src, dst) in enumerate(
            ((x, x_out), (h1n, h1n_out), (cols, cols_out), (h2n, h2n_out))
            + ((a2, a2_out), (w1, w1_out), (res, res_out))
        )
    ]
    writes[0].start()

    def a2_copy(t):
        return mesh_copy(a2_all.at[t], a2, a2_send.at[t], a2_recv, t, place)

    @pl.when(me == 0)
    def _():
        first_part(
            count,
            writes[1:3],
            x,
            w,
            k,
            gb,
            pack,
            tiles,
            a2_all,
            cols,
            h1n,
            h2n,
            stats_out,
            count_out,
            act,
            *sync[:6],
        )
        writes[3].start()
        for t in range(1, sections):
            a2_copy(t).start()
        a2[...] = a2_all[0]
        short_own.wait()

    @pl.when(me != 0)
    def _():
        slots, send1, recv1 = sync[:3]
        narrow = h1n.shape[1]
        stats_out[...] = jnp.zeros(stats_out.shape, F32)
        slots[place, :, 0:narrow] = jnp.zeros((8, narrow), F32)
        slots[place, 0:4, narrow:] = jnp.broadcast_to(by_batch(pack[:, 0:1]), (4, 128))
        slots[place, 4:8, narrow:] = jnp.broadcast_to(by_batch(tiles[:, 0:1]), (4, 128))
        count_out[...] = exchange(count, slots, send1, recv1)[:, narrow:]

    def spread_paced(i, after):
        @pl.when(me == parts[i][3])
        def _():
            spread_sent(after)
            for d in (3, 1, 2):
                spread_copy(i, parts[i][3] ^ d).start()

    spread_on(0)
    spread_paced(3, 1)
    spread_on(1)

    @pl.when(me != 0)
    def _():
        short_copy(0).wait_recv()
        short_relay.start()

    @pl.when(me == 1)
    def _():
        w1_own.wait()

    @pl.when(me != 1)
    def _():
        w1_copy(0).wait_recv()
        w1_relay.start()

    spread_on(2)

    @pl.when(me != 0)
    def _():
        short_relay.wait_recv()

    residual_part(x, wsc, rq, act)

    def res_copy(k_):
        other = jnp.bitwise_xor(me, k_)
        return mesh_copy(
            rq.at[other], res.at[me], res_send.at[k_], res_recv.at[k_], other, place
        )

    for k_ in range(1, sections):
        res_copy(k_).start()
    res[me] = rq[me]
    spread_paced(4, 2)

    @pl.when(me != 0)
    def _():
        a2_copy(0).wait_recv()

    @pl.when(me != 1)
    def _():
        w1_relay.wait_recv()

    for k_ in range(1, sections):
        g_copy(k_).wait_recv()
    g_out[...] = gslots[...]

    def before():
        spread_on(3)
        far_on(0)
        far_on(1)
        for k_ in range(1, sections):
            res_copy(k_).wait_recv()

    second_part(
        count,
        before,
        a2,
        w1,
        res,
        mask,
        gslots,
        batch_valid(count_out, 0),
        moves,
        y_out,
        u_out,
        h3n,
        stats3,
        *sync[6:],
    )
    spread_on(4)
    for copy in writes[4:]:
        copy.start()
    for i in range(2, len(parts)):
        far_on(i)
    for k_ in range(1, sections):
        g_copy(k_).wait_send()
        res_copy(k_).wait_send()

    @pl.when(me == 0)
    def _():
        for t in range(1, sections):
            short_copy(t).wait_send()
            a2_copy(t).wait_send()

    @pl.when(me != 0)
    def _():
        short_relay.wait_send()

    @pl.when(me == 1)
    def _():
        for t in (0, 2, 3):
            w1_copy(t).wait_send()

    @pl.when(me != 1)
    def _():
        w1_relay.wait_send()

    for i in range(len(parts)):
        owner = parts[i][3]

        if i not in (1, 2):
            pl.when(me == owner)(functools.partial(spread_sent, i))

        @pl.when(me != owner)
        def _(i=i):
            far_copy(i).wait_send()
            near_copy(i, 0).wait()
            near_copy(i, 1).wait()

    for owner, copy in keeps:
        pl.when(me == owner)(copy.wait)
    for i, copy in enumerate(writes):
        if i in (1, 2, 3):
            pl.when(me == 0)(copy.wait)
        else:
            copy.wait()


def back_sums(slots, me, at, grad, hn):
    slots[me, 0:1, at] = jnp.sum(grad, axis=0, keepdims=True)
    slots[me, 1:2, at] = jnp.sum(grad * hn, axis=0, keepdims=True)


def map_sender(sections, src, dst, owner, send_sem, recv_sem, own_sem):
    me, place = lax.axis_index("segment"), lax.axis_index("dp")
    own = pltpu.make_async_copy(src, dst.at[me], own_sem)

    def copy(k):
        return mesh_copy(src, dst.at[me], send_sem, recv_sem.at[k], owner, place)

    def start():
        @pl.when(me == owner)
        def _():
            own.start()

        for k in range(1, sections):

            @pl.when(me == owner ^ k)
            def _(k=k):
                copy(k).start()

    def finish():
        @pl.when(me == owner)
        def _():
            own.wait()
            for k in range(1, sections):
                copy(k).wait_recv()

        @pl.when(me != owner)
        def _():
            copy(0).wait_send()

    return start, finish


def tile_kernel(
    sections,
    count,
    u,
    w2,
    k2,
    w3,
    og3,
    pack,
    gains,
    counts,
    back,
    y1,
    y_out,
    a2,
    cols,
    dh3,
    dh2,
    dh1,
    dy,
    sums_out,
    map_one,
    h1n,
    h2n,
    h3n,
    act,
    dz,
    stats,
    og,
    map_send,
    map_recv,
    map_own,
    *sync,
):
    s1, send1, recv1, s2, send2, recv2, s3, send3, recv3 = sync[:9]
    b3, bsend3, brecv3, b2, bsend2, brecv2, b1, bsend1, brecv1 = sync[9:]
    rows, wide = u.shape
    narrow = h1n.shape[1]
    me = lax.axis_index("dp")
    section = lax.axis_index("segment")
    valid = batch_valid(counts, 4)
    gb3 = gains.at[3]

    def gb2(row, at):
        return gains[2, row % 2 : row % 2 + 1, pl.ds(at.start + row // 2 * narrow, at.size)]

    greet(count, sections)

    def project(at):
        h = dot(u[...], w2[:, at])
        h1n[:, at] = h
        norm_sums(s1, me, at, pack[:, 0:1] * h, h)

    over(narrow, TILE, project)
    greeted(count, sections)
    send_map, wait_map = map_sender(sections, y1, map_one, 1, map_send, map_recv, map_own)
    send_map()
    real = og3.shape[0]
    for m in range(sections):

        @pl.when(section == m)
        def _(m=m):
            def one(j, carry):
                at = pl.ds(pl.multiple_of(j * 128, 128), 128)
                og[0:real, at] = og3[:, m, at].astype(F32)
                return carry

            lax.fori_loop(0, wide // 128, one, 0)

    og[real:, :] = jnp.zeros((rows - real, wide), F32)
    finish_stats(exchange(count, s1, send1, recv1), valid, stats, 0)

    def activate(row, gain, source, store):
        def body(at):
            hn = (source[:, at] - stats[row : row + 1, at]) * stats[row + 1 : row + 2, at]
            source[:, at] = hn
            n = gb2(gain, at) * hn + gb2(gain + 1, at)
            store(at, pack[:, 0:1] * (n * sigmoid(n)))

        return body

    def to_act(at, value):
        act[:, at] = value

    def to_a2(at, value):
        a2[:, at] = value.astype(BF16)

    over(narrow, 128, activate(0, 0, h1n, to_act))
    for t, (vertical, lateral) in enumerate(OFFSETS):
        shift = 7 * vertical + lateral

        def place(j, carry, t=t, shift=shift):
            at = pl.ds(pl.multiple_of(j * 128, 128), 128)
            to = pl.ds(pl.multiple_of(t * narrow + j * 128, 128), 128)
            moved = unrolled_shift(act[:, at], shift)
            cols[:, to] = (pack[:, 1 + t : 2 + t] * moved).astype(BF16)
            return carry

        lax.fori_loop(0, narrow // 128, place, 0)

    def convolve(at):
        h = dot(cols[...], k2[:, at])
        h2n[:, at] = h
        norm_sums(s2, me, at, pack[:, 0:1] * h, h)

    over(narrow, TILE, convolve)
    finish_stats(exchange(count, s2, send2, recv2), valid, stats, 2)
    over(narrow, 128, activate(2, 2, h2n, to_a2))

    def expand(at):
        h = dot_t(a2[...], w3[at, :])
        h3n[:, at] = h
        norm_sums(s3, me, at, pack[:, 0:1] * h, h)

    over(wide, TILE, expand)
    finish_stats(exchange(count, s3, send3, recv3), valid, stats, 4)

    def result(at):
        hn = (h3n[:, at] - stats[4:5, at]) * stats[5:6, at]
        h3n[:, at] = hn
        z = gb3[0:1, at] * hn + gb3[1:2, at] + u[:, at].astype(F32)
        s = sigmoid(z)
        m = pack[:, 0:1]
        y_out[:, at] = (m * (z * s)).astype(BF16)
        grad = (og[:, at] * m * (s * (1.0 + z * (1.0 - s)))).astype(BF16)
        dz[:, at] = grad
        grad = grad.astype(F32)
        back_sums(b3, me, at, grad, hn)

    over(wide, 128, result)
    total = exchange(count, b3, bsend3, brecv3)
    sums_out[0:2, :] = total

    def through(at):
        offset, scale = sums_out[0:1, at], sums_out[1:2, at]
        dh3[:, at] = (
            pack[:, 0:1]
            * gb3[0:1, at]
            * stats[5:6, at]
            * (dz[:, at].astype(F32) - (offset + h3n[:, at] * scale) / valid)
        ).astype(BF16)

    over(wide, 128, through)

    def into_two(at):
        grad = dot(dh3[...], w3[:, at]).astype(BF16).astype(F32)
        hn = h2n[:, at]
        n = gb2(2, at) * hn + gb2(3, at)
        grad = grad * pack[:, 0:1] * slope(n)
        act[:, at] = grad
        back_sums(b2, me, at, grad, hn)

    over(narrow, TILE, into_two)
    total = exchange(count, b2, bsend2, brecv2)
    sums_out[2:4, 0:narrow] = total

    def through_two(at):
        offset, scale = sums_out[2:3, at], sums_out[3:4, at]
        grad = (
            pack[:, 0:1]
            * gb2(2, at)
            * stats[3:4, at]
            * (act[:, at] - (offset + h2n[:, at] * scale) / valid)
        )
        dh2[:, at] = grad.astype(BF16)
        act[:, at] = dh2[:, at].astype(F32)

    over(narrow, 128, through_two)
    h2n[...] = jnp.zeros((rows, narrow), F32)
    for t, (vertical, lateral) in enumerate(OFFSETS):
        shift = -(7 * vertical + lateral)
        other = 8 - t

        def place_back(j, carry, t=t, shift=shift, other=other):
            at = pl.ds(pl.multiple_of(j * 128, 128), 128)
            moved = unrolled_shift(act[:, at], shift)
            dy[:, at] = (pack[:, 1 + other : 2 + other] * moved).astype(BF16)
            return carry

        lax.fori_loop(0, narrow // 128, place_back, 0)

        def gather(at, t=t):
            row = pl.ds(pl.multiple_of(t * narrow + at.start, TILE), TILE)
            h2n[:, at] += dot_t(dy[:, 0:narrow], k2[row, :])

        over(narrow, TILE, gather)

    def into_one(at):
        hn = h1n[:, at]
        n = gb2(0, at) * hn + gb2(1, at)
        grad = h2n[:, at] * pack[:, 0:1] * slope(n)
        act[:, at] = grad
        back_sums(b1, me, at, grad, hn)

    over(narrow, 128, into_one)
    total = exchange(count, b1, bsend1, brecv1)
    sums_out[4:6, 0:narrow] = total

    def through_one(at):
        offset, scale = sums_out[4:5, at], sums_out[5:6, at]
        dh1[:, at] = (
            pack[:, 0:1]
            * gb2(0, at)
            * stats[1:2, at]
            * (act[:, at] - (offset + h1n[:, at] * scale) / valid)
        ).astype(BF16)

    over(narrow, 128, through_one)

    def into_input(at):
        grad = dot_t(dh1[...], w2[at, :]) + dz[:, at].astype(F32)
        dy[:, at] = dot(back[...], grad.astype(BF16)).astype(BF16)

    over(wide, TILE, into_input)
    wait_map()


def image_back_part(
    count, after, dy, res, h3n, mask, gb, stats, valid, w1, dz, dh3, da2, sums_out, b3, send3, recv3
):
    wide = dy.shape[1]
    quarter = res.shape[2]
    narrow = da2.shape[1]
    me = lax.axis_index("dp")
    for q in range(wide // quarter):

        def body(j, carry, q=q):
            at = pl.ds(pl.multiple_of(q * quarter + j * 128, 128), 128)
            own = pl.ds(pl.multiple_of(j * 128, 128), 128)
            hn = h3n[:, at]
            z = gb[0:1, at] * hn + gb[1:2, at] + res[q, :, own].astype(F32)
            grad = (dy[:, at].astype(F32) * mask[:, 0:1] * slope(z)).astype(BF16)
            dz[:, at] = grad
            back_sums(b3, me, at, grad.astype(F32), hn)
            return carry

        lax.fori_loop(0, quarter // 128, body, 0)
    after()
    total = exchange(count, b3, send3, recv3)
    sums_out[...] = total

    def through(at):
        offset, scale = sums_out[0:1, at], sums_out[1:2, at]
        dh3[:, at] = (
            mask[:, 0:1]
            * gb[0:1, at]
            * stats[1:2, at]
            * (dz[:, at].astype(F32) - (offset + h3n[:, at] * scale) / valid)
        ).astype(BF16)

    over(wide, 128, through)

    def into(at):
        da2[:, at] = dot(dh3[...], w1[:, at]).astype(BF16)

    over(narrow, TILE, into)


def last_part(
    count, da2, k, gb, pack, h1n, h2n, stats, counts, dh2, dh1, sums_out, act, acc, hold, *sync
):
    b2, send2, recv2, b1, send1, recv1 = sync
    rows, narrow = h1n.shape
    full = act.shape[1]
    me = lax.axis_index("dp")
    valid = counts[0:4, 0:1]

    def tile8(v):
        return v.reshape(rows // 8, 8, v.shape[1])

    for m in range(4):

        def put(j, carry, m=m):
            at = pl.ds(pl.multiple_of(j * 128, 128), 128)
            act[j, pl.ds(m, full // 4, stride=4), :] = da2[m, :, at].astype(F32)
            return carry

        lax.fori_loop(0, narrow // 128, put, 0)

    def into(gain, source, hidden, slots):
        def body(at):
            hn = hidden[:, at]
            n = gb[gain : gain + 1, at] * hn + gb[gain + 1 : gain + 2, at]
            grad = source(at) * pack[:, 0:1] * slope(n)
            act[lane(at), 0:rows, :] = grad
            slots[me, 0:4, at] = by_batch(grad)
            slots[me, 4:8, at] = by_batch(grad * hn)

        return body

    def through(gain, stat_at, row, hidden, out):
        def body(at):
            offset = spread8(sums_out[row : row + 4, at] / valid)
            scale = spread8(sums_out[row + 4 : row + 8, at] / valid)
            inv = spread8(stats[stat_at : stat_at + 4, at])
            g = tile8(act[lane(at), 0:rows, :])
            value = inv * gb[gain : gain + 1, at][None] * (g - (offset + tile8(hidden[:, at]) * scale))
            value = (pack[:, 0:1] * value.reshape(rows, value.shape[2])).astype(BF16)
            out[:, at] = value
            act[lane(at), 0:rows, :] = value.astype(F32)

        return body

    over(narrow, 128, into(2, lambda at: act[lane(at), 0:rows, :], h2n, b2))
    sums_out[0:8, :] = exchange(count, b2, send2, recv2)
    over(narrow, 128, through(2, 12, 0, h2n, dh2))
    acc[...] = jnp.zeros((rows, narrow), F32)
    for t, (vertical, lateral) in enumerate(OFFSETS):
        shift = -4 * (7 * vertical + lateral)
        other = 8 - t

        def place_back(j, carry, t=t, shift=shift, other=other):
            at = pl.ds(pl.multiple_of(j * 128, 128), 128)
            moved = unrolled_shift(act[j, 0:rows, :], shift)
            hold[:, at] = (pack[:, 1 + other : 2 + other] * moved).astype(BF16)
            return carry

        lax.fori_loop(0, narrow // 128, place_back, 0)

        def gather(at, t=t):
            row = pl.ds(pl.multiple_of(t * narrow + at.start, TILE), TILE)
            acc[:, at] += dot_t(hold[...], k[row, :])

        over(narrow, TILE, gather)
    over(narrow, 128, into(0, lambda at: acc[:, at], h1n, b1))
    sums_out[8:16, :] = exchange(count, b1, send1, recv1)
    over(narrow, 128, through(0, 4, 8, h1n, dh1))


def back_kernel(
    sections,
    count,
    dy,
    res,
    h3n,
    mask,
    gains,
    stats3,
    w1,
    k,
    gb,
    pack,
    h1n,
    h2n,
    stats,
    counts,
    p3,
    p2,
    k2,
    y2,
    dz,
    dh3,
    dh2,
    dh1,
    sums3,
    sums12,
    dzq_out,
    p3_out,
    p2_out,
    k2_out,
    dz_all,
    map_two,
    map_three,
    da2,
    da2_all,
    dzq,
    act,
    acc,
    hold,
    *rest,
):
    sync, rest = rest[:9], list(rest[9:])
    halves, theirs, pieces, totals, chips, wholes = (
        rest[:3], rest[3:6], rest[6:9], rest[9:11], rest[11:13], rest[13:16]
    )
    load_sem, swap_send, swap_recv, piece_send, piece_recv, next_send, next_recv, share_send, share_recv, out_sem = rest[16:26]
    rest = rest[26:]
    a_send, a_recv, q_send, q_recv = rest[:4]
    maps = [rest[4:7], rest[7:10], rest[10:13]]
    me, place = lax.axis_index("segment"), lax.axis_index("dp")
    quarter = dzq.shape[2]
    greet(count, sections)
    send_dz, wait_dz = map_sender(sections, dz, dz_all, 0, *maps[0])
    send_two, wait_two = map_sender(sections, dy, map_two, 2, *maps[1])
    send_three, wait_three = map_sender(sections, y2, map_three, 3, *maps[2])

    def q_copy(k_):
        other = jnp.bitwise_xor(me, k_)
        at = pl.ds(pl.multiple_of(other * quarter, 128), quarter)
        return mesh_copy(dz.at[:, at], dzq.at[me], q_send.at[k_], q_recv.at[k_], other, place)

    greeted(count, sections)
    core, z = lax.rem(place, 2), lax.div(place, 2)
    depth = count // 2
    terms = (p3, p2, k2)
    loads = [pltpu.make_async_copy(terms[i].at[core], halves[i], load_sem.at[i]) for i in range(3)]
    swaps = [
        mesh_copy(
            terms[i].at[1 - core],
            theirs[i],
            swap_send.at[i],
            swap_recv.at[i],
            me,
            place + 1 - 2 * core,
        )
        for i in range(3)
    ]
    for i in range(3):
        swaps[i].start()
        loads[i].start()

    def to_section(i, k_):
        other = jnp.bitwise_xor(me, k_)
        return mesh_copy(
            halves[i].at[other],
            pieces[i].at[k_],
            piece_send.at[i, k_],
            piece_recv.at[i, k_],
            other,
            place,
        )

    def to_chip(k_):
        to = lax.rem(z + k_, depth)
        return mesh_copy(
            halves[2].at[:, to],
            pieces[2].at[k_],
            piece_send.at[2, k_],
            piece_recv.at[2, k_],
            me,
            2 * to + core,
        )

    def add_cores(i):
        loads[i].wait()
        swaps[i].wait_recv()

        def add(n):
            q, y = lax.div(n, depth), lax.rem(n, depth)
            halves[i][q, y] = (
                halves[i][q, y].astype(F32) + theirs[i][q, y].astype(F32)
            ).astype(BF16)

        loop(0, sections * depth, add)

    send_three()

    def after():
        return

    image_back_part(
        count,
        after,
        dy,
        res,
        h3n,
        mask,
        gains.at[1],
        stats3,
        batch_valid(counts, 0),
        w1,
        dz,
        dh3,
        da2,
        sums3,
        *sync[:3],
    )

    def a_copy(k_):
        return mesh_copy(da2, da2_all.at[me], a_send, a_recv.at[k_], 0, place)

    for k_ in range(1, sections):

        @pl.when(me == k_)
        def _(k_=k_):
            a_copy(k_).start()

    for i in range(2):
        add_cores(i)
        for k_ in range(1, sections):
            to_section(i, k_).start()
    for k_ in range(1, sections):
        q_copy(k_).start()
    send_dz()
    send_two()
    add_cores(2)
    loop(1, depth, lambda k_: to_chip(k_).start())

    @pl.when(me == 0)
    def _():
        for k_ in range(1, sections):
            a_copy(k_).wait_recv()
        da2_all[0] = da2[...]
        last_part(
            count,
            da2_all,
            k,
            gb,
            pack,
            h1n,
            h2n,
            stats,
            counts,
            dh2,
            dh1,
            sums12,
            act,
            acc,
            hold,
            *sync[3:],
        )

    @pl.when(me != 0)
    def _():
        a_copy(0).wait_send()
        sums12[...] = jnp.zeros(sums12.shape, F32)

    def next_chip(i, k_):
        to = lax.rem(z + k_, depth)
        return mesh_copy(
            totals[i].at[to],
            chips[i].at[k_],
            next_send.at[i, k_],
            next_recv.at[i, k_],
            me,
            2 * to + core,
        )

    def share(i, k_):
        return mesh_copy(
            wholes[i].at[z],
            wholes[i].at[z],
            share_send.at[i, k_],
            share_recv.at[i, k_],
            me,
            2 * lax.rem(z + k_, depth) + core,
        )

    for i in range(2):
        for k_ in range(1, sections):
            to_section(i, k_).wait_recv()

        def p_sum(y, i=i):
            total = halves[i][me, y].astype(F32)
            for k_ in range(1, sections):
                total = total + pieces[i][k_, y].astype(F32)
            totals[i][y] = total.astype(BF16)

        loop(0, depth, p_sum)
        loop(1, depth, lambda k_, i=i: next_chip(i, k_).start())
    loop(1, depth, lambda k_: to_chip(k_).wait_recv())

    def k2_sum(q):
        total = halves[2][q, z].astype(F32)
        for k_ in range(1, depth):
            total = total + pieces[2][k_, q].astype(F32)
        wholes[2][q] = total.astype(BF16)

    loop(0, sections, k2_sum)
    for k_ in range(1, sections):
        q_copy(k_).wait_recv()
    dzq[me] = dz[:, pl.ds(pl.multiple_of(me * quarter, 128), quarter)]
    rows, full = dzq_out.shape[0], act.shape[1]
    for m in range(4):

        def put(j, carry, m=m):
            at = pl.ds(pl.multiple_of(j * 128, 128), 128)
            act[j, pl.ds(m, full // 4, stride=4), :] = dzq[m, :, at].astype(F32)
            return carry

        lax.fori_loop(0, quarter // 128, put, 0)

    def weave(j, carry):
        at = pl.ds(pl.multiple_of(j * 128, 128), 128)
        dzq_out[:, at] = act[j, 0:rows, :].astype(BF16)
        return carry

    lax.fori_loop(0, quarter // 128, weave, 0)
    for i in range(2):
        loop(1, depth, lambda k_, i=i: next_chip(i, k_).wait_recv())
        total = totals[i][z].astype(F32)
        for k_ in range(1, depth):
            total = total + chips[i][k_].astype(F32)
        wholes[i][z] = total.astype(BF16)
        loop(1, depth, lambda k_, i=i: share(i, k_).start())
    outs = []
    for i, out in enumerate((p3_out, p2_out, k2_out)):
        if i < 2:
            loop(1, depth, lambda k_, i=i: share(i, k_).wait_recv())
        outs.append(pltpu.make_async_copy(wholes[i], out, out_sem.at[i]))
        outs[i].start()
    for k_ in range(1, sections):
        q_copy(k_).wait_send()
        for i in range(2):
            to_section(i, k_).wait_send()
    loop(1, depth, lambda k_: to_chip(k_).wait_send())
    for i in range(2):
        loop(1, depth, lambda k_, i=i: next_chip(i, k_).wait_send())
    for i in range(3):
        swaps[i].wait_send()
        if i < 2:
            loop(1, depth, lambda k_, i=i: share(i, k_).wait_send())
        outs[i].wait()
    wait_dz()
    wait_two()
    wait_three()


SUMS = (
    ("k0", 0, "owner"),
    ("p0", 0, "owner"),
    ("p1", 1, "each"),
    ("p3", 3, "done"),
    ("p2", 2, "done"),
    ("k2", 2, "chips"),
)


def gradient_kernel(
    sections,
    count,
    sh,
    k0,
    p0,
    p1,
    p3,
    p2,
    k2,
    vec,
    dh1,
    w,
    short,
    map_zero,
    map_one,
    map_two,
    map_three,
    sh_out,
    p_out,
    k_out,
    vec_out,
    maps,
    *scratch,
):
    names = [name for name, _, _ in SUMS]
    terms = dict(zip(names, (k0, p0, p1, p3, p2, k2)))
    owner = {name: section for name, section, _ in SUMS}
    held = {name: kind for name, _, kind in SUMS}
    fresh = [name for name in names if held[name] in ("owner", "each")]
    depth = count // 2
    me, place = lax.axis_index("segment"), lax.axis_index("dp")
    core, z = lax.rem(place, 2), lax.div(place, 2)
    sibling = place + 1 - 2 * core
    scratch = list(scratch)
    take = lambda: scratch.pop(0)
    half, theirs, planes, total, others, whole = {}, {}, {}, {}, {}, {}
    for name in names:
        if name in fresh:
            half[name], theirs[name] = take(), take()
        if held[name] in ("each", "chips"):
            planes[name] = take()
        if name in fresh:
            total[name], others[name] = take(), take()
        whole[name] = terms[name] if held[name] == "done" else take()
    relay = {name: take() for name in names if owner[name] == 0}
    relay["sh"] = take()
    sh_half, sh_theirs, sh_others, sh_whole, vec_slots = take(), take(), take(), take(), take()
    load_sem, a_send, a_recv, b_send, b_recv, c_send, c_recv, d_send, d_recv = (take() for _ in range(9))
    e_send, e_recv, e_own, f_send, f_recv, v_send, v_recv = (take() for _ in range(7))
    r_send, r_recv = take(), take()
    pages, s_rows, w_rows, hold, stage, page_sem, s_sem, w_sem, stage_sem = (take() for _ in range(9))
    slot = {name: i for i, name in enumerate(names)}
    last = len(names)

    page_loads = [
        pltpu.make_async_copy(source, pages, page_sem)
        for source in (map_zero, map_one, map_two, map_three)
    ]
    for i, copy in enumerate(page_loads):
        pl.when(me == i)(copy.start)
    wide = pages.shape[2]
    full_rows, map_rows = hold.shape[1], maps.shape[0] * maps.shape[1]

    def tile_loads(j):
        at = pl.ds(pl.multiple_of(j * TILE, TILE), TILE)
        at_slot = lax.rem(j, 2)
        return (
            pltpu.make_async_copy(short.at[at], s_rows.at[at_slot], s_sem.at[at_slot]),
            pltpu.make_async_copy(w.at[at], w_rows.at[at_slot], w_sem.at[at_slot]),
        )

    def tile_store(j):
        at = pl.ds(pl.multiple_of(j * TILE, TILE), TILE)
        at_slot = lax.rem(j, 2)
        return pltpu.make_async_copy(stage.at[at_slot], maps.at[:, :, at], stage_sem.at[at_slot])

    @pl.when(me == 0)
    def _():
        for copy in tile_loads(0):
            copy.start()

    def map_tile(j):
        at = pl.ds(pl.multiple_of(j * TILE, TILE), TILE)
        at_slot = lax.rem(j, 2)

        def weave(m, value):
            for part in range(TILE // 128):
                hold[part, pl.ds(m, full_rows // 4, stride=4), :] = value[
                    :, part * 128 : part * 128 + 128
                ]

        @pl.when(j >= 2)
        def _():
            tile_store(j - 2).wait()

        @pl.when(me == 0)
        def _():
            @pl.when(j + 1 < wide // TILE)
            def _():
                for copy in tile_loads(j + 1):
                    copy.start()

            for copy in tile_loads(j):
                copy.wait()
            for m in range(4):
                weave(m, dot_t(pages[m], s_rows[at_slot]))
            extra = dot_t(dh1[...], w_rows[at_slot])
            for part in range(TILE // 128):
                cols = slice(part * 128, part * 128 + 128)
                value = (hold[part, 0:map_rows, :] + extra[:, cols]).astype(BF16)
                stage[at_slot, :, :, cols] = value.reshape(map_rows // 4, 4, 128)

        @pl.when(me != 0)
        def _():
            for m in range(4):
                weave(m, pages[m, :, at].astype(F32))
            for part in range(TILE // 128):
                cols = slice(part * 128, part * 128 + 128)
                value = hold[part, 0:map_rows, :].astype(BF16)
                stage[at_slot, :, :, cols] = value.reshape(map_rows // 4, 4, 128)

        tile_store(j).start()

    def chip(k):
        return 2 * lax.rem(z + k, depth) + core

    barrier = pltpu.get_barrier_semaphore()
    pl.semaphore_signal(barrier, inc=1, device_id=(me, sibling), device_id_type=MESH)
    for k in range(1, sections):
        pl.semaphore_signal(
            barrier, inc=1, device_id=(jnp.bitwise_xor(me, k), place), device_id_type=MESH
        )
    loop(
        1,
        depth,
        lambda k: pl.semaphore_signal(
            barrier, inc=1, device_id=(me, chip(k)), device_id_type=MESH
        ),
    )
    pl.semaphore_wait(barrier, 1 + sections - 1 + depth - 1)

    def swap(name):
        return mesh_copy(
            terms[name].at[1 - core],
            theirs[name],
            a_send.at[slot[name]],
            a_recv.at[slot[name]],
            me,
            sibling,
        )

    def load(name):
        return pltpu.make_async_copy(terms[name].at[core], half[name], load_sem.at[slot[name]])

    def when_held(name, body):
        if held[name] == "each":
            body()
        else:
            pl.when(me == owner[name])(body)

    sh_rows = sh_half.shape[0]
    sh_swap = mesh_copy(
        sh.at[1 - core], sh_theirs, a_send.at[last], a_recv.at[last], me, sibling
    )
    sh_load = pltpu.make_async_copy(sh.at[core], sh_half, load_sem.at[last])
    sh_swap.start()
    sh_load.start()

    def vec_copy(k):
        other = jnp.bitwise_xor(me, k)
        return mesh_copy(
            vec.at[other], vec_slots.at[k], v_send.at[k], v_recv.at[k], other, place
        )

    for k in range(1, sections):
        vec_copy(k).start()
    for name in fresh:

        def begin(name=name):
            swap(name).start()
            load(name).start()

        when_held(name, begin)

    def final(name):
        return k_out if name[0] == "k" else p_out

    def deliver(name, k):
        return mesh_copy(
            whole[name],
            final(name).at[core, me],
            e_send.at[slot[name]],
            e_recv.at[slot[name], k],
            owner[name],
            place,
        )

    def keep_own(name):
        return pltpu.make_async_copy(whole[name], final(name).at[core, me], e_own.at[slot[name]])

    def to_plane(name, k):
        other = jnp.bitwise_xor(me, k)
        return mesh_copy(
            terms[name].at[other],
            planes[name].at[k],
            b_send.at[slot[name], k],
            b_recv.at[slot[name], k],
            other,
            place,
        )

    def load_plane(name):
        return pltpu.make_async_copy(terms[name].at[me], planes[name].at[0], load_sem.at[slot[name]])

    for name in names:
        if held[name] == "chips":
            for k in range(1, sections):
                to_plane(name, k).start()
            load_plane(name).start()
        if held[name] == "done":

            @pl.when(me == owner[name])
            def _(name=name):
                keep_own(name).start()

            for k in range(1, sections):

                @pl.when(me == owner[name] ^ k)
                def _(name=name, k=k):
                    deliver(name, k).start()

    piece = sh_rows // depth
    step = 32

    def sh_at(i):
        return pl.ds(pl.multiple_of(i * piece, 16), piece)

    def sh_send(k):
        to = lax.rem(z + k, depth)
        return mesh_copy(
            sh_half.at[sh_at(to)],
            sh_others.at[k],
            c_send.at[last, k],
            c_recv.at[last, k],
            me,
            2 * to + core,
        )

    sh_load.wait()
    sh_swap.wait_recv()

    def sh_add(i):
        at = pl.ds(pl.multiple_of(i * step, step), step)
        sh_half[at, :] = (sh_half[at, :].astype(F32) + sh_theirs[at, :].astype(F32)).astype(BF16)

    loop(0, sh_rows // step, sh_add)
    loop(1, depth, lambda k: sh_send(k).start())

    def to_section(name, k):
        other = jnp.bitwise_xor(me, k)
        target = planes[name].at[k] if held[name] == "each" else total[name]
        return mesh_copy(
            half[name].at[other],
            target,
            b_send.at[slot[name], k],
            b_recv.at[slot[name], k],
            other,
            place,
        )

    for name in fresh:

        def combine(name=name):
            load(name).wait()
            swap(name).wait_recv()

            def add(i):
                q, y = lax.div(i, depth), lax.rem(i, depth)
                half[name][q, y] = (
                    half[name][q, y].astype(F32) + theirs[name][q, y].astype(F32)
                ).astype(BF16)

            loop(0, sections * depth, add)
            for k in range(1, sections):
                to_section(name, k).start()

        when_held(name, combine)

    for i, copy in enumerate(page_loads):
        pl.when(me == i)(copy.wait)
    loop(0, 2, map_tile)

    def share(name, k):
        return mesh_copy(
            whole[name].at[z],
            whole[name].at[z],
            d_send.at[slot[name], k],
            d_recv.at[slot[name], k],
            me,
            chip(k),
        )

    loop(1, depth, lambda k: sh_send(k).wait_recv())
    mine = sh_at(z)
    acc = sh_half[mine, :].astype(F32)
    for k in range(1, depth):
        acc = acc + sh_others[k].astype(F32)
    sh_whole[mine, :] = acc.astype(BF16)

    def sh_share(k):
        return mesh_copy(
            sh_whole.at[mine],
            sh_whole.at[mine],
            d_send.at[last, k],
            d_recv.at[last, k],
            me,
            chip(k),
        )

    loop(1, depth, lambda k: sh_share(k).start())
    loop(2, wide // TILE, map_tile)

    for name in names:
        if held[name] == "chips":
            load_plane(name).wait()
            acc = planes[name][0].astype(F32)
            for k in range(1, sections):
                to_plane(name, k).wait_recv()
                acc = acc + planes[name][k].astype(F32)
            whole[name][z] = acc.astype(BF16)
            loop(1, depth, lambda k, name=name: share(name, k).start())

    def to_chip(name, k):
        to = lax.rem(z + k, depth)
        return mesh_copy(
            total[name].at[to],
            others[name].at[k],
            c_send.at[slot[name], k],
            c_recv.at[slot[name], k],
            me,
            2 * to + core,
        )

    for name in fresh:
        if held[name] == "each":
            for k in range(1, sections):
                to_section(name, k).wait_recv()

            def plane_add(y, name=name):
                acc = half[name][me, y].astype(F32)
                for k in range(1, sections):
                    acc = acc + planes[name][k, y].astype(F32)
                total[name][y] = acc.astype(BF16)

            loop(0, depth, plane_add)
        else:

            @pl.when(me == owner[name])
            def _(name=name):
                def keep(y):
                    total[name][y] = half[name][owner[name], y]

                loop(0, depth, keep)

            for k in range(1, sections):

                @pl.when(me == owner[name] ^ k)
                def _(name=name, k=k):
                    to_section(name, k).wait_recv()

        loop(1, depth, lambda k, name=name: to_chip(name, k).start())

    def sh_deliver(k):
        at = pl.ds(pl.multiple_of(me * sh_whole.shape[1], 128), sh_whole.shape[1])
        return mesh_copy(
            sh_whole,
            sh_out.at[core, :, at],
            e_send.at[last],
            e_recv.at[last, k],
            0,
            place,
        )

    loop(1, depth, lambda k: sh_share(k).wait_recv())
    at_zero = pl.ds(0, sh_whole.shape[1])
    sh_keep = pltpu.make_async_copy(sh_whole, sh_out.at[core, :, at_zero], e_own.at[last])

    @pl.when(me == 0)
    def _():
        sh_keep.start()

    for name in fresh:
        loop(1, depth, lambda k, name=name: to_chip(name, k).wait_recv())
        acc = total[name][z].astype(F32)
        for k in range(1, depth):
            acc = acc + others[name][k].astype(F32)
        whole[name][z] = acc.astype(BF16)
        loop(1, depth, lambda k, name=name: share(name, k).start())

    def relayed(name, onward):
        index = last if name == "sh" else slot[name]
        at = pl.ds(3 * sh_whole.shape[1], sh_whole.shape[1])
        src, dst = (sh_whole, sh_out.at[core, :, at]) if name == "sh" else (whole[name], final(name).at[core, 3])
        if onward:
            return mesh_copy(relay[name], dst, r_send.at[index], e_recv.at[index, 3], 0, place)
        return mesh_copy(src, relay[name], e_send.at[index], r_recv.at[index], 1, place)

    def start_delivery(name):
        index = last if name == "sh" else slot[name]
        section = 0 if name == "sh" else owner[name]
        copy = sh_deliver if name == "sh" else functools.partial(deliver, name)
        for k in range(1, sections):
            direct = me == section ^ k
            if section == 0 and k == 3:
                direct = direct & (core == 0)

                @pl.when((me == 3) & (core == 1))
                def _():
                    relayed(name, False).start()

            @pl.when(direct)
            def _(k=k):
                copy(k).start()

    def pass_on(name):
        @pl.when((me == 1) & (core == 1))
        def _():
            relayed(name, False).wait_recv()
            relayed(name, True).start()

    start_delivery("sh")
    for name in ["k2"] + fresh:
        if name == fresh[-1]:
            pass_on("sh")
        loop(1, depth, lambda k, name=name: share(name, k).wait_recv())

        @pl.when(me == owner[name])
        def _(name=name):
            keep_own(name).start()

        start_delivery(name)
    for name in fresh:
        if owner[name] == 0:
            pass_on(name)

    def cross(name):
        return mesh_copy(
            final(name).at[core],
            final(name).at[core],
            f_send.at[slot[name]],
            f_recv.at[slot[name]],
            me,
            sibling,
        )

    sh_cross = mesh_copy(
        sh_out.at[core], sh_out.at[core], f_send.at[last], f_recv.at[last], me, sibling
    )

    @pl.when(me == 0)
    def _():
        sh_keep.wait()
        for k in range(1, sections):
            sh_deliver(k).wait_recv()
        sh_cross.start()

    for name in names:

        @pl.when(me == owner[name])
        def _(name=name):
            keep_own(name).wait()
            for k in range(1, sections):
                deliver(name, k).wait_recv()
            cross(name).start()

    for k in range(1, sections):
        vec_copy(k).wait_recv()
    sums = vec[me]
    for k in range(1, sections):
        sums = sums + vec_slots[k]
    vec_out[...] = sums

    tile_store(wide // TILE - 2).wait()
    tile_store(wide // TILE - 1).wait()
    for k in range(1, sections):
        vec_copy(k).wait_send()
    sh_swap.wait_send()
    loop(1, depth, lambda k: sh_send(k).wait_send())
    loop(1, depth, lambda k: sh_share(k).wait_send())

    @pl.when(me == 0)
    def _():
        sh_cross.wait()

    @pl.when(me != 0)
    def _():
        sh_deliver(0).wait_send()

    @pl.when((me == 1) & (core == 1))
    def _():
        for name in relay:
            relayed(name, True).wait_send()

    for name in names:

        def sent(name=name):
            swap(name).wait_send()
            for k in range(1, sections):
                to_section(name, k).wait_send()

        if name in fresh:
            when_held(name, sent)
            loop(1, depth, lambda k, name=name: to_chip(name, k).wait_send())
        if held[name] == "chips":
            for k in range(1, sections):
                to_plane(name, k).wait_send()
        if held[name] != "done":
            loop(1, depth, lambda k, name=name: share(name, k).wait_send())

        @pl.when(me == owner[name])
        def _(name=name):
            cross(name).wait()

        @pl.when(me != owner[name])
        def _(name=name):
            deliver(name, 0).wait_send()


def sum_gradients(sections, count, short, terms, vectors, dh1, w, weights, map_sources, real):
    narrow = short.shape[1]
    depth = count // 2
    args, scratch = [], []
    relays = []
    for name, section, kind in SUMS:
        args.append(terms[name])
        full = (sections, depth) + terms[name].shape[-2:]
        shapes = []
        if kind in ("owner", "each"):
            shapes += [full, full]
        if kind == "each":
            shapes.append(full)
        if kind == "chips":
            shapes.append((sections,) + full[2:])
        if kind in ("owner", "each"):
            shapes += [full[1:]] * 2
        if kind != "done":
            shapes.append(full[1:])
        if section == 0:
            relays.append(pltpu.VMEM(full[1:], BF16))
        scratch += [pltpu.VMEM(a, BF16) for a in shapes]
    scratch += relays + [pltpu.VMEM((short.shape[0] // 2, narrow), BF16)]
    sh_rows = short.shape[0] // 2
    scratch += [
        pltpu.VMEM((sh_rows, narrow), BF16),
        pltpu.VMEM((sh_rows, narrow), BF16),
        pltpu.VMEM((depth, sh_rows // depth, narrow), BF16),
        pltpu.VMEM((sh_rows, narrow), BF16),
        pltpu.VMEM((sections,) + vectors.shape[1:], F32),
    ]
    kinds = len(SUMS) + 1
    for shape in [(kinds,)] * 3 + [(kinds, sections)] * 2 + [(kinds, depth)] * 4:
        scratch.append(pltpu.SemaphoreType.DMA(shape))
    for shape in [(kinds,), (kinds, sections), (kinds,), (kinds,), (kinds,), (sections,), (sections,), (kinds,), (kinds,)]:
        scratch.append(pltpu.SemaphoreType.DMA(shape))
    wide = w.shape[0]
    padded = map_sources[0].shape[1]
    scratch += [
        pltpu.VMEM(map_sources[0].shape, BF16),
        pltpu.VMEM((2, TILE, wide), BF16),
        pltpu.VMEM((2, TILE, narrow), BF16),
        pltpu.VMEM((TILE // 128, 4 * padded, 128), F32),
        pltpu.VMEM((2, real, 4, TILE), BF16),
        pltpu.SemaphoreType.DMA,
        pltpu.SemaphoreType.DMA((2,)),
        pltpu.SemaphoreType.DMA((2,)),
        pltpu.SemaphoreType.DMA((2,)),
    ]
    hbm = pl.BlockSpec(memory_space=pl.ANY)
    vmem = pl.BlockSpec(memory_space=pltpu.VMEM)
    taps_shape, proj_shape = args[0].shape, args[1].shape
    return pl.pallas_call(
        functools.partial(gradient_kernel, sections, count),
        out_shape=[
            shape_of((2, sh_rows, narrow * sections), BF16),
            shape_of(proj_shape, BF16),
            shape_of(taps_shape, BF16),
            shape_of(vectors.shape[1:], F32),
            shape_of((real, 4, wide), BF16),
        ],
        in_specs=[hbm] * 7 + [vmem, vmem] + [hbm] * 6,
        out_specs=[hbm, hbm, hbm, vmem, hbm],
        scratch_shapes=scratch,
        compiler_params=pltpu.CompilerParams(
            has_side_effects=True, vmem_limit_bytes=VMEM_BYTES, collective_id=5
        ),
        cost_estimate=pl.CostEstimate(flops=0, bytes_accessed=400 * 2**20, transcendentals=0),
    )(short.reshape(2, sh_rows, narrow), *args, vectors, dh1, w, weights, *map_sources)


def layouts(resolution_ids, order_ids):
    pixels = jnp.arange(MAP * MAP, dtype=jnp.int32)
    row_of = pixels // MAP
    column_of = pixels % MAP
    extent = 5 + resolution_ids[:, None]
    image_mask = ((row_of[None, :] < extent) & (column_of[None, :] < extent)).astype(F32)
    inside = (row_of < 6) & (column_of < 6)
    position = jnp.where(inside, row_of // 2 * 3 + column_of // 2, 0)
    onehot_tile = (position[:, None] == jnp.arange(9)[None, :]).astype(jnp.int32)
    picked = jnp.sum(onehot_tile[None] * order_ids[:, None, :], axis=2)
    row_to = 2 * (picked // 3) + row_of % 2
    column_to = 2 * (picked % 3) + column_of % 2
    target = row_to * MAP + column_to
    tile_mask = (inside & (row_to < extent) & (column_to < extent)).astype(F32)
    return image_mask, tile_mask, jnp.where(inside, target, -1)


def tap_tables(tiled):
    lattice = np.arange(MAP)
    tables = []
    for vertical, lateral in OFFSETS:
        row, column = lattice + vertical, lattice + lateral
        in_row = (row >= 0) & (row < MAP)
        in_column = (column >= 0) & (column < MAP)
        if tiled:
            in_row &= row // 2 == lattice // 2
            in_column &= column // 2 == lattice // 2
        tables.append((in_row[:, None] & in_column[None, :]).reshape(-1))
    return np.stack(tables, axis=1).astype(np.float32)


def mm(a, b, dims="rk,kn->rn"):
    return jnp.einsum(dims, a, b, preferred_element_type=F32)


def body(
    layer_input,
    output_grad,
    resolution,
    tile_order,
    proj_weight,
    spatial_weight,
    shortcut_weight,
    bn_gain,
    bn_bias,
):
    micro, images, pixels, wide = layer_input.shape
    narrow = proj_weight.shape[2]
    rows = images * pixels
    padded = -(-rows // 16) * 16
    sections = lax.axis_size("segment")
    count = lax.axis_size("dp")
    section = lax.axis_index("segment")
    first = section == 0
    proj, spatial, shortcut = proj_weight[0], spatial_weight[0], shortcut_weight[0]
    pick = lambda a: lax.dynamic_index_in_dim(a, section, 0, keepdims=False)

    image_masks, tile_masks, targets = layouts(
        resolution.reshape(-1), tile_order.reshape(micro * images, -1)
    )
    interleave = lambda a: jnp.transpose(a.reshape(micro, rows), (1, 0)).reshape(rows * micro, 1)
    taps_image = np.tile(np.repeat(tap_tables(False), micro, axis=0), (images, 1))
    pack_all = jnp.concatenate(
        [interleave(image_masks), jnp.asarray(taps_image), jnp.zeros((rows * micro, 6), F32)], axis=1
    )
    tiles_all = interleave(tile_masks)
    pad_rows = lambda a: jnp.pad(a, ((0, padded - rows), (0, 0)))
    image_mask = pad_rows(pick(image_masks.reshape(micro, rows, 1)))
    tile_mask = pad_rows(pick(tile_masks.reshape(micro, rows, 1)))
    taps_tile = np.pad(np.tile(tap_tables(True), (images, 1)), ((0, padded - rows), (0, 6)))
    pack_tile = jnp.concatenate([tile_mask, jnp.asarray(taps_tile)], axis=1)
    target = pick(targets.reshape(micro, images, pixels))
    base = (jnp.arange(images) * pixels)[:, None]
    target = jnp.where(target >= 0, target + base, -1).reshape(rows)
    target = jnp.pad(target, (0, padded - rows), constant_values=-1)
    index = jnp.arange(padded)
    moves = (target[:, None] == index[None, :]).astype(BF16)
    moves_back = (target[None, :] == index[:, None]).astype(BF16)

    x_in = jnp.transpose(layer_input, (1, 2, 0, 3)).reshape(rows, micro, wide)
    og_in = jnp.transpose(output_grad, (1, 2, 0, 3)).reshape(rows, micro, wide)
    gb_first = jnp.stack(
        [bn_gain[0, :narrow], bn_bias[0, :narrow]]
        + [bn_gain[0, narrow : 2 * narrow], bn_bias[0, narrow : 2 * narrow]]
    )
    gains_here = jnp.concatenate([bn_gain, bn_bias])
    total = rows * micro
    quarter = wide // sections
    dma = pltpu.SemaphoreType.DMA
    stats_all, counts, gains, y1, u, h3n, stats3, *far = kernel_call(
        functools.partial(head_kernel, sections, count),
        [
            shape_of((16, narrow), F32),
            shape_of((8, 128), F32),
            shape_of((sections, 2, wide), F32),
            shape_of((padded, wide), BF16),
            shape_of((padded, wide), BF16),
            shape_of((padded, wide), F32),
            shape_of((2, wide), F32),
            shape_of((padded, narrow), BF16),
            shape_of((wide, narrow), BF16),
            shape_of((sections, padded, quarter), BF16),
            shape_of((total, wide), BF16),
            shape_of((total, 9 * narrow), BF16),
            shape_of((total, narrow), F32),
            shape_of((total, narrow), F32),
            shape_of((wide, narrow), BF16),
            shape_of((wide, narrow), BF16),
            shape_of((9 * narrow, narrow), BF16),
        ],
        [x_in, proj, shortcut, spatial, gb_first, gains_here, pack_all, tiles_all, image_mask, moves],
        [
            pltpu.VMEM((total, wide), BF16),
            pltpu.VMEM((total, 9 * narrow), BF16),
            pltpu.VMEM((total, narrow), F32),
            pltpu.VMEM((total, narrow), F32),
            pltpu.VMEM((narrow // 128, 4 * padded, 128), F32),
            pltpu.VMEM((micro, padded, narrow), BF16),
            pltpu.VMEM((padded, narrow), BF16),
            pltpu.VMEM((wide, quarter), BF16),
            pltpu.VMEM((wide, narrow), BF16),
            pltpu.VMEM((micro, padded, quarter), BF16),
            pltpu.VMEM((sections, padded, quarter), BF16),
            pltpu.VMEM((sections, 2, wide), F32),
        ]
        + sync_scratch(count, [(8, narrow + 128), (8, narrow), (2, wide)])
        + [dma((sections,)), dma, dma, dma]
        + [dma((sections,)), dma, dma, dma]
        + [dma((sections,)), dma((sections,)), dma((sections,)), dma]
        + [dma((sections,)), dma((sections,)), dma((2,)), dma((7,))]
        + [dma((5, sections)), dma((5,)), dma((5,)), dma((5,))]
        + [dma((5, 2)), dma((5, 2)), dma((3,))],
        0,
        2 * total * (narrow * (wide + 9 * narrow) + wide * quarter),
        60 * 2**20,
        far_in=(2,),
        far_out=tuple(range(7, 17)),
    )
    a2, w1, res, x_all, cols_all, h1n_all, h2n_all, w3, w2, k2 = far
    paged = shape_of((sections, padded, wide), BF16)
    y2, t_a2, t_cols, t_dh3, t_dh2, t_dh1, dy1, t_sums, map_one = kernel_call(
        functools.partial(tile_kernel, sections, count),
        [
            shape_of((padded, wide), BF16),
            shape_of((padded, narrow), BF16),
            shape_of((padded, 9 * narrow), BF16),
            shape_of((padded, wide), BF16),
            shape_of((padded, narrow), BF16),
            shape_of((padded, narrow), BF16),
            shape_of((padded, wide), BF16),
            shape_of((6, wide), F32),
            paged,
        ],
        [u, w2, k2, w3, og_in, pack_tile, gains, counts, moves_back, y1],
        [
            pltpu.VMEM((padded, narrow), F32),
            pltpu.VMEM((padded, narrow), F32),
            pltpu.VMEM((padded, wide), F32),
            pltpu.VMEM((padded, narrow), F32),
            pltpu.VMEM((padded, wide), BF16),
            pltpu.VMEM((6, wide), F32),
            pltpu.VMEM((padded, wide), F32),
        ]
        + [dma, dma((sections,)), dma]
        + sync_scratch(
            count, [(2, narrow), (2, narrow), (2, wide), (2, wide), (2, narrow), (2, narrow)]
        ),
        1,
        4 * padded * narrow * (2 * wide + 9 * narrow),
        30 * 2**20,
        far_in=(9,),
        far_out=(8,),
    )
    depth = count // 2

    def split(term):
        return term.astype(BF16).reshape(
            2, sections, depth, term.shape[0] // (2 * sections * depth), narrow
        )

    p3_term = split(mm(t_dh3, t_a2, "rd,rk->dk"))
    k2_term = split(mm(t_cols, t_dh2, "rk,rn->kn"))
    p2_term = split(mm(u, t_dh1, "rc,rn->cn"))
    proj_piece, taps_piece = p3_term.shape[3], k2_term.shape[3]
    dz, dh3, dh2_all, dh1_all, i_sums, f_sums, dz_quarter, p3_part, p2_part, k2_part, map_zero, map_two, map_three = (
        kernel_call(
            functools.partial(back_kernel, sections, count),
            [
                shape_of((padded, wide), BF16),
                shape_of((padded, wide), BF16),
                shape_of((total, narrow), BF16),
                shape_of((total, narrow), BF16),
                shape_of((2, wide), F32),
                shape_of((16, narrow), F32),
                shape_of((total, quarter), BF16),
                shape_of((depth, proj_piece, narrow), BF16),
                shape_of((depth, proj_piece, narrow), BF16),
                shape_of((sections, taps_piece, narrow), BF16),
                paged,
                paged,
                paged,
            ],
            [dy1, res, h3n, image_mask, gains, stats3, w1, spatial, gb_first, pack_all]
            + [h1n_all, h2n_all, stats_all, counts, p3_term, p2_term, k2_term, y2],
            [
                pltpu.VMEM((padded, narrow), BF16),
                pltpu.VMEM((micro, padded, narrow), BF16),
                pltpu.VMEM((micro, padded, quarter), BF16),
                pltpu.VMEM((narrow // 128, 4 * padded, 128), F32),
                pltpu.VMEM((total, narrow), F32),
                pltpu.VMEM((total, narrow), BF16),
            ]
            + sync_scratch(count, [(2, wide), (8, narrow), (8, narrow)])
            + [pltpu.VMEM(a.shape[1:], BF16) for a in (p3_term, p2_term, k2_term)] * 2
            + [pltpu.VMEM(p3_term.shape[1:], BF16)] * 2
            + [pltpu.VMEM((depth, sections, taps_piece, narrow), BF16)]
            + [pltpu.VMEM((depth, proj_piece, narrow), BF16)] * 6
            + [pltpu.VMEM((sections, taps_piece, narrow), BF16)]
            + [dma((3,))] * 3
            + [dma((3, max(sections, depth)))] * 6
            + [dma((3,))]
            + [dma, dma((sections,)), dma((sections,)), dma((sections,))]
            + [dma, dma((sections,)), dma] * 3,
            2,
            2 * total * narrow * 9 * narrow,
            40 * 2**20,
            far_in=(14, 15, 16, 17),
            far_out=(7, 8, 9, 10, 11, 12),
        )
    )

    terms = {
        "p3": p3_part,
        "k2": k2_part,
        "p2": p2_part,
        "p1": split(mm(dh3, a2, "rd,rk->dk")),
        "k0": split(mm(cols_all, dh2_all, "rk,rn->kn")),
        "p0": split(mm(x_all, dh1_all, "rc,rn->cn")),
    }
    short_term = mm(x_all, dz_quarter, "rc,rd->cd").astype(BF16)

    blank = jnp.zeros((wide,), F32)
    pad = jnp.zeros((wide - 2 * narrow,), F32)
    of_batches = lambda at: jnp.sum(f_sums[at : at + 4], axis=0)
    zero_gain = jnp.where(first, jnp.concatenate([of_batches(12), of_batches(4), pad]), blank)
    zero_bias = jnp.where(first, jnp.concatenate([of_batches(8), of_batches(0), pad]), blank)
    vectors = jnp.stack(
        [
            zero_gain,
            zero_bias,
            i_sums[1],
            i_sums[0],
            jnp.concatenate([t_sums[5, :narrow], t_sums[3, :narrow], pad]),
            jnp.concatenate([t_sums[4, :narrow], t_sums[2, :narrow], pad]),
            t_sums[1],
            t_sums[0],
        ]
    )
    short_sum, proj_sum, taps_sum, vectors, maps = sum_gradients(
        sections,
        count,
        short_term,
        terms,
        vectors.reshape(sections, 2, wide),
        dh1_all,
        proj,
        shortcut,
        (map_zero, map_one, map_two, map_three),
        rows,
    )
    maps = jnp.transpose(maps.reshape(images, pixels, micro, wide), (2, 0, 1, 3))
    proj_grad = proj_sum.reshape(wide, narrow).astype(F32)
    spatial_grad = taps_sum.reshape(9 * narrow, narrow).astype(F32)
    spatial_grad = jnp.where((section % 2) == 0, spatial_grad, jnp.zeros_like(spatial_grad))
    short_grad = short_sum.reshape(wide, wide).astype(F32)
    short_grad = jnp.where(first, short_grad, jnp.zeros_like(short_grad))
    return (
        maps[None],
        proj_grad[None],
        spatial_grad[None],
        short_grad[None],
        vectors[:1],
        vectors[1:],
    )


def solution(mesh):
    return jax.shard_map(
        body,
        mesh=mesh,
        in_specs=(
            P(None, "dp", None, None),
            P(None, "dp", None, None),
            P(None, "dp"),
            P(None, "dp", None),
            P("segment", None, None),
            P("segment", None, None),
            P("segment", None, None),
            P("segment", None),
            P("segment", None),
        ),
        out_specs=(
            P("segment", None, "dp", None, None),
            P("segment", None, None),
            P("segment", None, None),
            P("segment", None, None),
            P("segment", None),
            P("segment", None),
        ),
        check_vma=False,
    )
```

```python
import functools

import jax
import jax.numpy as jnp
import numpy as np
from jax import lax
from jax.experimental import pallas as pl
from jax.experimental.pallas import tpu as pltpu
from jax.sharding import PartitionSpec as P

MAP = 7
EPSILON = 1e-05
OFFSETS = ((-1, -1), (-1, 0), (-1, 1), (0, -1), (0, 0), (0, 1), (1, -1), (1, 0), (1, 1))
MESH = pl.DeviceIdType.MESH
F32 = jnp.float32
BF16 = jnp.bfloat16
VMEM_BYTES = 60 * 2**20
TILE = 256


def greet(count, sections=0):
    segment, me = lax.axis_index("segment"), lax.axis_index("dp")
    barrier = pltpu.get_barrier_semaphore()

    def one(k, carry):
        pl.semaphore_signal(
            barrier, inc=1, device_id=(segment, lax.rem(me + k, count)), device_id_type=MESH
        )
        return carry

    lax.fori_loop(1, count, one, 0)
    for k in range(1, sections):
        pl.semaphore_signal(
            barrier, inc=1, device_id=(jnp.bitwise_xor(segment, k), me), device_id_type=MESH
        )


def greeted(count, sections=1):
    pl.semaphore_wait(pltpu.get_barrier_semaphore(), count - 1 + sections - 1)


def exchange(count, slots, send_sem, recv_sem):
    segment, me = lax.axis_index("segment"), lax.axis_index("dp")

    def copy(k):
        return pltpu.make_async_remote_copy(
            src_ref=slots.at[me],
            dst_ref=slots.at[me],
            send_sem=send_sem.at[k],
            recv_sem=recv_sem.at[k],
            device_id=(segment, lax.rem(me + k, count)),
            device_id_type=MESH,
        )

    def start(k, carry):
        copy(k).start()
        return carry

    def finish(k, carry):
        copy(k).wait_recv()
        copy(k).wait_send()
        return carry

    lax.fori_loop(1, count, start, 0)
    lax.fori_loop(1, count, finish, 0)
    total = slots[0]
    for k in range(1, count):
        total = total + slots[k]
    return total


def mesh_copy(src, dst, send_sem, recv_sem, segment, place):
    return pltpu.make_async_remote_copy(
        src_ref=src,
        dst_ref=dst,
        send_sem=send_sem,
        recv_sem=recv_sem,
        device_id=(segment, place),
        device_id_type=MESH,
    )


def loop(low, high, body):
    def one(k, carry):
        body(k)
        return carry

    lax.fori_loop(low, high, one, 0)


def sync_scratch(count, shapes):
    out = []
    for shape in shapes:
        out += [
            pltpu.VMEM((count,) + shape, F32),
            pltpu.SemaphoreType.DMA((count,)),
            pltpu.SemaphoreType.DMA((count,)),
        ]
    return out


def kernel_call(kernel, outs, args, scratch, ident, flops, moved, far_in=(), far_out=()):
    params = dict(has_side_effects=True, vmem_limit_bytes=VMEM_BYTES)
    if ident is not None:
        params["collective_id"] = ident
    return pl.pallas_call(
        kernel,
        out_shape=outs,
        in_specs=[
            pl.BlockSpec(memory_space=pl.ANY if i in far_in else pltpu.VMEM) for i in range(len(args))
        ],
        out_specs=[
            pl.BlockSpec(memory_space=pl.ANY if i in far_out else pltpu.VMEM) for i in range(len(outs))
        ],
        scratch_shapes=scratch,
        compiler_params=pltpu.CompilerParams(**params),
        cost_estimate=pl.CostEstimate(flops=flops, bytes_accessed=moved, transcendentals=0),
    )(*args)


def shape_of(shape, dtype):
    return jax.ShapeDtypeStruct(shape, dtype)


def dot(a, b):
    return jnp.dot(a, b, preferred_element_type=F32)


def dot_t(a, b):
    return lax.dot_general(a, b, (((1,), (1,)), ((), ())), preferred_element_type=F32)


def dot_0(a, b):
    return lax.dot_general(a, b, (((0,), (0,)), ((), ())), preferred_element_type=F32)


class Writer:
    def __init__(self, stage, sems):
        self.stage, self.sems, self.open, self.turn = stage, sems, [None, None], 0

    def put(self, value, dst):
        at = self.turn % 2
        self.turn += 1
        if self.open[at] is not None:
            self.open[at].wait()
        self.stage[at] = value.astype(BF16)
        self.open[at] = pltpu.make_async_copy(self.stage.at[at], dst, self.sems.at[at])
        self.open[at].start()

    def rows_of_dot(self, left, right, out):
        tall = self.stage.shape[1]
        for j in range(out.shape[0] // tall):
            at = pl.ds(j * tall, tall)
            self.put(dot_0(left[:, at], right[...]), out.at[at])

    def drain(self):
        for at in range(2):
            if self.open[at] is not None:
                self.open[at].wait()
        self.open = [None, None]


def sigmoid(v):
    return 1.0 / (1.0 + jnp.exp(-v))


def slope(v):
    s = sigmoid(v)
    return s * (1.0 + v * (1.0 - s))


def over(width, step, body):
    def one(j, carry):
        body(pl.ds(pl.multiple_of(j * step, step), step))
        return carry

    lax.fori_loop(0, width // step, one, 0)


def lane(at):
    return lax.div(at.start, 128)


def unrolled_shift(ref_value, shift):
    rows = ref_value.shape[0]
    return ref_value if shift % rows == 0 else pltpu.roll(ref_value, (-shift) % rows, 0)


def by_batch(values):
    rows, width = values.shape
    part = jnp.sum(values.reshape(rows // 8, 8, width), axis=0)
    return part[:4] + part[4:]


def spread8(values):
    return jnp.concatenate([values, values], axis=0)[None]


def first_part(
    count, hooks, writes, x, w, k, gb, pack, tiles, a2_out, cols, h1n, h2n, stats_out, count_out, act, *sync
):
    s1, send1, recv1, s2, send2, recv2 = sync
    rows, narrow = h1n.shape
    me = lax.axis_index("dp")
    full = act.shape[1]

    def tile8(v):
        return v.reshape(rows // 8, 8, v.shape[1])

    def project(at):
        h = dot(x[...], w[:, at])
        h1n[:, at] = h
        m = pack[:, 0:1] * h
        s1[me, 0:4, at] = by_batch(m)
        s1[me, 4:8, at] = by_batch(m * h)

    over(narrow, TILE, project)
    s1[me, 0:4, narrow:] = jnp.broadcast_to(by_batch(pack[:, 0:1]), (4, 128))
    s1[me, 4:8, narrow:] = jnp.broadcast_to(by_batch(tiles[:, 0:1]), (4, 128))
    total = exchange(count, s1, send1, recv1)
    counts = total[:, narrow:]
    count_out[...] = counts
    valid = counts[0:4, 0:1]
    average = total[0:4, :narrow] / valid
    inverse = lax.rsqrt(total[4:8, :narrow] / valid - average * average + EPSILON)
    stats_out[0:4, :] = average
    stats_out[4:8, :] = inverse
    hooks[0]()

    def activate(stat_at, gain_at, source):
        def body(at):
            mean = spread8(stats_out[stat_at : stat_at + 4, at])
            inv = spread8(stats_out[stat_at + 4 : stat_at + 8, at])
            hn = (tile8(source[:, at]) - mean) * inv
            source[:, at] = hn.reshape(rows, hn.shape[2])
            n = gb[gain_at : gain_at + 1, at][None] * hn + gb[gain_at + 1 : gain_at + 2, at][None]
            n = n.reshape(rows, n.shape[2])
            act[lane(at), 0:rows, :] = pack[:, 0:1] * (n * sigmoid(n))

        return body

    over(narrow, 128, activate(0, 0, h1n))

    for t, (vertical, lateral) in enumerate(OFFSETS):
        shift = 4 * (7 * vertical + lateral)

        def place(j, carry, t=t, shift=shift):
            at = pl.ds(pl.multiple_of(j * 128, 128), 128)
            to = pl.ds(pl.multiple_of(t * narrow + j * 128, 128), 128)
            moved = unrolled_shift(act[j, 0:rows, :], shift)
            cols[:, to] = (pack[:, 1 + t : 2 + t] * moved).astype(BF16)
            return carry

        lax.fori_loop(0, narrow // 128, place, 0)

    def convolve(at):
        h = dot(cols[...], k[:, at])
        h2n[:, at] = h
        m = pack[:, 0:1] * h
        s2[me, 0:4, at] = by_batch(m)
        s2[me, 4:8, at] = by_batch(m * h)

    for write in writes:
        write.start()
    hooks[1]()
    over(narrow, TILE, convolve)
    total = exchange(count, s2, send2, recv2)
    average = total[0:4] / valid
    hooks[2]()
    stats_out[8:12, :] = average
    stats_out[12:16, :] = lax.rsqrt(total[4:8] / valid - average * average + EPSILON)
    over(narrow, 128, activate(8, 2, h2n))
    act[:, rows:, :] = jnp.zeros((narrow // 128, full - rows, 128), F32)
    for m in range(4):

        def pick(j, carry, m=m):
            at = pl.ds(pl.multiple_of(j * 128, 128), 128)
            a2_out[m, :, at] = act[j, pl.ds(m, full // 4, stride=4), :].astype(BF16)
            return carry

        lax.fori_loop(0, narrow // 128, pick, 0)


def residual_part(x, w, out, hold):
    rows, full, quarter = x.shape[0], hold.shape[1], out.shape[2]
    hold[:, rows:, :] = jnp.zeros((quarter // 128, full - rows, 128), F32)

    def body(at):
        value = dot(x[...], w[:, at])
        for part in range(TILE // 128):
            hold[lane(at) + part, 0:rows, :] = value[:, part * 128 : part * 128 + 128]

    over(quarter, TILE, body)
    for m in range(4):

        def pick(j, carry, m=m):
            at = pl.ds(pl.multiple_of(j * 128, 128), 128)
            out[m, :, at] = hold[j, pl.ds(m, full // 4, stride=4), :].astype(BF16)
            return carry

        lax.fori_loop(0, quarter // 128, pick, 0)


def norm_sums(slots, me, at, masked, h):
    slots[me, 0:1, at] = jnp.sum(masked, axis=0, keepdims=True)
    slots[me, 1:2, at] = jnp.sum(masked * h, axis=0, keepdims=True)


def finish_stats(total, valid, stats_out, at_row):
    average = total[0:1] / valid
    width = average.shape[1]
    stats_out[at_row : at_row + 1, 0:width] = average
    stats_out[at_row + 1 : at_row + 2, 0:width] = lax.rsqrt(
        total[1:2] / valid - average * average + EPSILON
    )


def second_part(
    count, before, a2, w1, res, mask, gb, valid, moves, y_out, u_out, h3n, stats_out, s1, send1, recv1
):
    wide = h3n.shape[1]
    quarter = res.shape[2]
    me = lax.axis_index("dp")

    def project(at):
        h = dot_t(a2[...], w1[at, :])
        h3n[:, at] = h
        norm_sums(s1, me, at, mask[:, 0:1] * h, h)

    over(wide, TILE, project)
    finish_stats(exchange(count, s1, send1, recv1), valid, stats_out, 0)
    before()
    for q in range(wide // quarter):

        def body(j, carry, q=q):
            at = pl.ds(pl.multiple_of(q * quarter + j * 128, 128), 128)
            own = pl.ds(pl.multiple_of(j * 128, 128), 128)
            hn = (h3n[:, at] - stats_out[0:1, at]) * stats_out[1:2, at]
            h3n[:, at] = hn
            z = gb[1, 0:1, at] * hn + gb[1, 1:2, at] + res[q, :, own].astype(F32)
            y_out[:, at] = (mask[:, 0:1] * (z * sigmoid(z))).astype(BF16)
            return carry

        lax.fori_loop(0, quarter // 128, body, 0)

    def permute(at):
        u_out[:, at] = dot(moves[...], y_out[:, at]).astype(BF16)

    over(wide, TILE, permute)


def batch_valid(counts, row):
    me = lax.axis_index("segment")
    value = counts[row : row + 1, 0:1]
    for m in range(1, 4):
        value = jnp.where(me == m, counts[row + m : row + m + 1, 0:1], value)
    return value


def head_kernel(
    sections,
    count,
    x3,
    w,
    short,
    k,
    gb,
    vec,
    pack,
    tiles,
    mask,
    moves,
    stats_out,
    count_out,
    g_out,
    y_out,
    u_out,
    h3n,
    stats3,
    a2_out,
    w1_out,
    res_out,
    x_out,
    a1_out,
    h1n_out,
    h2n_out,
    w3_out,
    w2_out,
    k2_out,
    x,
    cols,
    h1n,
    h2n,
    act,
    a2_all,
    a2,
    wsc,
    w1,
    rq,
    res,
    gslots,
    *rest,
):
    sync, rest = rest[:9], list(rest[9:])
    short_send, short_recv, short_relay_send, short_relay_recv = rest[:4]
    w1_send, w1_recv, w1_relay_send, w1_relay_recv = rest[4:8]
    g_send, g_recv, a2_send, a2_recv, res_send, res_recv, own_sem, out_sem = rest[8:16]
    spread_send, spread_recv, far_send, far_recv, near_send, near_recv, keep_sem = rest[16:23]
    pass_send, kv, kv_sem = rest[23:]
    me, place = lax.axis_index("segment"), lax.axis_index("dp")
    core = lax.rem(place, 2)
    sibling = place + 1 - 2 * core
    wide = x.shape[1]
    quarter = wide // sections
    half_rows = wide // 2
    mine = pl.ds(pl.multiple_of(core * half_rows, 16), half_rows)
    greet(count, sections)
    k_load = pltpu.make_async_copy(k, kv, kv_sem)
    k_load.start()

    odd = lax.rem(lax.div(place, 2), 2)
    beside = place + 2 - 4 * odd
    parts = [("w3", w, w3_out, 3, 0, 1), ("w2", w, w2_out, 2, 0, 1)]
    parts += [("k2", k, k2_out, 2, i, 3) for i in range(3)]

    def part_rows(i, at_odd):
        _, src, _, _, piece, pieces = parts[i]
        fine = src.shape[0] // (4 * pieces)
        start = ((2 * at_odd + core) * pieces + piece) * fine
        return pl.ds(pl.multiple_of(start, 16), fine)

    def spread_copy(i, t):
        _, src, dst, _, _, _ = parts[i]
        at = part_rows(i, odd)
        return mesh_copy(src.at[at], dst.at[at], spread_send.at[i, t], spread_recv.at[i], t, place)

    def far_copy(i):
        dst, at = parts[i][2], part_rows(i, odd)
        return mesh_copy(dst.at[at], dst.at[at], far_send.at[i], far_recv.at[i], me, beside)

    def near_copy(i, second):
        dst = parts[i][2]
        at = part_rows(i, 1 - odd if second else odd)
        sems = near_send.at[i, second], near_recv.at[i, second]
        return mesh_copy(dst.at[at], dst.at[at], *sems, me, sibling)

    keeps = [
        (3, pltpu.make_async_copy(w, w3_out, keep_sem.at[0])),
        (2, pltpu.make_async_copy(w, w2_out, keep_sem.at[1])),
        (2, pltpu.make_async_copy(kv, k2_out, keep_sem.at[2])),
    ]

    def spread_start(i):
        owner = parts[i][3]

        @pl.when(me == owner)
        def _():
            for d in (1, 2):
                spread_copy(i, owner ^ d).start()

    def spread_sent(i):
        for d in (1, 2):
            spread_copy(i, parts[i][3] ^ d).wait_send()

    def pass_copy(i):
        dst, at = parts[i][2], part_rows(i, odd)
        return mesh_copy(
            dst.at[at], dst.at[at], pass_send.at[i], spread_recv.at[i], parts[i][3] ^ 3, place
        )

    def spread_on(i):
        owner = parts[i][3]

        @pl.when(me == owner ^ 1)
        def _():
            spread_copy(i, 0).wait_recv()
            pass_copy(i).start()

        @pl.when((me != owner) & (me != owner ^ 1))
        def _():
            spread_copy(i, 0).wait_recv()

        @pl.when(me != owner)
        def _():
            far_copy(i).start()
            near_copy(i, 0).start()

    def far_on(i):
        @pl.when(me != parts[i][3])
        def _():
            far_copy(i).wait_recv()
            near_copy(i, 1).start()

    def short_copy(t):
        src = short.at[mine, pl.ds(t * quarter, quarter)]
        return mesh_copy(src, wsc.at[mine], short_send.at[t], short_recv, t, place)

    def w1_copy(t):
        return mesh_copy(w.at[mine], w1.at[mine], w1_send.at[t], w1_recv, t, place)

    short_own = pltpu.make_async_copy(short.at[:, pl.ds(0, quarter)], wsc, own_sem.at[0])
    w1_own = pltpu.make_async_copy(w, w1, own_sem.at[1])
    short_relay = mesh_copy(
        wsc.at[mine], wsc.at[mine], short_relay_send, short_relay_recv, me, sibling
    )
    w1_relay = mesh_copy(w1.at[mine], w1.at[mine], w1_relay_send, w1_relay_recv, me, sibling)

    def g_copy(k_):
        return mesh_copy(
            gslots.at[me],
            gslots.at[me],
            g_send.at[k_],
            g_recv.at[k_],
            jnp.bitwise_xor(me, k_),
            place,
        )

    gslots[me] = vec[...]
    greeted(count, sections)

    @pl.when(me == 0)
    def _():
        for t in (3, 1, 2):
            short_copy(t).start()
        short_own.start()

    @pl.when(me == 1)
    def _():
        for t in (2, 0, 3):
            w1_copy(t).start()
        w1_own.start()

    for k_ in range(1, sections):
        g_copy(k_).start()
    for i in range(3):
        spread_start(i)
    for owner, copy in keeps[:2]:
        pl.when(me == owner)(copy.start)

    def relayout(j, carry):
        at = pl.ds(pl.multiple_of(j * 128, 128), 128)
        x[:, at] = x3[:, :, at].reshape(x.shape[0], 128)
        return carry

    lax.fori_loop(0, wide // 128, relayout, 0)
    writes = [
        pltpu.make_async_copy(src, dst, out_sem.at[i])
        for i, (src, dst) in enumerate(
            ((x, x_out), (h1n, h1n_out), (cols.at[:, pl.ds(4 * h1n.shape[1], h1n.shape[1])], a1_out), (h2n, h2n_out))
            + ((a2, a2_out), (w1, w1_out), (res, res_out))
        )
    ]
    writes[0].start()

    def a2_copy(t):
        return mesh_copy(a2_all.at[t], a2, a2_send.at[t], a2_recv, t, place)

    @pl.when(me == 0)
    def _():
        def between():
            spread_on(0)
            spread_on(1)

        first_part(
            count,
            (lambda: spread_on(1), k_load.wait, lambda: spread_on(0)),
            writes[1:3],
            x,
            w,
            kv,
            gb,
            pack,
            tiles,
            a2_all,
            cols,
            h1n,
            h2n,
            stats_out,
            count_out,
            act,
            *sync[:6],
        )
        writes[3].start()
        for t in range(1, sections):
            a2_copy(t).start()
        a2[...] = a2_all[0]
        short_own.wait()
        for i in (2, 3, 4):
            spread_on(i)

    @pl.when(me != 0)
    def _():
        k_load.wait()
        pl.when(me == keeps[2][0])(keeps[2][1].start)
        slots, send1, recv1 = sync[:3]
        narrow = h1n.shape[1]
        stats_out[...] = jnp.zeros(stats_out.shape, F32)
        slots[place, :, 0:narrow] = jnp.zeros((8, narrow), F32)
        slots[place, 0:4, narrow:] = jnp.broadcast_to(by_batch(pack[:, 0:1]), (4, 128))
        slots[place, 4:8, narrow:] = jnp.broadcast_to(by_batch(tiles[:, 0:1]), (4, 128))
        count_out[...] = exchange(count, slots, send1, recv1)[:, narrow:]

    def spread_paced(i, after):
        @pl.when(me == parts[i][3])
        def _():
            spread_sent(after)
            for d in (1, 2):
                spread_copy(i, parts[i][3] ^ d).start()

    def unless_zero(i):
        pl.when(me != 0)(lambda: spread_on(i))

    unless_zero(0)
    spread_paced(3, 1)
    unless_zero(1)
    spread_paced(4, 2)
    unless_zero(2)
    unless_zero(3)

    @pl.when(me != 0)
    def _():
        short_copy(0).wait_recv()
        short_relay.start()

    @pl.when(me == 1)
    def _():
        w1_own.wait()

    @pl.when(me != 1)
    def _():
        w1_copy(0).wait_recv()
        w1_relay.start()

    @pl.when(me != 0)
    def _():
        short_relay.wait_recv()

    residual_part(x, wsc, rq, act)

    def res_copy(k_):
        other = jnp.bitwise_xor(me, k_)
        return mesh_copy(
            rq.at[other], res.at[me], res_send.at[k_], res_recv.at[k_], other, place
        )

    for k_ in range(1, sections):
        res_copy(k_).start()
    res[me] = rq[me]
    unless_zero(4)

    @pl.when(me != 0)
    def _():
        a2_copy(0).wait_recv()

    @pl.when(me != 1)
    def _():
        w1_relay.wait_recv()

    for k_ in range(1, sections):
        g_copy(k_).wait_recv()
    g_out[...] = gslots[...]

    def before():
        far_on(0)
        far_on(1)
        for k_ in range(1, sections):
            res_copy(k_).wait_recv()

    second_part(
        count,
        before,
        a2,
        w1,
        res,
        mask,
        gslots,
        batch_valid(count_out, 0),
        moves,
        y_out,
        u_out,
        h3n,
        stats3,
        *sync[6:],
    )
    for copy in writes[4:]:
        copy.start()
    for i in range(2, len(parts)):
        far_on(i)
    for k_ in range(1, sections):
        g_copy(k_).wait_send()
        res_copy(k_).wait_send()

    @pl.when(me == 0)
    def _():
        for t in range(1, sections):
            short_copy(t).wait_send()
            a2_copy(t).wait_send()

    @pl.when(me != 0)
    def _():
        short_relay.wait_send()

    @pl.when(me == 1)
    def _():
        for t in (0, 2, 3):
            w1_copy(t).wait_send()

    @pl.when(me != 1)
    def _():
        w1_relay.wait_send()

    for i in range(len(parts)):
        owner = parts[i][3]

        if i not in (1, 2):
            pl.when(me == owner)(functools.partial(spread_sent, i))
        pl.when(me == owner ^ 1)(lambda i=i: pass_copy(i).wait_send())

        @pl.when(me != owner)
        def _(i=i):
            far_copy(i).wait_send()
            near_copy(i, 0).wait()
            near_copy(i, 1).wait()

    for owner, copy in keeps:
        pl.when(me == owner)(copy.wait)
    for i, copy in enumerate(writes):
        if i in (1, 2, 3):
            pl.when(me == 0)(copy.wait)
        else:
            copy.wait()


def back_sums(slots, me, at, grad, hn):
    slots[me, 0:1, at] = jnp.sum(grad, axis=0, keepdims=True)
    slots[me, 1:2, at] = jnp.sum(grad * hn, axis=0, keepdims=True)


def map_sender(sections, src, dst, owner, send_sem, recv_sem, own_sem):
    me, place = lax.axis_index("segment"), lax.axis_index("dp")
    own = pltpu.make_async_copy(src, dst.at[me], own_sem)

    def copy(k):
        return mesh_copy(src, dst.at[me], send_sem, recv_sem.at[k], owner, place)

    def start():
        @pl.when(me == owner)
        def _():
            own.start()

        for k in range(1, sections):

            @pl.when(me == owner ^ k)
            def _(k=k):
                copy(k).start()

    def finish():
        @pl.when(me == owner)
        def _():
            own.wait()
            for k in range(1, sections):
                copy(k).wait_recv()

        @pl.when(me != owner)
        def _():
            copy(0).wait_send()

    return start, finish


def tile_kernel(
    sections,
    count,
    u,
    w2,
    k2_far,
    w3_far,
    og_far,
    pack,
    gains,
    counts,
    back,
    y1,
    y_out,
    dy,
    sums_out,
    map_one,
    p3_out,
    p2_out,
    k2_out,
    a2,
    cols,
    dh3,
    dh2,
    dh1,
    stage,
    stage_sem,
    k2,
    w3,
    og3,
    load_sem,
    h1n,
    h2n,
    h3n,
    act,
    dz,
    stats,
    og,
    map_send,
    map_recv,
    map_own,
    *sync,
):
    s1, send1, recv1, s2, send2, recv2, s3, send3, recv3 = sync[:9]
    b3, bsend3, brecv3, b2, bsend2, brecv2, b1, bsend1, brecv1 = sync[9:]
    rows, wide = u.shape
    narrow = h1n.shape[1]
    me = lax.axis_index("dp")
    section = lax.axis_index("segment")
    valid = batch_valid(counts, 4)
    gb3 = gains.at[3]
    loads = [
        pltpu.make_async_copy(src, dst, load_sem.at[i])
        for i, (src, dst) in enumerate(((og_far, og3), (k2_far, k2), (w3_far, w3)))
    ]
    for load in loads:
        load.start()

    def gb2(row, at):
        return gains[2, row % 2 : row % 2 + 1, pl.ds(at.start + row // 2 * narrow, at.size)]

    greet(count, sections)

    def project(at):
        h = dot(u[...], w2[:, at])
        h1n[:, at] = h
        norm_sums(s1, me, at, pack[:, 0:1] * h, h)

    over(narrow, TILE, project)
    greeted(count, sections)
    send_map, wait_map = map_sender(sections, y1, map_one, 1, map_send, map_recv, map_own)
    send_map()
    loads[0].wait()
    real = og3.shape[0]
    for m in range(sections):

        @pl.when(section == m)
        def _(m=m):
            def one(j, carry):
                at = pl.ds(pl.multiple_of(j * 128, 128), 128)
                og[0:real, at] = og3[:, m, at].astype(F32)
                return carry

            lax.fori_loop(0, wide // 128, one, 0)

    og[real:, :] = jnp.zeros((rows - real, wide), F32)
    finish_stats(exchange(count, s1, send1, recv1), valid, stats, 0)

    def activate(row, gain, source, store):
        def body(at):
            hn = (source[:, at] - stats[row : row + 1, at]) * stats[row + 1 : row + 2, at]
            source[:, at] = hn
            n = gb2(gain, at) * hn + gb2(gain + 1, at)
            store(at, pack[:, 0:1] * (n * sigmoid(n)))

        return body

    def to_act(at, value):
        act[:, at] = value

    def to_a2(at, value):
        a2[:, at] = value.astype(BF16)

    over(narrow, 128, activate(0, 0, h1n, to_act))
    for t, (vertical, lateral) in enumerate(OFFSETS):
        shift = 7 * vertical + lateral

        def place(j, carry, t=t, shift=shift):
            at = pl.ds(pl.multiple_of(j * 128, 128), 128)
            to = pl.ds(pl.multiple_of(t * narrow + j * 128, 128), 128)
            moved = unrolled_shift(act[:, at], shift)
            cols[:, to] = (pack[:, 1 + t : 2 + t] * moved).astype(BF16)
            return carry

        lax.fori_loop(0, narrow // 128, place, 0)

    def convolve(at):
        h = dot(cols[...], k2[:, at])
        h2n[:, at] = h
        norm_sums(s2, me, at, pack[:, 0:1] * h, h)

    loads[1].wait()
    over(narrow, TILE, convolve)
    finish_stats(exchange(count, s2, send2, recv2), valid, stats, 2)
    over(narrow, 128, activate(2, 2, h2n, to_a2))

    def expand(at):
        h = dot_t(a2[...], w3[at, :])
        h3n[:, at] = h
        norm_sums(s3, me, at, pack[:, 0:1] * h, h)

    loads[2].wait()
    over(wide, TILE, expand)
    finish_stats(exchange(count, s3, send3, recv3), valid, stats, 4)

    def result(at):
        hn = (h3n[:, at] - stats[4:5, at]) * stats[5:6, at]
        h3n[:, at] = hn
        z = gb3[0:1, at] * hn + gb3[1:2, at] + u[:, at].astype(F32)
        s = sigmoid(z)
        m = pack[:, 0:1]
        y_out[:, at] = (m * (z * s)).astype(BF16)
        grad = (og[:, at] * m * (s * (1.0 + z * (1.0 - s)))).astype(BF16)
        dz[:, at] = grad
        grad = grad.astype(F32)
        back_sums(b3, me, at, grad, hn)

    over(wide, 128, result)
    total = exchange(count, b3, bsend3, brecv3)
    sums_out[0:2, :] = total

    def through(at):
        offset, scale = sums_out[0:1, at], sums_out[1:2, at]
        dh3[:, at] = (
            pack[:, 0:1]
            * gb3[0:1, at]
            * stats[5:6, at]
            * (dz[:, at].astype(F32) - (offset + h3n[:, at] * scale) / valid)
        ).astype(BF16)

    over(wide, 128, through)

    def into_two(at):
        grad = dot(dh3[...], w3[:, at]).astype(BF16).astype(F32)
        hn = h2n[:, at]
        n = gb2(2, at) * hn + gb2(3, at)
        grad = grad * pack[:, 0:1] * slope(n)
        act[:, at] = grad
        back_sums(b2, me, at, grad, hn)

    over(narrow, TILE, into_two)
    total = exchange(count, b2, bsend2, brecv2)
    sums_out[2:4, 0:narrow] = total

    def through_two(at):
        offset, scale = sums_out[2:3, at], sums_out[3:4, at]
        grad = (
            pack[:, 0:1]
            * gb2(2, at)
            * stats[3:4, at]
            * (act[:, at] - (offset + h2n[:, at] * scale) / valid)
        )
        dh2[:, at] = grad.astype(BF16)
        act[:, at] = dh2[:, at].astype(F32)

    over(narrow, 128, through_two)
    h2n[...] = jnp.zeros((rows, narrow), F32)
    for t, (vertical, lateral) in enumerate(OFFSETS):
        shift = -(7 * vertical + lateral)
        other = 8 - t

        def place_back(j, carry, t=t, shift=shift, other=other):
            at = pl.ds(pl.multiple_of(j * 128, 128), 128)
            moved = unrolled_shift(act[:, at], shift)
            dy[:, at] = (pack[:, 1 + other : 2 + other] * moved).astype(BF16)
            return carry

        lax.fori_loop(0, narrow // 128, place_back, 0)

        def gather(at, t=t):
            row = pl.ds(pl.multiple_of(t * narrow + at.start, TILE), TILE)
            h2n[:, at] += dot_t(dy[:, 0:narrow], k2[row, :])

        over(narrow, TILE, gather)

    def into_one(at):
        hn = h1n[:, at]
        n = gb2(0, at) * hn + gb2(1, at)
        grad = h2n[:, at] * pack[:, 0:1] * slope(n)
        act[:, at] = grad
        back_sums(b1, me, at, grad, hn)

    over(narrow, 128, into_one)
    total = exchange(count, b1, bsend1, brecv1)
    sums_out[4:6, 0:narrow] = total

    def through_one(at):
        offset, scale = sums_out[4:5, at], sums_out[5:6, at]
        dh1[:, at] = (
            pack[:, 0:1]
            * gb2(0, at)
            * stats[1:2, at]
            * (act[:, at] - (offset + h1n[:, at] * scale) / valid)
        ).astype(BF16)

    over(narrow, 128, through_one)

    def into_input(at):
        grad = dot_t(dh1[...], w2[at, :]) + dz[:, at].astype(F32)
        dy[:, at] = dot(back[...], grad.astype(BF16)).astype(BF16)

    over(wide, TILE, into_input)
    writer = Writer(stage, stage_sem)
    writer.rows_of_dot(dh3, a2, p3_out)
    writer.rows_of_dot(cols, dh2, k2_out)
    writer.rows_of_dot(u, dh1, p2_out)
    writer.drain()
    wait_map()


def image_back_part(
    count, after, dy, res, h3n, mask, gb, stats, valid, w1, dz, dh3, da2, sums_out, b3, send3, recv3
):
    wide = dy.shape[1]
    quarter = res.shape[2]
    narrow = da2.shape[1]
    me = lax.axis_index("dp")
    for q in range(wide // quarter):

        def body(j, carry, q=q):
            at = pl.ds(pl.multiple_of(q * quarter + j * 128, 128), 128)
            own = pl.ds(pl.multiple_of(j * 128, 128), 128)
            hn = h3n[:, at]
            z = gb[0:1, at] * hn + gb[1:2, at] + res[q, :, own].astype(F32)
            grad = (dy[:, at].astype(F32) * mask[:, 0:1] * slope(z)).astype(BF16)
            dz[:, at] = grad
            back_sums(b3, me, at, grad.astype(F32), hn)
            return carry

        lax.fori_loop(0, quarter // 128, body, 0)
    after()
    total = exchange(count, b3, send3, recv3)
    sums_out[...] = total

    def through(at):
        offset, scale = sums_out[0:1, at], sums_out[1:2, at]
        dh3[:, at] = (
            mask[:, 0:1]
            * gb[0:1, at]
            * stats[1:2, at]
            * (dz[:, at].astype(F32) - (offset + h3n[:, at] * scale) / valid)
        ).astype(BF16)

    over(wide, 128, through)

    def into(at):
        da2[:, at] = dot(dh3[...], w1[:, at]).astype(BF16)

    over(narrow, TILE, into)


def last_part(
    count, between, taps_term, da2, k, gb, pack, h1n, h2n, stats, counts, dh2, dh1, sums_out, act, acc, hold, *sync
):
    b2, send2, recv2, b1, send1, recv1 = sync
    rows, narrow = h1n.shape
    full = act.shape[1]
    me = lax.axis_index("dp")
    valid = counts[0:4, 0:1]

    def tile8(v):
        return v.reshape(rows // 8, 8, v.shape[1])

    for m in range(4):

        def put(j, carry, m=m):
            at = pl.ds(pl.multiple_of(j * 128, 128), 128)
            act[j, pl.ds(m, full // 4, stride=4), :] = da2[m, :, at].astype(F32)
            return carry

        lax.fori_loop(0, narrow // 128, put, 0)

    def into(gain, source, hidden, slots):
        def body(at):
            hn = hidden[:, at]
            n = gb[gain : gain + 1, at] * hn + gb[gain + 1 : gain + 2, at]
            grad = source(at) * pack[:, 0:1] * slope(n)
            act[lane(at), 0:rows, :] = grad
            slots[me, 0:4, at] = by_batch(grad)
            slots[me, 4:8, at] = by_batch(grad * hn)

        return body

    def through(gain, stat_at, row, hidden, out):
        def body(at):
            offset = spread8(sums_out[row : row + 4, at] / valid)
            scale = spread8(sums_out[row + 4 : row + 8, at] / valid)
            inv = spread8(stats[stat_at : stat_at + 4, at])
            g = tile8(act[lane(at), 0:rows, :])
            value = inv * gb[gain : gain + 1, at][None] * (g - (offset + tile8(hidden[:, at]) * scale))
            value = (pack[:, 0:1] * value.reshape(rows, value.shape[2])).astype(BF16)
            out[:, at] = value
            act[lane(at), 0:rows, :] = value.astype(F32)

        return body

    over(narrow, 128, into(2, lambda at: act[lane(at), 0:rows, :], h2n, b2))
    sums_out[0:8, :] = exchange(count, b2, send2, recv2)
    between()
    over(narrow, 128, through(2, 12, 0, h2n, dh2))
    acc[...] = jnp.zeros((rows, narrow), F32)
    for t, (vertical, lateral) in enumerate(OFFSETS):
        shift = -4 * (7 * vertical + lateral)
        other = 8 - t

        def place_back(j, carry, t=t, shift=shift, other=other):
            at = pl.ds(pl.multiple_of(j * 128, 128), 128)
            moved = unrolled_shift(act[j, 0:rows, :], shift)
            hold[:, at] = (pack[:, 1 + other : 2 + other] * moved).astype(BF16)
            return carry

        lax.fori_loop(0, narrow // 128, place_back, 0)

        def gather(at, t=t):
            row = pl.ds(pl.multiple_of(t * narrow + at.start, TILE), TILE)
            acc[:, at] += dot_t(hold[...], k[row, :])

        over(narrow, TILE, gather)
        taps_term(t)
    over(narrow, 128, into(0, lambda at: acc[:, at], h1n, b1))
    sums_out[8:16, :] = exchange(count, b1, send1, recv1)
    over(narrow, 128, through(0, 4, 8, h1n, dh1))


def back_kernel(
    sections,
    count,
    dy,
    res,
    h3n,
    mask,
    gains,
    stats3,
    w1,
    k_far,
    gb,
    pack,
    h1n_far,
    h2n_far,
    stats,
    counts,
    p3,
    p2,
    k2,
    y2,
    a2,
    a1_in,
    x_in,
    dh1,
    sums3,
    sums12,
    p3_out,
    p2_out,
    k2_out,
    dz_all,
    map_two,
    map_three,
    p1_out,
    k0_out,
    p0_out,
    sh_out,
    dz,
    dh3,
    dh2,
    dzq_out,
    a1,
    x,
    k,
    h1n,
    h2n,
    stage,
    stage_sem,
    x_sem,
    da2,
    da2_all,
    dzq,
    act,
    acc,
    hold,
    *rest,
):
    sync, rest = rest[:9], list(rest[9:])
    halves, theirs, pieces, totals, chips, wholes = (
        rest[:3], rest[3:6], rest[6:9], rest[9:11], rest[11:13], rest[13:16]
    )
    load_sem, swap_send, swap_recv, piece_send, piece_recv, next_send, next_recv, share_send, share_recv, out_sem = rest[16:26]
    rest = rest[26:]
    a_send, a_recv, q_send, q_recv = rest[:4]
    maps = [rest[4:7], rest[7:10], rest[10:13]]
    me, place = lax.axis_index("segment"), lax.axis_index("dp")
    quarter, narrow = dzq.shape[2], da2.shape[1]
    greet(count, sections)
    send_dz, wait_dz = map_sender(sections, dz, dz_all, 0, *maps[0])
    send_two, wait_two = map_sender(sections, dy, map_two, 2, *maps[1])
    send_three, wait_three = map_sender(sections, y2, map_three, 3, *maps[2])

    def q_copy(k_):
        other = jnp.bitwise_xor(me, k_)
        at = pl.ds(pl.multiple_of(other * quarter, 128), quarter)
        return mesh_copy(dz.at[:, at], dzq.at[me], q_send.at[k_], q_recv.at[k_], other, place)

    greeted(count, sections)
    core, z = lax.rem(place, 2), lax.div(place, 2)
    depth = count // 2
    x_loads = [
        pltpu.make_async_copy(src, dst, x_sem.at[i])
        for i, (src, dst) in enumerate(
            ((h2n_far, h2n), (k_far, k), (h1n_far, h1n), (a1_in, a1), (x_in, x))
        )
    ]
    for copy in x_loads:
        copy.start()
    terms = (p3, p2, k2)
    loads = [pltpu.make_async_copy(terms[i].at[core], halves[i], load_sem.at[i]) for i in range(3)]
    swaps = [
        mesh_copy(
            terms[i].at[1 - core],
            theirs[i],
            swap_send.at[i],
            swap_recv.at[i],
            me,
            place + 1 - 2 * core,
        )
        for i in range(3)
    ]
    for i in range(3):
        swaps[i].start()
        loads[i].start()

    def to_section(i, k_):
        other = jnp.bitwise_xor(me, k_)
        return mesh_copy(
            halves[i].at[other],
            pieces[i].at[k_],
            piece_send.at[i, k_],
            piece_recv.at[i, k_],
            other,
            place,
        )

    def to_chip(k_):
        to = lax.rem(z + k_, depth)
        return mesh_copy(
            halves[2].at[:, to],
            pieces[2].at[k_],
            piece_send.at[2, k_],
            piece_recv.at[2, k_],
            me,
            2 * to + core,
        )

    def add_cores(i):
        loads[i].wait()
        swaps[i].wait_recv()

        def add(n):
            q, y = lax.div(n, depth), lax.rem(n, depth)
            halves[i][q, y] = (
                halves[i][q, y].astype(F32) + theirs[i][q, y].astype(F32)
            ).astype(BF16)

        loop(0, sections * depth, add)

    send_three()

    def after():
        return

    image_back_part(
        count,
        after,
        dy,
        res,
        h3n,
        mask,
        gains.at[1],
        stats3,
        batch_valid(counts, 0),
        w1,
        dz,
        dh3,
        da2,
        sums3,
        *sync[:3],
    )

    def a_copy(k_):
        return mesh_copy(da2, da2_all.at[me], a_send, a_recv.at[k_], 0, place)

    for k_ in range(1, sections):

        @pl.when(me == k_)
        def _(k_=k_):
            a_copy(k_).start()

    for i in range(2):
        add_cores(i)
        for k_ in range(1, sections):
            to_section(i, k_).start()
    for k_ in range(1, sections):
        q_copy(k_).start()
    send_dz()
    send_two()
    add_cores(2)

    def to_chips():
        loop(1, depth, lambda k_: to_chip(k_).start())

    pl.when(me != 0)(to_chips)

    @pl.when(me == 0)
    def _():
        for k_ in range(1, sections):
            a_copy(k_).wait_recv()
        da2_all[0] = da2[...]
        for copy in x_loads:
            copy.wait()
        writer = Writer(stage, stage_sem)

        def taps_term(t):
            tall = narrow
            writer.put(dot_0(a1[...], hold[...]), k0_out.at[pl.ds(t * tall, tall)])

        last_part(
            count,
            to_chips,
            taps_term,
            da2_all,
            k,
            gb,
            pack,
            h1n,
            h2n,
            stats,
            counts,
            dh2,
            dh1,
            sums12,
            act,
            acc,
            hold,
            *sync[3:],
        )
        writer.rows_of_dot(x, dh1, p0_out)
        writer.drain()

    @pl.when(me != 0)
    def _():
        for copy in x_loads:
            copy.wait()
        a_copy(0).wait_send()
        sums12[...] = jnp.zeros(sums12.shape, F32)

    def next_chip(i, k_):
        to = lax.rem(z + k_, depth)
        return mesh_copy(
            totals[i].at[to],
            chips[i].at[k_],
            next_send.at[i, k_],
            next_recv.at[i, k_],
            me,
            2 * to + core,
        )

    def share(i, k_):
        return mesh_copy(
            wholes[i].at[z],
            wholes[i].at[z],
            share_send.at[i, k_],
            share_recv.at[i, k_],
            me,
            2 * lax.rem(z + k_, depth) + core,
        )

    for i in range(2):
        for k_ in range(1, sections):
            to_section(i, k_).wait_recv()

        def p_sum(y, i=i):
            total = halves[i][me, y].astype(F32)
            for k_ in range(1, sections):
                total = total + pieces[i][k_, y].astype(F32)
            totals[i][y] = total.astype(BF16)

        loop(0, depth, p_sum)
        loop(1, depth, lambda k_, i=i: next_chip(i, k_).start())
    loop(1, depth, lambda k_: to_chip(k_).wait_recv())

    def k2_sum(q):
        total = halves[2][q, z].astype(F32)
        for k_ in range(1, depth):
            total = total + pieces[2][k_, q].astype(F32)
        wholes[2][q] = total.astype(BF16)

    loop(0, sections, k2_sum)
    for k_ in range(1, sections):
        q_copy(k_).wait_recv()
    dzq[me] = dz[:, pl.ds(pl.multiple_of(me * quarter, 128), quarter)]
    rows, full = dzq_out.shape[0], act.shape[1]
    for m in range(4):

        def put(j, carry, m=m):
            at = pl.ds(pl.multiple_of(j * 128, 128), 128)
            act[j, pl.ds(m, full // 4, stride=4), :] = dzq[m, :, at].astype(F32)
            return carry

        lax.fori_loop(0, quarter // 128, put, 0)

    def weave(j, carry):
        at = pl.ds(pl.multiple_of(j * 128, 128), 128)
        dzq_out[:, at] = act[j, 0:rows, :].astype(BF16)
        return carry

    lax.fori_loop(0, quarter // 128, weave, 0)
    writer = Writer(stage, stage_sem)
    writer.rows_of_dot(x, dzq_out, sh_out)
    writer.rows_of_dot(dh3, a2, p1_out)
    writer.drain()
    for i in range(2):
        loop(1, depth, lambda k_, i=i: next_chip(i, k_).wait_recv())
        total = totals[i][z].astype(F32)
        for k_ in range(1, depth):
            total = total + chips[i][k_].astype(F32)
        wholes[i][z] = total.astype(BF16)
        loop(1, depth, lambda k_, i=i: share(i, k_).start())
    outs = []
    for i, out in enumerate((p3_out, p2_out, k2_out)):
        if i < 2:
            loop(1, depth, lambda k_, i=i: share(i, k_).wait_recv())
        outs.append(pltpu.make_async_copy(wholes[i], out, out_sem.at[i]))
        outs[i].start()
    for k_ in range(1, sections):
        q_copy(k_).wait_send()
        for i in range(2):
            to_section(i, k_).wait_send()
    loop(1, depth, lambda k_: to_chip(k_).wait_send())
    for i in range(2):
        loop(1, depth, lambda k_, i=i: next_chip(i, k_).wait_send())
    for i in range(3):
        swaps[i].wait_send()
        if i < 2:
            loop(1, depth, lambda k_, i=i: share(i, k_).wait_send())
        outs[i].wait()
    wait_dz()
    wait_two()
    wait_three()


SUMS = (
    ("k0", 0, "owner"),
    ("p0", 0, "owner"),
    ("p1", 1, "each"),
    ("p3", 3, "done"),
    ("p2", 2, "done"),
    ("k2", 2, "chips"),
)


def gradient_kernel(
    sections,
    count,
    sh,
    k0,
    p0,
    p1,
    p3,
    p2,
    k2,
    vec,
    dh1,
    w,
    short,
    map_zero,
    map_one,
    map_two,
    map_three,
    sh_out,
    p_out,
    k_out,
    vec_out,
    maps,
    *scratch,
):
    names = [name for name, _, _ in SUMS]
    terms = dict(zip(names, (k0, p0, p1, p3, p2, k2)))
    owner = {name: section for name, section, _ in SUMS}
    held = {name: kind for name, _, kind in SUMS}
    fresh = [name for name in names if held[name] in ("owner", "each")]
    depth = count // 2
    me, place = lax.axis_index("segment"), lax.axis_index("dp")
    core, z = lax.rem(place, 2), lax.div(place, 2)
    sibling = place + 1 - 2 * core
    scratch = list(scratch)
    take = lambda: scratch.pop(0)
    half, theirs, planes, total, others, whole = {}, {}, {}, {}, {}, {}
    for name in names:
        if name in fresh:
            half[name], theirs[name] = take(), take()
        if held[name] in ("each", "chips"):
            planes[name] = take()
        if name in fresh:
            total[name], others[name] = take(), take()
        whole[name] = terms[name] if held[name] == "done" else take()
    relay = {name: take() for name in names if owner[name] == 0}
    relay["sh"] = take()
    sh_half, sh_theirs, sh_others, sh_whole, vec_slots = take(), take(), take(), take(), take()
    load_sem, a_send, a_recv, b_send, b_recv, c_send, c_recv, d_send, d_recv = (take() for _ in range(9))
    e_send, e_recv, e_own, f_send, f_recv, v_send, v_recv = (take() for _ in range(7))
    r_send, r_recv = take(), take()
    pages, s_rows, w_rows, hold, stage, page_sem, s_sem, w_sem, stage_sem = (take() for _ in range(9))
    slot = {name: i for i, name in enumerate(names)}
    last = len(names)

    page_loads = [
        pltpu.make_async_copy(source, pages, page_sem)
        for source in (map_zero, map_one, map_two, map_three)
    ]
    for i, copy in enumerate(page_loads):
        pl.when(me == i)(copy.start)
    wide = pages.shape[2]
    full_rows, map_rows = hold.shape[1], maps.shape[0] * maps.shape[1]

    def tile_loads(j):
        at = pl.ds(pl.multiple_of(j * TILE, TILE), TILE)
        at_slot = lax.rem(j, 2)
        return (
            pltpu.make_async_copy(short.at[at], s_rows.at[at_slot], s_sem.at[at_slot]),
            pltpu.make_async_copy(w.at[at], w_rows.at[at_slot], w_sem.at[at_slot]),
        )

    def tile_store(j):
        at = pl.ds(pl.multiple_of(j * TILE, TILE), TILE)
        at_slot = lax.rem(j, 2)
        return pltpu.make_async_copy(stage.at[at_slot], maps.at[:, :, at], stage_sem.at[at_slot])

    @pl.when(me == 0)
    def _():
        for copy in tile_loads(0):
            copy.start()

    def map_tile(j):
        at = pl.ds(pl.multiple_of(j * TILE, TILE), TILE)
        at_slot = lax.rem(j, 2)

        def weave(m, value):
            for part in range(TILE // 128):
                hold[part, pl.ds(m, full_rows // 4, stride=4), :] = value[
                    :, part * 128 : part * 128 + 128
                ]

        @pl.when(j >= 2)
        def _():
            tile_store(j - 2).wait()

        @pl.when(me == 0)
        def _():
            @pl.when(j + 1 < wide // TILE)
            def _():
                for copy in tile_loads(j + 1):
                    copy.start()

            for copy in tile_loads(j):
                copy.wait()
            for m in range(4):
                weave(m, dot_t(pages[m], s_rows[at_slot]))
            extra = dot_t(dh1[...], w_rows[at_slot])
            for part in range(TILE // 128):
                cols = slice(part * 128, part * 128 + 128)
                value = (hold[part, 0:map_rows, :] + extra[:, cols]).astype(BF16)
                stage[at_slot, :, :, cols] = value.reshape(map_rows // 4, 4, 128)

        @pl.when(me != 0)
        def _():
            for m in range(4):
                weave(m, pages[m, :, at].astype(F32))
            for part in range(TILE // 128):
                cols = slice(part * 128, part * 128 + 128)
                value = hold[part, 0:map_rows, :].astype(BF16)
                stage[at_slot, :, :, cols] = value.reshape(map_rows // 4, 4, 128)

        tile_store(j).start()

    def chip(k):
        return 2 * lax.rem(z + k, depth) + core

    barrier = pltpu.get_barrier_semaphore()
    pl.semaphore_signal(barrier, inc=1, device_id=(me, sibling), device_id_type=MESH)
    for k in range(1, sections):
        pl.semaphore_signal(
            barrier, inc=1, device_id=(jnp.bitwise_xor(me, k), place), device_id_type=MESH
        )
    loop(
        1,
        depth,
        lambda k: pl.semaphore_signal(
            barrier, inc=1, device_id=(me, chip(k)), device_id_type=MESH
        ),
    )
    pl.semaphore_wait(barrier, 1 + sections - 1 + depth - 1)

    def swap(name):
        return mesh_copy(
            terms[name].at[1 - core],
            theirs[name],
            a_send.at[slot[name]],
            a_recv.at[slot[name]],
            me,
            sibling,
        )

    def load(name):
        return pltpu.make_async_copy(terms[name].at[core], half[name], load_sem.at[slot[name]])

    def when_held(name, body):
        if held[name] == "each":
            body()
        else:
            pl.when(me == owner[name])(body)

    sh_rows = sh_half.shape[0]
    sh_swap = mesh_copy(
        sh.at[1 - core], sh_theirs, a_send.at[last], a_recv.at[last], me, sibling
    )
    sh_load = pltpu.make_async_copy(sh.at[core], sh_half, load_sem.at[last])
    sh_swap.start()
    sh_load.start()

    def vec_copy(k):
        other = jnp.bitwise_xor(me, k)
        return mesh_copy(
            vec.at[other], vec_slots.at[k], v_send.at[k], v_recv.at[k], other, place
        )

    for k in range(1, sections):
        vec_copy(k).start()
    for name in fresh:

        def begin(name=name):
            swap(name).start()
            load(name).start()

        when_held(name, begin)

    def final(name):
        return k_out if name[0] == "k" else p_out

    def deliver(name, k):
        return mesh_copy(
            whole[name],
            final(name).at[core, me],
            e_send.at[slot[name]],
            e_recv.at[slot[name], k],
            owner[name],
            place,
        )

    def keep_own(name):
        return pltpu.make_async_copy(whole[name], final(name).at[core, me], e_own.at[slot[name]])

    def to_plane(name, k):
        other = jnp.bitwise_xor(me, k)
        return mesh_copy(
            terms[name].at[other],
            planes[name].at[k],
            b_send.at[slot[name], k],
            b_recv.at[slot[name], k],
            other,
            place,
        )

    def load_plane(name):
        return pltpu.make_async_copy(terms[name].at[me], planes[name].at[0], load_sem.at[slot[name]])

    for name in names:
        if held[name] == "chips":
            for k in range(1, sections):
                to_plane(name, k).start()
            load_plane(name).start()
        if held[name] == "done":

            @pl.when(me == owner[name])
            def _(name=name):
                keep_own(name).start()

            for k in range(1, sections):

                @pl.when(me == owner[name] ^ k)
                def _(name=name, k=k):
                    deliver(name, k).start()

    piece = sh_rows // depth
    step = 32

    def sh_at(i):
        return pl.ds(pl.multiple_of(i * piece, 16), piece)

    def sh_send(k):
        to = lax.rem(z + k, depth)
        return mesh_copy(
            sh_half.at[sh_at(to)],
            sh_others.at[k],
            c_send.at[last, k],
            c_recv.at[last, k],
            me,
            2 * to + core,
        )

    sh_load.wait()
    sh_swap.wait_recv()

    def sh_add(i):
        at = pl.ds(pl.multiple_of(i * step, step), step)
        sh_half[at, :] = (sh_half[at, :].astype(F32) + sh_theirs[at, :].astype(F32)).astype(BF16)

    loop(0, sh_rows // step, sh_add)
    loop(1, depth, lambda k: sh_send(k).start())

    def to_section(name, k):
        other = jnp.bitwise_xor(me, k)
        target = planes[name].at[k] if held[name] == "each" else total[name]
        return mesh_copy(
            half[name].at[other],
            target,
            b_send.at[slot[name], k],
            b_recv.at[slot[name], k],
            other,
            place,
        )

    for name in fresh:

        def combine(name=name):
            load(name).wait()
            swap(name).wait_recv()

            def add(i):
                q, y = lax.div(i, depth), lax.rem(i, depth)
                half[name][q, y] = (
                    half[name][q, y].astype(F32) + theirs[name][q, y].astype(F32)
                ).astype(BF16)

            loop(0, sections * depth, add)
            for k in range(1, sections):
                to_section(name, k).start()

        when_held(name, combine)

    for i, copy in enumerate(page_loads):
        pl.when(me == i)(copy.wait)
    loop(0, 2, map_tile)

    def share(name, k):
        return mesh_copy(
            whole[name].at[z],
            whole[name].at[z],
            d_send.at[slot[name], k],
            d_recv.at[slot[name], k],
            me,
            chip(k),
        )

    loop(1, depth, lambda k: sh_send(k).wait_recv())
    mine = sh_at(z)
    acc = sh_half[mine, :].astype(F32)
    for k in range(1, depth):
        acc = acc + sh_others[k].astype(F32)
    sh_whole[mine, :] = acc.astype(BF16)

    def sh_share(k):
        return mesh_copy(
            sh_whole.at[mine],
            sh_whole.at[mine],
            d_send.at[last, k],
            d_recv.at[last, k],
            me,
            chip(k),
        )

    loop(1, depth, lambda k: sh_share(k).start())
    loop(2, wide // TILE, map_tile)

    for name in names:
        if held[name] == "chips":
            load_plane(name).wait()
            acc = planes[name][0].astype(F32)
            for k in range(1, sections):
                to_plane(name, k).wait_recv()
                acc = acc + planes[name][k].astype(F32)
            whole[name][z] = acc.astype(BF16)
            loop(1, depth, lambda k, name=name: share(name, k).start())

    def to_chip(name, k):
        to = lax.rem(z + k, depth)
        return mesh_copy(
            total[name].at[to],
            others[name].at[k],
            c_send.at[slot[name], k],
            c_recv.at[slot[name], k],
            me,
            2 * to + core,
        )

    for name in fresh:
        if held[name] == "each":
            for k in range(1, sections):
                to_section(name, k).wait_recv()

            def plane_add(y, name=name):
                acc = half[name][me, y].astype(F32)
                for k in range(1, sections):
                    acc = acc + planes[name][k, y].astype(F32)
                total[name][y] = acc.astype(BF16)

            loop(0, depth, plane_add)
        else:

            @pl.when(me == owner[name])
            def _(name=name):
                def keep(y):
                    total[name][y] = half[name][owner[name], y]

                loop(0, depth, keep)

            for k in range(1, sections):

                @pl.when(me == owner[name] ^ k)
                def _(name=name, k=k):
                    to_section(name, k).wait_recv()

        loop(1, depth, lambda k, name=name: to_chip(name, k).start())

    def sh_deliver(k):
        at = pl.ds(pl.multiple_of(me * sh_whole.shape[1], 128), sh_whole.shape[1])
        return mesh_copy(
            sh_whole,
            sh_out.at[core, :, at],
            e_send.at[last],
            e_recv.at[last, k],
            0,
            place,
        )

    loop(1, depth, lambda k: sh_share(k).wait_recv())
    at_zero = pl.ds(0, sh_whole.shape[1])
    sh_keep = pltpu.make_async_copy(sh_whole, sh_out.at[core, :, at_zero], e_own.at[last])

    @pl.when(me == 0)
    def _():
        sh_keep.start()

    for name in fresh:
        loop(1, depth, lambda k, name=name: to_chip(name, k).wait_recv())
        acc = total[name][z].astype(F32)
        for k in range(1, depth):
            acc = acc + others[name][k].astype(F32)
        whole[name][z] = acc.astype(BF16)
        loop(1, depth, lambda k, name=name: share(name, k).start())

    def relayed(name, onward):
        index = last if name == "sh" else slot[name]
        at = pl.ds(3 * sh_whole.shape[1], sh_whole.shape[1])
        src, dst = (sh_whole, sh_out.at[core, :, at]) if name == "sh" else (whole[name], final(name).at[core, 3])
        if onward:
            return mesh_copy(relay[name], dst, r_send.at[index], e_recv.at[index, 3], 0, place)
        return mesh_copy(src, relay[name], e_send.at[index], r_recv.at[index], 1, place)

    def start_delivery(name):
        index = last if name == "sh" else slot[name]
        section = 0 if name == "sh" else owner[name]
        copy = sh_deliver if name == "sh" else functools.partial(deliver, name)
        for k in range(1, sections):
            direct = me == section ^ k
            if section == 0 and k == 3:
                direct = direct & (core == 0)

                @pl.when((me == 3) & (core == 1))
                def _():
                    relayed(name, False).start()

            @pl.when(direct)
            def _(k=k):
                copy(k).start()

    def pass_on(name):
        @pl.when((me == 1) & (core == 1))
        def _():
            relayed(name, False).wait_recv()
            relayed(name, True).start()

    start_delivery("sh")
    for name in ["k2"] + fresh:
        if name == fresh[-1]:
            pass_on("sh")
        loop(1, depth, lambda k, name=name: share(name, k).wait_recv())

        @pl.when(me == owner[name])
        def _(name=name):
            keep_own(name).start()

        start_delivery(name)
    for name in fresh:
        if owner[name] == 0:
            pass_on(name)

    def cross(name):
        return mesh_copy(
            final(name).at[core],
            final(name).at[core],
            f_send.at[slot[name]],
            f_recv.at[slot[name]],
            me,
            sibling,
        )

    sh_cross = mesh_copy(
        sh_out.at[core], sh_out.at[core], f_send.at[last], f_recv.at[last], me, sibling
    )

    @pl.when(me == 0)
    def _():
        sh_keep.wait()
        for k in range(1, sections):
            sh_deliver(k).wait_recv()
        sh_cross.start()

    for name in names:

        @pl.when(me == owner[name])
        def _(name=name):
            keep_own(name).wait()
            for k in range(1, sections):
                deliver(name, k).wait_recv()
            cross(name).start()

    for k in range(1, sections):
        vec_copy(k).wait_recv()
    sums = vec[me]
    for k in range(1, sections):
        sums = sums + vec_slots[k]
    vec_out[...] = sums

    tile_store(wide // TILE - 2).wait()
    tile_store(wide // TILE - 1).wait()
    for k in range(1, sections):
        vec_copy(k).wait_send()
    sh_swap.wait_send()
    loop(1, depth, lambda k: sh_send(k).wait_send())
    loop(1, depth, lambda k: sh_share(k).wait_send())

    @pl.when(me == 0)
    def _():
        sh_cross.wait()

    @pl.when(me != 0)
    def _():
        sh_deliver(0).wait_send()

    @pl.when((me == 1) & (core == 1))
    def _():
        for name in relay:
            relayed(name, True).wait_send()

    for name in names:

        def sent(name=name):
            swap(name).wait_send()
            for k in range(1, sections):
                to_section(name, k).wait_send()

        if name in fresh:
            when_held(name, sent)
            loop(1, depth, lambda k, name=name: to_chip(name, k).wait_send())
        if held[name] == "chips":
            for k in range(1, sections):
                to_plane(name, k).wait_send()
        if held[name] != "done":
            loop(1, depth, lambda k, name=name: share(name, k).wait_send())

        @pl.when(me == owner[name])
        def _(name=name):
            cross(name).wait()

        @pl.when(me != owner[name])
        def _(name=name):
            deliver(name, 0).wait_send()


def sum_gradients(sections, count, short, terms, vectors, dh1, w, weights, map_sources, real):
    narrow = short.shape[1]
    depth = count // 2
    args, scratch = [], []
    relays = []
    for name, section, kind in SUMS:
        args.append(terms[name])
        full = (sections, depth) + terms[name].shape[-2:]
        shapes = []
        if kind in ("owner", "each"):
            shapes += [full, full]
        if kind == "each":
            shapes.append(full)
        if kind == "chips":
            shapes.append((sections,) + full[2:])
        if kind in ("owner", "each"):
            shapes += [full[1:]] * 2
        if kind != "done":
            shapes.append(full[1:])
        if section == 0:
            relays.append(pltpu.VMEM(full[1:], BF16))
        scratch += [pltpu.VMEM(a, BF16) for a in shapes]
    scratch += relays + [pltpu.VMEM((short.shape[0] // 2, narrow), BF16)]
    sh_rows = short.shape[0] // 2
    scratch += [
        pltpu.VMEM((sh_rows, narrow), BF16),
        pltpu.VMEM((sh_rows, narrow), BF16),
        pltpu.VMEM((depth, sh_rows // depth, narrow), BF16),
        pltpu.VMEM((sh_rows, narrow), BF16),
        pltpu.VMEM((sections,) + vectors.shape[1:], F32),
    ]
    kinds = len(SUMS) + 1
    for shape in [(kinds,)] * 3 + [(kinds, sections)] * 2 + [(kinds, depth)] * 4:
        scratch.append(pltpu.SemaphoreType.DMA(shape))
    for shape in [(kinds,), (kinds, sections), (kinds,), (kinds,), (kinds,), (sections,), (sections,), (kinds,), (kinds,)]:
        scratch.append(pltpu.SemaphoreType.DMA(shape))
    wide = w.shape[0]
    padded = map_sources[0].shape[1]
    scratch += [
        pltpu.VMEM(map_sources[0].shape, BF16),
        pltpu.VMEM((2, TILE, wide), BF16),
        pltpu.VMEM((2, TILE, narrow), BF16),
        pltpu.VMEM((TILE // 128, 4 * padded, 128), F32),
        pltpu.VMEM((2, real, 4, TILE), BF16),
        pltpu.SemaphoreType.DMA,
        pltpu.SemaphoreType.DMA((2,)),
        pltpu.SemaphoreType.DMA((2,)),
        pltpu.SemaphoreType.DMA((2,)),
    ]
    hbm = pl.BlockSpec(memory_space=pl.ANY)
    vmem = pl.BlockSpec(memory_space=pltpu.VMEM)
    taps_shape, proj_shape = args[0].shape, args[1].shape
    return pl.pallas_call(
        functools.partial(gradient_kernel, sections, count),
        out_shape=[
            shape_of((2, sh_rows, narrow * sections), BF16),
            shape_of(proj_shape, BF16),
            shape_of(taps_shape, BF16),
            shape_of(vectors.shape[1:], F32),
            shape_of((real, 4, wide), BF16),
        ],
        in_specs=[hbm] * 7 + [vmem, vmem] + [hbm] * 6,
        out_specs=[hbm, hbm, hbm, vmem, hbm],
        scratch_shapes=scratch,
        compiler_params=pltpu.CompilerParams(
            has_side_effects=True, vmem_limit_bytes=VMEM_BYTES, collective_id=5
        ),
        cost_estimate=pl.CostEstimate(flops=0, bytes_accessed=400 * 2**20, transcendentals=0),
    )(short.reshape(2, sh_rows, narrow), *args, vectors, dh1, w, weights, *map_sources)


def cast_kernel(proj, taps, short, proj_out, taps_out, short_out):
    me = lax.axis_index("segment")
    proj_out[...] = proj[...].astype(F32)
    for held, src, out in (
        ((me == 0) | (me == 2), taps, taps_out),
        (me == 0, short, short_out),
    ):

        @pl.when(held)
        def _(src=src, out=out):
            out[...] = src[...].astype(F32)

        @pl.when(jnp.logical_not(held))
        def _(out=out):
            out[...] = jnp.zeros(out.shape, F32)


def cast_sums(*sums):
    steps = 8
    blocks = [pl.BlockSpec((a.shape[0] // steps, a.shape[1]), lambda i: (i, 0)) for a in sums]
    return pl.pallas_call(
        cast_kernel,
        grid=(steps,),
        out_shape=[shape_of(a.shape, F32) for a in sums],
        in_specs=blocks,
        out_specs=blocks,
        compiler_params=pltpu.CompilerParams(vmem_limit_bytes=VMEM_BYTES),
        cost_estimate=pl.CostEstimate(flops=0, bytes_accessed=45 * 2**20, transcendentals=0),
    )(*sums)


def layouts(resolution_ids, order_ids):
    pixels = jnp.arange(MAP * MAP, dtype=jnp.int32)
    row_of = pixels // MAP
    column_of = pixels % MAP
    extent = 5 + resolution_ids[:, None]
    image_mask = ((row_of[None, :] < extent) & (column_of[None, :] < extent)).astype(F32)
    inside = (row_of < 6) & (column_of < 6)
    position = jnp.where(inside, row_of // 2 * 3 + column_of // 2, 0)
    onehot_tile = (position[:, None] == jnp.arange(9)[None, :]).astype(jnp.int32)
    picked = jnp.sum(onehot_tile[None] * order_ids[:, None, :], axis=2)
    row_to = 2 * (picked // 3) + row_of % 2
    column_to = 2 * (picked % 3) + column_of % 2
    target = row_to * MAP + column_to
    tile_mask = (inside & (row_to < extent) & (column_to < extent)).astype(F32)
    return image_mask, tile_mask, jnp.where(inside, target, -1)


def tap_tables(tiled):
    lattice = np.arange(MAP)
    tables = []
    for vertical, lateral in OFFSETS:
        row, column = lattice + vertical, lattice + lateral
        in_row = (row >= 0) & (row < MAP)
        in_column = (column >= 0) & (column < MAP)
        if tiled:
            in_row &= row // 2 == lattice // 2
            in_column &= column // 2 == lattice // 2
        tables.append((in_row[:, None] & in_column[None, :]).reshape(-1))
    return np.stack(tables, axis=1).astype(np.float32)


def body(
    layer_input,
    output_grad,
    resolution,
    tile_order,
    proj_weight,
    spatial_weight,
    shortcut_weight,
    bn_gain,
    bn_bias,
):
    micro, images, pixels, wide = layer_input.shape
    narrow = proj_weight.shape[2]
    rows = images * pixels
    padded = -(-rows // 16) * 16
    sections = lax.axis_size("segment")
    count = lax.axis_size("dp")
    section = lax.axis_index("segment")
    first = section == 0
    proj, spatial, shortcut = proj_weight[0], spatial_weight[0], shortcut_weight[0]
    pick = lambda a: lax.dynamic_index_in_dim(a, section, 0, keepdims=False)

    image_masks, tile_masks, targets = layouts(
        resolution.reshape(-1), tile_order.reshape(micro * images, -1)
    )
    interleave = lambda a: jnp.transpose(a.reshape(micro, rows), (1, 0)).reshape(rows * micro, 1)
    taps_image = np.tile(np.repeat(tap_tables(False), micro, axis=0), (images, 1))
    pack_all = jnp.concatenate(
        [interleave(image_masks), jnp.asarray(taps_image), jnp.zeros((rows * micro, 6), F32)], axis=1
    )
    tiles_all = interleave(tile_masks)
    pad_rows = lambda a: jnp.pad(a, ((0, padded - rows), (0, 0)))
    image_mask = pad_rows(pick(image_masks.reshape(micro, rows, 1)))
    tile_mask = pad_rows(pick(tile_masks.reshape(micro, rows, 1)))
    taps_tile = np.pad(np.tile(tap_tables(True), (images, 1)), ((0, padded - rows), (0, 6)))
    pack_tile = jnp.concatenate([tile_mask, jnp.asarray(taps_tile)], axis=1)
    target = pick(targets.reshape(micro, images, pixels))
    base = (jnp.arange(images) * pixels)[:, None]
    target = jnp.where(target >= 0, target + base, -1).reshape(rows)
    target = jnp.pad(target, (0, padded - rows), constant_values=-1)
    index = jnp.arange(padded)
    moves = (target[:, None] == index[None, :]).astype(BF16)
    moves_back = (target[None, :] == index[:, None]).astype(BF16)

    x_in = jnp.transpose(layer_input, (1, 2, 0, 3)).reshape(rows, micro, wide)
    og_in = jnp.transpose(output_grad, (1, 2, 0, 3)).reshape(rows, micro, wide)
    gb_first = jnp.stack(
        [bn_gain[0, :narrow], bn_bias[0, :narrow]]
        + [bn_gain[0, narrow : 2 * narrow], bn_bias[0, narrow : 2 * narrow]]
    )
    gains_here = jnp.concatenate([bn_gain, bn_bias])
    total = rows * micro
    quarter = wide // sections
    dma = pltpu.SemaphoreType.DMA
    stats_all, counts, gains, y1, u, h3n, stats3, *far = kernel_call(
        functools.partial(head_kernel, sections, count),
        [
            shape_of((16, narrow), F32),
            shape_of((8, 128), F32),
            shape_of((sections, 2, wide), F32),
            shape_of((padded, wide), BF16),
            shape_of((padded, wide), BF16),
            shape_of((padded, wide), F32),
            shape_of((2, wide), F32),
            shape_of((padded, narrow), BF16),
            shape_of((wide, narrow), BF16),
            shape_of((sections, padded, quarter), BF16),
            shape_of((total, wide), BF16),
            shape_of((total, narrow), BF16),
            shape_of((total, narrow), F32),
            shape_of((total, narrow), F32),
            shape_of((wide, narrow), BF16),
            shape_of((wide, narrow), BF16),
            shape_of((9 * narrow, narrow), BF16),
        ],
        [x_in, proj, shortcut, spatial, gb_first, gains_here, pack_all, tiles_all, image_mask, moves],
        [
            pltpu.VMEM((total, wide), BF16),
            pltpu.VMEM((total, 9 * narrow), BF16),
            pltpu.VMEM((total, narrow), F32),
            pltpu.VMEM((total, narrow), F32),
            pltpu.VMEM((narrow // 128, 4 * padded, 128), F32),
            pltpu.VMEM((micro, padded, narrow), BF16),
            pltpu.VMEM((padded, narrow), BF16),
            pltpu.VMEM((wide, quarter), BF16),
            pltpu.VMEM((wide, narrow), BF16),
            pltpu.VMEM((micro, padded, quarter), BF16),
            pltpu.VMEM((sections, padded, quarter), BF16),
            pltpu.VMEM((sections, 2, wide), F32),
        ]
        + sync_scratch(count, [(8, narrow + 128), (8, narrow), (2, wide)])
        + [dma((sections,)), dma, dma, dma]
        + [dma((sections,)), dma, dma, dma]
        + [dma((sections,)), dma((sections,)), dma((sections,)), dma]
        + [dma((sections,)), dma((sections,)), dma((2,)), dma((7,))]
        + [dma((5, sections)), dma((5,)), dma((5,)), dma((5,))]
        + [dma((5, 2)), dma((5, 2)), dma((3,))]
        + [dma((5,)), pltpu.VMEM((9 * narrow, narrow), BF16), dma],
        0,
        2 * total * (narrow * (wide + 9 * narrow) + wide * quarter),
        60 * 2**20,
        far_in=(2, 3),
        far_out=tuple(range(7, 17)),
    )
    a2, w1, res, x_all, a1_all, h1n_all, h2n_all, w3, w2, k2 = far
    paged = shape_of((sections, padded, wide), BF16)
    y2, dy1, t_sums, map_one, p3_term, p2_term, k2_term = kernel_call(
        functools.partial(tile_kernel, sections, count),
        [
            shape_of((padded, wide), BF16),
            shape_of((padded, wide), BF16),
            shape_of((6, wide), F32),
            paged,
            shape_of((wide, narrow), BF16),
            shape_of((wide, narrow), BF16),
            shape_of((9 * narrow, narrow), BF16),
        ],
        [u, w2, k2, w3, og_in, pack_tile, gains, counts, moves_back, y1],
        [
            pltpu.VMEM((padded, narrow), BF16),
            pltpu.VMEM((padded, 9 * narrow), BF16),
            pltpu.VMEM((padded, wide), BF16),
            pltpu.VMEM((padded, narrow), BF16),
            pltpu.VMEM((padded, narrow), BF16),
            pltpu.VMEM((2, 512, narrow), BF16),
            dma((2,)),
            pltpu.VMEM((9 * narrow, narrow), BF16),
            pltpu.VMEM((wide, narrow), BF16),
            pltpu.VMEM((rows, micro, wide), BF16),
            dma((3,)),
            pltpu.VMEM((padded, narrow), F32),
            pltpu.VMEM((padded, narrow), F32),
            pltpu.VMEM((padded, wide), F32),
            pltpu.VMEM((padded, narrow), F32),
            pltpu.VMEM((padded, wide), BF16),
            pltpu.VMEM((6, wide), F32),
            pltpu.VMEM((padded, wide), F32),
        ]
        + [dma, dma((sections,)), dma]
        + sync_scratch(
            count, [(2, narrow), (2, narrow), (2, wide), (2, wide), (2, narrow), (2, narrow)]
        ),
        1,
        4 * padded * narrow * (2 * wide + 9 * narrow),
        30 * 2**20,
        far_in=(2, 3, 4, 9),
        far_out=(3, 4, 5, 6),
    )
    depth = count // 2

    def split(term):
        return term.reshape(2, sections, depth, term.shape[0] // (2 * sections * depth), narrow)

    p3_term, p2_term, k2_term = split(p3_term), split(p2_term), split(k2_term)
    proj_piece, taps_piece = p3_term.shape[3], k2_term.shape[3]
    dh1_all, i_sums, f_sums, p3_part, p2_part, k2_part, *far = kernel_call(
        functools.partial(back_kernel, sections, count),
        [
            shape_of((total, narrow), BF16),
            shape_of((2, wide), F32),
            shape_of((16, narrow), F32),
            shape_of((depth, proj_piece, narrow), BF16),
            shape_of((depth, proj_piece, narrow), BF16),
            shape_of((sections, taps_piece, narrow), BF16),
            paged,
            paged,
            paged,
            shape_of((wide, narrow), BF16),
            shape_of((9 * narrow, narrow), BF16),
            shape_of((wide, narrow), BF16),
            shape_of((wide, narrow), BF16),
        ],
        [dy1, res, h3n, image_mask, gains, stats3, w1, spatial, gb_first, pack_all]
        + [h1n_all, h2n_all, stats_all, counts, p3_term, p2_term, k2_term, y2, a2, a1_all, x_all],
        [
            pltpu.VMEM((padded, wide), BF16),
            pltpu.VMEM((padded, wide), BF16),
            pltpu.VMEM((total, narrow), BF16),
            pltpu.VMEM((total, quarter), BF16),
            pltpu.VMEM((total, narrow), BF16),
            pltpu.VMEM((total, wide), BF16),
            pltpu.VMEM((9 * narrow, narrow), BF16),
            pltpu.VMEM((total, narrow), F32),
            pltpu.VMEM((total, narrow), F32),
            pltpu.VMEM((2, 512, narrow), BF16),
            dma((2,)),
            dma((5,)),
            pltpu.VMEM((padded, narrow), BF16),
            pltpu.VMEM((micro, padded, narrow), BF16),
            pltpu.VMEM((micro, padded, quarter), BF16),
            pltpu.VMEM((narrow // 128, 4 * padded, 128), F32),
            pltpu.VMEM((total, narrow), F32),
            pltpu.VMEM((total, narrow), BF16),
        ]
        + sync_scratch(count, [(2, wide), (8, narrow), (8, narrow)])
        + [pltpu.VMEM(a.shape[1:], BF16) for a in (p3_term, p2_term, k2_term)] * 2
        + [pltpu.VMEM(p3_term.shape[1:], BF16)] * 2
        + [pltpu.VMEM((depth, sections, taps_piece, narrow), BF16)]
        + [pltpu.VMEM((depth, proj_piece, narrow), BF16)] * 6
        + [pltpu.VMEM((sections, taps_piece, narrow), BF16)]
        + [dma((3,))] * 3
        + [dma((3, max(sections, depth)))] * 6
        + [dma((3,))]
        + [dma, dma((sections,)), dma((sections,)), dma((sections,))]
        + [dma, dma((sections,)), dma] * 3,
        2,
        2 * total * narrow * 9 * narrow,
        40 * 2**20,
        far_in=(7, 10, 11, 14, 15, 16, 17, 19, 20),
        far_out=tuple(range(3, 13)),
    )
    map_zero, map_two, map_three, p1_term, k0_term, p0_term, short_term = far

    terms = {
        "p3": p3_part,
        "k2": k2_part,
        "p2": p2_part,
        "p1": split(p1_term),
        "k0": split(k0_term),
        "p0": split(p0_term),
    }

    blank = jnp.zeros((wide,), F32)
    pad = jnp.zeros((wide - 2 * narrow,), F32)
    of_batches = lambda at: jnp.sum(f_sums[at : at + 4], axis=0)
    zero_gain = jnp.where(first, jnp.concatenate([of_batches(12), of_batches(4), pad]), blank)
    zero_bias = jnp.where(first, jnp.concatenate([of_batches(8), of_batches(0), pad]), blank)
    vectors = jnp.stack(
        [
            zero_gain,
            zero_bias,
            i_sums[1],
            i_sums[0],
            jnp.concatenate([t_sums[5, :narrow], t_sums[3, :narrow], pad]),
            jnp.concatenate([t_sums[4, :narrow], t_sums[2, :narrow], pad]),
            t_sums[1],
            t_sums[0],
        ]
    )
    short_sum, proj_sum, taps_sum, vectors, maps = sum_gradients(
        sections,
        count,
        short_term,
        terms,
        vectors.reshape(sections, 2, wide),
        dh1_all,
        proj,
        shortcut,
        (map_zero, map_one, map_two, map_three),
        rows,
    )
    maps = jnp.transpose(maps.reshape(images, pixels, micro, wide), (2, 0, 1, 3))
    proj_grad, spatial_grad, short_grad = cast_sums(
        proj_sum.reshape(wide, narrow),
        taps_sum.reshape(9 * narrow, narrow),
        short_sum.reshape(wide, wide),
    )
    return (
        maps[None],
        proj_grad[None],
        spatial_grad[None],
        short_grad[None],
        vectors[:1],
        vectors[1:],
    )


def solution(mesh):
    return jax.shard_map(
        body,
        mesh=mesh,
        in_specs=(
            P(None, "dp", None, None),
            P(None, "dp", None, None),
            P(None, "dp"),
            P(None, "dp", None),
            P("segment", None, None),
            P("segment", None, None),
            P("segment", None, None),
            P("segment", None),
            P("segment", None),
        ),
        out_specs=(
            P("segment", None, "dp", None, None),
            P("segment", None, None),
            P("segment", None, None),
            P("segment", None, None),
            P("segment", None),
            P("segment", None),
        ),
        check_vma=False,
    )
```

```python
import functools

import jax
import jax.numpy as jnp
import numpy as np
from jax import lax
from jax.experimental import pallas as pl
from jax.experimental.pallas import tpu as pltpu
from jax.sharding import PartitionSpec as P

MAP = 7
EPSILON = 1e-05
OFFSETS = ((-1, -1), (-1, 0), (-1, 1), (0, -1), (0, 0), (0, 1), (1, -1), (1, 0), (1, 1))
MESH = pl.DeviceIdType.MESH
F32 = jnp.float32
BF16 = jnp.bfloat16
VMEM_BYTES = 60 * 2**20
TILE = 256


def greet(count, sections=0):
    segment, me = lax.axis_index("segment"), lax.axis_index("dp")
    barrier = pltpu.get_barrier_semaphore()

    def one(k, carry):
        pl.semaphore_signal(
            barrier, inc=1, device_id=(segment, lax.rem(me + k, count)), device_id_type=MESH
        )
        return carry

    lax.fori_loop(1, count, one, 0)
    for k in range(1, sections):
        pl.semaphore_signal(
            barrier, inc=1, device_id=(jnp.bitwise_xor(segment, k), me), device_id_type=MESH
        )


def greeted(count, sections=1):
    pl.semaphore_wait(pltpu.get_barrier_semaphore(), count - 1 + sections - 1)


def exchange(count, slots, send_sem, recv_sem):
    segment, me = lax.axis_index("segment"), lax.axis_index("dp")

    def copy(k):
        return pltpu.make_async_remote_copy(
            src_ref=slots.at[me],
            dst_ref=slots.at[me],
            send_sem=send_sem.at[k],
            recv_sem=recv_sem.at[k],
            device_id=(segment, lax.rem(me + k, count)),
            device_id_type=MESH,
        )

    def start(k, carry):
        copy(k).start()
        return carry

    def finish(k, carry):
        copy(k).wait_recv()
        copy(k).wait_send()
        return carry

    lax.fori_loop(1, count, start, 0)
    lax.fori_loop(1, count, finish, 0)
    total = slots[0]
    for k in range(1, count):
        total = total + slots[k]
    return total


def mesh_copy(src, dst, send_sem, recv_sem, segment, place):
    return pltpu.make_async_remote_copy(
        src_ref=src,
        dst_ref=dst,
        send_sem=send_sem,
        recv_sem=recv_sem,
        device_id=(segment, place),
        device_id_type=MESH,
    )


def loop(low, high, body):
    def one(k, carry):
        body(k)
        return carry

    lax.fori_loop(low, high, one, 0)


def sync_scratch(count, shapes):
    out = []
    for shape in shapes:
        out += [
            pltpu.VMEM((count,) + shape, F32),
            pltpu.SemaphoreType.DMA((count,)),
            pltpu.SemaphoreType.DMA((count,)),
        ]
    return out


def kernel_call(kernel, outs, args, scratch, ident, flops, moved, far_in=(), far_out=()):
    params = dict(has_side_effects=True, vmem_limit_bytes=VMEM_BYTES)
    if ident is not None:
        params["collective_id"] = ident
    return pl.pallas_call(
        kernel,
        out_shape=outs,
        in_specs=[
            pl.BlockSpec(memory_space=pl.ANY if i in far_in else pltpu.VMEM) for i in range(len(args))
        ],
        out_specs=[
            pl.BlockSpec(memory_space=pl.ANY if i in far_out else pltpu.VMEM) for i in range(len(outs))
        ],
        scratch_shapes=scratch,
        compiler_params=pltpu.CompilerParams(**params),
        cost_estimate=pl.CostEstimate(flops=flops, bytes_accessed=moved, transcendentals=0),
    )(*args)


def shape_of(shape, dtype):
    return jax.ShapeDtypeStruct(shape, dtype)


def dot(a, b):
    return jnp.dot(a, b, preferred_element_type=F32)


def dot_t(a, b):
    return lax.dot_general(a, b, (((1,), (1,)), ((), ())), preferred_element_type=F32)


def dot_0(a, b):
    return lax.dot_general(a, b, (((0,), (0,)), ((), ())), preferred_element_type=F32)


class Writer:
    def __init__(self, stage, sems):
        self.stage, self.sems, self.open, self.turn = stage, sems, [None, None], 0

    def put(self, value, dst):
        at = self.turn % 2
        self.turn += 1
        if self.open[at] is not None:
            self.open[at].wait()
        self.stage[at] = value.astype(BF16)
        self.open[at] = pltpu.make_async_copy(self.stage.at[at], dst, self.sems.at[at])
        self.open[at].start()

    def rows_of_dot(self, left, right, out):
        tall = self.stage.shape[1]
        for j in range(out.shape[0] // tall):
            at = pl.ds(j * tall, tall)
            self.put(dot_0(left[:, at], right[...]), out.at[at])

    def drain(self):
        for at in range(2):
            if self.open[at] is not None:
                self.open[at].wait()
        self.open = [None, None]


def sigmoid(v):
    return 1.0 / (1.0 + jnp.exp(-v))


def slope(v):
    s = sigmoid(v)
    return s * (1.0 + v * (1.0 - s))


def over(width, step, body):
    def one(j, carry):
        body(pl.ds(pl.multiple_of(j * step, step), step))
        return carry

    lax.fori_loop(0, width // step, one, 0)


def lane(at):
    return lax.div(at.start, 128)


def unrolled_shift(ref_value, shift):
    rows = ref_value.shape[0]
    return ref_value if shift % rows == 0 else pltpu.roll(ref_value, (-shift) % rows, 0)


def by_batch(values):
    rows, width = values.shape
    part = jnp.sum(values.reshape(rows // 8, 8, width), axis=0)
    return part[:4] + part[4:]


def spread8(values):
    return jnp.concatenate([values, values], axis=0)[None]


def first_part(
    count, hooks, writes, x, w, k, gb, pack, tiles, a2_out, cols, h1n, h2n, stats_out, count_out, act, *sync
):
    s1, send1, recv1, s2, send2, recv2 = sync
    rows, narrow = h1n.shape
    me = lax.axis_index("dp")
    full = act.shape[1]

    def tile8(v):
        return v.reshape(rows // 8, 8, v.shape[1])

    def project(at):
        h = dot(x[...], w[:, at])
        h1n[:, at] = h
        m = pack[:, 0:1] * h
        s1[me, 0:4, at] = by_batch(m)
        s1[me, 4:8, at] = by_batch(m * h)

    over(narrow, TILE, project)
    s1[me, 0:4, narrow:] = jnp.broadcast_to(by_batch(pack[:, 0:1]), (4, 128))
    s1[me, 4:8, narrow:] = jnp.broadcast_to(by_batch(tiles[:, 0:1]), (4, 128))
    total = exchange(count, s1, send1, recv1)
    counts = total[:, narrow:]
    count_out[...] = counts
    valid = counts[0:4, 0:1]
    average = total[0:4, :narrow] / valid
    inverse = lax.rsqrt(total[4:8, :narrow] / valid - average * average + EPSILON)
    stats_out[0:4, :] = average
    stats_out[4:8, :] = inverse
    hooks[0]()

    def activate(stat_at, gain_at, source):
        def body(at):
            mean = spread8(stats_out[stat_at : stat_at + 4, at])
            inv = spread8(stats_out[stat_at + 4 : stat_at + 8, at])
            hn = (tile8(source[:, at]) - mean) * inv
            source[:, at] = hn.reshape(rows, hn.shape[2])
            n = gb[gain_at : gain_at + 1, at][None] * hn + gb[gain_at + 1 : gain_at + 2, at][None]
            n = n.reshape(rows, n.shape[2])
            act[lane(at), 0:rows, :] = pack[:, 0:1] * (n * sigmoid(n))

        return body

    over(narrow, 128, activate(0, 0, h1n))

    for t, (vertical, lateral) in enumerate(OFFSETS):
        shift = 4 * (7 * vertical + lateral)

        def place(j, carry, t=t, shift=shift):
            at = pl.ds(pl.multiple_of(j * 128, 128), 128)
            to = pl.ds(pl.multiple_of(t * narrow + j * 128, 128), 128)
            moved = unrolled_shift(act[j, 0:rows, :], shift)
            cols[:, to] = (pack[:, 1 + t : 2 + t] * moved).astype(BF16)
            return carry

        lax.fori_loop(0, narrow // 128, place, 0)

    def convolve(at):
        h = dot(cols[...], k[:, at])
        h2n[:, at] = h
        m = pack[:, 0:1] * h
        s2[me, 0:4, at] = by_batch(m)
        s2[me, 4:8, at] = by_batch(m * h)

    for write in writes:
        write.start()
    hooks[1]()
    over(narrow, TILE, convolve)
    total = exchange(count, s2, send2, recv2)
    average = total[0:4] / valid
    hooks[2]()
    stats_out[8:12, :] = average
    stats_out[12:16, :] = lax.rsqrt(total[4:8] / valid - average * average + EPSILON)
    over(narrow, 128, activate(8, 2, h2n))
    act[:, rows:, :] = jnp.zeros((narrow // 128, full - rows, 128), F32)
    for m in range(4):

        def pick(j, carry, m=m):
            at = pl.ds(pl.multiple_of(j * 128, 128), 128)
            a2_out[m, :, at] = act[j, pl.ds(m, full // 4, stride=4), :].astype(BF16)
            return carry

        lax.fori_loop(0, narrow // 128, pick, 0)


def residual_part(x, w, out, hold):
    rows, full, quarter = x.shape[0], hold.shape[1], out.shape[2]
    hold[:, rows:, :] = jnp.zeros((quarter // 128, full - rows, 128), F32)

    def body(at):
        value = dot(x[...], w[:, at])
        for part in range(TILE // 128):
            hold[lane(at) + part, 0:rows, :] = value[:, part * 128 : part * 128 + 128]

    over(quarter, TILE, body)
    for m in range(4):

        def pick(j, carry, m=m):
            at = pl.ds(pl.multiple_of(j * 128, 128), 128)
            out[m, :, at] = hold[j, pl.ds(m, full // 4, stride=4), :].astype(BF16)
            return carry

        lax.fori_loop(0, quarter // 128, pick, 0)


def norm_sums(slots, me, at, masked, h):
    slots[me, 0:1, at] = jnp.sum(masked, axis=0, keepdims=True)
    slots[me, 1:2, at] = jnp.sum(masked * h, axis=0, keepdims=True)


def finish_stats(total, valid, stats_out, at_row):
    average = total[0:1] / valid
    width = average.shape[1]
    stats_out[at_row : at_row + 1, 0:width] = average
    stats_out[at_row + 1 : at_row + 2, 0:width] = lax.rsqrt(
        total[1:2] / valid - average * average + EPSILON
    )


def second_part(
    count, before, a2, w1, res, mask, gb, valid, moves, y_out, u_out, h3n, stats_out, s1, send1, recv1
):
    wide = h3n.shape[1]
    quarter = res.shape[2]
    me = lax.axis_index("dp")

    def project(at):
        h = dot_t(a2[...], w1[at, :])
        h3n[:, at] = h
        norm_sums(s1, me, at, mask[:, 0:1] * h, h)

    over(wide, TILE, project)
    finish_stats(exchange(count, s1, send1, recv1), valid, stats_out, 0)
    before()
    for q in range(wide // quarter):

        def body(j, carry, q=q):
            at = pl.ds(pl.multiple_of(q * quarter + j * 128, 128), 128)
            own = pl.ds(pl.multiple_of(j * 128, 128), 128)
            hn = (h3n[:, at] - stats_out[0:1, at]) * stats_out[1:2, at]
            h3n[:, at] = hn
            z = gb[1, 0:1, at] * hn + gb[1, 1:2, at] + res[q, :, own].astype(F32)
            y_out[:, at] = (mask[:, 0:1] * (z * sigmoid(z))).astype(BF16)
            return carry

        lax.fori_loop(0, quarter // 128, body, 0)

    def permute(at):
        u_out[:, at] = dot(moves[...], y_out[:, at]).astype(BF16)

    over(wide, TILE, permute)


def batch_valid(counts, row):
    me = lax.axis_index("segment")
    value = counts[row : row + 1, 0:1]
    for m in range(1, 4):
        value = jnp.where(me == m, counts[row + m : row + m + 1, 0:1], value)
    return value


def head_kernel(
    sections,
    count,
    x3,
    w,
    short,
    k,
    gb,
    vec,
    pack,
    tiles,
    mask,
    moves,
    stats_out,
    count_out,
    g_out,
    y_out,
    u_out,
    h3n,
    stats3,
    a2_out,
    w1_out,
    res_out,
    x_out,
    a1_out,
    h1n_out,
    h2n_out,
    w3_out,
    w2_out,
    k2_out,
    x,
    cols,
    h1n,
    h2n,
    act,
    a2_all,
    a2,
    wsc,
    w1,
    rq,
    res,
    gslots,
    *rest,
):
    sync, rest = rest[:9], list(rest[9:])
    short_send, short_recv, short_relay_send, short_relay_recv = rest[:4]
    w1_send, w1_recv, w1_relay_send, w1_relay_recv = rest[4:8]
    g_send, g_recv, a2_send, a2_recv, res_send, res_recv, own_sem, out_sem = rest[8:16]
    spread_send, spread_recv, far_send, far_recv, near_send, near_recv, keep_sem = rest[16:23]
    pass_send, kv, kv_sem = rest[23:]
    me, place = lax.axis_index("segment"), lax.axis_index("dp")
    core = lax.rem(place, 2)
    sibling = place + 1 - 2 * core
    wide = x.shape[1]
    quarter = wide // sections
    half_rows = wide // 2
    mine = pl.ds(pl.multiple_of(core * half_rows, 16), half_rows)
    greet(count, sections)
    k_load = pltpu.make_async_copy(k, kv, kv_sem)
    k_load.start()

    odd = lax.rem(lax.div(place, 2), 2)
    beside = place + 2 - 4 * odd
    parts = [("w3", w, w3_out, 3, 0, 1), ("w2", w, w2_out, 2, 0, 1)]
    parts += [("k2", k, k2_out, 2, i, 3) for i in range(3)]

    def part_rows(i, at_odd):
        _, src, _, _, piece, pieces = parts[i]
        fine = src.shape[0] // (4 * pieces)
        start = ((2 * at_odd + core) * pieces + piece) * fine
        return pl.ds(pl.multiple_of(start, 16), fine)

    def spread_copy(i, t):
        _, src, dst, _, _, _ = parts[i]
        at = part_rows(i, odd)
        return mesh_copy(src.at[at], dst.at[at], spread_send.at[i, t], spread_recv.at[i], t, place)

    def far_copy(i):
        dst, at = parts[i][2], part_rows(i, odd)
        return mesh_copy(dst.at[at], dst.at[at], far_send.at[i], far_recv.at[i], me, beside)

    def near_copy(i, second):
        dst = parts[i][2]
        at = part_rows(i, 1 - odd if second else odd)
        sems = near_send.at[i, second], near_recv.at[i, second]
        return mesh_copy(dst.at[at], dst.at[at], *sems, me, sibling)

    keeps = [
        (3, pltpu.make_async_copy(w, w3_out, keep_sem.at[0])),
        (2, pltpu.make_async_copy(w, w2_out, keep_sem.at[1])),
        (2, pltpu.make_async_copy(kv, k2_out, keep_sem.at[2])),
    ]

    def spread_start(i):
        owner = parts[i][3]

        @pl.when(me == owner)
        def _():
            for d in (1, 2):
                spread_copy(i, owner ^ d).start()

    def spread_sent(i):
        for d in (1, 2):
            spread_copy(i, parts[i][3] ^ d).wait_send()

    def pass_copy(i):
        dst, at = parts[i][2], part_rows(i, odd)
        return mesh_copy(
            dst.at[at], dst.at[at], pass_send.at[i], spread_recv.at[i], parts[i][3] ^ 3, place
        )

    def spread_on(i):
        owner = parts[i][3]

        @pl.when(me == owner ^ 1)
        def _():
            spread_copy(i, 0).wait_recv()
            pass_copy(i).start()

        @pl.when((me != owner) & (me != owner ^ 1))
        def _():
            spread_copy(i, 0).wait_recv()

        @pl.when(me != owner)
        def _():
            far_copy(i).start()
            near_copy(i, 0).start()

    def far_on(i):
        @pl.when(me != parts[i][3])
        def _():
            far_copy(i).wait_recv()
            near_copy(i, 1).start()

    def short_copy(t):
        src = short.at[mine, pl.ds(t * quarter, quarter)]
        return mesh_copy(src, wsc.at[mine], short_send.at[t], short_recv, t, place)

    def w1_copy(t):
        return mesh_copy(w.at[mine], w1.at[mine], w1_send.at[t], w1_recv, t, place)

    short_own = pltpu.make_async_copy(short.at[:, pl.ds(0, quarter)], wsc, own_sem.at[0])
    w1_own = pltpu.make_async_copy(w, w1, own_sem.at[1])
    short_relay = mesh_copy(
        wsc.at[mine], wsc.at[mine], short_relay_send, short_relay_recv, me, sibling
    )
    w1_relay = mesh_copy(w1.at[mine], w1.at[mine], w1_relay_send, w1_relay_recv, me, sibling)

    def g_copy(k_):
        return mesh_copy(
            gslots.at[me],
            gslots.at[me],
            g_send.at[k_],
            g_recv.at[k_],
            jnp.bitwise_xor(me, k_),
            place,
        )

    gslots[me] = vec[...]
    greeted(count, sections)

    @pl.when(me == 0)
    def _():
        for t in (3, 1, 2):
            short_copy(t).start()
        short_own.start()

    @pl.when(me == 1)
    def _():
        for t in (2, 0, 3):
            w1_copy(t).start()
        w1_own.start()

    for k_ in range(1, sections):
        g_copy(k_).start()
    for i in range(3):
        spread_start(i)
    for owner, copy in keeps[:2]:
        pl.when(me == owner)(copy.start)

    def relayout(j, carry):
        at = pl.ds(pl.multiple_of(j * 128, 128), 128)
        x[:, at] = x3[:, :, at].reshape(x.shape[0], 128)
        return carry

    lax.fori_loop(0, wide // 128, relayout, 0)
    writes = [
        pltpu.make_async_copy(src, dst, out_sem.at[i])
        for i, (src, dst) in enumerate(
            ((x, x_out), (h1n, h1n_out), (cols.at[:, pl.ds(4 * h1n.shape[1], h1n.shape[1])], a1_out), (h2n, h2n_out))
            + ((a2, a2_out), (w1, w1_out), (res, res_out))
        )
    ]
    writes[0].start()

    def a2_copy(t):
        return mesh_copy(a2_all.at[t], a2, a2_send.at[t], a2_recv, t, place)

    @pl.when(me == 0)
    def _():
        def between():
            spread_on(0)
            spread_on(1)

        first_part(
            count,
            (lambda: spread_on(1), k_load.wait, lambda: spread_on(0)),
            writes[1:3],
            x,
            w,
            kv,
            gb,
            pack,
            tiles,
            a2_all,
            cols,
            h1n,
            h2n,
            stats_out,
            count_out,
            act,
            *sync[:6],
        )
        writes[3].start()
        for t in range(1, sections):
            a2_copy(t).start()
        a2[...] = a2_all[0]
        short_own.wait()
        for i in (2, 3, 4):
            spread_on(i)

    @pl.when(me != 0)
    def _():
        k_load.wait()
        pl.when(me == keeps[2][0])(keeps[2][1].start)
        slots, send1, recv1 = sync[:3]
        narrow = h1n.shape[1]
        stats_out[...] = jnp.zeros(stats_out.shape, F32)
        slots[place, :, 0:narrow] = jnp.zeros((8, narrow), F32)
        slots[place, 0:4, narrow:] = jnp.broadcast_to(by_batch(pack[:, 0:1]), (4, 128))
        slots[place, 4:8, narrow:] = jnp.broadcast_to(by_batch(tiles[:, 0:1]), (4, 128))
        count_out[...] = exchange(count, slots, send1, recv1)[:, narrow:]

    def spread_paced(i, after):
        @pl.when(me == parts[i][3])
        def _():
            spread_sent(after)
            for d in (1, 2):
                spread_copy(i, parts[i][3] ^ d).start()

    def unless_zero(i):
        pl.when(me != 0)(lambda: spread_on(i))

    unless_zero(0)
    spread_paced(3, 1)
    unless_zero(1)
    spread_paced(4, 2)
    unless_zero(2)
    unless_zero(3)
    pl.when(me == parts[4][3] ^ 1)(lambda: spread_on(4))

    @pl.when(me != 0)
    def _():
        short_copy(0).wait_recv()
        short_relay.start()

    @pl.when(me == 1)
    def _():
        w1_own.wait()

    @pl.when(me != 1)
    def _():
        w1_copy(0).wait_recv()
        w1_relay.start()

    @pl.when(me != 0)
    def _():
        short_relay.wait_recv()

    residual_part(x, wsc, rq, act)

    def res_copy(k_):
        other = jnp.bitwise_xor(me, k_)
        return mesh_copy(
            rq.at[other], res.at[me], res_send.at[k_], res_recv.at[k_], other, place
        )

    for k_ in range(1, sections):
        res_copy(k_).start()
    res[me] = rq[me]
    pl.when((me != 0) & (me != parts[4][3] ^ 1))(lambda: spread_on(4))

    @pl.when(me != 0)
    def _():
        a2_copy(0).wait_recv()

    @pl.when(me != 1)
    def _():
        w1_relay.wait_recv()

    for k_ in range(1, sections):
        g_copy(k_).wait_recv()
    g_out[...] = gslots[...]

    def before():
        far_on(0)
        far_on(1)
        for k_ in range(1, sections):
            res_copy(k_).wait_recv()

    second_part(
        count,
        before,
        a2,
        w1,
        res,
        mask,
        gslots,
        batch_valid(count_out, 0),
        moves,
        y_out,
        u_out,
        h3n,
        stats3,
        *sync[6:],
    )
    for copy in writes[4:]:
        copy.start()
    for i in range(2, len(parts)):
        far_on(i)
    for k_ in range(1, sections):
        g_copy(k_).wait_send()
        res_copy(k_).wait_send()

    @pl.when(me == 0)
    def _():
        for t in range(1, sections):
            short_copy(t).wait_send()
            a2_copy(t).wait_send()

    @pl.when(me != 0)
    def _():
        short_relay.wait_send()

    @pl.when(me == 1)
    def _():
        for t in (0, 2, 3):
            w1_copy(t).wait_send()

    @pl.when(me != 1)
    def _():
        w1_relay.wait_send()

    for i in range(len(parts)):
        owner = parts[i][3]

        if i not in (1, 2):
            pl.when(me == owner)(functools.partial(spread_sent, i))
        pl.when(me == owner ^ 1)(lambda i=i: pass_copy(i).wait_send())

        @pl.when(me != owner)
        def _(i=i):
            far_copy(i).wait_send()
            near_copy(i, 0).wait()
            near_copy(i, 1).wait()

    for owner, copy in keeps:
        pl.when(me == owner)(copy.wait)
    for i, copy in enumerate(writes):
        if i in (1, 2, 3):
            pl.when(me == 0)(copy.wait)
        else:
            copy.wait()


def back_sums(slots, me, at, grad, hn):
    slots[me, 0:1, at] = jnp.sum(grad, axis=0, keepdims=True)
    slots[me, 1:2, at] = jnp.sum(grad * hn, axis=0, keepdims=True)


def map_sender(sections, src, dst, owner, send_sem, recv_sem, own_sem):
    me, place = lax.axis_index("segment"), lax.axis_index("dp")
    own = pltpu.make_async_copy(src, dst.at[me], own_sem)

    def copy(k):
        return mesh_copy(src, dst.at[me], send_sem, recv_sem.at[k], owner, place)

    def start():
        @pl.when(me == owner)
        def _():
            own.start()

        for k in range(1, sections):

            @pl.when(me == owner ^ k)
            def _(k=k):
                copy(k).start()

    def finish():
        @pl.when(me == owner)
        def _():
            own.wait()
            for k in range(1, sections):
                copy(k).wait_recv()

        @pl.when(me != owner)
        def _():
            copy(0).wait_send()

    return start, finish


def tile_kernel(
    sections,
    count,
    u,
    w2,
    k2_far,
    w3_far,
    og_far,
    pack,
    gains,
    counts,
    back,
    y1,
    y_out,
    dy,
    sums_out,
    map_one,
    p3_out,
    p2_out,
    k2_out,
    a2,
    cols,
    dh3,
    dh2,
    dh1,
    stage,
    stage_sem,
    k2,
    w3,
    og3,
    load_sem,
    h1n,
    h2n,
    h3n,
    act,
    dz,
    stats,
    og,
    map_send,
    map_recv,
    map_own,
    *sync,
):
    s1, send1, recv1, s2, send2, recv2, s3, send3, recv3 = sync[:9]
    b3, bsend3, brecv3, b2, bsend2, brecv2, b1, bsend1, brecv1 = sync[9:]
    rows, wide = u.shape
    narrow = h1n.shape[1]
    me = lax.axis_index("dp")
    section = lax.axis_index("segment")
    valid = batch_valid(counts, 4)
    gb3 = gains.at[3]
    loads = [
        pltpu.make_async_copy(src, dst, load_sem.at[i])
        for i, (src, dst) in enumerate(((og_far, og3), (k2_far, k2), (w3_far, w3)))
    ]
    for load in loads:
        load.start()

    def gb2(row, at):
        return gains[2, row % 2 : row % 2 + 1, pl.ds(at.start + row // 2 * narrow, at.size)]

    greet(count, sections)

    def project(at):
        h = dot(u[...], w2[:, at])
        h1n[:, at] = h
        norm_sums(s1, me, at, pack[:, 0:1] * h, h)

    over(narrow, TILE, project)
    greeted(count, sections)
    send_map, wait_map = map_sender(sections, y1, map_one, 1, map_send, map_recv, map_own)
    send_map()
    loads[0].wait()
    real = og3.shape[0]
    for m in range(sections):

        @pl.when(section == m)
        def _(m=m):
            def one(j, carry):
                at = pl.ds(pl.multiple_of(j * 128, 128), 128)
                og[0:real, at] = og3[:, m, at].astype(F32)
                return carry

            lax.fori_loop(0, wide // 128, one, 0)

    og[real:, :] = jnp.zeros((rows - real, wide), F32)
    finish_stats(exchange(count, s1, send1, recv1), valid, stats, 0)

    def activate(row, gain, source, store):
        def body(at):
            hn = (source[:, at] - stats[row : row + 1, at]) * stats[row + 1 : row + 2, at]
            source[:, at] = hn
            n = gb2(gain, at) * hn + gb2(gain + 1, at)
            store(at, pack[:, 0:1] * (n * sigmoid(n)))

        return body

    def to_act(at, value):
        act[:, at] = value

    def to_a2(at, value):
        a2[:, at] = value.astype(BF16)

    over(narrow, 128, activate(0, 0, h1n, to_act))
    for t, (vertical, lateral) in enumerate(OFFSETS):
        shift = 7 * vertical + lateral

        def place(j, carry, t=t, shift=shift):
            at = pl.ds(pl.multiple_of(j * 128, 128), 128)
            to = pl.ds(pl.multiple_of(t * narrow + j * 128, 128), 128)
            moved = unrolled_shift(act[:, at], shift)
            cols[:, to] = (pack[:, 1 + t : 2 + t] * moved).astype(BF16)
            return carry

        lax.fori_loop(0, narrow // 128, place, 0)

    def convolve(at):
        h = dot(cols[...], k2[:, at])
        h2n[:, at] = h
        norm_sums(s2, me, at, pack[:, 0:1] * h, h)

    loads[1].wait()
    over(narrow, TILE, convolve)
    finish_stats(exchange(count, s2, send2, recv2), valid, stats, 2)
    over(narrow, 128, activate(2, 2, h2n, to_a2))

    def expand(at):
        h = dot_t(a2[...], w3[at, :])
        h3n[:, at] = h
        norm_sums(s3, me, at, pack[:, 0:1] * h, h)

    loads[2].wait()
    over(wide, TILE, expand)
    finish_stats(exchange(count, s3, send3, recv3), valid, stats, 4)

    def result(at):
        hn = (h3n[:, at] - stats[4:5, at]) * stats[5:6, at]
        h3n[:, at] = hn
        z = gb3[0:1, at] * hn + gb3[1:2, at] + u[:, at].astype(F32)
        s = sigmoid(z)
        m = pack[:, 0:1]
        y_out[:, at] = (m * (z * s)).astype(BF16)
        grad = (og[:, at] * m * (s * (1.0 + z * (1.0 - s)))).astype(BF16)
        dz[:, at] = grad
        grad = grad.astype(F32)
        back_sums(b3, me, at, grad, hn)

    over(wide, 128, result)
    total = exchange(count, b3, bsend3, brecv3)
    sums_out[0:2, :] = total

    def through(at):
        offset, scale = sums_out[0:1, at], sums_out[1:2, at]
        dh3[:, at] = (
            pack[:, 0:1]
            * gb3[0:1, at]
            * stats[5:6, at]
            * (dz[:, at].astype(F32) - (offset + h3n[:, at] * scale) / valid)
        ).astype(BF16)

    over(wide, 128, through)

    def into_two(at):
        grad = dot(dh3[...], w3[:, at]).astype(BF16).astype(F32)
        hn = h2n[:, at]
        n = gb2(2, at) * hn + gb2(3, at)
        grad = grad * pack[:, 0:1] * slope(n)
        act[:, at] = grad
        back_sums(b2, me, at, grad, hn)

    over(narrow, TILE, into_two)
    total = exchange(count, b2, bsend2, brecv2)
    sums_out[2:4, 0:narrow] = total

    def through_two(at):
        offset, scale = sums_out[2:3, at], sums_out[3:4, at]
        grad = (
            pack[:, 0:1]
            * gb2(2, at)
            * stats[3:4, at]
            * (act[:, at] - (offset + h2n[:, at] * scale) / valid)
        )
        dh2[:, at] = grad.astype(BF16)
        act[:, at] = dh2[:, at].astype(F32)

    over(narrow, 128, through_two)
    h2n[...] = jnp.zeros((rows, narrow), F32)
    for t, (vertical, lateral) in enumerate(OFFSETS):
        shift = -(7 * vertical + lateral)
        other = 8 - t

        def place_back(j, carry, t=t, shift=shift, other=other):
            at = pl.ds(pl.multiple_of(j * 128, 128), 128)
            moved = unrolled_shift(act[:, at], shift)
            dy[:, at] = (pack[:, 1 + other : 2 + other] * moved).astype(BF16)
            return carry

        lax.fori_loop(0, narrow // 128, place_back, 0)

        def gather(at, t=t):
            row = pl.ds(pl.multiple_of(t * narrow + at.start, TILE), TILE)
            h2n[:, at] += dot_t(dy[:, 0:narrow], k2[row, :])

        over(narrow, TILE, gather)

    def into_one(at):
        hn = h1n[:, at]
        n = gb2(0, at) * hn + gb2(1, at)
        grad = h2n[:, at] * pack[:, 0:1] * slope(n)
        act[:, at] = grad
        back_sums(b1, me, at, grad, hn)

    over(narrow, 128, into_one)
    total = exchange(count, b1, bsend1, brecv1)
    sums_out[4:6, 0:narrow] = total

    def through_one(at):
        offset, scale = sums_out[4:5, at], sums_out[5:6, at]
        dh1[:, at] = (
            pack[:, 0:1]
            * gb2(0, at)
            * stats[1:2, at]
            * (act[:, at] - (offset + h1n[:, at] * scale) / valid)
        ).astype(BF16)

    over(narrow, 128, through_one)

    def into_input(at):
        grad = dot_t(dh1[...], w2[at, :]) + dz[:, at].astype(F32)
        dy[:, at] = dot(back[...], grad.astype(BF16)).astype(BF16)

    over(wide, TILE, into_input)
    writer = Writer(stage, stage_sem)
    writer.rows_of_dot(dh3, a2, p3_out)
    writer.rows_of_dot(cols, dh2, k2_out)
    writer.rows_of_dot(u, dh1, p2_out)
    writer.drain()
    wait_map()


def image_back_part(
    count, after, dy, res, h3n, mask, gb, stats, valid, w1, dz, dh3, da2, sums_out, b3, send3, recv3
):
    wide = dy.shape[1]
    quarter = res.shape[2]
    narrow = da2.shape[1]
    me = lax.axis_index("dp")
    for q in range(wide // quarter):

        def body(j, carry, q=q):
            at = pl.ds(pl.multiple_of(q * quarter + j * 128, 128), 128)
            own = pl.ds(pl.multiple_of(j * 128, 128), 128)
            hn = h3n[:, at]
            z = gb[0:1, at] * hn + gb[1:2, at] + res[q, :, own].astype(F32)
            grad = (dy[:, at].astype(F32) * mask[:, 0:1] * slope(z)).astype(BF16)
            dz[:, at] = grad
            back_sums(b3, me, at, grad.astype(F32), hn)
            return carry

        lax.fori_loop(0, quarter // 128, body, 0)
    after()
    total = exchange(count, b3, send3, recv3)
    sums_out[...] = total

    def through(at):
        offset, scale = sums_out[0:1, at], sums_out[1:2, at]
        dh3[:, at] = (
            mask[:, 0:1]
            * gb[0:1, at]
            * stats[1:2, at]
            * (dz[:, at].astype(F32) - (offset + h3n[:, at] * scale) / valid)
        ).astype(BF16)

    over(wide, 128, through)

    def into(at):
        da2[:, at] = dot(dh3[...], w1[:, at]).astype(BF16)

    over(narrow, TILE, into)


def last_part(
    count, between, taps_term, da2, k, gb, pack, h1n, h2n, stats, counts, dh2, dh1, sums_out, act, acc, hold, *sync
):
    b2, send2, recv2, b1, send1, recv1 = sync
    rows, narrow = h1n.shape
    full = act.shape[1]
    me = lax.axis_index("dp")
    valid = counts[0:4, 0:1]

    def tile8(v):
        return v.reshape(rows // 8, 8, v.shape[1])

    for m in range(4):

        def put(j, carry, m=m):
            at = pl.ds(pl.multiple_of(j * 128, 128), 128)
            act[j, pl.ds(m, full // 4, stride=4), :] = da2[m, :, at].astype(F32)
            return carry

        lax.fori_loop(0, narrow // 128, put, 0)

    def into(gain, source, hidden, slots):
        def body(at):
            hn = hidden[:, at]
            n = gb[gain : gain + 1, at] * hn + gb[gain + 1 : gain + 2, at]
            grad = source(at) * pack[:, 0:1] * slope(n)
            act[lane(at), 0:rows, :] = grad
            slots[me, 0:4, at] = by_batch(grad)
            slots[me, 4:8, at] = by_batch(grad * hn)

        return body

    def through(gain, stat_at, row, hidden, out):
        def body(at):
            offset = spread8(sums_out[row : row + 4, at] / valid)
            scale = spread8(sums_out[row + 4 : row + 8, at] / valid)
            inv = spread8(stats[stat_at : stat_at + 4, at])
            g = tile8(act[lane(at), 0:rows, :])
            value = inv * gb[gain : gain + 1, at][None] * (g - (offset + tile8(hidden[:, at]) * scale))
            value = (pack[:, 0:1] * value.reshape(rows, value.shape[2])).astype(BF16)
            out[:, at] = value
            act[lane(at), 0:rows, :] = value.astype(F32)

        return body

    over(narrow, 128, into(2, lambda at: act[lane(at), 0:rows, :], h2n, b2))
    sums_out[0:8, :] = exchange(count, b2, send2, recv2)
    between()
    over(narrow, 128, through(2, 12, 0, h2n, dh2))
    acc[...] = jnp.zeros((rows, narrow), F32)
    for t, (vertical, lateral) in enumerate(OFFSETS):
        shift = -4 * (7 * vertical + lateral)
        other = 8 - t

        def place_back(j, carry, t=t, shift=shift, other=other):
            at = pl.ds(pl.multiple_of(j * 128, 128), 128)
            moved = unrolled_shift(act[j, 0:rows, :], shift)
            hold[:, at] = (pack[:, 1 + other : 2 + other] * moved).astype(BF16)
            return carry

        lax.fori_loop(0, narrow // 128, place_back, 0)

        def gather(at, t=t):
            row = pl.ds(pl.multiple_of(t * narrow + at.start, TILE), TILE)
            acc[:, at] += dot_t(hold[...], k[row, :])

        over(narrow, TILE, gather)
        taps_term(t)
    over(narrow, 128, into(0, lambda at: acc[:, at], h1n, b1))
    sums_out[8:16, :] = exchange(count, b1, send1, recv1)
    over(narrow, 128, through(0, 4, 8, h1n, dh1))


def back_kernel(
    sections,
    count,
    dy,
    res,
    h3n,
    mask,
    gains,
    stats3,
    w1,
    k_far,
    gb,
    pack,
    h1n_far,
    h2n_far,
    stats,
    counts,
    k2,
    y2,
    a2,
    a1_in,
    x_in,
    dh1,
    sums3,
    sums12,
    k2_out,
    dz_all,
    map_two,
    map_three,
    p1_out,
    k0_out,
    p0_out,
    sh_out,
    dz,
    dh3,
    dh2,
    dzq_out,
    a1,
    x,
    k,
    h1n,
    h2n,
    stage,
    stage_sem,
    x_sem,
    da2,
    da2_all,
    dzq,
    act,
    acc,
    hold,
    *rest,
):
    sync, rest = rest[:9], list(rest[9:])
    half, theirs, pieces, whole = rest[:4]
    load_sem, swap_send, swap_recv, piece_send, piece_recv, out_sem = rest[4:10]
    rest = rest[10:]
    a_send, a_recv, q_send, q_recv = rest[:4]
    maps = [rest[4:7], rest[7:10], rest[10:13]]
    me, place = lax.axis_index("segment"), lax.axis_index("dp")
    quarter, narrow = dzq.shape[2], da2.shape[1]
    greet(count, sections)
    send_dz, wait_dz = map_sender(sections, dz, dz_all, 0, *maps[0])
    send_two, wait_two = map_sender(sections, dy, map_two, 2, *maps[1])
    send_three, wait_three = map_sender(sections, y2, map_three, 3, *maps[2])

    def q_copy(k_):
        other = jnp.bitwise_xor(me, k_)
        at = pl.ds(pl.multiple_of(other * quarter, 128), quarter)
        return mesh_copy(dz.at[:, at], dzq.at[me], q_send.at[k_], q_recv.at[k_], other, place)

    greeted(count, sections)
    core, z = lax.rem(place, 2), lax.div(place, 2)
    depth = count // 2
    x_loads = [
        pltpu.make_async_copy(src, dst, x_sem.at[i])
        for i, (src, dst) in enumerate(
            ((h2n_far, h2n), (k_far, k), (h1n_far, h1n), (a1_in, a1), (x_in, x))
        )
    ]
    for copy in x_loads:
        copy.start()
    load = pltpu.make_async_copy(k2.at[core], half, load_sem)
    swap = mesh_copy(k2.at[1 - core], theirs, swap_send, swap_recv, me, place + 1 - 2 * core)
    swap.start()
    load.start()

    def to_chip(k_):
        to = lax.rem(z + k_, depth)
        return mesh_copy(
            half.at[:, to],
            pieces.at[k_],
            piece_send.at[k_],
            piece_recv.at[k_],
            me,
            2 * to + core,
        )

    def add_cores():
        load.wait()
        swap.wait_recv()

        def add(n):
            q, y = lax.div(n, depth), lax.rem(n, depth)
            half[q, y] = (half[q, y].astype(F32) + theirs[q, y].astype(F32)).astype(BF16)

        loop(0, sections * depth, add)

    send_three()

    def after():
        return

    image_back_part(
        count,
        after,
        dy,
        res,
        h3n,
        mask,
        gains.at[1],
        stats3,
        batch_valid(counts, 0),
        w1,
        dz,
        dh3,
        da2,
        sums3,
        *sync[:3],
    )

    def a_copy(k_):
        return mesh_copy(da2, da2_all.at[me], a_send, a_recv.at[k_], 0, place)

    for k_ in range(1, sections):

        @pl.when(me == k_)
        def _(k_=k_):
            a_copy(k_).start()

    for k_ in range(1, sections):
        q_copy(k_).start()
    send_dz()
    send_two()
    add_cores()

    def to_chips():
        loop(1, depth, lambda k_: to_chip(k_).start())

    pl.when(me != 0)(to_chips)

    @pl.when(me == 0)
    def _():
        for k_ in range(1, sections):
            a_copy(k_).wait_recv()
        da2_all[0] = da2[...]
        for copy in x_loads:
            copy.wait()
        writer = Writer(stage, stage_sem)

        def taps_term(t):
            tall = narrow
            writer.put(dot_0(a1[...], hold[...]), k0_out.at[pl.ds(t * tall, tall)])

        last_part(
            count,
            to_chips,
            taps_term,
            da2_all,
            k,
            gb,
            pack,
            h1n,
            h2n,
            stats,
            counts,
            dh2,
            dh1,
            sums12,
            act,
            acc,
            hold,
            *sync[3:],
        )
        writer.rows_of_dot(x, dh1, p0_out)
        writer.drain()

    @pl.when(me != 0)
    def _():
        for copy in x_loads:
            copy.wait()
        a_copy(0).wait_send()
        sums12[...] = jnp.zeros(sums12.shape, F32)

    loop(1, depth, lambda k_: to_chip(k_).wait_recv())

    def k2_sum(q):
        total = half[q, z].astype(F32)
        for k_ in range(1, depth):
            total = total + pieces[k_, q].astype(F32)
        whole[q] = total.astype(BF16)

    loop(0, sections, k2_sum)
    out = pltpu.make_async_copy(whole, k2_out, out_sem)
    out.start()
    for k_ in range(1, sections):
        q_copy(k_).wait_recv()
    dzq[me] = dz[:, pl.ds(pl.multiple_of(me * quarter, 128), quarter)]
    rows, full = dzq_out.shape[0], act.shape[1]
    for m in range(4):

        def put(j, carry, m=m):
            at = pl.ds(pl.multiple_of(j * 128, 128), 128)
            act[j, pl.ds(m, full // 4, stride=4), :] = dzq[m, :, at].astype(F32)
            return carry

        lax.fori_loop(0, quarter // 128, put, 0)

    def weave(j, carry):
        at = pl.ds(pl.multiple_of(j * 128, 128), 128)
        dzq_out[:, at] = act[j, 0:rows, :].astype(BF16)
        return carry

    lax.fori_loop(0, quarter // 128, weave, 0)
    writer = Writer(stage, stage_sem)
    writer.rows_of_dot(x, dzq_out, sh_out)
    writer.rows_of_dot(dh3, a2, p1_out)
    writer.drain()
    for k_ in range(1, sections):
        q_copy(k_).wait_send()
    loop(1, depth, lambda k_: to_chip(k_).wait_send())
    swap.wait_send()
    out.wait()
    wait_dz()
    wait_two()
    wait_three()


SUMS = (
    ("k0", 0, "owner"),
    ("p0", 0, "owner"),
    ("p1", 1, "each"),
    ("p2", 2, "each"),
    ("p3", 3, "each"),
    ("k2", 2, "chips"),
)


def gradient_kernel(
    sections,
    count,
    sh,
    k0,
    p0,
    p1,
    p2,
    p3,
    k2,
    vec,
    dh1,
    w,
    short,
    map_zero,
    map_one,
    map_two,
    map_three,
    sh_out,
    p_out,
    k_out,
    vec_out,
    maps,
    *scratch,
):
    names = [name for name, _, _ in SUMS]
    terms = dict(zip(names, (k0, p0, p1, p2, p3, k2)))
    owner = {name: section for name, section, _ in SUMS}
    held = {name: kind for name, _, kind in SUMS}
    fresh = [name for name in names if held[name] in ("owner", "each")]
    depth = count // 2
    me, place = lax.axis_index("segment"), lax.axis_index("dp")
    core, z = lax.rem(place, 2), lax.div(place, 2)
    sibling = place + 1 - 2 * core
    scratch = list(scratch)
    take = lambda: scratch.pop(0)
    half, theirs, planes, total, others, whole = {}, {}, {}, {}, {}, {}
    for name in names:
        if name in fresh:
            half[name], theirs[name] = take(), take()
        if held[name] in ("each", "chips"):
            planes[name] = take()
        if name in fresh:
            total[name], others[name] = take(), take()
        whole[name] = terms[name] if held[name] == "done" else take()
    relay = {name: take() for name in names if owner[name] == 0}
    relay["sh"] = take()
    sh_half, sh_theirs, sh_others, sh_whole, vec_slots = take(), take(), take(), take(), take()
    load_sem, a_send, a_recv, b_send, b_recv, c_send, c_recv, d_send, d_recv = (take() for _ in range(9))
    e_send, e_recv, e_own, f_send, f_recv, v_send, v_recv = (take() for _ in range(7))
    r_send, r_recv = take(), take()
    pages, s_rows, w_rows, hold, stage, page_sem, s_sem, w_sem, stage_sem = (take() for _ in range(9))
    slot = {name: i for i, name in enumerate(names)}
    last = len(names)

    page_loads = [
        pltpu.make_async_copy(source, pages, page_sem)
        for source in (map_zero, map_one, map_two, map_three)
    ]
    for i, copy in enumerate(page_loads):
        pl.when(me == i)(copy.start)
    wide = pages.shape[2]
    full_rows, map_rows = hold.shape[1], maps.shape[0] * maps.shape[1]

    def tile_loads(j):
        at = pl.ds(pl.multiple_of(j * TILE, TILE), TILE)
        at_slot = lax.rem(j, 2)
        return (
            pltpu.make_async_copy(short.at[at], s_rows.at[at_slot], s_sem.at[at_slot]),
            pltpu.make_async_copy(w.at[at], w_rows.at[at_slot], w_sem.at[at_slot]),
        )

    def tile_store(j):
        at = pl.ds(pl.multiple_of(j * TILE, TILE), TILE)
        at_slot = lax.rem(j, 2)
        return pltpu.make_async_copy(stage.at[at_slot], maps.at[:, :, at], stage_sem.at[at_slot])

    @pl.when(me == 0)
    def _():
        for copy in tile_loads(0):
            copy.start()

    def map_tile(j):
        at = pl.ds(pl.multiple_of(j * TILE, TILE), TILE)
        at_slot = lax.rem(j, 2)

        def weave(m, value):
            for part in range(TILE // 128):
                hold[part, pl.ds(m, full_rows // 4, stride=4), :] = value[
                    :, part * 128 : part * 128 + 128
                ]

        @pl.when(j >= 2)
        def _():
            tile_store(j - 2).wait()

        @pl.when(me == 0)
        def _():
            @pl.when(j + 1 < wide // TILE)
            def _():
                for copy in tile_loads(j + 1):
                    copy.start()

            for copy in tile_loads(j):
                copy.wait()
            for m in range(4):
                weave(m, dot_t(pages[m], s_rows[at_slot]))
            extra = dot_t(dh1[...], w_rows[at_slot])
            for part in range(TILE // 128):
                cols = slice(part * 128, part * 128 + 128)
                value = (hold[part, 0:map_rows, :] + extra[:, cols]).astype(BF16)
                stage[at_slot, :, :, cols] = value.reshape(map_rows // 4, 4, 128)

        @pl.when(me != 0)
        def _():
            for m in range(4):
                weave(m, pages[m, :, at].astype(F32))
            for part in range(TILE // 128):
                cols = slice(part * 128, part * 128 + 128)
                value = hold[part, 0:map_rows, :].astype(BF16)
                stage[at_slot, :, :, cols] = value.reshape(map_rows // 4, 4, 128)

        tile_store(j).start()

    def chip(k):
        return 2 * lax.rem(z + k, depth) + core

    barrier = pltpu.get_barrier_semaphore()
    pl.semaphore_signal(barrier, inc=1, device_id=(me, sibling), device_id_type=MESH)
    for k in range(1, sections):
        pl.semaphore_signal(
            barrier, inc=1, device_id=(jnp.bitwise_xor(me, k), place), device_id_type=MESH
        )
    loop(
        1,
        depth,
        lambda k: pl.semaphore_signal(
            barrier, inc=1, device_id=(me, chip(k)), device_id_type=MESH
        ),
    )
    pl.semaphore_wait(barrier, 1 + sections - 1 + depth - 1)

    def swap(name):
        return mesh_copy(
            terms[name].at[1 - core],
            theirs[name],
            a_send.at[slot[name]],
            a_recv.at[slot[name]],
            me,
            sibling,
        )

    def load(name):
        return pltpu.make_async_copy(terms[name].at[core], half[name], load_sem.at[slot[name]])

    def when_held(name, body):
        if held[name] == "each":
            body()
        else:
            pl.when(me == owner[name])(body)

    sh_rows = sh_half.shape[0]
    sh_swap = mesh_copy(
        sh.at[1 - core], sh_theirs, a_send.at[last], a_recv.at[last], me, sibling
    )
    sh_load = pltpu.make_async_copy(sh.at[core], sh_half, load_sem.at[last])
    sh_swap.start()
    sh_load.start()

    def vec_copy(k):
        other = jnp.bitwise_xor(me, k)
        return mesh_copy(
            vec.at[other], vec_slots.at[k], v_send.at[k], v_recv.at[k], other, place
        )

    for k in range(1, sections):
        vec_copy(k).start()
    for name in fresh:

        def begin(name=name):
            swap(name).start()
            load(name).start()

        when_held(name, begin)

    def final(name):
        return k_out if name[0] == "k" else p_out

    def deliver(name, k):
        return mesh_copy(
            whole[name],
            final(name).at[core, me],
            e_send.at[slot[name]],
            e_recv.at[slot[name], k],
            owner[name],
            place,
        )

    def keep_own(name):
        return pltpu.make_async_copy(whole[name], final(name).at[core, me], e_own.at[slot[name]])

    def to_plane(name, k):
        other = jnp.bitwise_xor(me, k)
        return mesh_copy(
            terms[name].at[other],
            planes[name].at[k],
            b_send.at[slot[name], k],
            b_recv.at[slot[name], k],
            other,
            place,
        )

    def load_plane(name):
        return pltpu.make_async_copy(terms[name].at[me], planes[name].at[0], load_sem.at[slot[name]])

    for name in names:
        if held[name] == "chips":
            for k in range(1, sections):
                to_plane(name, k).start()
            load_plane(name).start()
        if held[name] == "done":

            @pl.when(me == owner[name])
            def _(name=name):
                keep_own(name).start()

            for k in range(1, sections):

                @pl.when(me == owner[name] ^ k)
                def _(name=name, k=k):
                    deliver(name, k).start()

    piece = sh_rows // depth
    step = 32

    def sh_at(i):
        return pl.ds(pl.multiple_of(i * piece, 16), piece)

    def sh_send(k):
        to = lax.rem(z + k, depth)
        return mesh_copy(
            sh_half.at[sh_at(to)],
            sh_others.at[k],
            c_send.at[last, k],
            c_recv.at[last, k],
            me,
            2 * to + core,
        )

    sh_load.wait()
    sh_swap.wait_recv()

    def sh_add(i):
        at = pl.ds(pl.multiple_of(i * step, step), step)
        sh_half[at, :] = (sh_half[at, :].astype(F32) + sh_theirs[at, :].astype(F32)).astype(BF16)

    loop(0, sh_rows // step, sh_add)
    loop(1, depth, lambda k: sh_send(k).start())

    def to_section(name, k):
        other = jnp.bitwise_xor(me, k)
        target = planes[name].at[k] if held[name] == "each" else total[name]
        return mesh_copy(
            half[name].at[other],
            target,
            b_send.at[slot[name], k],
            b_recv.at[slot[name], k],
            other,
            place,
        )

    for name in fresh:

        def combine(name=name):
            load(name).wait()
            swap(name).wait_recv()

            def add(i):
                q, y = lax.div(i, depth), lax.rem(i, depth)
                half[name][q, y] = (
                    half[name][q, y].astype(F32) + theirs[name][q, y].astype(F32)
                ).astype(BF16)

            loop(0, sections * depth, add)
            for k in range(1, sections):
                to_section(name, k).start()

        when_held(name, combine)

    for i, copy in enumerate(page_loads):
        pl.when(me == i)(copy.wait)
    loop(0, 2, map_tile)

    def share(name, k):
        return mesh_copy(
            whole[name].at[z],
            whole[name].at[z],
            d_send.at[slot[name], k],
            d_recv.at[slot[name], k],
            me,
            chip(k),
        )

    loop(1, depth, lambda k: sh_send(k).wait_recv())
    mine = sh_at(z)
    acc = sh_half[mine, :].astype(F32)
    for k in range(1, depth):
        acc = acc + sh_others[k].astype(F32)
    sh_whole[mine, :] = acc.astype(BF16)

    def sh_share(k):
        return mesh_copy(
            sh_whole.at[mine],
            sh_whole.at[mine],
            d_send.at[last, k],
            d_recv.at[last, k],
            me,
            chip(k),
        )

    loop(1, depth, lambda k: sh_share(k).start())
    loop(2, wide // TILE, map_tile)

    def planes_end(name):
        load_plane(name).wait()
        acc = planes[name][0].astype(F32)
        for k in range(1, sections):
            to_plane(name, k).wait_recv()
            acc = acc + planes[name][k].astype(F32)
        whole[name][z] = acc.astype(BF16)
        loop(1, depth, lambda k: share(name, k).start())

    def to_chip(name, k):
        to = lax.rem(z + k, depth)
        return mesh_copy(
            total[name].at[to],
            others[name].at[k],
            c_send.at[slot[name], k],
            c_recv.at[slot[name], k],
            me,
            2 * to + core,
        )

    def b_end(name):
        if held[name] == "each":
            for k in range(1, sections):
                to_section(name, k).wait_recv()

            def plane_add(y, name=name):
                acc = half[name][me, y].astype(F32)
                for k in range(1, sections):
                    acc = acc + planes[name][k, y].astype(F32)
                total[name][y] = acc.astype(BF16)

            loop(0, depth, plane_add)
        else:

            @pl.when(me == owner[name])
            def _(name=name):
                def keep(y):
                    total[name][y] = half[name][owner[name], y]

                loop(0, depth, keep)

            for k in range(1, sections):

                @pl.when(me == owner[name] ^ k)
                def _(name=name, k=k):
                    to_section(name, k).wait_recv()

        loop(1, depth, lambda k, name=name: to_chip(name, k).start())

    for name in ("k0", "p0"):
        b_end(name)

    def sh_deliver(k):
        at = pl.ds(pl.multiple_of(me * sh_whole.shape[1], 128), sh_whole.shape[1])
        return mesh_copy(
            sh_whole,
            sh_out.at[core, :, at],
            e_send.at[last],
            e_recv.at[last, k],
            0,
            place,
        )

    loop(1, depth, lambda k: sh_share(k).wait_recv())
    at_zero = pl.ds(0, sh_whole.shape[1])
    sh_keep = pltpu.make_async_copy(sh_whole, sh_out.at[core, :, at_zero], e_own.at[last])

    @pl.when(me == 0)
    def _():
        sh_keep.start()

    def relayed(name, onward):
        index = last if name == "sh" else slot[name]
        at = pl.ds(3 * sh_whole.shape[1], sh_whole.shape[1])
        src, dst = (sh_whole, sh_out.at[core, :, at]) if name == "sh" else (whole[name], final(name).at[core, 3])
        if onward:
            return mesh_copy(relay[name], dst, r_send.at[index], e_recv.at[index, 3], 0, place)
        return mesh_copy(src, relay[name], e_send.at[index], r_recv.at[index], 1, place)

    def start_delivery(name):
        index = last if name == "sh" else slot[name]
        section = 0 if name == "sh" else owner[name]
        copy = sh_deliver if name == "sh" else functools.partial(deliver, name)
        for k in range(1, sections):
            direct = me == section ^ k
            if section == 0 and k == 3:
                direct = direct & (core == 0)

                @pl.when((me == 3) & (core == 1))
                def _():
                    relayed(name, False).start()

            @pl.when(direct)
            def _(k=k):
                copy(k).start()

    def pass_on(name):
        @pl.when((me == 1) & (core == 1))
        def _():
            relayed(name, False).wait_recv()
            relayed(name, True).start()

    start_delivery("sh")

    def c_end(name):
        loop(1, depth, lambda k: to_chip(name, k).wait_recv())
        acc = total[name][z].astype(F32)
        for k in range(1, depth):
            acc = acc + others[name][k].astype(F32)
        whole[name][z] = acc.astype(BF16)
        loop(1, depth, lambda k: share(name, k).start())

    def d_end(name):
        loop(1, depth, lambda k: share(name, k).wait_recv())

        @pl.when(me == owner[name])
        def _():
            keep_own(name).start()

        start_delivery(name)

    later = ("p1", "p2", "p3")
    planes_end("k2")
    for name in ("k0", "p0"):
        c_end(name)
    for name in later:
        b_end(name)
    pass_on("sh")
    for name in ("k0", "p0", "k2"):
        d_end(name)
    for name in later:
        c_end(name)
    for name in ("k0", "p0"):
        pass_on(name)
    for name in later:
        d_end(name)

    def cross(name):
        return mesh_copy(
            final(name).at[core],
            final(name).at[core],
            f_send.at[slot[name]],
            f_recv.at[slot[name]],
            me,
            sibling,
        )

    sh_cross = mesh_copy(
        sh_out.at[core], sh_out.at[core], f_send.at[last], f_recv.at[last], me, sibling
    )

    @pl.when(me == 0)
    def _():
        sh_keep.wait()
        for k in range(1, sections):
            sh_deliver(k).wait_recv()
        sh_cross.start()

    for name in names:

        @pl.when(me == owner[name])
        def _(name=name):
            keep_own(name).wait()
            for k in range(1, sections):
                deliver(name, k).wait_recv()
            cross(name).start()

    for k in range(1, sections):
        vec_copy(k).wait_recv()
    sums = vec[me]
    for k in range(1, sections):
        sums = sums + vec_slots[k]
    vec_out[...] = sums

    tile_store(wide // TILE - 2).wait()
    tile_store(wide // TILE - 1).wait()
    for k in range(1, sections):
        vec_copy(k).wait_send()
    sh_swap.wait_send()
    loop(1, depth, lambda k: sh_send(k).wait_send())
    loop(1, depth, lambda k: sh_share(k).wait_send())

    @pl.when(me == 0)
    def _():
        sh_cross.wait()

    @pl.when(me != 0)
    def _():
        sh_deliver(0).wait_send()

    @pl.when((me == 1) & (core == 1))
    def _():
        for name in relay:
            relayed(name, True).wait_send()

    for name in names:

        def sent(name=name):
            swap(name).wait_send()
            for k in range(1, sections):
                to_section(name, k).wait_send()

        if name in fresh:
            when_held(name, sent)
            loop(1, depth, lambda k, name=name: to_chip(name, k).wait_send())
        if held[name] == "chips":
            for k in range(1, sections):
                to_plane(name, k).wait_send()
        if held[name] != "done":
            loop(1, depth, lambda k, name=name: share(name, k).wait_send())

        @pl.when(me == owner[name])
        def _(name=name):
            cross(name).wait()

        @pl.when(me != owner[name])
        def _(name=name):
            deliver(name, 0).wait_send()


def sum_gradients(sections, count, short, terms, vectors, dh1, w, weights, map_sources, real):
    narrow = short.shape[1]
    depth = count // 2
    args, scratch = [], []
    relays = []
    for name, section, kind in SUMS:
        args.append(terms[name])
        full = (sections, depth) + terms[name].shape[-2:]
        shapes = []
        if kind in ("owner", "each"):
            shapes += [full, full]
        if kind == "each":
            shapes.append(full)
        if kind == "chips":
            shapes.append((sections,) + full[2:])
        if kind in ("owner", "each"):
            shapes += [full[1:]] * 2
        if kind != "done":
            shapes.append(full[1:])
        if section == 0:
            relays.append(pltpu.VMEM(full[1:], BF16))
        scratch += [pltpu.VMEM(a, BF16) for a in shapes]
    scratch += relays + [pltpu.VMEM((short.shape[0] // 2, narrow), BF16)]
    sh_rows = short.shape[0] // 2
    scratch += [
        pltpu.VMEM((sh_rows, narrow), BF16),
        pltpu.VMEM((sh_rows, narrow), BF16),
        pltpu.VMEM((depth, sh_rows // depth, narrow), BF16),
        pltpu.VMEM((sh_rows, narrow), BF16),
        pltpu.VMEM((sections,) + vectors.shape[1:], F32),
    ]
    kinds = len(SUMS) + 1
    for shape in [(kinds,)] * 3 + [(kinds, sections)] * 2 + [(kinds, depth)] * 4:
        scratch.append(pltpu.SemaphoreType.DMA(shape))
    for shape in [(kinds,), (kinds, sections), (kinds,), (kinds,), (kinds,), (sections,), (sections,), (kinds,), (kinds,)]:
        scratch.append(pltpu.SemaphoreType.DMA(shape))
    wide = w.shape[0]
    padded = map_sources[0].shape[1]
    scratch += [
        pltpu.VMEM(map_sources[0].shape, BF16),
        pltpu.VMEM((2, TILE, wide), BF16),
        pltpu.VMEM((2, TILE, narrow), BF16),
        pltpu.VMEM((TILE // 128, 4 * padded, 128), F32),
        pltpu.VMEM((2, real, 4, TILE), BF16),
        pltpu.SemaphoreType.DMA,
        pltpu.SemaphoreType.DMA((2,)),
        pltpu.SemaphoreType.DMA((2,)),
        pltpu.SemaphoreType.DMA((2,)),
    ]
    hbm = pl.BlockSpec(memory_space=pl.ANY)
    vmem = pl.BlockSpec(memory_space=pltpu.VMEM)
    taps_shape, proj_shape = args[0].shape, args[1].shape
    return pl.pallas_call(
        functools.partial(gradient_kernel, sections, count),
        out_shape=[
            shape_of((2, sh_rows, narrow * sections), BF16),
            shape_of(proj_shape, BF16),
            shape_of(taps_shape, BF16),
            shape_of(vectors.shape[1:], F32),
            shape_of((real, 4, wide), BF16),
        ],
        in_specs=[hbm] * 7 + [vmem, vmem] + [hbm] * 6,
        out_specs=[hbm, hbm, hbm, vmem, hbm],
        scratch_shapes=scratch,
        compiler_params=pltpu.CompilerParams(
            has_side_effects=True, vmem_limit_bytes=VMEM_BYTES, collective_id=5
        ),
        cost_estimate=pl.CostEstimate(flops=0, bytes_accessed=400 * 2**20, transcendentals=0),
    )(short.reshape(2, sh_rows, narrow), *args, vectors, dh1, w, weights, *map_sources)


def cast_kernel(proj, taps, short, proj_out, taps_out, short_out):
    me = lax.axis_index("segment")
    proj_out[...] = proj[...].astype(F32)
    for held, src, out in (
        ((me == 0) | (me == 2), taps, taps_out),
        (me == 0, short, short_out),
    ):

        @pl.when(held)
        def _(src=src, out=out):
            out[...] = src[...].astype(F32)

        @pl.when(jnp.logical_not(held))
        def _(out=out):
            out[...] = jnp.zeros(out.shape, F32)


def cast_sums(*sums):
    steps = 8
    blocks = [pl.BlockSpec((a.shape[0] // steps, a.shape[1]), lambda i: (i, 0)) for a in sums]
    return pl.pallas_call(
        cast_kernel,
        grid=(steps,),
        out_shape=[shape_of(a.shape, F32) for a in sums],
        in_specs=blocks,
        out_specs=blocks,
        compiler_params=pltpu.CompilerParams(vmem_limit_bytes=VMEM_BYTES),
        cost_estimate=pl.CostEstimate(flops=0, bytes_accessed=45 * 2**20, transcendentals=0),
    )(*sums)


def layouts(resolution_ids, order_ids):
    pixels = jnp.arange(MAP * MAP, dtype=jnp.int32)
    row_of = pixels // MAP
    column_of = pixels % MAP
    extent = 5 + resolution_ids[:, None]
    image_mask = ((row_of[None, :] < extent) & (column_of[None, :] < extent)).astype(F32)
    inside = (row_of < 6) & (column_of < 6)
    position = jnp.where(inside, row_of // 2 * 3 + column_of // 2, 0)
    onehot_tile = (position[:, None] == jnp.arange(9)[None, :]).astype(jnp.int32)
    picked = jnp.sum(onehot_tile[None] * order_ids[:, None, :], axis=2)
    row_to = 2 * (picked // 3) + row_of % 2
    column_to = 2 * (picked % 3) + column_of % 2
    target = row_to * MAP + column_to
    tile_mask = (inside & (row_to < extent) & (column_to < extent)).astype(F32)
    return image_mask, tile_mask, jnp.where(inside, target, -1)


def tap_tables(tiled):
    lattice = np.arange(MAP)
    tables = []
    for vertical, lateral in OFFSETS:
        row, column = lattice + vertical, lattice + lateral
        in_row = (row >= 0) & (row < MAP)
        in_column = (column >= 0) & (column < MAP)
        if tiled:
            in_row &= row // 2 == lattice // 2
            in_column &= column // 2 == lattice // 2
        tables.append((in_row[:, None] & in_column[None, :]).reshape(-1))
    return np.stack(tables, axis=1).astype(np.float32)


def body(
    layer_input,
    output_grad,
    resolution,
    tile_order,
    proj_weight,
    spatial_weight,
    shortcut_weight,
    bn_gain,
    bn_bias,
):
    micro, images, pixels, wide = layer_input.shape
    narrow = proj_weight.shape[2]
    rows = images * pixels
    padded = -(-rows // 16) * 16
    sections = lax.axis_size("segment")
    count = lax.axis_size("dp")
    section = lax.axis_index("segment")
    first = section == 0
    proj, spatial, shortcut = proj_weight[0], spatial_weight[0], shortcut_weight[0]
    pick = lambda a: lax.dynamic_index_in_dim(a, section, 0, keepdims=False)

    image_masks, tile_masks, targets = layouts(
        resolution.reshape(-1), tile_order.reshape(micro * images, -1)
    )
    interleave = lambda a: jnp.transpose(a.reshape(micro, rows), (1, 0)).reshape(rows * micro, 1)
    taps_image = np.tile(np.repeat(tap_tables(False), micro, axis=0), (images, 1))
    pack_all = jnp.concatenate(
        [interleave(image_masks), jnp.asarray(taps_image), jnp.zeros((rows * micro, 6), F32)], axis=1
    )
    tiles_all = interleave(tile_masks)
    pad_rows = lambda a: jnp.pad(a, ((0, padded - rows), (0, 0)))
    image_mask = pad_rows(pick(image_masks.reshape(micro, rows, 1)))
    tile_mask = pad_rows(pick(tile_masks.reshape(micro, rows, 1)))
    taps_tile = np.pad(np.tile(tap_tables(True), (images, 1)), ((0, padded - rows), (0, 6)))
    pack_tile = jnp.concatenate([tile_mask, jnp.asarray(taps_tile)], axis=1)
    target = pick(targets.reshape(micro, images, pixels))
    base = (jnp.arange(images) * pixels)[:, None]
    target = jnp.where(target >= 0, target + base, -1).reshape(rows)
    target = jnp.pad(target, (0, padded - rows), constant_values=-1)
    index = jnp.arange(padded)
    moves = (target[:, None] == index[None, :]).astype(BF16)
    moves_back = (target[None, :] == index[:, None]).astype(BF16)

    x_in = jnp.transpose(layer_input, (1, 2, 0, 3)).reshape(rows, micro, wide)
    og_in = jnp.transpose(output_grad, (1, 2, 0, 3)).reshape(rows, micro, wide)
    gb_first = jnp.stack(
        [bn_gain[0, :narrow], bn_bias[0, :narrow]]
        + [bn_gain[0, narrow : 2 * narrow], bn_bias[0, narrow : 2 * narrow]]
    )
    gains_here = jnp.concatenate([bn_gain, bn_bias])
    total = rows * micro
    quarter = wide // sections
    dma = pltpu.SemaphoreType.DMA
    stats_all, counts, gains, y1, u, h3n, stats3, *far = kernel_call(
        functools.partial(head_kernel, sections, count),
        [
            shape_of((16, narrow), F32),
            shape_of((8, 128), F32),
            shape_of((sections, 2, wide), F32),
            shape_of((padded, wide), BF16),
            shape_of((padded, wide), BF16),
            shape_of((padded, wide), F32),
            shape_of((2, wide), F32),
            shape_of((padded, narrow), BF16),
            shape_of((wide, narrow), BF16),
            shape_of((sections, padded, quarter), BF16),
            shape_of((total, wide), BF16),
            shape_of((total, narrow), BF16),
            shape_of((total, narrow), F32),
            shape_of((total, narrow), F32),
            shape_of((wide, narrow), BF16),
            shape_of((wide, narrow), BF16),
            shape_of((9 * narrow, narrow), BF16),
        ],
        [x_in, proj, shortcut, spatial, gb_first, gains_here, pack_all, tiles_all, image_mask, moves],
        [
            pltpu.VMEM((total, wide), BF16),
            pltpu.VMEM((total, 9 * narrow), BF16),
            pltpu.VMEM((total, narrow), F32),
            pltpu.VMEM((total, narrow), F32),
            pltpu.VMEM((narrow // 128, 4 * padded, 128), F32),
            pltpu.VMEM((micro, padded, narrow), BF16),
            pltpu.VMEM((padded, narrow), BF16),
            pltpu.VMEM((wide, quarter), BF16),
            pltpu.VMEM((wide, narrow), BF16),
            pltpu.VMEM((micro, padded, quarter), BF16),
            pltpu.VMEM((sections, padded, quarter), BF16),
            pltpu.VMEM((sections, 2, wide), F32),
        ]
        + sync_scratch(count, [(8, narrow + 128), (8, narrow), (2, wide)])
        + [dma((sections,)), dma, dma, dma]
        + [dma((sections,)), dma, dma, dma]
        + [dma((sections,)), dma((sections,)), dma((sections,)), dma]
        + [dma((sections,)), dma((sections,)), dma((2,)), dma((7,))]
        + [dma((5, sections)), dma((5,)), dma((5,)), dma((5,))]
        + [dma((5, 2)), dma((5, 2)), dma((3,))]
        + [dma((5,)), pltpu.VMEM((9 * narrow, narrow), BF16), dma],
        0,
        2 * total * (narrow * (wide + 9 * narrow) + wide * quarter),
        60 * 2**20,
        far_in=(2, 3),
        far_out=tuple(range(7, 17)),
    )
    a2, w1, res, x_all, a1_all, h1n_all, h2n_all, w3, w2, k2 = far
    paged = shape_of((sections, padded, wide), BF16)
    y2, dy1, t_sums, map_one, p3_term, p2_term, k2_term = kernel_call(
        functools.partial(tile_kernel, sections, count),
        [
            shape_of((padded, wide), BF16),
            shape_of((padded, wide), BF16),
            shape_of((6, wide), F32),
            paged,
            shape_of((wide, narrow), BF16),
            shape_of((wide, narrow), BF16),
            shape_of((9 * narrow, narrow), BF16),
        ],
        [u, w2, k2, w3, og_in, pack_tile, gains, counts, moves_back, y1],
        [
            pltpu.VMEM((padded, narrow), BF16),
            pltpu.VMEM((padded, 9 * narrow), BF16),
            pltpu.VMEM((padded, wide), BF16),
            pltpu.VMEM((padded, narrow), BF16),
            pltpu.VMEM((padded, narrow), BF16),
            pltpu.VMEM((2, 512, narrow), BF16),
            dma((2,)),
            pltpu.VMEM((9 * narrow, narrow), BF16),
            pltpu.VMEM((wide, narrow), BF16),
            pltpu.VMEM((rows, micro, wide), BF16),
            dma((3,)),
            pltpu.VMEM((padded, narrow), F32),
            pltpu.VMEM((padded, narrow), F32),
            pltpu.VMEM((padded, wide), F32),
            pltpu.VMEM((padded, narrow), F32),
            pltpu.VMEM((padded, wide), BF16),
            pltpu.VMEM((6, wide), F32),
            pltpu.VMEM((padded, wide), F32),
        ]
        + [dma, dma((sections,)), dma]
        + sync_scratch(
            count, [(2, narrow), (2, narrow), (2, wide), (2, wide), (2, narrow), (2, narrow)]
        ),
        1,
        4 * padded * narrow * (2 * wide + 9 * narrow),
        30 * 2**20,
        far_in=(2, 3, 4, 9),
        far_out=(3, 4, 5, 6),
    )
    depth = count // 2

    def split(term):
        return term.reshape(2, sections, depth, term.shape[0] // (2 * sections * depth), narrow)

    p3_term, p2_term, k2_term = split(p3_term), split(p2_term), split(k2_term)
    taps_piece = k2_term.shape[3]
    dh1_all, i_sums, f_sums, k2_part, *far = kernel_call(
        functools.partial(back_kernel, sections, count),
        [
            shape_of((total, narrow), BF16),
            shape_of((2, wide), F32),
            shape_of((16, narrow), F32),
            shape_of((sections, taps_piece, narrow), BF16),
            paged,
            paged,
            paged,
            shape_of((wide, narrow), BF16),
            shape_of((9 * narrow, narrow), BF16),
            shape_of((wide, narrow), BF16),
            shape_of((wide, narrow), BF16),
        ],
        [dy1, res, h3n, image_mask, gains, stats3, w1, spatial, gb_first, pack_all]
        + [h1n_all, h2n_all, stats_all, counts, k2_term, y2, a2, a1_all, x_all],
        [
            pltpu.VMEM((padded, wide), BF16),
            pltpu.VMEM((padded, wide), BF16),
            pltpu.VMEM((total, narrow), BF16),
            pltpu.VMEM((total, quarter), BF16),
            pltpu.VMEM((total, narrow), BF16),
            pltpu.VMEM((total, wide), BF16),
            pltpu.VMEM((9 * narrow, narrow), BF16),
            pltpu.VMEM((total, narrow), F32),
            pltpu.VMEM((total, narrow), F32),
            pltpu.VMEM((2, 512, narrow), BF16),
            dma((2,)),
            dma((5,)),
            pltpu.VMEM((padded, narrow), BF16),
            pltpu.VMEM((micro, padded, narrow), BF16),
            pltpu.VMEM((micro, padded, quarter), BF16),
            pltpu.VMEM((narrow // 128, 4 * padded, 128), F32),
            pltpu.VMEM((total, narrow), F32),
            pltpu.VMEM((total, narrow), BF16),
        ]
        + sync_scratch(count, [(2, wide), (8, narrow), (8, narrow)])
        + [pltpu.VMEM(k2_term.shape[1:], BF16)] * 2
        + [pltpu.VMEM((depth, sections, taps_piece, narrow), BF16)]
        + [pltpu.VMEM((sections, taps_piece, narrow), BF16)]
        + [dma, dma, dma, dma((depth,)), dma((depth,)), dma]
        + [dma, dma((sections,)), dma((sections,)), dma((sections,))]
        + [dma, dma((sections,)), dma] * 3,
        2,
        2 * total * narrow * 9 * narrow,
        40 * 2**20,
        far_in=(7, 10, 11, 14, 15, 17, 18),
        far_out=tuple(range(3, 11)),
    )
    map_zero, map_two, map_three, p1_term, k0_term, p0_term, short_term = far

    terms = {
        "p3": p3_term,
        "k2": k2_part,
        "p2": p2_term,
        "p1": split(p1_term),
        "k0": split(k0_term),
        "p0": split(p0_term),
    }

    blank = jnp.zeros((wide,), F32)
    pad = jnp.zeros((wide - 2 * narrow,), F32)
    of_batches = lambda at: jnp.sum(f_sums[at : at + 4], axis=0)
    zero_gain = jnp.where(first, jnp.concatenate([of_batches(12), of_batches(4), pad]), blank)
    zero_bias = jnp.where(first, jnp.concatenate([of_batches(8), of_batches(0), pad]), blank)
    vectors = jnp.stack(
        [
            zero_gain,
            zero_bias,
            i_sums[1],
            i_sums[0],
            jnp.concatenate([t_sums[5, :narrow], t_sums[3, :narrow], pad]),
            jnp.concatenate([t_sums[4, :narrow], t_sums[2, :narrow], pad]),
            t_sums[1],
            t_sums[0],
        ]
    )
    short_sum, proj_sum, taps_sum, vectors, maps = sum_gradients(
        sections,
        count,
        short_term,
        terms,
        vectors.reshape(sections, 2, wide),
        dh1_all,
        proj,
        shortcut,
        (map_zero, map_one, map_two, map_three),
        rows,
    )
    maps = jnp.transpose(maps.reshape(images, pixels, micro, wide), (2, 0, 1, 3))
    proj_grad, spatial_grad, short_grad = cast_sums(
        proj_sum.reshape(wide, narrow),
        taps_sum.reshape(9 * narrow, narrow),
        short_sum.reshape(wide, wide),
    )
    return (
        maps[None],
        proj_grad[None],
        spatial_grad[None],
        short_grad[None],
        vectors[:1],
        vectors[1:],
    )


def solution(mesh):
    return jax.shard_map(
        body,
        mesh=mesh,
        in_specs=(
            P(None, "dp", None, None),
            P(None, "dp", None, None),
            P(None, "dp"),
            P(None, "dp", None),
            P("segment", None, None),
            P("segment", None, None),
            P("segment", None, None),
            P("segment", None),
            P("segment", None),
        ),
        out_specs=(
            P("segment", None, "dp", None, None),
            P("segment", None, None),
            P("segment", None, None),
            P("segment", None, None),
            P("segment", None),
            P("segment", None),
        ),
        check_vma=False,
    )
```

```python
import functools

import jax
import jax.numpy as jnp
import numpy as np
from jax import lax
from jax.experimental import pallas as pl
from jax.experimental.pallas import tpu as pltpu
from jax.sharding import PartitionSpec as P

MAP = 7
EPSILON = 1e-05
OFFSETS = ((-1, -1), (-1, 0), (-1, 1), (0, -1), (0, 0), (0, 1), (1, -1), (1, 0), (1, 1))
MESH = pl.DeviceIdType.MESH
F32 = jnp.float32
BF16 = jnp.bfloat16
VMEM_BYTES = 60 * 2**20
TILE = 256


def greet(count, sections=0):
    segment, me = lax.axis_index("segment"), lax.axis_index("dp")
    barrier = pltpu.get_barrier_semaphore()

    def one(k, carry):
        pl.semaphore_signal(
            barrier, inc=1, device_id=(segment, lax.rem(me + k, count)), device_id_type=MESH
        )
        return carry

    lax.fori_loop(1, count, one, 0)
    for k in range(1, sections):
        pl.semaphore_signal(
            barrier, inc=1, device_id=(jnp.bitwise_xor(segment, k), me), device_id_type=MESH
        )


def greeted(count, sections=1):
    pl.semaphore_wait(pltpu.get_barrier_semaphore(), count - 1 + sections - 1)


def exchange(count, slots, send_sem, recv_sem):
    segment, me = lax.axis_index("segment"), lax.axis_index("dp")

    def copy(k):
        return pltpu.make_async_remote_copy(
            src_ref=slots.at[me],
            dst_ref=slots.at[me],
            send_sem=send_sem.at[k],
            recv_sem=recv_sem.at[k],
            device_id=(segment, lax.rem(me + k, count)),
            device_id_type=MESH,
        )

    def start(k, carry):
        copy(k).start()
        return carry

    def finish(k, carry):
        copy(k).wait_recv()
        copy(k).wait_send()
        return carry

    lax.fori_loop(1, count, start, 0)
    lax.fori_loop(1, count, finish, 0)
    total = slots[0]
    for k in range(1, count):
        total = total + slots[k]
    return total


def mesh_copy(src, dst, send_sem, recv_sem, segment, place):
    return pltpu.make_async_remote_copy(
        src_ref=src,
        dst_ref=dst,
        send_sem=send_sem,
        recv_sem=recv_sem,
        device_id=(segment, place),
        device_id_type=MESH,
    )


def loop(low, high, body):
    def one(k, carry):
        body(k)
        return carry

    lax.fori_loop(low, high, one, 0)


def sync_scratch(count, shapes):
    out = []
    for shape in shapes:
        out += [
            pltpu.VMEM((count,) + shape, F32),
            pltpu.SemaphoreType.DMA((count,)),
            pltpu.SemaphoreType.DMA((count,)),
        ]
    return out


def kernel_call(kernel, outs, args, scratch, ident, flops, moved, far_in=(), far_out=()):
    params = dict(has_side_effects=True, vmem_limit_bytes=VMEM_BYTES)
    if ident is not None:
        params["collective_id"] = ident
    return pl.pallas_call(
        kernel,
        out_shape=outs,
        in_specs=[
            pl.BlockSpec(memory_space=pl.ANY if i in far_in else pltpu.VMEM) for i in range(len(args))
        ],
        out_specs=[
            pl.BlockSpec(memory_space=pl.ANY if i in far_out else pltpu.VMEM) for i in range(len(outs))
        ],
        scratch_shapes=scratch,
        compiler_params=pltpu.CompilerParams(**params),
        cost_estimate=pl.CostEstimate(flops=flops, bytes_accessed=moved, transcendentals=0),
    )(*args)


def shape_of(shape, dtype):
    return jax.ShapeDtypeStruct(shape, dtype)


def dot(a, b):
    return jnp.dot(a, b, preferred_element_type=F32)


def dot_t(a, b):
    return lax.dot_general(a, b, (((1,), (1,)), ((), ())), preferred_element_type=F32)


def dot_0(a, b):
    return lax.dot_general(a, b, (((0,), (0,)), ((), ())), preferred_element_type=F32)


class Writer:
    def __init__(self, stage, sems):
        self.stage, self.sems, self.open, self.turn = stage, sems, [None, None], 0

    def put(self, value, dst):
        at = self.turn % 2
        self.turn += 1
        if self.open[at] is not None:
            self.open[at].wait()
        self.stage[at] = value.astype(BF16)
        self.open[at] = pltpu.make_async_copy(self.stage.at[at], dst, self.sems.at[at])
        self.open[at].start()

    def rows_of_dot(self, left, right, out):
        tall = self.stage.shape[1]
        for j in range(out.shape[0] // tall):
            at = pl.ds(j * tall, tall)
            self.put(dot_0(left[:, at], right[...]), out.at[at])

    def drain(self):
        for at in range(2):
            if self.open[at] is not None:
                self.open[at].wait()
        self.open = [None, None]


def sigmoid(v):
    return 1.0 / (1.0 + jnp.exp(-v))


def slope(v):
    s = sigmoid(v)
    return s * (1.0 + v * (1.0 - s))


def over(width, step, body):
    def one(j, carry):
        body(pl.ds(pl.multiple_of(j * step, step), step))
        return carry

    lax.fori_loop(0, width // step, one, 0)


def lane(at):
    return lax.div(at.start, 128)


def unrolled_shift(ref_value, shift):
    rows = ref_value.shape[0]
    return ref_value if shift % rows == 0 else pltpu.roll(ref_value, (-shift) % rows, 0)


def by_batch(values):
    rows, width = values.shape
    part = jnp.sum(values.reshape(rows // 8, 8, width), axis=0)
    return part[:4] + part[4:]


def spread8(values):
    return jnp.concatenate([values, values], axis=0)[None]


def first_part(
    count, hooks, writes, x, w, k, gb, pack, tiles, a2_out, cols, h1n, h2n, stats_out, count_out, act, *sync
):
    s1, send1, recv1, s2, send2, recv2 = sync
    rows, narrow = h1n.shape
    me = lax.axis_index("dp")
    full = act.shape[1]

    def tile8(v):
        return v.reshape(rows // 8, 8, v.shape[1])

    def project(at):
        h = dot(x[...], w[:, at])
        h1n[:, at] = h
        m = pack[:, 0:1] * h
        s1[me, 0:4, at] = by_batch(m)
        s1[me, 4:8, at] = by_batch(m * h)

    over(narrow, TILE, project)
    s1[me, 0:4, narrow:] = jnp.broadcast_to(by_batch(pack[:, 0:1]), (4, 128))
    s1[me, 4:8, narrow:] = jnp.broadcast_to(by_batch(tiles[:, 0:1]), (4, 128))
    total = exchange(count, s1, send1, recv1)
    counts = total[:, narrow:]
    count_out[...] = counts
    valid = counts[0:4, 0:1]
    average = total[0:4, :narrow] / valid
    inverse = lax.rsqrt(total[4:8, :narrow] / valid - average * average + EPSILON)
    stats_out[0:4, :] = average
    stats_out[4:8, :] = inverse
    hooks[0]()

    def activate(stat_at, gain_at, source):
        def body(at):
            mean = spread8(stats_out[stat_at : stat_at + 4, at])
            inv = spread8(stats_out[stat_at + 4 : stat_at + 8, at])
            hn = (tile8(source[:, at]) - mean) * inv
            source[:, at] = hn.reshape(rows, hn.shape[2])
            n = gb[gain_at : gain_at + 1, at][None] * hn + gb[gain_at + 1 : gain_at + 2, at][None]
            n = n.reshape(rows, n.shape[2])
            act[lane(at), 0:rows, :] = pack[:, 0:1] * (n * sigmoid(n))

        return body

    over(narrow, 128, activate(0, 0, h1n))

    for t, (vertical, lateral) in enumerate(OFFSETS):
        shift = 4 * (7 * vertical + lateral)

        def place(j, carry, t=t, shift=shift):
            at = pl.ds(pl.multiple_of(j * 128, 128), 128)
            to = pl.ds(pl.multiple_of(t * narrow + j * 128, 128), 128)
            moved = unrolled_shift(act[j, 0:rows, :], shift)
            cols[:, to] = (pack[:, 1 + t : 2 + t] * moved).astype(BF16)
            return carry

        lax.fori_loop(0, narrow // 128, place, 0)

    def convolve(at):
        h = dot(cols[...], k[:, at])
        h2n[:, at] = h
        m = pack[:, 0:1] * h
        s2[me, 0:4, at] = by_batch(m)
        s2[me, 4:8, at] = by_batch(m * h)

    for write in writes:
        write.start()
    hooks[1]()
    over(narrow, TILE, convolve)
    total = exchange(count, s2, send2, recv2)
    average = total[0:4] / valid
    hooks[2]()
    stats_out[8:12, :] = average
    stats_out[12:16, :] = lax.rsqrt(total[4:8] / valid - average * average + EPSILON)
    over(narrow, 128, activate(8, 2, h2n))
    act[:, rows:, :] = jnp.zeros((narrow // 128, full - rows, 128), F32)
    for m in range(4):

        def pick(j, carry, m=m):
            at = pl.ds(pl.multiple_of(j * 128, 128), 128)
            a2_out[m, :, at] = act[j, pl.ds(m, full // 4, stride=4), :].astype(BF16)
            return carry

        lax.fori_loop(0, narrow // 128, pick, 0)


def residual_part(x, w, out, hold):
    rows, full, quarter = x.shape[0], hold.shape[1], out.shape[2]
    hold[:, rows:, :] = jnp.zeros((quarter // 128, full - rows, 128), F32)

    def body(at):
        value = dot(x[...], w[:, at])
        for part in range(TILE // 128):
            hold[lane(at) + part, 0:rows, :] = value[:, part * 128 : part * 128 + 128]

    over(quarter, TILE, body)
    for m in range(4):

        def pick(j, carry, m=m):
            at = pl.ds(pl.multiple_of(j * 128, 128), 128)
            out[m, :, at] = hold[j, pl.ds(m, full // 4, stride=4), :].astype(BF16)
            return carry

        lax.fori_loop(0, quarter // 128, pick, 0)


def norm_sums(slots, me, at, masked, h):
    slots[me, 0:1, at] = jnp.sum(masked, axis=0, keepdims=True)
    slots[me, 1:2, at] = jnp.sum(masked * h, axis=0, keepdims=True)


def finish_stats(total, valid, stats_out, at_row):
    average = total[0:1] / valid
    width = average.shape[1]
    stats_out[at_row : at_row + 1, 0:width] = average
    stats_out[at_row + 1 : at_row + 2, 0:width] = lax.rsqrt(
        total[1:2] / valid - average * average + EPSILON
    )


def second_part(
    count, before, a2, w1, res, mask, gb, valid, moves, y_out, u_out, h3n, stats_out, s1, send1, recv1
):
    wide = h3n.shape[1]
    quarter = res.shape[2]
    me = lax.axis_index("dp")

    def project(at):
        h = dot_t(a2[...], w1[at, :])
        h3n[:, at] = h
        norm_sums(s1, me, at, mask[:, 0:1] * h, h)

    over(wide, TILE, project)
    finish_stats(exchange(count, s1, send1, recv1), valid, stats_out, 0)
    before()
    for q in range(wide // quarter):

        def body(j, carry, q=q):
            at = pl.ds(pl.multiple_of(q * quarter + j * 128, 128), 128)
            own = pl.ds(pl.multiple_of(j * 128, 128), 128)
            hn = (h3n[:, at] - stats_out[0:1, at]) * stats_out[1:2, at]
            h3n[:, at] = hn
            z = gb[1, 0:1, at] * hn + gb[1, 1:2, at] + res[q, :, own].astype(F32)
            y_out[:, at] = (mask[:, 0:1] * (z * sigmoid(z))).astype(BF16)
            return carry

        lax.fori_loop(0, quarter // 128, body, 0)

    def permute(at):
        u_out[:, at] = dot(moves[...], y_out[:, at]).astype(BF16)

    over(wide, TILE, permute)


def batch_valid(counts, row):
    me = lax.axis_index("segment")
    value = counts[row : row + 1, 0:1]
    for m in range(1, 4):
        value = jnp.where(me == m, counts[row + m : row + m + 1, 0:1], value)
    return value


def head_kernel(
    sections,
    count,
    x3,
    w,
    short,
    k,
    gb,
    vec,
    pack,
    tiles,
    mask,
    moves,
    stats_out,
    count_out,
    g_out,
    y_out,
    u_out,
    h3n,
    stats3,
    a2_out,
    w1_out,
    res_out,
    x_out,
    a1_out,
    h1n_out,
    h2n_out,
    w3_out,
    w2_out,
    k2_out,
    x,
    cols,
    h1n,
    h2n,
    act,
    a2_all,
    a2,
    wsc,
    w1,
    rq,
    res,
    gslots,
    *rest,
):
    sync, rest = rest[:9], list(rest[9:])
    short_send, short_recv, short_relay_send, short_relay_recv = rest[:4]
    w1_send, w1_recv, w1_relay_send, w1_relay_recv = rest[4:8]
    g_send, g_recv, a2_send, a2_recv, res_send, res_recv, own_sem, out_sem = rest[8:16]
    spread_send, spread_recv, far_send, far_recv, near_send, near_recv, keep_sem = rest[16:23]
    pass_send, kv, kv_sem = rest[23:]
    me, place = lax.axis_index("segment"), lax.axis_index("dp")
    core = lax.rem(place, 2)
    sibling = place + 1 - 2 * core
    wide = x.shape[1]
    quarter = wide // sections
    half_rows = wide // 2
    mine = pl.ds(pl.multiple_of(core * half_rows, 16), half_rows)
    greet(count, sections)
    k_load = pltpu.make_async_copy(k, kv, kv_sem)
    k_load.start()

    odd = lax.rem(lax.div(place, 2), 2)
    beside = place + 2 - 4 * odd
    parts = [("w3", w, w3_out, 3, 0, 1), ("w2", w, w2_out, 2, 0, 1)]
    parts += [("k2", k, k2_out, 2, i, 3) for i in range(3)]

    def part_rows(i, at_odd):
        _, src, _, _, piece, pieces = parts[i]
        fine = src.shape[0] // (4 * pieces)
        start = ((2 * at_odd + core) * pieces + piece) * fine
        return pl.ds(pl.multiple_of(start, 16), fine)

    def spread_copy(i, t):
        _, src, dst, _, _, _ = parts[i]
        at = part_rows(i, odd)
        return mesh_copy(src.at[at], dst.at[at], spread_send.at[i, t], spread_recv.at[i], t, place)

    def far_copy(i):
        dst, at = parts[i][2], part_rows(i, odd)
        return mesh_copy(dst.at[at], dst.at[at], far_send.at[i], far_recv.at[i], me, beside)

    def near_copy(i, second):
        dst = parts[i][2]
        at = part_rows(i, 1 - odd if second else odd)
        sems = near_send.at[i, second], near_recv.at[i, second]
        return mesh_copy(dst.at[at], dst.at[at], *sems, me, sibling)

    keeps = [
        (3, pltpu.make_async_copy(w, w3_out, keep_sem.at[0])),
        (2, pltpu.make_async_copy(w, w2_out, keep_sem.at[1])),
        (2, pltpu.make_async_copy(kv, k2_out, keep_sem.at[2])),
    ]

    def spread_start(i):
        owner = parts[i][3]

        @pl.when(me == owner)
        def _():
            for d in (1, 2):
                spread_copy(i, owner ^ d).start()

    def spread_sent(i):
        for d in (1, 2):
            spread_copy(i, parts[i][3] ^ d).wait_send()

    def pass_copy(i):
        dst, at = parts[i][2], part_rows(i, odd)
        return mesh_copy(
            dst.at[at], dst.at[at], pass_send.at[i], spread_recv.at[i], parts[i][3] ^ 3, place
        )

    def spread_on(i):
        owner = parts[i][3]

        @pl.when(me == owner ^ 1)
        def _():
            spread_copy(i, 0).wait_recv()
            pass_copy(i).start()

        @pl.when((me != owner) & (me != owner ^ 1))
        def _():
            spread_copy(i, 0).wait_recv()

        @pl.when(me != owner)
        def _():
            far_copy(i).start()
            near_copy(i, 0).start()

    def far_on(i):
        @pl.when(me != parts[i][3])
        def _():
            far_copy(i).wait_recv()
            near_copy(i, 1).start()

    def short_copy(t):
        src = short.at[mine, pl.ds(t * quarter, quarter)]
        return mesh_copy(src, wsc.at[mine], short_send.at[t], short_recv, t, place)

    def w1_copy(t):
        return mesh_copy(w.at[mine], w1.at[mine], w1_send.at[t], w1_recv, t, place)

    short_own = pltpu.make_async_copy(short.at[:, pl.ds(0, quarter)], wsc, own_sem.at[0])
    w1_own = pltpu.make_async_copy(w, w1, own_sem.at[1])
    short_relay = mesh_copy(
        wsc.at[mine], wsc.at[mine], short_relay_send, short_relay_recv, me, sibling
    )
    w1_relay = mesh_copy(w1.at[mine], w1.at[mine], w1_relay_send, w1_relay_recv, me, sibling)

    def g_copy(k_):
        return mesh_copy(
            gslots.at[me],
            gslots.at[me],
            g_send.at[k_],
            g_recv.at[k_],
            jnp.bitwise_xor(me, k_),
            place,
        )

    gslots[me] = vec[...]
    greeted(count, sections)

    @pl.when(me == 0)
    def _():
        for t in (3, 1, 2):
            short_copy(t).start()
        short_own.start()

    @pl.when(me == 1)
    def _():
        for t in (2, 0, 3):
            w1_copy(t).start()
        w1_own.start()

    for k_ in range(1, sections):
        g_copy(k_).start()
    for i in range(3):
        spread_start(i)
    for owner, copy in keeps[:2]:
        pl.when(me == owner)(copy.start)

    def relayout(j, carry):
        at = pl.ds(pl.multiple_of(j * 128, 128), 128)
        x[:, at] = x3[:, :, at].reshape(x.shape[0], 128)
        return carry

    lax.fori_loop(0, wide // 128, relayout, 0)
    writes = [
        pltpu.make_async_copy(src, dst, out_sem.at[i])
        for i, (src, dst) in enumerate(
            ((x, x_out), (h1n, h1n_out), (cols.at[:, pl.ds(4 * h1n.shape[1], h1n.shape[1])], a1_out), (h2n, h2n_out))
            + ((a2, a2_out), (w1, w1_out), (res, res_out))
        )
    ]
    writes[0].start()

    def a2_copy(t):
        return mesh_copy(a2_all.at[t], a2, a2_send.at[t], a2_recv, t, place)

    @pl.when(me == 0)
    def _():
        def between():
            spread_on(0)
            spread_on(1)

        first_part(
            count,
            (lambda: spread_on(1), k_load.wait, lambda: spread_on(0)),
            writes[1:3],
            x,
            w,
            kv,
            gb,
            pack,
            tiles,
            a2_all,
            cols,
            h1n,
            h2n,
            stats_out,
            count_out,
            act,
            *sync[:6],
        )
        writes[3].start()
        for t in range(1, sections):
            a2_copy(t).start()
        a2[...] = a2_all[0]
        short_own.wait()
        for i in (2, 3, 4):
            spread_on(i)

    @pl.when(me != 0)
    def _():
        k_load.wait()
        pl.when(me == keeps[2][0])(keeps[2][1].start)
        slots, send1, recv1 = sync[:3]
        narrow = h1n.shape[1]
        stats_out[...] = jnp.zeros(stats_out.shape, F32)
        slots[place, :, 0:narrow] = jnp.zeros((8, narrow), F32)
        slots[place, 0:4, narrow:] = jnp.broadcast_to(by_batch(pack[:, 0:1]), (4, 128))
        slots[place, 4:8, narrow:] = jnp.broadcast_to(by_batch(tiles[:, 0:1]), (4, 128))
        count_out[...] = exchange(count, slots, send1, recv1)[:, narrow:]

    def spread_paced(i, after):
        @pl.when(me == parts[i][3])
        def _():
            spread_sent(after)
            for d in (1, 2):
                spread_copy(i, parts[i][3] ^ d).start()

    def unless_zero(i):
        pl.when(me != 0)(lambda: spread_on(i))

    unless_zero(0)
    spread_paced(3, 1)
    unless_zero(1)
    spread_paced(4, 2)
    unless_zero(2)
    unless_zero(3)
    pl.when(me == parts[4][3] ^ 1)(lambda: spread_on(4))

    @pl.when(me != 0)
    def _():
        short_copy(0).wait_recv()
        short_relay.start()

    @pl.when(me == 1)
    def _():
        w1_own.wait()

    @pl.when(me != 1)
    def _():
        w1_copy(0).wait_recv()
        w1_relay.start()

    @pl.when(me != 0)
    def _():
        short_relay.wait_recv()

    residual_part(x, wsc, rq, act)

    def res_copy(k_):
        other = jnp.bitwise_xor(me, k_)
        return mesh_copy(
            rq.at[other], res.at[me], res_send.at[k_], res_recv.at[k_], other, place
        )

    for k_ in range(1, sections):
        res_copy(k_).start()
    res[me] = rq[me]
    pl.when((me != 0) & (me != parts[4][3] ^ 1))(lambda: spread_on(4))

    @pl.when(me != 0)
    def _():
        a2_copy(0).wait_recv()

    @pl.when(me != 1)
    def _():
        w1_relay.wait_recv()

    for k_ in range(1, sections):
        g_copy(k_).wait_recv()
    g_out[...] = gslots[...]

    def before():
        far_on(0)
        far_on(1)
        for k_ in range(1, sections):
            res_copy(k_).wait_recv()

    second_part(
        count,
        before,
        a2,
        w1,
        res,
        mask,
        gslots,
        batch_valid(count_out, 0),
        moves,
        y_out,
        u_out,
        h3n,
        stats3,
        *sync[6:],
    )
    for copy in writes[4:]:
        copy.start()
    for i in range(2, len(parts)):
        far_on(i)
    for k_ in range(1, sections):
        g_copy(k_).wait_send()
        res_copy(k_).wait_send()

    @pl.when(me == 0)
    def _():
        for t in range(1, sections):
            short_copy(t).wait_send()
            a2_copy(t).wait_send()

    @pl.when(me != 0)
    def _():
        short_relay.wait_send()

    @pl.when(me == 1)
    def _():
        for t in (0, 2, 3):
            w1_copy(t).wait_send()

    @pl.when(me != 1)
    def _():
        w1_relay.wait_send()

    for i in range(len(parts)):
        owner = parts[i][3]

        if i not in (1, 2):
            pl.when(me == owner)(functools.partial(spread_sent, i))
        pl.when(me == owner ^ 1)(lambda i=i: pass_copy(i).wait_send())

        @pl.when(me != owner)
        def _(i=i):
            far_copy(i).wait_send()
            near_copy(i, 0).wait()
            near_copy(i, 1).wait()

    for owner, copy in keeps:
        pl.when(me == owner)(copy.wait)
    for i, copy in enumerate(writes):
        if i in (1, 2, 3):
            pl.when(me == 0)(copy.wait)
        else:
            copy.wait()


def back_sums(slots, me, at, grad, hn):
    slots[me, 0:1, at] = jnp.sum(grad, axis=0, keepdims=True)
    slots[me, 1:2, at] = jnp.sum(grad * hn, axis=0, keepdims=True)


def map_sender(sections, src, dst, owner, send_sem, recv_sem, own_sem):
    me, place = lax.axis_index("segment"), lax.axis_index("dp")
    own = pltpu.make_async_copy(src, dst.at[me], own_sem)

    def copy(k):
        return mesh_copy(src, dst.at[me], send_sem, recv_sem.at[k], owner, place)

    def start():
        @pl.when(me == owner)
        def _():
            own.start()

        for k in range(1, sections):

            @pl.when(me == owner ^ k)
            def _(k=k):
                copy(k).start()

    def finish():
        @pl.when(me == owner)
        def _():
            own.wait()
            for k in range(1, sections):
                copy(k).wait_recv()

        @pl.when(me != owner)
        def _():
            copy(0).wait_send()

    return start, finish


def tile_kernel(
    sections,
    count,
    u,
    w2,
    k2_far,
    w3_far,
    og_far,
    pack,
    gains,
    counts,
    back,
    y1,
    y_out,
    dy,
    sums_out,
    map_one,
    p3_out,
    p2_out,
    k2_out,
    a2,
    cols,
    dh3,
    dh2,
    dh1,
    stage,
    stage_sem,
    k2,
    w3,
    og3,
    load_sem,
    h1n,
    h2n,
    h3n,
    act,
    dz,
    stats,
    og,
    map_send,
    map_recv,
    map_own,
    *sync,
):
    s1, send1, recv1, s2, send2, recv2, s3, send3, recv3 = sync[:9]
    b3, bsend3, brecv3, b2, bsend2, brecv2, b1, bsend1, brecv1 = sync[9:]
    rows, wide = u.shape
    narrow = h1n.shape[1]
    me = lax.axis_index("dp")
    section = lax.axis_index("segment")
    valid = batch_valid(counts, 4)
    gb3 = gains.at[3]
    loads = [
        pltpu.make_async_copy(src, dst, load_sem.at[i])
        for i, (src, dst) in enumerate(((og_far, og3), (k2_far, k2), (w3_far, w3)))
    ]
    for load in loads:
        load.start()

    def gb2(row, at):
        return gains[2, row % 2 : row % 2 + 1, pl.ds(at.start + row // 2 * narrow, at.size)]

    greet(count, sections)

    def project(at):
        h = dot(u[...], w2[:, at])
        h1n[:, at] = h
        norm_sums(s1, me, at, pack[:, 0:1] * h, h)

    over(narrow, TILE, project)
    greeted(count, sections)
    send_map, wait_map = map_sender(sections, y1, map_one, 1, map_send, map_recv, map_own)
    send_map()
    loads[0].wait()
    real = og3.shape[0]
    for m in range(sections):

        @pl.when(section == m)
        def _(m=m):
            def one(j, carry):
                at = pl.ds(pl.multiple_of(j * 128, 128), 128)
                og[0:real, at] = og3[:, m, at].astype(F32)
                return carry

            lax.fori_loop(0, wide // 128, one, 0)

    og[real:, :] = jnp.zeros((rows - real, wide), F32)
    finish_stats(exchange(count, s1, send1, recv1), valid, stats, 0)

    def activate(row, gain, source, store):
        def body(at):
            hn = (source[:, at] - stats[row : row + 1, at]) * stats[row + 1 : row + 2, at]
            source[:, at] = hn
            n = gb2(gain, at) * hn + gb2(gain + 1, at)
            store(at, pack[:, 0:1] * (n * sigmoid(n)))

        return body

    def to_act(at, value):
        act[:, at] = value

    def to_a2(at, value):
        a2[:, at] = value.astype(BF16)

    over(narrow, 128, activate(0, 0, h1n, to_act))
    for t, (vertical, lateral) in enumerate(OFFSETS):
        shift = 7 * vertical + lateral

        def place(j, carry, t=t, shift=shift):
            at = pl.ds(pl.multiple_of(j * 128, 128), 128)
            to = pl.ds(pl.multiple_of(t * narrow + j * 128, 128), 128)
            moved = unrolled_shift(act[:, at], shift)
            cols[:, to] = (pack[:, 1 + t : 2 + t] * moved).astype(BF16)
            return carry

        lax.fori_loop(0, narrow // 128, place, 0)

    def convolve(at):
        h = dot(cols[...], k2[:, at])
        h2n[:, at] = h
        norm_sums(s2, me, at, pack[:, 0:1] * h, h)

    loads[1].wait()
    over(narrow, TILE, convolve)
    finish_stats(exchange(count, s2, send2, recv2), valid, stats, 2)
    over(narrow, 128, activate(2, 2, h2n, to_a2))

    def expand(at):
        h = dot_t(a2[...], w3[at, :])
        h3n[:, at] = h
        norm_sums(s3, me, at, pack[:, 0:1] * h, h)

    loads[2].wait()
    over(wide, TILE, expand)
    finish_stats(exchange(count, s3, send3, recv3), valid, stats, 4)

    def result(at):
        hn = (h3n[:, at] - stats[4:5, at]) * stats[5:6, at]
        h3n[:, at] = hn
        z = gb3[0:1, at] * hn + gb3[1:2, at] + u[:, at].astype(F32)
        s = sigmoid(z)
        m = pack[:, 0:1]
        y_out[:, at] = (m * (z * s)).astype(BF16)
        grad = (og[:, at] * m * (s * (1.0 + z * (1.0 - s)))).astype(BF16)
        dz[:, at] = grad
        grad = grad.astype(F32)
        back_sums(b3, me, at, grad, hn)

    over(wide, 128, result)
    total = exchange(count, b3, bsend3, brecv3)
    sums_out[0:2, :] = total

    def through(at):
        offset, scale = sums_out[0:1, at], sums_out[1:2, at]
        dh3[:, at] = (
            pack[:, 0:1]
            * gb3[0:1, at]
            * stats[5:6, at]
            * (dz[:, at].astype(F32) - (offset + h3n[:, at] * scale) / valid)
        ).astype(BF16)

    over(wide, 128, through)

    def into_two(at):
        grad = dot(dh3[...], w3[:, at]).astype(BF16).astype(F32)
        hn = h2n[:, at]
        n = gb2(2, at) * hn + gb2(3, at)
        grad = grad * pack[:, 0:1] * slope(n)
        act[:, at] = grad
        back_sums(b2, me, at, grad, hn)

    over(narrow, TILE, into_two)
    total = exchange(count, b2, bsend2, brecv2)
    sums_out[2:4, 0:narrow] = total

    def through_two(at):
        offset, scale = sums_out[2:3, at], sums_out[3:4, at]
        grad = (
            pack[:, 0:1]
            * gb2(2, at)
            * stats[3:4, at]
            * (act[:, at] - (offset + h2n[:, at] * scale) / valid)
        )
        dh2[:, at] = grad.astype(BF16)
        act[:, at] = dh2[:, at].astype(F32)

    over(narrow, 128, through_two)
    h2n[...] = jnp.zeros((rows, narrow), F32)
    for t, (vertical, lateral) in enumerate(OFFSETS):
        shift = -(7 * vertical + lateral)
        other = 8 - t

        def place_back(j, carry, t=t, shift=shift, other=other):
            at = pl.ds(pl.multiple_of(j * 128, 128), 128)
            moved = unrolled_shift(act[:, at], shift)
            dy[:, at] = (pack[:, 1 + other : 2 + other] * moved).astype(BF16)
            return carry

        lax.fori_loop(0, narrow // 128, place_back, 0)

        def gather(at, t=t):
            row = pl.ds(pl.multiple_of(t * narrow + at.start, TILE), TILE)
            h2n[:, at] += dot_t(dy[:, 0:narrow], k2[row, :])

        over(narrow, TILE, gather)

    def into_one(at):
        hn = h1n[:, at]
        n = gb2(0, at) * hn + gb2(1, at)
        grad = h2n[:, at] * pack[:, 0:1] * slope(n)
        act[:, at] = grad
        back_sums(b1, me, at, grad, hn)

    over(narrow, 128, into_one)
    total = exchange(count, b1, bsend1, brecv1)
    sums_out[4:6, 0:narrow] = total

    def through_one(at):
        offset, scale = sums_out[4:5, at], sums_out[5:6, at]
        dh1[:, at] = (
            pack[:, 0:1]
            * gb2(0, at)
            * stats[1:2, at]
            * (act[:, at] - (offset + h1n[:, at] * scale) / valid)
        ).astype(BF16)

    over(narrow, 128, through_one)

    def into_input(at):
        grad = dot_t(dh1[...], w2[at, :]) + dz[:, at].astype(F32)
        dy[:, at] = dot(back[...], grad.astype(BF16)).astype(BF16)

    over(wide, TILE, into_input)
    writer = Writer(stage, stage_sem)
    writer.rows_of_dot(dh3, a2, p3_out)
    writer.rows_of_dot(cols, dh2, k2_out)
    writer.rows_of_dot(u, dh1, p2_out)
    writer.drain()
    wait_map()


def image_back_part(
    count, after, dy, res, h3n, mask, gb, stats, valid, w1, dz, dh3, da2, sums_out, b3, send3, recv3
):
    wide = dy.shape[1]
    quarter = res.shape[2]
    narrow = da2.shape[1]
    me = lax.axis_index("dp")
    for q in range(wide // quarter):

        def body(j, carry, q=q):
            at = pl.ds(pl.multiple_of(q * quarter + j * 128, 128), 128)
            own = pl.ds(pl.multiple_of(j * 128, 128), 128)
            hn = h3n[:, at]
            z = gb[0:1, at] * hn + gb[1:2, at] + res[q, :, own].astype(F32)
            grad = (dy[:, at].astype(F32) * mask[:, 0:1] * slope(z)).astype(BF16)
            dz[:, at] = grad
            back_sums(b3, me, at, grad.astype(F32), hn)
            return carry

        lax.fori_loop(0, quarter // 128, body, 0)
    after()
    total = exchange(count, b3, send3, recv3)
    sums_out[...] = total

    def through(at):
        offset, scale = sums_out[0:1, at], sums_out[1:2, at]
        dh3[:, at] = (
            mask[:, 0:1]
            * gb[0:1, at]
            * stats[1:2, at]
            * (dz[:, at].astype(F32) - (offset + h3n[:, at] * scale) / valid)
        ).astype(BF16)

    over(wide, 128, through)

    def into(at):
        da2[:, at] = dot(dh3[...], w1[:, at]).astype(BF16)

    over(narrow, TILE, into)


def last_part(
    count, between, taps_term, da2, k, gb, pack, h1n, h2n, stats, counts, dh2, dh1, sums_out, act, acc, hold, *sync
):
    b2, send2, recv2, b1, send1, recv1 = sync
    rows, narrow = h1n.shape
    full = act.shape[1]
    me = lax.axis_index("dp")
    valid = counts[0:4, 0:1]

    def tile8(v):
        return v.reshape(rows // 8, 8, v.shape[1])

    for m in range(4):

        def put(j, carry, m=m):
            at = pl.ds(pl.multiple_of(j * 128, 128), 128)
            act[j, pl.ds(m, full // 4, stride=4), :] = da2[m, :, at].astype(F32)
            return carry

        lax.fori_loop(0, narrow // 128, put, 0)

    def into(gain, source, hidden, slots):
        def body(at):
            hn = hidden[:, at]
            n = gb[gain : gain + 1, at] * hn + gb[gain + 1 : gain + 2, at]
            grad = source(at) * pack[:, 0:1] * slope(n)
            act[lane(at), 0:rows, :] = grad
            slots[me, 0:4, at] = by_batch(grad)
            slots[me, 4:8, at] = by_batch(grad * hn)

        return body

    def through(gain, stat_at, row, hidden, out):
        def body(at):
            offset = spread8(sums_out[row : row + 4, at] / valid)
            scale = spread8(sums_out[row + 4 : row + 8, at] / valid)
            inv = spread8(stats[stat_at : stat_at + 4, at])
            g = tile8(act[lane(at), 0:rows, :])
            value = inv * gb[gain : gain + 1, at][None] * (g - (offset + tile8(hidden[:, at]) * scale))
            value = (pack[:, 0:1] * value.reshape(rows, value.shape[2])).astype(BF16)
            out[:, at] = value
            act[lane(at), 0:rows, :] = value.astype(F32)

        return body

    over(narrow, 128, into(2, lambda at: act[lane(at), 0:rows, :], h2n, b2))
    sums_out[0:8, :] = exchange(count, b2, send2, recv2)
    between()
    over(narrow, 128, through(2, 12, 0, h2n, dh2))
    acc[...] = jnp.zeros((rows, narrow), F32)
    for t, (vertical, lateral) in enumerate(OFFSETS):
        shift = -4 * (7 * vertical + lateral)
        other = 8 - t

        def place_back(j, carry, t=t, shift=shift, other=other):
            at = pl.ds(pl.multiple_of(j * 128, 128), 128)
            moved = unrolled_shift(act[j, 0:rows, :], shift)
            hold[:, at] = (pack[:, 1 + other : 2 + other] * moved).astype(BF16)
            return carry

        lax.fori_loop(0, narrow // 128, place_back, 0)

        def gather(at, t=t):
            row = pl.ds(pl.multiple_of(t * narrow + at.start, TILE), TILE)
            acc[:, at] += dot_t(hold[...], k[row, :])

        over(narrow, TILE, gather)
        taps_term(t)
    over(narrow, 128, into(0, lambda at: acc[:, at], h1n, b1))
    sums_out[8:16, :] = exchange(count, b1, send1, recv1)
    over(narrow, 128, through(0, 4, 8, h1n, dh1))


def back_kernel(
    sections,
    count,
    dy,
    res,
    h3n,
    mask,
    gains,
    stats3,
    w1,
    k_far,
    gb,
    pack,
    h1n_far,
    h2n_far,
    stats,
    counts,
    k2,
    y2,
    a2,
    a1_in,
    x_in,
    dh1,
    sums3,
    sums12,
    k2_out,
    dz_all,
    map_two,
    map_three,
    p1_out,
    k0_out,
    p0_out,
    sh_out,
    piece_out,
    dz,
    dh3,
    dh2,
    dzq_out,
    a1,
    x,
    k,
    h1n,
    h2n,
    stage,
    stage_sem,
    x_sem,
    da2,
    da2_all,
    dzq,
    act,
    acc,
    hold,
    *rest,
):
    sync, rest = rest[:9], list(rest[9:])
    half, theirs, pieces, whole = rest[:4]
    load_sem, swap_send, swap_recv, piece_send, piece_recv, out_sem = rest[4:10]
    sh_half, sh_other, sh_theirs, sh_pieces, sh_sum = rest[10:15]
    sh_swap_send, sh_swap_recv, sh_send, sh_recv, sh_sem = rest[15:20]
    rest = rest[20:]
    a_send, a_recv, q_send, q_recv = rest[:4]
    maps = [rest[4:7], rest[7:10], rest[10:13]]
    me, place = lax.axis_index("segment"), lax.axis_index("dp")
    quarter, narrow = dzq.shape[2], da2.shape[1]
    greet(count, sections)
    send_dz, wait_dz = map_sender(sections, dz, dz_all, 0, *maps[0])
    send_two, wait_two = map_sender(sections, dy, map_two, 2, *maps[1])
    send_three, wait_three = map_sender(sections, y2, map_three, 3, *maps[2])

    def q_copy(k_):
        other = jnp.bitwise_xor(me, k_)
        at = pl.ds(pl.multiple_of(other * quarter, 128), quarter)
        return mesh_copy(dz.at[:, at], dzq.at[me], q_send.at[k_], q_recv.at[k_], other, place)

    greeted(count, sections)
    core, z = lax.rem(place, 2), lax.div(place, 2)
    depth = count // 2
    x_loads = [
        pltpu.make_async_copy(src, dst, x_sem.at[i])
        for i, (src, dst) in enumerate(
            ((h2n_far, h2n), (k_far, k), (h1n_far, h1n), (a1_in, a1), (x_in, x))
        )
    ]
    for copy in x_loads:
        copy.start()
    load = pltpu.make_async_copy(k2.at[core], half, load_sem)
    swap = mesh_copy(k2.at[1 - core], theirs, swap_send, swap_recv, me, place + 1 - 2 * core)
    swap.start()
    load.start()

    def to_chip(k_):
        to = lax.rem(z + k_, depth)
        return mesh_copy(
            half.at[:, to],
            pieces.at[k_],
            piece_send.at[k_],
            piece_recv.at[k_],
            me,
            2 * to + core,
        )

    def add_cores():
        load.wait()
        swap.wait_recv()

        def add(n):
            q, y = lax.div(n, depth), lax.rem(n, depth)
            half[q, y] = (half[q, y].astype(F32) + theirs[q, y].astype(F32)).astype(BF16)

        loop(0, sections * depth, add)

    send_three()

    def after():
        return

    image_back_part(
        count,
        after,
        dy,
        res,
        h3n,
        mask,
        gains.at[1],
        stats3,
        batch_valid(counts, 0),
        w1,
        dz,
        dh3,
        da2,
        sums3,
        *sync[:3],
    )

    def a_copy(k_):
        return mesh_copy(da2, da2_all.at[me], a_send, a_recv.at[k_], 0, place)

    for k_ in range(1, sections):

        @pl.when(me == k_)
        def _(k_=k_):
            a_copy(k_).start()

    for k_ in range(1, sections):
        q_copy(k_).start()
    send_dz()
    send_two()
    add_cores()

    def to_chips():
        loop(1, depth, lambda k_: to_chip(k_).start())

    pl.when(me != 0)(to_chips)

    @pl.when(me == 0)
    def _():
        for k_ in range(1, sections):
            a_copy(k_).wait_recv()
        da2_all[0] = da2[...]
        for copy in x_loads:
            copy.wait()
        writer = Writer(stage, stage_sem)

        def taps_term(t):
            tall = narrow
            writer.put(dot_0(a1[...], hold[...]), k0_out.at[pl.ds(t * tall, tall)])

        last_part(
            count,
            to_chips,
            taps_term,
            da2_all,
            k,
            gb,
            pack,
            h1n,
            h2n,
            stats,
            counts,
            dh2,
            dh1,
            sums12,
            act,
            acc,
            hold,
            *sync[3:],
        )
        writer.rows_of_dot(x, dh1, p0_out)
        writer.drain()

    @pl.when(me != 0)
    def _():
        for copy in x_loads:
            copy.wait()
        a_copy(0).wait_send()
        sums12[...] = jnp.zeros(sums12.shape, F32)

    for k_ in range(1, sections):
        q_copy(k_).wait_recv()
    dzq[me] = dz[:, pl.ds(pl.multiple_of(me * quarter, 128), quarter)]
    rows, full = dzq_out.shape[0], act.shape[1]
    for m in range(4):

        def put(j, carry, m=m):
            at = pl.ds(pl.multiple_of(j * 128, 128), 128)
            act[j, pl.ds(m, full // 4, stride=4), :] = dzq[m, :, at].astype(F32)
            return carry

        lax.fori_loop(0, quarter // 128, put, 0)

    def weave(j, carry):
        at = pl.ds(pl.multiple_of(j * 128, 128), 128)
        dzq_out[:, at] = act[j, 0:rows, :].astype(BF16)
        return carry

    lax.fori_loop(0, quarter // 128, weave, 0)
    tall = stage.shape[1]
    sh_rows = sh_half.shape[0]
    fine = sh_rows // depth
    sh_swap = mesh_copy(
        sh_other, sh_theirs, sh_swap_send, sh_swap_recv, me, place + 1 - 2 * core
    )

    def sh_to_chip(k_):
        to = lax.rem(z + k_, depth)
        return mesh_copy(
            sh_half.at[pl.ds(pl.multiple_of(to * fine, 16), fine)],
            sh_pieces.at[k_],
            sh_send.at[k_],
            sh_recv.at[k_],
            me,
            2 * to + core,
        )

    @pl.when(me != 0)
    def _():
        for half_of, target in ((1 - core, sh_other), (core, sh_half)):
            for j in range(sh_rows // tall):
                at = pl.ds(pl.multiple_of(half_of * sh_rows + j * tall, 128), tall)
                target[j * tall : j * tall + tall, :] = dot_0(x[:, at], dzq_out[...]).astype(BF16)
            if target is sh_other:
                sh_swap.start()
        sh_swap.wait_recv()

        def add(n):
            at = pl.ds(pl.multiple_of(n * 32, 32), 32)
            sh_half[at, :] = (sh_half[at, :].astype(F32) + sh_theirs[at, :].astype(F32)).astype(BF16)

        loop(0, sh_rows // 32, add)
        loop(1, depth, lambda k_: sh_to_chip(k_).start())

    writer = Writer(stage, stage_sem)
    writer.rows_of_dot(dh3, a2, p1_out)
    writer.drain()
    loop(1, depth, lambda k_: to_chip(k_).wait_recv())

    def k2_sum(q):
        total = half[q, z].astype(F32)
        for k_ in range(1, depth):
            total = total + pieces[k_, q].astype(F32)
        whole[q] = total.astype(BF16)

    loop(0, sections, k2_sum)
    out = pltpu.make_async_copy(whole, k2_out, out_sem)
    out.start()

    @pl.when(me == 0)
    def _():
        writer = Writer(stage, stage_sem)
        writer.rows_of_dot(x, dzq_out, sh_out)
        writer.drain()

    @pl.when(me != 0)
    def _():
        loop(1, depth, lambda k_: sh_to_chip(k_).wait_recv())
        acc = sh_half[pl.ds(pl.multiple_of(z * fine, 16), fine), :].astype(F32)
        for k_ in range(1, depth):
            acc = acc + sh_pieces[k_].astype(F32)
        sh_sum[...] = acc.astype(BF16)
        written = pltpu.make_async_copy(sh_sum, piece_out, sh_sem)
        written.start()
        sh_swap.wait_send()
        loop(1, depth, lambda k_: sh_to_chip(k_).wait_send())
        written.wait()

    for k_ in range(1, sections):
        q_copy(k_).wait_send()
    loop(1, depth, lambda k_: to_chip(k_).wait_send())
    swap.wait_send()
    out.wait()
    wait_dz()
    wait_two()
    wait_three()


SUMS = (
    ("k0", 0, "owner"),
    ("p0", 0, "owner"),
    ("p1", 1, "each"),
    ("p2", 2, "each"),
    ("p3", 3, "each"),
    ("k2", 2, "chips"),
)


def gradient_kernel(
    sections,
    count,
    sh,
    sh_piece,
    k0,
    p0,
    p1,
    p2,
    p3,
    k2,
    vec,
    dh1,
    w,
    short,
    map_zero,
    map_one,
    map_two,
    map_three,
    sh_out,
    p_out,
    k_out,
    vec_out,
    maps,
    *scratch,
):
    names = [name for name, _, _ in SUMS]
    terms = dict(zip(names, (k0, p0, p1, p2, p3, k2)))
    owner = {name: section for name, section, _ in SUMS}
    held = {name: kind for name, _, kind in SUMS}
    fresh = [name for name in names if held[name] in ("owner", "each")]
    depth = count // 2
    me, place = lax.axis_index("segment"), lax.axis_index("dp")
    core, z = lax.rem(place, 2), lax.div(place, 2)
    sibling = place + 1 - 2 * core
    scratch = list(scratch)
    take = lambda: scratch.pop(0)
    half, theirs, planes, total, others, whole = {}, {}, {}, {}, {}, {}
    for name in names:
        if name in fresh:
            half[name], theirs[name] = take(), take()
        if held[name] in ("each", "chips"):
            planes[name] = take()
        if name in fresh:
            total[name], others[name] = take(), take()
        whole[name] = terms[name] if held[name] == "done" else take()
    relay = {name: take() for name in names if owner[name] == 0}
    relay["sh"] = take()
    sh_half, sh_theirs, sh_others, sh_whole, vec_slots = take(), take(), take(), take(), take()
    load_sem, a_send, a_recv, b_send, b_recv, c_send, c_recv, d_send, d_recv = (take() for _ in range(9))
    e_send, e_recv, e_own, f_send, f_recv, v_send, v_recv = (take() for _ in range(7))
    r_send, r_recv = take(), take()
    pages, s_rows, w_rows, hold, stage, page_sem, s_sem, w_sem, stage_sem = (take() for _ in range(9))
    slot = {name: i for i, name in enumerate(names)}
    last = len(names)

    page_loads = [
        pltpu.make_async_copy(source, pages, page_sem)
        for source in (map_zero, map_one, map_two, map_three)
    ]
    for i, copy in enumerate(page_loads):
        pl.when(me == i)(copy.start)
    wide = pages.shape[2]
    full_rows, map_rows = hold.shape[1], maps.shape[0] * maps.shape[1]

    def tile_loads(j):
        at = pl.ds(pl.multiple_of(j * TILE, TILE), TILE)
        at_slot = lax.rem(j, 2)
        return (
            pltpu.make_async_copy(short.at[at], s_rows.at[at_slot], s_sem.at[at_slot]),
            pltpu.make_async_copy(w.at[at], w_rows.at[at_slot], w_sem.at[at_slot]),
        )

    def tile_store(j):
        at = pl.ds(pl.multiple_of(j * TILE, TILE), TILE)
        at_slot = lax.rem(j, 2)
        return pltpu.make_async_copy(stage.at[at_slot], maps.at[:, :, at], stage_sem.at[at_slot])

    @pl.when(me == 0)
    def _():
        for copy in tile_loads(0):
            copy.start()

    def map_tile(j):
        at = pl.ds(pl.multiple_of(j * TILE, TILE), TILE)
        at_slot = lax.rem(j, 2)

        def weave(m, value):
            for part in range(TILE // 128):
                hold[part, pl.ds(m, full_rows // 4, stride=4), :] = value[
                    :, part * 128 : part * 128 + 128
                ]

        @pl.when(j >= 2)
        def _():
            tile_store(j - 2).wait()

        @pl.when(me == 0)
        def _():
            @pl.when(j + 1 < wide // TILE)
            def _():
                for copy in tile_loads(j + 1):
                    copy.start()

            for copy in tile_loads(j):
                copy.wait()
            for m in range(4):
                weave(m, dot_t(pages[m], s_rows[at_slot]))
            extra = dot_t(dh1[...], w_rows[at_slot])
            for part in range(TILE // 128):
                cols = slice(part * 128, part * 128 + 128)
                value = (hold[part, 0:map_rows, :] + extra[:, cols]).astype(BF16)
                stage[at_slot, :, :, cols] = value.reshape(map_rows // 4, 4, 128)

        @pl.when(me != 0)
        def _():
            for m in range(4):
                weave(m, pages[m, :, at].astype(F32))
            for part in range(TILE // 128):
                cols = slice(part * 128, part * 128 + 128)
                value = hold[part, 0:map_rows, :].astype(BF16)
                stage[at_slot, :, :, cols] = value.reshape(map_rows // 4, 4, 128)

        tile_store(j).start()

    def chip(k):
        return 2 * lax.rem(z + k, depth) + core

    barrier = pltpu.get_barrier_semaphore()
    pl.semaphore_signal(barrier, inc=1, device_id=(me, sibling), device_id_type=MESH)
    for k in range(1, sections):
        pl.semaphore_signal(
            barrier, inc=1, device_id=(jnp.bitwise_xor(me, k), place), device_id_type=MESH
        )
    loop(
        1,
        depth,
        lambda k: pl.semaphore_signal(
            barrier, inc=1, device_id=(me, chip(k)), device_id_type=MESH
        ),
    )
    pl.semaphore_wait(barrier, 1 + sections - 1 + depth - 1)

    def swap(name):
        return mesh_copy(
            terms[name].at[1 - core],
            theirs[name],
            a_send.at[slot[name]],
            a_recv.at[slot[name]],
            me,
            sibling,
        )

    def load(name):
        return pltpu.make_async_copy(terms[name].at[core], half[name], load_sem.at[slot[name]])

    def when_held(name, body):
        if held[name] == "each":
            body()
        else:
            pl.when(me == owner[name])(body)

    sh_rows = sh_half.shape[0]
    sh_swap = mesh_copy(
        sh.at[1 - core], sh_theirs, a_send.at[last], a_recv.at[last], me, sibling
    )
    sh_load = pltpu.make_async_copy(sh.at[core], sh_half, load_sem.at[last])
    piece = sh_rows // depth

    def sh_at(i):
        return pl.ds(pl.multiple_of(i * piece, 16), piece)

    mine = sh_at(z)
    piece_load = pltpu.make_async_copy(sh_piece, sh_whole.at[mine], load_sem.at[last])

    def sh_share(k):
        return mesh_copy(
            sh_whole.at[mine],
            sh_whole.at[mine],
            d_send.at[last, k],
            d_recv.at[last, k],
            me,
            chip(k),
        )

    @pl.when(me == 0)
    def _():
        sh_swap.start()
        sh_load.start()

    @pl.when(me != 0)
    def _():
        piece_load.start()
        piece_load.wait()
        loop(1, depth, lambda k: sh_share(k).start())


    def vec_copy(k):
        other = jnp.bitwise_xor(me, k)
        return mesh_copy(
            vec.at[other], vec_slots.at[k], v_send.at[k], v_recv.at[k], other, place
        )

    for k in range(1, sections):
        vec_copy(k).start()
    for name in fresh:

        def begin(name=name):
            swap(name).start()
            load(name).start()

        when_held(name, begin)

    def final(name):
        return k_out if name[0] == "k" else p_out

    def deliver(name, k):
        return mesh_copy(
            whole[name],
            final(name).at[core, me],
            e_send.at[slot[name]],
            e_recv.at[slot[name], k],
            owner[name],
            place,
        )

    def keep_own(name):
        return pltpu.make_async_copy(whole[name], final(name).at[core, me], e_own.at[slot[name]])

    def to_plane(name, k):
        other = jnp.bitwise_xor(me, k)
        return mesh_copy(
            terms[name].at[other],
            planes[name].at[k],
            b_send.at[slot[name], k],
            b_recv.at[slot[name], k],
            other,
            place,
        )

    def load_plane(name):
        return pltpu.make_async_copy(terms[name].at[me], planes[name].at[0], load_sem.at[slot[name]])

    for name in names:
        if held[name] == "chips":
            for k in range(1, sections):
                to_plane(name, k).start()
            load_plane(name).start()
        if held[name] == "done":

            @pl.when(me == owner[name])
            def _(name=name):
                keep_own(name).start()

            for k in range(1, sections):

                @pl.when(me == owner[name] ^ k)
                def _(name=name, k=k):
                    deliver(name, k).start()

    step = 32

    def sh_send(k):
        to = lax.rem(z + k, depth)
        return mesh_copy(
            sh_half.at[sh_at(to)],
            sh_others.at[k],
            c_send.at[last, k],
            c_recv.at[last, k],
            me,
            2 * to + core,
        )

    @pl.when(me == 0)
    def _():
        sh_load.wait()
        sh_swap.wait_recv()

        def sh_add(i):
            at = pl.ds(pl.multiple_of(i * step, step), step)
            sh_half[at, :] = (sh_half[at, :].astype(F32) + sh_theirs[at, :].astype(F32)).astype(BF16)

        loop(0, sh_rows // step, sh_add)
        loop(1, depth, lambda k: sh_send(k).start())

    def to_section(name, k):
        other = jnp.bitwise_xor(me, k)
        target = planes[name].at[k] if held[name] == "each" else total[name]
        return mesh_copy(
            half[name].at[other],
            target,
            b_send.at[slot[name], k],
            b_recv.at[slot[name], k],
            other,
            place,
        )

    def scattered(name, onward):
        if onward:
            return mesh_copy(
                relay[name], total[name], r_send.at[slot[name]], b_recv.at[slot[name], 3], 3, place
            )
        return mesh_copy(
            half[name].at[3], relay[name], b_send.at[slot[name], 3], r_recv.at[slot[name]], 2, place
        )

    for name in fresh:

        def combine(name=name):
            load(name).wait()
            swap(name).wait_recv()

            def add(i):
                q, y = lax.div(i, depth), lax.rem(i, depth)
                half[name][q, y] = (
                    half[name][q, y].astype(F32) + theirs[name][q, y].astype(F32)
                ).astype(BF16)

            loop(0, sections * depth, add)
            for k in range(1, sections):
                if held[name] == "owner" and k == 3:
                    pl.when(core == 0)(to_section(name, k).start)
                    pl.when(core == 1)(scattered(name, False).start)
                else:
                    to_section(name, k).start()

        when_held(name, combine)

    def share(name, k):
        return mesh_copy(
            whole[name].at[z],
            whole[name].at[z],
            d_send.at[slot[name], k],
            d_recv.at[slot[name], k],
            me,
            chip(k),
        )

    def planes_end(name):
        load_plane(name).wait()
        acc = planes[name][0].astype(F32)
        for k in range(1, sections):
            to_plane(name, k).wait_recv()
            acc = acc + planes[name][k].astype(F32)
        whole[name][z] = acc.astype(BF16)
        loop(1, depth, lambda k: share(name, k).start())

    planes_end("k2")
    for i, copy in enumerate(page_loads):
        pl.when(me == i)(copy.wait)
    loop(0, 2, map_tile)

    @pl.when((me == 2) & (core == 1))
    def _():
        for name in ("k0", "p0"):
            scattered(name, False).wait_recv()
            scattered(name, True).start()


    @pl.when(me == 0)
    def _():
        loop(1, depth, lambda k: sh_send(k).wait_recv())
        acc = sh_half[mine, :].astype(F32)
        for k in range(1, depth):
            acc = acc + sh_others[k].astype(F32)
        sh_whole[mine, :] = acc.astype(BF16)
        loop(1, depth, lambda k: sh_share(k).start())

    loop(2, wide // TILE, map_tile)

    def to_chip(name, k):
        to = lax.rem(z + k, depth)
        return mesh_copy(
            total[name].at[to],
            others[name].at[k],
            c_send.at[slot[name], k],
            c_recv.at[slot[name], k],
            me,
            2 * to + core,
        )

    def b_end(name):
        if held[name] == "each":
            for k in range(1, sections):
                to_section(name, k).wait_recv()

            def plane_add(y, name=name):
                acc = half[name][me, y].astype(F32)
                for k in range(1, sections):
                    acc = acc + planes[name][k, y].astype(F32)
                total[name][y] = acc.astype(BF16)

            loop(0, depth, plane_add)
        else:

            @pl.when(me == owner[name])
            def _(name=name):
                def keep(y):
                    total[name][y] = half[name][owner[name], y]

                loop(0, depth, keep)

            for k in range(1, sections):

                @pl.when(me == owner[name] ^ k)
                def _(name=name, k=k):
                    to_section(name, k).wait_recv()

        loop(1, depth, lambda k, name=name: to_chip(name, k).start())

    for name in ("k0", "p0"):
        b_end(name)

    def sh_deliver(k):
        at = pl.ds(pl.multiple_of(me * sh_whole.shape[1], 128), sh_whole.shape[1])
        return mesh_copy(
            sh_whole,
            sh_out.at[core, :, at],
            e_send.at[last],
            e_recv.at[last, k],
            0,
            place,
        )

    loop(1, depth, lambda k: sh_share(k).wait_recv())
    at_zero = pl.ds(0, sh_whole.shape[1])
    sh_keep = pltpu.make_async_copy(sh_whole, sh_out.at[core, :, at_zero], e_own.at[last])

    @pl.when(me == 0)
    def _():
        sh_keep.start()

    def relayed(name, onward):
        index = last if name == "sh" else slot[name]
        at = pl.ds(3 * sh_whole.shape[1], sh_whole.shape[1])
        src, dst = (sh_whole, sh_out.at[core, :, at]) if name == "sh" else (whole[name], final(name).at[core, 3])
        if onward:
            return mesh_copy(relay[name], dst, r_send.at[index], e_recv.at[index, 3], 0, place)
        return mesh_copy(src, relay[name], e_send.at[index], r_recv.at[index], 1, place)

    def start_delivery(name):
        index = last if name == "sh" else slot[name]
        section = 0 if name == "sh" else owner[name]
        copy = sh_deliver if name == "sh" else functools.partial(deliver, name)
        for k in range(1, sections):
            direct = me == section ^ k
            if section == 0 and k == 3:
                direct = direct & (core == 0)

                @pl.when((me == 3) & (core == 1))
                def _():
                    relayed(name, False).start()

            @pl.when(direct)
            def _(k=k):
                copy(k).start()

    def pass_on(name):
        @pl.when((me == 1) & (core == 1))
        def _():
            relayed(name, False).wait_recv()
            relayed(name, True).start()

    start_delivery("sh")

    def c_end(name):
        loop(1, depth, lambda k: to_chip(name, k).wait_recv())
        acc = total[name][z].astype(F32)
        for k in range(1, depth):
            acc = acc + others[name][k].astype(F32)
        whole[name][z] = acc.astype(BF16)
        loop(1, depth, lambda k: share(name, k).start())

    def d_end(name):
        loop(1, depth, lambda k: share(name, k).wait_recv())

        @pl.when(me == owner[name])
        def _():
            keep_own(name).start()

        start_delivery(name)

    later = ("p1", "p2", "p3")
    for name in ("k0", "p0"):
        c_end(name)
    for name in later:
        b_end(name)
    pass_on("sh")
    for name in ("k0", "p0", "k2"):
        d_end(name)
    for name in later:
        c_end(name)
    for name in ("k0", "p0"):
        pass_on(name)
    for name in later:
        d_end(name)

    def cross(name):
        return mesh_copy(
            final(name).at[core],
            final(name).at[core],
            f_send.at[slot[name]],
            f_recv.at[slot[name]],
            me,
            sibling,
        )

    sh_cross = mesh_copy(
        sh_out.at[core], sh_out.at[core], f_send.at[last], f_recv.at[last], me, sibling
    )

    @pl.when(me == 0)
    def _():
        sh_keep.wait()
        for k in range(1, sections):
            sh_deliver(k).wait_recv()
        sh_cross.start()

    for name in names:

        @pl.when(me == owner[name])
        def _(name=name):
            keep_own(name).wait()
            for k in range(1, sections):
                deliver(name, k).wait_recv()
            cross(name).start()

    for k in range(1, sections):
        vec_copy(k).wait_recv()
    sums = vec[me]
    for k in range(1, sections):
        sums = sums + vec_slots[k]
    vec_out[...] = sums

    tile_store(wide // TILE - 2).wait()
    tile_store(wide // TILE - 1).wait()
    for k in range(1, sections):
        vec_copy(k).wait_send()

    @pl.when(me == 0)
    def _():
        sh_swap.wait_send()
        loop(1, depth, lambda k: sh_send(k).wait_send())

    loop(1, depth, lambda k: sh_share(k).wait_send())

    @pl.when(me == 0)
    def _():
        sh_cross.wait()

    @pl.when(me != 0)
    def _():
        sh_deliver(0).wait_send()

    @pl.when((me == 1) & (core == 1))
    def _():
        for name in relay:
            relayed(name, True).wait_send()

    @pl.when((me == 2) & (core == 1))
    def _():
        for name in ("k0", "p0"):
            scattered(name, True).wait_send()

    for name in names:

        def sent(name=name):
            swap(name).wait_send()
            for k in range(1, sections):
                to_section(name, k).wait_send()

        if name in fresh:
            when_held(name, sent)
            loop(1, depth, lambda k, name=name: to_chip(name, k).wait_send())
        if held[name] == "chips":
            for k in range(1, sections):
                to_plane(name, k).wait_send()
        if held[name] != "done":
            loop(1, depth, lambda k, name=name: share(name, k).wait_send())

        @pl.when(me == owner[name])
        def _(name=name):
            cross(name).wait()

        @pl.when(me != owner[name])
        def _(name=name):
            deliver(name, 0).wait_send()


def sum_gradients(sections, count, short, piece, terms, vectors, dh1, w, weights, map_sources, real):
    narrow = short.shape[1]
    depth = count // 2
    args, scratch = [], []
    relays = []
    for name, section, kind in SUMS:
        args.append(terms[name])
        full = (sections, depth) + terms[name].shape[-2:]
        shapes = []
        if kind in ("owner", "each"):
            shapes += [full, full]
        if kind == "each":
            shapes.append(full)
        if kind == "chips":
            shapes.append((sections,) + full[2:])
        if kind in ("owner", "each"):
            shapes += [full[1:]] * 2
        if kind != "done":
            shapes.append(full[1:])
        if section == 0:
            relays.append(pltpu.VMEM(full[1:], BF16))
        scratch += [pltpu.VMEM(a, BF16) for a in shapes]
    scratch += relays + [pltpu.VMEM((short.shape[0] // 2, narrow), BF16)]
    sh_rows = short.shape[0] // 2
    scratch += [
        pltpu.VMEM((sh_rows, narrow), BF16),
        pltpu.VMEM((sh_rows, narrow), BF16),
        pltpu.VMEM((depth, sh_rows // depth, narrow), BF16),
        pltpu.VMEM((sh_rows, narrow), BF16),
        pltpu.VMEM((sections,) + vectors.shape[1:], F32),
    ]
    kinds = len(SUMS) + 1
    for shape in [(kinds,)] * 3 + [(kinds, sections)] * 2 + [(kinds, depth)] * 4:
        scratch.append(pltpu.SemaphoreType.DMA(shape))
    for shape in [(kinds,), (kinds, sections), (kinds,), (kinds,), (kinds,), (sections,), (sections,), (kinds,), (kinds,)]:
        scratch.append(pltpu.SemaphoreType.DMA(shape))
    wide = w.shape[0]
    padded = map_sources[0].shape[1]
    scratch += [
        pltpu.VMEM(map_sources[0].shape, BF16),
        pltpu.VMEM((2, TILE, wide), BF16),
        pltpu.VMEM((2, TILE, narrow), BF16),
        pltpu.VMEM((TILE // 128, 4 * padded, 128), F32),
        pltpu.VMEM((2, real, 4, TILE), BF16),
        pltpu.SemaphoreType.DMA,
        pltpu.SemaphoreType.DMA((2,)),
        pltpu.SemaphoreType.DMA((2,)),
        pltpu.SemaphoreType.DMA((2,)),
    ]
    hbm = pl.BlockSpec(memory_space=pl.ANY)
    vmem = pl.BlockSpec(memory_space=pltpu.VMEM)
    taps_shape, proj_shape = args[0].shape, args[1].shape
    return pl.pallas_call(
        functools.partial(gradient_kernel, sections, count),
        out_shape=[
            shape_of((2, sh_rows, narrow * sections), BF16),
            shape_of(proj_shape, BF16),
            shape_of(taps_shape, BF16),
            shape_of(vectors.shape[1:], F32),
            shape_of((real, 4, wide), BF16),
        ],
        in_specs=[hbm] * 8 + [vmem, vmem] + [hbm] * 6,
        out_specs=[hbm, hbm, hbm, vmem, hbm],
        scratch_shapes=scratch,
        compiler_params=pltpu.CompilerParams(
            has_side_effects=True, vmem_limit_bytes=VMEM_BYTES, collective_id=5
        ),
        cost_estimate=pl.CostEstimate(flops=0, bytes_accessed=400 * 2**20, transcendentals=0),
    )(short.reshape(2, sh_rows, narrow), piece, *args, vectors, dh1, w, weights, *map_sources)


def cast_kernel(proj, taps, short, proj_out, taps_out, short_out):
    me = lax.axis_index("segment")
    proj_out[...] = proj[...].astype(F32)
    for held, src, out in (
        ((me == 0) | (me == 2), taps, taps_out),
        (me == 0, short, short_out),
    ):

        @pl.when(held)
        def _(src=src, out=out):
            out[...] = src[...].astype(F32)

        @pl.when(jnp.logical_not(held))
        def _(out=out):
            out[...] = jnp.zeros(out.shape, F32)


def cast_sums(*sums):
    steps = 8
    blocks = [pl.BlockSpec((a.shape[0] // steps, a.shape[1]), lambda i: (i, 0)) for a in sums]
    return pl.pallas_call(
        cast_kernel,
        grid=(steps,),
        out_shape=[shape_of(a.shape, F32) for a in sums],
        in_specs=blocks,
        out_specs=blocks,
        compiler_params=pltpu.CompilerParams(vmem_limit_bytes=VMEM_BYTES),
        cost_estimate=pl.CostEstimate(flops=0, bytes_accessed=45 * 2**20, transcendentals=0),
    )(*sums)


def layouts(resolution_ids, order_ids):
    pixels = jnp.arange(MAP * MAP, dtype=jnp.int32)
    row_of = pixels // MAP
    column_of = pixels % MAP
    extent = 5 + resolution_ids[:, None]
    image_mask = ((row_of[None, :] < extent) & (column_of[None, :] < extent)).astype(F32)
    inside = (row_of < 6) & (column_of < 6)
    position = jnp.where(inside, row_of // 2 * 3 + column_of // 2, 0)
    onehot_tile = (position[:, None] == jnp.arange(9)[None, :]).astype(jnp.int32)
    picked = jnp.sum(onehot_tile[None] * order_ids[:, None, :], axis=2)
    row_to = 2 * (picked // 3) + row_of % 2
    column_to = 2 * (picked % 3) + column_of % 2
    target = row_to * MAP + column_to
    tile_mask = (inside & (row_to < extent) & (column_to < extent)).astype(F32)
    return image_mask, tile_mask, jnp.where(inside, target, -1)


def tap_tables(tiled):
    lattice = np.arange(MAP)
    tables = []
    for vertical, lateral in OFFSETS:
        row, column = lattice + vertical, lattice + lateral
        in_row = (row >= 0) & (row < MAP)
        in_column = (column >= 0) & (column < MAP)
        if tiled:
            in_row &= row // 2 == lattice // 2
            in_column &= column // 2 == lattice // 2
        tables.append((in_row[:, None] & in_column[None, :]).reshape(-1))
    return np.stack(tables, axis=1).astype(np.float32)


def body(
    layer_input,
    output_grad,
    resolution,
    tile_order,
    proj_weight,
    spatial_weight,
    shortcut_weight,
    bn_gain,
    bn_bias,
):
    micro, images, pixels, wide = layer_input.shape
    narrow = proj_weight.shape[2]
    rows = images * pixels
    padded = -(-rows // 16) * 16
    sections = lax.axis_size("segment")
    count = lax.axis_size("dp")
    section = lax.axis_index("segment")
    first = section == 0
    proj, spatial, shortcut = proj_weight[0], spatial_weight[0], shortcut_weight[0]
    pick = lambda a: lax.dynamic_index_in_dim(a, section, 0, keepdims=False)

    image_masks, tile_masks, targets = layouts(
        resolution.reshape(-1), tile_order.reshape(micro * images, -1)
    )
    interleave = lambda a: jnp.transpose(a.reshape(micro, rows), (1, 0)).reshape(rows * micro, 1)
    taps_image = np.tile(np.repeat(tap_tables(False), micro, axis=0), (images, 1))
    pack_all = jnp.concatenate(
        [interleave(image_masks), jnp.asarray(taps_image), jnp.zeros((rows * micro, 6), F32)], axis=1
    )
    tiles_all = interleave(tile_masks)
    pad_rows = lambda a: jnp.pad(a, ((0, padded - rows), (0, 0)))
    image_mask = pad_rows(pick(image_masks.reshape(micro, rows, 1)))
    tile_mask = pad_rows(pick(tile_masks.reshape(micro, rows, 1)))
    taps_tile = np.pad(np.tile(tap_tables(True), (images, 1)), ((0, padded - rows), (0, 6)))
    pack_tile = jnp.concatenate([tile_mask, jnp.asarray(taps_tile)], axis=1)
    target = pick(targets.reshape(micro, images, pixels))
    base = (jnp.arange(images) * pixels)[:, None]
    target = jnp.where(target >= 0, target + base, -1).reshape(rows)
    target = jnp.pad(target, (0, padded - rows), constant_values=-1)
    index = jnp.arange(padded)
    moves = (target[:, None] == index[None, :]).astype(BF16)
    moves_back = (target[None, :] == index[:, None]).astype(BF16)

    x_in = jnp.transpose(layer_input, (1, 2, 0, 3)).reshape(rows, micro, wide)
    og_in = jnp.transpose(output_grad, (1, 2, 0, 3)).reshape(rows, micro, wide)
    gb_first = jnp.stack(
        [bn_gain[0, :narrow], bn_bias[0, :narrow]]
        + [bn_gain[0, narrow : 2 * narrow], bn_bias[0, narrow : 2 * narrow]]
    )
    gains_here = jnp.concatenate([bn_gain, bn_bias])
    total = rows * micro
    quarter = wide // sections
    dma = pltpu.SemaphoreType.DMA
    stats_all, counts, gains, y1, u, h3n, stats3, *far = kernel_call(
        functools.partial(head_kernel, sections, count),
        [
            shape_of((16, narrow), F32),
            shape_of((8, 128), F32),
            shape_of((sections, 2, wide), F32),
            shape_of((padded, wide), BF16),
            shape_of((padded, wide), BF16),
            shape_of((padded, wide), F32),
            shape_of((2, wide), F32),
            shape_of((padded, narrow), BF16),
            shape_of((wide, narrow), BF16),
            shape_of((sections, padded, quarter), BF16),
            shape_of((total, wide), BF16),
            shape_of((total, narrow), BF16),
            shape_of((total, narrow), F32),
            shape_of((total, narrow), F32),
            shape_of((wide, narrow), BF16),
            shape_of((wide, narrow), BF16),
            shape_of((9 * narrow, narrow), BF16),
        ],
        [x_in, proj, shortcut, spatial, gb_first, gains_here, pack_all, tiles_all, image_mask, moves],
        [
            pltpu.VMEM((total, wide), BF16),
            pltpu.VMEM((total, 9 * narrow), BF16),
            pltpu.VMEM((total, narrow), F32),
            pltpu.VMEM((total, narrow), F32),
            pltpu.VMEM((narrow // 128, 4 * padded, 128), F32),
            pltpu.VMEM((micro, padded, narrow), BF16),
            pltpu.VMEM((padded, narrow), BF16),
            pltpu.VMEM((wide, quarter), BF16),
            pltpu.VMEM((wide, narrow), BF16),
            pltpu.VMEM((micro, padded, quarter), BF16),
            pltpu.VMEM((sections, padded, quarter), BF16),
            pltpu.VMEM((sections, 2, wide), F32),
        ]
        + sync_scratch(count, [(8, narrow + 128), (8, narrow), (2, wide)])
        + [dma((sections,)), dma, dma, dma]
        + [dma((sections,)), dma, dma, dma]
        + [dma((sections,)), dma((sections,)), dma((sections,)), dma]
        + [dma((sections,)), dma((sections,)), dma((2,)), dma((7,))]
        + [dma((5, sections)), dma((5,)), dma((5,)), dma((5,))]
        + [dma((5, 2)), dma((5, 2)), dma((3,))]
        + [dma((5,)), pltpu.VMEM((9 * narrow, narrow), BF16), dma],
        0,
        2 * total * (narrow * (wide + 9 * narrow) + wide * quarter),
        60 * 2**20,
        far_in=(2, 3),
        far_out=tuple(range(7, 17)),
    )
    a2, w1, res, x_all, a1_all, h1n_all, h2n_all, w3, w2, k2 = far
    paged = shape_of((sections, padded, wide), BF16)
    y2, dy1, t_sums, map_one, p3_term, p2_term, k2_term = kernel_call(
        functools.partial(tile_kernel, sections, count),
        [
            shape_of((padded, wide), BF16),
            shape_of((padded, wide), BF16),
            shape_of((6, wide), F32),
            paged,
            shape_of((wide, narrow), BF16),
            shape_of((wide, narrow), BF16),
            shape_of((9 * narrow, narrow), BF16),
        ],
        [u, w2, k2, w3, og_in, pack_tile, gains, counts, moves_back, y1],
        [
            pltpu.VMEM((padded, narrow), BF16),
            pltpu.VMEM((padded, 9 * narrow), BF16),
            pltpu.VMEM((padded, wide), BF16),
            pltpu.VMEM((padded, narrow), BF16),
            pltpu.VMEM((padded, narrow), BF16),
            pltpu.VMEM((2, 512, narrow), BF16),
            dma((2,)),
            pltpu.VMEM((9 * narrow, narrow), BF16),
            pltpu.VMEM((wide, narrow), BF16),
            pltpu.VMEM((rows, micro, wide), BF16),
            dma((3,)),
            pltpu.VMEM((padded, narrow), F32),
            pltpu.VMEM((padded, narrow), F32),
            pltpu.VMEM((padded, wide), F32),
            pltpu.VMEM((padded, narrow), F32),
            pltpu.VMEM((padded, wide), BF16),
            pltpu.VMEM((6, wide), F32),
            pltpu.VMEM((padded, wide), F32),
        ]
        + [dma, dma((sections,)), dma]
        + sync_scratch(
            count, [(2, narrow), (2, narrow), (2, wide), (2, wide), (2, narrow), (2, narrow)]
        ),
        1,
        4 * padded * narrow * (2 * wide + 9 * narrow),
        30 * 2**20,
        far_in=(2, 3, 4, 9),
        far_out=(3, 4, 5, 6),
    )
    depth = count // 2

    def split(term):
        return term.reshape(2, sections, depth, term.shape[0] // (2 * sections * depth), narrow)

    p3_term, p2_term, k2_term = split(p3_term), split(p2_term), split(k2_term)
    taps_piece = k2_term.shape[3]
    dh1_all, i_sums, f_sums, k2_part, *far = kernel_call(
        functools.partial(back_kernel, sections, count),
        [
            shape_of((total, narrow), BF16),
            shape_of((2, wide), F32),
            shape_of((16, narrow), F32),
            shape_of((sections, taps_piece, narrow), BF16),
            paged,
            paged,
            paged,
            shape_of((wide, narrow), BF16),
            shape_of((9 * narrow, narrow), BF16),
            shape_of((wide, narrow), BF16),
            shape_of((wide, narrow), BF16),
            shape_of((wide // count, narrow), BF16),
        ],
        [dy1, res, h3n, image_mask, gains, stats3, w1, spatial, gb_first, pack_all]
        + [h1n_all, h2n_all, stats_all, counts, k2_term, y2, a2, a1_all, x_all],
        [
            pltpu.VMEM((padded, wide), BF16),
            pltpu.VMEM((padded, wide), BF16),
            pltpu.VMEM((total, narrow), BF16),
            pltpu.VMEM((total, quarter), BF16),
            pltpu.VMEM((total, narrow), BF16),
            pltpu.VMEM((total, wide), BF16),
            pltpu.VMEM((9 * narrow, narrow), BF16),
            pltpu.VMEM((total, narrow), F32),
            pltpu.VMEM((total, narrow), F32),
            pltpu.VMEM((2, 512, narrow), BF16),
            dma((2,)),
            dma((5,)),
            pltpu.VMEM((padded, narrow), BF16),
            pltpu.VMEM((micro, padded, narrow), BF16),
            pltpu.VMEM((micro, padded, quarter), BF16),
            pltpu.VMEM((narrow // 128, 4 * padded, 128), F32),
            pltpu.VMEM((total, narrow), F32),
            pltpu.VMEM((total, narrow), BF16),
        ]
        + sync_scratch(count, [(2, wide), (8, narrow), (8, narrow)])
        + [pltpu.VMEM(k2_term.shape[1:], BF16)] * 2
        + [pltpu.VMEM((depth, sections, taps_piece, narrow), BF16)]
        + [pltpu.VMEM((sections, taps_piece, narrow), BF16)]
        + [dma, dma, dma, dma((depth,)), dma((depth,)), dma]
        + [pltpu.VMEM((wide // 2, narrow), BF16)] * 3
        + [pltpu.VMEM((depth, wide // count, narrow), BF16), pltpu.VMEM((wide // count, narrow), BF16)]
        + [dma, dma, dma((depth,)), dma((depth,)), dma]
        + [dma, dma((sections,)), dma((sections,)), dma((sections,))]
        + [dma, dma((sections,)), dma] * 3,
        2,
        2 * total * narrow * 9 * narrow,
        40 * 2**20,
        far_in=(7, 10, 11, 14, 15, 17, 18),
        far_out=tuple(range(3, 12)),
    )
    map_zero, map_two, map_three, p1_term, k0_term, p0_term, short_term, short_piece = far

    terms = {
        "p3": p3_term,
        "k2": k2_part,
        "p2": p2_term,
        "p1": split(p1_term),
        "k0": split(k0_term),
        "p0": split(p0_term),
    }

    blank = jnp.zeros((wide,), F32)
    pad = jnp.zeros((wide - 2 * narrow,), F32)
    of_batches = lambda at: jnp.sum(f_sums[at : at + 4], axis=0)
    zero_gain = jnp.where(first, jnp.concatenate([of_batches(12), of_batches(4), pad]), blank)
    zero_bias = jnp.where(first, jnp.concatenate([of_batches(8), of_batches(0), pad]), blank)
    vectors = jnp.stack(
        [
            zero_gain,
            zero_bias,
            i_sums[1],
            i_sums[0],
            jnp.concatenate([t_sums[5, :narrow], t_sums[3, :narrow], pad]),
            jnp.concatenate([t_sums[4, :narrow], t_sums[2, :narrow], pad]),
            t_sums[1],
            t_sums[0],
        ]
    )
    short_sum, proj_sum, taps_sum, vectors, maps = sum_gradients(
        sections,
        count,
        short_term,
        short_piece,
        terms,
        vectors.reshape(sections, 2, wide),
        dh1_all,
        proj,
        shortcut,
        (map_zero, map_one, map_two, map_three),
        rows,
    )
    maps = jnp.transpose(maps.reshape(images, pixels, micro, wide), (2, 0, 1, 3))
    proj_grad, spatial_grad, short_grad = cast_sums(
        proj_sum.reshape(wide, narrow),
        taps_sum.reshape(9 * narrow, narrow),
        short_sum.reshape(wide, wide),
    )
    return (
        maps[None],
        proj_grad[None],
        spatial_grad[None],
        short_grad[None],
        vectors[:1],
        vectors[1:],
    )


def solution(mesh):
    return jax.shard_map(
        body,
        mesh=mesh,
        in_specs=(
            P(None, "dp", None, None),
            P(None, "dp", None, None),
            P(None, "dp"),
            P(None, "dp", None),
            P("segment", None, None),
            P("segment", None, None),
            P("segment", None, None),
            P("segment", None),
            P("segment", None),
        ),
        out_specs=(
            P("segment", None, "dp", None, None),
            P("segment", None, None),
            P("segment", None, None),
            P("segment", None, None),
            P("segment", None),
            P("segment", None),
        ),
        check_vma=False,
    )
```

```python
import functools

import jax
import jax.numpy as jnp
import numpy as np
from jax import lax
from jax.experimental import pallas as pl
from jax.experimental.pallas import tpu as pltpu
from jax.sharding import PartitionSpec as P

MAP = 7
EPSILON = 1e-05
OFFSETS = ((-1, -1), (-1, 0), (-1, 1), (0, -1), (0, 0), (0, 1), (1, -1), (1, 0), (1, 1))
MESH = pl.DeviceIdType.MESH
F32 = jnp.float32
BF16 = jnp.bfloat16
VMEM_BYTES = 60 * 2**20
TILE = 256


def greet(count, sections=0):
    segment, me = lax.axis_index("segment"), lax.axis_index("dp")
    barrier = pltpu.get_barrier_semaphore()

    def one(k, carry):
        pl.semaphore_signal(
            barrier, inc=1, device_id=(segment, lax.rem(me + k, count)), device_id_type=MESH
        )
        return carry

    lax.fori_loop(1, count, one, 0)
    for k in range(1, sections):
        pl.semaphore_signal(
            barrier, inc=1, device_id=(jnp.bitwise_xor(segment, k), me), device_id_type=MESH
        )


def greeted(count, sections=1):
    pl.semaphore_wait(pltpu.get_barrier_semaphore(), count - 1 + sections - 1)


def exchange(count, slots, send_sem, recv_sem):
    segment, me = lax.axis_index("segment"), lax.axis_index("dp")

    def copy(k):
        return pltpu.make_async_remote_copy(
            src_ref=slots.at[me],
            dst_ref=slots.at[me],
            send_sem=send_sem.at[k],
            recv_sem=recv_sem.at[k],
            device_id=(segment, lax.rem(me + k, count)),
            device_id_type=MESH,
        )

    def start(k, carry):
        copy(k).start()
        return carry

    def finish(k, carry):
        copy(k).wait_recv()
        copy(k).wait_send()
        return carry

    lax.fori_loop(1, count, start, 0)
    lax.fori_loop(1, count, finish, 0)
    total = slots[0]
    for k in range(1, count):
        total = total + slots[k]
    return total


def mesh_copy(src, dst, send_sem, recv_sem, segment, place):
    return pltpu.make_async_remote_copy(
        src_ref=src,
        dst_ref=dst,
        send_sem=send_sem,
        recv_sem=recv_sem,
        device_id=(segment, place),
        device_id_type=MESH,
    )


def loop(low, high, body):
    def one(k, carry):
        body(k)
        return carry

    lax.fori_loop(low, high, one, 0)


def sync_scratch(count, shapes):
    out = []
    for shape in shapes:
        out += [
            pltpu.VMEM((count,) + shape, F32),
            pltpu.SemaphoreType.DMA((count,)),
            pltpu.SemaphoreType.DMA((count,)),
        ]
    return out


def kernel_call(kernel, outs, args, scratch, ident, flops, moved, far_in=(), far_out=()):
    params = dict(has_side_effects=True, vmem_limit_bytes=VMEM_BYTES)
    if ident is not None:
        params["collective_id"] = ident
    return pl.pallas_call(
        kernel,
        out_shape=outs,
        in_specs=[
            pl.BlockSpec(memory_space=pl.ANY if i in far_in else pltpu.VMEM) for i in range(len(args))
        ],
        out_specs=[
            pl.BlockSpec(memory_space=pl.ANY if i in far_out else pltpu.VMEM) for i in range(len(outs))
        ],
        scratch_shapes=scratch,
        compiler_params=pltpu.CompilerParams(**params),
        cost_estimate=pl.CostEstimate(flops=flops, bytes_accessed=moved, transcendentals=0),
    )(*args)


def shape_of(shape, dtype):
    return jax.ShapeDtypeStruct(shape, dtype)


def dot(a, b):
    return jnp.dot(a, b, preferred_element_type=F32)


def dot_t(a, b):
    return lax.dot_general(a, b, (((1,), (1,)), ((), ())), preferred_element_type=F32)


def dot_0(a, b):
    return lax.dot_general(a, b, (((0,), (0,)), ((), ())), preferred_element_type=F32)


class Writer:
    def __init__(self, stage, sems):
        self.stage, self.sems, self.open, self.turn = stage, sems, [None, None], 0

    def put(self, value, dst):
        at = self.turn % 2
        self.turn += 1
        if self.open[at] is not None:
            self.open[at].wait()
        self.stage[at] = value.astype(BF16)
        self.open[at] = pltpu.make_async_copy(self.stage.at[at], dst, self.sems.at[at])
        self.open[at].start()

    def rows_of_dot(self, left, right, out):
        tall = self.stage.shape[1]
        for j in range(out.shape[0] // tall):
            at = pl.ds(j * tall, tall)
            self.put(dot_0(left[:, at], right[...]), out.at[at])

    def drain(self):
        for at in range(2):
            if self.open[at] is not None:
                self.open[at].wait()
        self.open = [None, None]


def sigmoid(v):
    return 1.0 / (1.0 + jnp.exp(-v))


def slope(v):
    s = sigmoid(v)
    return s * (1.0 + v * (1.0 - s))


def over(width, step, body):
    def one(j, carry):
        body(pl.ds(pl.multiple_of(j * step, step), step))
        return carry

    lax.fori_loop(0, width // step, one, 0)


def lane(at):
    return lax.div(at.start, 128)


def unrolled_shift(ref_value, shift):
    rows = ref_value.shape[0]
    return ref_value if shift % rows == 0 else pltpu.roll(ref_value, (-shift) % rows, 0)


def by_batch(values):
    rows, width = values.shape
    part = jnp.sum(values.reshape(rows // 8, 8, width), axis=0)
    return part[:4] + part[4:]


def spread8(values):
    return jnp.concatenate([values, values], axis=0)[None]


def first_part(
    count, hooks, writes, x, w, k, gb, pack, tiles, a2_out, cols, h1n, h2n, stats_out, count_out, act, *sync
):
    s1, send1, recv1, s2, send2, recv2 = sync
    rows, narrow = h1n.shape
    me = lax.axis_index("dp")
    full = act.shape[1]

    def tile8(v):
        return v.reshape(rows // 8, 8, v.shape[1])

    def project(at):
        h = dot(x[...], w[:, at])
        h1n[:, at] = h
        m = pack[:, 0:1] * h
        s1[me, 0:4, at] = by_batch(m)
        s1[me, 4:8, at] = by_batch(m * h)

    over(narrow, TILE, project)
    s1[me, 0:4, narrow:] = jnp.broadcast_to(by_batch(pack[:, 0:1]), (4, 128))
    s1[me, 4:8, narrow:] = jnp.broadcast_to(by_batch(tiles[:, 0:1]), (4, 128))
    total = exchange(count, s1, send1, recv1)
    counts = total[:, narrow:]
    count_out[...] = counts
    valid = counts[0:4, 0:1]
    average = total[0:4, :narrow] / valid
    inverse = lax.rsqrt(total[4:8, :narrow] / valid - average * average + EPSILON)
    stats_out[0:4, :] = average
    stats_out[4:8, :] = inverse
    hooks[0]()

    def activate(stat_at, gain_at, source):
        def body(at):
            mean = spread8(stats_out[stat_at : stat_at + 4, at])
            inv = spread8(stats_out[stat_at + 4 : stat_at + 8, at])
            hn = (tile8(source[:, at]) - mean) * inv
            source[:, at] = hn.reshape(rows, hn.shape[2])
            n = gb[gain_at : gain_at + 1, at][None] * hn + gb[gain_at + 1 : gain_at + 2, at][None]
            n = n.reshape(rows, n.shape[2])
            act[lane(at), 0:rows, :] = pack[:, 0:1] * (n * sigmoid(n))

        return body

    over(narrow, 128, activate(0, 0, h1n))

    for t, (vertical, lateral) in enumerate(OFFSETS):
        shift = 4 * (7 * vertical + lateral)

        def place(j, carry, t=t, shift=shift):
            at = pl.ds(pl.multiple_of(j * 128, 128), 128)
            to = pl.ds(pl.multiple_of(t * narrow + j * 128, 128), 128)
            moved = unrolled_shift(act[j, 0:rows, :], shift)
            cols[:, to] = (pack[:, 1 + t : 2 + t] * moved).astype(BF16)
            return carry

        lax.fori_loop(0, narrow // 128, place, 0)

    def convolve(at):
        h = dot(cols[...], k[:, at])
        h2n[:, at] = h
        m = pack[:, 0:1] * h
        s2[me, 0:4, at] = by_batch(m)
        s2[me, 4:8, at] = by_batch(m * h)

    for write in writes:
        write.start()
    hooks[1]()
    over(narrow, TILE, convolve)
    total = exchange(count, s2, send2, recv2)
    average = total[0:4] / valid
    hooks[2]()
    stats_out[8:12, :] = average
    stats_out[12:16, :] = lax.rsqrt(total[4:8] / valid - average * average + EPSILON)
    over(narrow, 128, activate(8, 2, h2n))
    act[:, rows:, :] = jnp.zeros((narrow // 128, full - rows, 128), F32)
    for m in range(4):

        def pick(j, carry, m=m):
            at = pl.ds(pl.multiple_of(j * 128, 128), 128)
            a2_out[m, :, at] = act[j, pl.ds(m, full // 4, stride=4), :].astype(BF16)
            return carry

        lax.fori_loop(0, narrow // 128, pick, 0)


def residual_part(x, w, out, hold):
    rows, full, quarter = x.shape[0], hold.shape[1], out.shape[2]
    hold[:, rows:, :] = jnp.zeros((quarter // 128, full - rows, 128), F32)

    def body(at):
        value = dot(x[...], w[:, at])
        for part in range(TILE // 128):
            hold[lane(at) + part, 0:rows, :] = value[:, part * 128 : part * 128 + 128]

    over(quarter, TILE, body)
    for m in range(4):

        def pick(j, carry, m=m):
            at = pl.ds(pl.multiple_of(j * 128, 128), 128)
            out[m, :, at] = hold[j, pl.ds(m, full // 4, stride=4), :].astype(BF16)
            return carry

        lax.fori_loop(0, quarter // 128, pick, 0)


def norm_sums(slots, me, at, masked, h):
    slots[me, 0:1, at] = jnp.sum(masked, axis=0, keepdims=True)
    slots[me, 1:2, at] = jnp.sum(masked * h, axis=0, keepdims=True)


def finish_stats(total, valid, stats_out, at_row):
    average = total[0:1] / valid
    width = average.shape[1]
    stats_out[at_row : at_row + 1, 0:width] = average
    stats_out[at_row + 1 : at_row + 2, 0:width] = lax.rsqrt(
        total[1:2] / valid - average * average + EPSILON
    )


def second_part(
    count, before, a2, w1, res, mask, gb, valid, moves, y_out, u_out, h3n, stats_out, s1, send1, recv1
):
    wide = h3n.shape[1]
    quarter = res.shape[2]
    me = lax.axis_index("dp")

    def project(at):
        h = dot_t(a2[...], w1[at, :])
        h3n[:, at] = h
        norm_sums(s1, me, at, mask[:, 0:1] * h, h)

    over(wide, TILE, project)
    finish_stats(exchange(count, s1, send1, recv1), valid, stats_out, 0)
    before()
    for q in range(wide // quarter):

        def body(j, carry, q=q):
            at = pl.ds(pl.multiple_of(q * quarter + j * 128, 128), 128)
            own = pl.ds(pl.multiple_of(j * 128, 128), 128)
            hn = (h3n[:, at] - stats_out[0:1, at]) * stats_out[1:2, at]
            h3n[:, at] = hn
            z = gb[1, 0:1, at] * hn + gb[1, 1:2, at] + res[q, :, own].astype(F32)
            y_out[:, at] = (mask[:, 0:1] * (z * sigmoid(z))).astype(BF16)
            return carry

        lax.fori_loop(0, quarter // 128, body, 0)

    def permute(at):
        u_out[:, at] = dot(moves[...], y_out[:, at]).astype(BF16)

    over(wide, TILE, permute)


def batch_valid(counts, row):
    me = lax.axis_index("segment")
    value = counts[row : row + 1, 0:1]
    for m in range(1, 4):
        value = jnp.where(me == m, counts[row + m : row + m + 1, 0:1], value)
    return value


def head_kernel(
    sections,
    count,
    x3,
    w,
    short,
    k,
    gb,
    vec,
    pack,
    tiles,
    mask,
    moves,
    stats_out,
    count_out,
    g_out,
    y_out,
    u_out,
    h3n,
    stats3,
    a2_out,
    w1_out,
    res_out,
    x_out,
    a1_out,
    h1n_out,
    h2n_out,
    w3_out,
    w2_out,
    k2_out,
    x,
    cols,
    h1n,
    h2n,
    act,
    a2_all,
    a2,
    wsc,
    w1,
    rq,
    res,
    gslots,
    *rest,
):
    sync, rest = rest[:9], list(rest[9:])
    short_send, short_recv, short_relay_send, short_relay_recv = rest[:4]
    w1_send, w1_recv, w1_relay_send, w1_relay_recv = rest[4:8]
    g_send, g_recv, a2_send, a2_recv, res_send, res_recv, own_sem, out_sem = rest[8:16]
    spread_send, spread_recv, far_send, far_recv, near_send, near_recv, keep_sem = rest[16:23]
    pass_send, kv, kv_sem = rest[23:]
    me, place = lax.axis_index("segment"), lax.axis_index("dp")
    core = lax.rem(place, 2)
    sibling = place + 1 - 2 * core
    wide = x.shape[1]
    quarter = wide // sections
    half_rows = wide // 2
    mine = pl.ds(pl.multiple_of(core * half_rows, 16), half_rows)
    greet(count, sections)
    k_load = pltpu.make_async_copy(k, kv, kv_sem)
    k_load.start()

    odd = lax.rem(lax.div(place, 2), 2)
    beside = place + 2 - 4 * odd
    parts = [("w3", w, w3_out, 3, 0, 1), ("w2", w, w2_out, 2, 0, 1)]
    parts += [("k2", k, k2_out, 2, i, 3) for i in range(3)]

    def part_rows(i, at_odd):
        _, src, _, _, piece, pieces = parts[i]
        fine = src.shape[0] // (4 * pieces)
        start = ((2 * at_odd + core) * pieces + piece) * fine
        return pl.ds(pl.multiple_of(start, 16), fine)

    def spread_copy(i, t):
        _, src, dst, _, _, _ = parts[i]
        at = part_rows(i, odd)
        return mesh_copy(src.at[at], dst.at[at], spread_send.at[i, t], spread_recv.at[i], t, place)

    def far_copy(i):
        dst, at = parts[i][2], part_rows(i, odd)
        return mesh_copy(dst.at[at], dst.at[at], far_send.at[i], far_recv.at[i], me, beside)

    def near_copy(i, second):
        dst = parts[i][2]
        at = part_rows(i, 1 - odd if second else odd)
        sems = near_send.at[i, second], near_recv.at[i, second]
        return mesh_copy(dst.at[at], dst.at[at], *sems, me, sibling)

    keeps = [
        (3, pltpu.make_async_copy(w, w3_out, keep_sem.at[0])),
        (2, pltpu.make_async_copy(w, w2_out, keep_sem.at[1])),
        (2, pltpu.make_async_copy(kv, k2_out, keep_sem.at[2])),
    ]

    def spread_start(i):
        owner = parts[i][3]

        @pl.when(me == owner)
        def _():
            for d in (1, 2):
                spread_copy(i, owner ^ d).start()

    def spread_sent(i):
        for d in (1, 2):
            spread_copy(i, parts[i][3] ^ d).wait_send()

    def pass_copy(i):
        dst, at = parts[i][2], part_rows(i, odd)
        return mesh_copy(
            dst.at[at], dst.at[at], pass_send.at[i], spread_recv.at[i], parts[i][3] ^ 3, place
        )

    def spread_on(i):
        owner = parts[i][3]

        @pl.when(me == owner ^ 1)
        def _():
            spread_copy(i, 0).wait_recv()
            pass_copy(i).start()

        @pl.when((me != owner) & (me != owner ^ 1))
        def _():
            spread_copy(i, 0).wait_recv()

        @pl.when(me != owner)
        def _():
            far_copy(i).start()
            near_copy(i, 0).start()

    def far_on(i):
        @pl.when(me != parts[i][3])
        def _():
            far_copy(i).wait_recv()
            near_copy(i, 1).start()

    def short_copy(t):
        src = short.at[mine, pl.ds(t * quarter, quarter)]
        return mesh_copy(src, wsc.at[mine], short_send.at[t], short_recv, t, place)

    def w1_copy(t):
        return mesh_copy(w.at[mine], w1.at[mine], w1_send.at[t], w1_recv, t, place)

    short_own = pltpu.make_async_copy(short.at[:, pl.ds(0, quarter)], wsc, own_sem.at[0])
    w1_own = pltpu.make_async_copy(w, w1, own_sem.at[1])
    short_relay = mesh_copy(
        wsc.at[mine], wsc.at[mine], short_relay_send, short_relay_recv, me, sibling
    )
    w1_relay = mesh_copy(w1.at[mine], w1.at[mine], w1_relay_send, w1_relay_recv, me, sibling)

    def g_copy(k_):
        return mesh_copy(
            gslots.at[me],
            gslots.at[me],
            g_send.at[k_],
            g_recv.at[k_],
            jnp.bitwise_xor(me, k_),
            place,
        )

    gslots[me] = vec[...]
    greeted(count, sections)

    @pl.when(me == 0)
    def _():
        for t in (3, 1, 2):
            short_copy(t).start()
        short_own.start()

    @pl.when(me == 1)
    def _():
        for t in (2, 0, 3):
            w1_copy(t).start()
        w1_own.start()

    for k_ in range(1, sections):
        g_copy(k_).start()
    for i in range(3):
        spread_start(i)
    for owner, copy in keeps[:2]:
        pl.when(me == owner)(copy.start)

    def relayout(j, carry):
        at = pl.ds(pl.multiple_of(j * 128, 128), 128)
        x[:, at] = x3[:, :, at].reshape(x.shape[0], 128)
        return carry

    lax.fori_loop(0, wide // 128, relayout, 0)
    writes = [
        pltpu.make_async_copy(src, dst, out_sem.at[i])
        for i, (src, dst) in enumerate(
            ((x, x_out), (h1n, h1n_out), (cols.at[:, pl.ds(4 * h1n.shape[1], h1n.shape[1])], a1_out), (h2n, h2n_out))
            + ((a2, a2_out), (w1, w1_out), (res, res_out))
        )
    ]
    writes[0].start()

    def a2_copy(t):
        return mesh_copy(a2_all.at[t], a2, a2_send.at[t], a2_recv, t, place)

    @pl.when(me == 0)
    def _():
        def between():
            spread_on(0)
            spread_on(1)

        first_part(
            count,
            (lambda: spread_on(1), k_load.wait, lambda: spread_on(0)),
            writes[1:3],
            x,
            w,
            kv,
            gb,
            pack,
            tiles,
            a2_all,
            cols,
            h1n,
            h2n,
            stats_out,
            count_out,
            act,
            *sync[:6],
        )
        writes[3].start()
        for t in range(1, sections):
            a2_copy(t).start()
        a2[...] = a2_all[0]
        short_own.wait()
        for i in (2, 3, 4):
            spread_on(i)

    @pl.when(me != 0)
    def _():
        k_load.wait()
        pl.when(me == keeps[2][0])(keeps[2][1].start)
        slots, send1, recv1 = sync[:3]
        narrow = h1n.shape[1]
        stats_out[...] = jnp.zeros(stats_out.shape, F32)
        slots[place, :, 0:narrow] = jnp.zeros((8, narrow), F32)
        slots[place, 0:4, narrow:] = jnp.broadcast_to(by_batch(pack[:, 0:1]), (4, 128))
        slots[place, 4:8, narrow:] = jnp.broadcast_to(by_batch(tiles[:, 0:1]), (4, 128))
        count_out[...] = exchange(count, slots, send1, recv1)[:, narrow:]

    def spread_paced(i, after):
        @pl.when(me == parts[i][3])
        def _():
            spread_sent(after)
            for d in (1, 2):
                spread_copy(i, parts[i][3] ^ d).start()

    def unless_zero(i):
        pl.when(me != 0)(lambda: spread_on(i))

    unless_zero(0)
    spread_paced(3, 1)
    unless_zero(1)
    spread_paced(4, 2)
    unless_zero(2)
    unless_zero(3)
    pl.when(me == parts[4][3] ^ 1)(lambda: spread_on(4))

    @pl.when(me != 0)
    def _():
        short_copy(0).wait_recv()
        short_relay.start()

    @pl.when(me == 1)
    def _():
        w1_own.wait()

    @pl.when(me != 1)
    def _():
        w1_copy(0).wait_recv()
        w1_relay.start()

    @pl.when(me != 0)
    def _():
        short_relay.wait_recv()

    residual_part(x, wsc, rq, act)

    def res_copy(k_):
        other = jnp.bitwise_xor(me, k_)
        return mesh_copy(
            rq.at[other], res.at[me], res_send.at[k_], res_recv.at[k_], other, place
        )

    for k_ in range(1, sections):
        res_copy(k_).start()
    res[me] = rq[me]
    pl.when((me != 0) & (me != parts[4][3] ^ 1))(lambda: spread_on(4))

    @pl.when(me != 0)
    def _():
        a2_copy(0).wait_recv()

    @pl.when(me != 1)
    def _():
        w1_relay.wait_recv()

    for k_ in range(1, sections):
        g_copy(k_).wait_recv()
    g_out[...] = gslots[...]

    def before():
        far_on(0)
        far_on(1)
        for k_ in range(1, sections):
            res_copy(k_).wait_recv()

    second_part(
        count,
        before,
        a2,
        w1,
        res,
        mask,
        gslots,
        batch_valid(count_out, 0),
        moves,
        y_out,
        u_out,
        h3n,
        stats3,
        *sync[6:],
    )
    for copy in writes[4:]:
        copy.start()
    for i in range(2, len(parts)):
        far_on(i)
    for k_ in range(1, sections):
        g_copy(k_).wait_send()
        res_copy(k_).wait_send()

    @pl.when(me == 0)
    def _():
        for t in range(1, sections):
            short_copy(t).wait_send()
            a2_copy(t).wait_send()

    @pl.when(me != 0)
    def _():
        short_relay.wait_send()

    @pl.when(me == 1)
    def _():
        for t in (0, 2, 3):
            w1_copy(t).wait_send()

    @pl.when(me != 1)
    def _():
        w1_relay.wait_send()

    for i in range(len(parts)):
        owner = parts[i][3]

        if i not in (1, 2):
            pl.when(me == owner)(functools.partial(spread_sent, i))
        pl.when(me == owner ^ 1)(lambda i=i: pass_copy(i).wait_send())

        @pl.when(me != owner)
        def _(i=i):
            far_copy(i).wait_send()
            near_copy(i, 0).wait()
            near_copy(i, 1).wait()

    for owner, copy in keeps:
        pl.when(me == owner)(copy.wait)
    for i, copy in enumerate(writes):
        if i in (1, 2, 3):
            pl.when(me == 0)(copy.wait)
        else:
            copy.wait()


def back_sums(slots, me, at, grad, hn):
    slots[me, 0:1, at] = jnp.sum(grad, axis=0, keepdims=True)
    slots[me, 1:2, at] = jnp.sum(grad * hn, axis=0, keepdims=True)


def map_sender(sections, src, dst, owner, send_sem, recv_sem, own_sem):
    me, place = lax.axis_index("segment"), lax.axis_index("dp")
    own = pltpu.make_async_copy(src, dst.at[me], own_sem)

    def copy(k):
        return mesh_copy(src, dst.at[me], send_sem, recv_sem.at[k], owner, place)

    def start():
        @pl.when(me == owner)
        def _():
            own.start()

        for k in range(1, sections):

            @pl.when(me == owner ^ k)
            def _(k=k):
                copy(k).start()

    def finish():
        @pl.when(me == owner)
        def _():
            own.wait()
            for k in range(1, sections):
                copy(k).wait_recv()

        @pl.when(me != owner)
        def _():
            copy(0).wait_send()

    return start, finish


def tile_kernel(
    sections,
    count,
    u,
    w2,
    k2_far,
    w3_far,
    og_far,
    pack,
    gains,
    counts,
    back,
    y1,
    y_out,
    dy,
    sums_out,
    map_one,
    p3_out,
    p2_out,
    k2_out,
    a2,
    cols,
    dh3,
    dh2,
    dh1,
    stage,
    stage_sem,
    k2,
    w3,
    og3,
    load_sem,
    h1n,
    h2n,
    h3n,
    act,
    dz,
    stats,
    og,
    map_send,
    map_recv,
    map_own,
    *sync,
):
    s1, send1, recv1, s2, send2, recv2, s3, send3, recv3 = sync[:9]
    b3, bsend3, brecv3, b2, bsend2, brecv2, b1, bsend1, brecv1 = sync[9:]
    rows, wide = u.shape
    narrow = h1n.shape[1]
    me = lax.axis_index("dp")
    section = lax.axis_index("segment")
    valid = batch_valid(counts, 4)
    gb3 = gains.at[3]
    loads = [
        pltpu.make_async_copy(src, dst, load_sem.at[i])
        for i, (src, dst) in enumerate(((og_far, og3), (k2_far, k2), (w3_far, w3)))
    ]
    for load in loads:
        load.start()

    def gb2(row, at):
        return gains[2, row % 2 : row % 2 + 1, pl.ds(at.start + row // 2 * narrow, at.size)]

    greet(count, sections)

    def project(at):
        h = dot(u[...], w2[:, at])
        h1n[:, at] = h
        norm_sums(s1, me, at, pack[:, 0:1] * h, h)

    over(narrow, TILE, project)
    greeted(count, sections)
    send_map, wait_map = map_sender(sections, y1, map_one, 1, map_send, map_recv, map_own)
    send_map()
    loads[0].wait()
    real = og3.shape[0]
    for m in range(sections):

        @pl.when(section == m)
        def _(m=m):
            def one(j, carry):
                at = pl.ds(pl.multiple_of(j * 128, 128), 128)
                og[0:real, at] = og3[:, m, at].astype(F32)
                return carry

            lax.fori_loop(0, wide // 128, one, 0)

    og[real:, :] = jnp.zeros((rows - real, wide), F32)
    finish_stats(exchange(count, s1, send1, recv1), valid, stats, 0)

    def activate(row, gain, source, store):
        def body(at):
            hn = (source[:, at] - stats[row : row + 1, at]) * stats[row + 1 : row + 2, at]
            source[:, at] = hn
            n = gb2(gain, at) * hn + gb2(gain + 1, at)
            store(at, pack[:, 0:1] * (n * sigmoid(n)))

        return body

    def to_act(at, value):
        act[:, at] = value

    def to_a2(at, value):
        a2[:, at] = value.astype(BF16)

    over(narrow, 128, activate(0, 0, h1n, to_act))
    for t, (vertical, lateral) in enumerate(OFFSETS):
        shift = 7 * vertical + lateral

        def place(j, carry, t=t, shift=shift):
            at = pl.ds(pl.multiple_of(j * 128, 128), 128)
            to = pl.ds(pl.multiple_of(t * narrow + j * 128, 128), 128)
            moved = unrolled_shift(act[:, at], shift)
            cols[:, to] = (pack[:, 1 + t : 2 + t] * moved).astype(BF16)
            return carry

        lax.fori_loop(0, narrow // 128, place, 0)

    def convolve(at):
        h = dot(cols[...], k2[:, at])
        h2n[:, at] = h
        norm_sums(s2, me, at, pack[:, 0:1] * h, h)

    loads[1].wait()
    over(narrow, TILE, convolve)
    finish_stats(exchange(count, s2, send2, recv2), valid, stats, 2)
    over(narrow, 128, activate(2, 2, h2n, to_a2))

    def expand(at):
        h = dot_t(a2[...], w3[at, :])
        h3n[:, at] = h
        norm_sums(s3, me, at, pack[:, 0:1] * h, h)

    loads[2].wait()
    over(wide, TILE, expand)
    finish_stats(exchange(count, s3, send3, recv3), valid, stats, 4)

    def result(at):
        hn = (h3n[:, at] - stats[4:5, at]) * stats[5:6, at]
        h3n[:, at] = hn
        z = gb3[0:1, at] * hn + gb3[1:2, at] + u[:, at].astype(F32)
        s = sigmoid(z)
        m = pack[:, 0:1]
        y_out[:, at] = (m * (z * s)).astype(BF16)
        grad = (og[:, at] * m * (s * (1.0 + z * (1.0 - s)))).astype(BF16)
        dz[:, at] = grad
        grad = grad.astype(F32)
        back_sums(b3, me, at, grad, hn)

    over(wide, 128, result)
    total = exchange(count, b3, bsend3, brecv3)
    sums_out[0:2, :] = total

    def through(at):
        offset, scale = sums_out[0:1, at], sums_out[1:2, at]
        dh3[:, at] = (
            pack[:, 0:1]
            * gb3[0:1, at]
            * stats[5:6, at]
            * (dz[:, at].astype(F32) - (offset + h3n[:, at] * scale) / valid)
        ).astype(BF16)

    over(wide, 128, through)

    def into_two(at):
        grad = dot(dh3[...], w3[:, at]).astype(BF16).astype(F32)
        hn = h2n[:, at]
        n = gb2(2, at) * hn + gb2(3, at)
        grad = grad * pack[:, 0:1] * slope(n)
        act[:, at] = grad
        back_sums(b2, me, at, grad, hn)

    over(narrow, TILE, into_two)
    total = exchange(count, b2, bsend2, brecv2)
    sums_out[2:4, 0:narrow] = total

    def through_two(at):
        offset, scale = sums_out[2:3, at], sums_out[3:4, at]
        grad = (
            pack[:, 0:1]
            * gb2(2, at)
            * stats[3:4, at]
            * (act[:, at] - (offset + h2n[:, at] * scale) / valid)
        )
        dh2[:, at] = grad.astype(BF16)
        act[:, at] = dh2[:, at].astype(F32)

    over(narrow, 128, through_two)
    h2n[...] = jnp.zeros((rows, narrow), F32)
    for t, (vertical, lateral) in enumerate(OFFSETS):
        shift = -(7 * vertical + lateral)
        other = 8 - t

        def place_back(j, carry, t=t, shift=shift, other=other):
            at = pl.ds(pl.multiple_of(j * 128, 128), 128)
            moved = unrolled_shift(act[:, at], shift)
            dy[:, at] = (pack[:, 1 + other : 2 + other] * moved).astype(BF16)
            return carry

        lax.fori_loop(0, narrow // 128, place_back, 0)

        def gather(at, t=t):
            row = pl.ds(pl.multiple_of(t * narrow + at.start, TILE), TILE)
            h2n[:, at] += dot_t(dy[:, 0:narrow], k2[row, :])

        over(narrow, TILE, gather)

    def into_one(at):
        hn = h1n[:, at]
        n = gb2(0, at) * hn + gb2(1, at)
        grad = h2n[:, at] * pack[:, 0:1] * slope(n)
        act[:, at] = grad
        back_sums(b1, me, at, grad, hn)

    over(narrow, 128, into_one)
    total = exchange(count, b1, bsend1, brecv1)
    sums_out[4:6, 0:narrow] = total

    def through_one(at):
        offset, scale = sums_out[4:5, at], sums_out[5:6, at]
        dh1[:, at] = (
            pack[:, 0:1]
            * gb2(0, at)
            * stats[1:2, at]
            * (act[:, at] - (offset + h1n[:, at] * scale) / valid)
        ).astype(BF16)

    over(narrow, 128, through_one)

    def into_input(at):
        grad = dot_t(dh1[...], w2[at, :]) + dz[:, at].astype(F32)
        dy[:, at] = dot(back[...], grad.astype(BF16)).astype(BF16)

    over(wide, TILE, into_input)
    writer = Writer(stage, stage_sem)
    writer.rows_of_dot(dh3, a2, p3_out)
    writer.rows_of_dot(cols, dh2, k2_out)
    writer.rows_of_dot(u, dh1, p2_out)
    writer.drain()
    wait_map()


def image_back_part(
    count, after, dy, res, h3n, mask, gb, stats, valid, w1, dz, dh3, da2, sums_out, b3, send3, recv3
):
    wide = dy.shape[1]
    quarter = res.shape[2]
    narrow = da2.shape[1]
    me = lax.axis_index("dp")
    for q in range(wide // quarter):

        def body(j, carry, q=q):
            at = pl.ds(pl.multiple_of(q * quarter + j * 128, 128), 128)
            own = pl.ds(pl.multiple_of(j * 128, 128), 128)
            hn = h3n[:, at]
            z = gb[0:1, at] * hn + gb[1:2, at] + res[q, :, own].astype(F32)
            grad = (dy[:, at].astype(F32) * mask[:, 0:1] * slope(z)).astype(BF16)
            dz[:, at] = grad
            back_sums(b3, me, at, grad.astype(F32), hn)
            return carry

        lax.fori_loop(0, quarter // 128, body, 0)
    after()
    total = exchange(count, b3, send3, recv3)
    sums_out[...] = total

    def through(at):
        offset, scale = sums_out[0:1, at], sums_out[1:2, at]
        dh3[:, at] = (
            mask[:, 0:1]
            * gb[0:1, at]
            * stats[1:2, at]
            * (dz[:, at].astype(F32) - (offset + h3n[:, at] * scale) / valid)
        ).astype(BF16)

    over(wide, 128, through)

    def into(at):
        da2[:, at] = dot(dh3[...], w1[:, at]).astype(BF16)

    over(narrow, TILE, into)


def last_part(
    count, between, taps_term, da2, k, gb, pack, h1n, h2n, stats, counts, dh2, dh1, sums_out, act, acc, hold, *sync
):
    b2, send2, recv2, b1, send1, recv1 = sync
    rows, narrow = h1n.shape
    full = act.shape[1]
    me = lax.axis_index("dp")
    valid = counts[0:4, 0:1]

    def tile8(v):
        return v.reshape(rows // 8, 8, v.shape[1])

    for m in range(4):

        def put(j, carry, m=m):
            at = pl.ds(pl.multiple_of(j * 128, 128), 128)
            act[j, pl.ds(m, full // 4, stride=4), :] = da2[m, :, at].astype(F32)
            return carry

        lax.fori_loop(0, narrow // 128, put, 0)

    def into(gain, source, hidden, slots):
        def body(at):
            hn = hidden[:, at]
            n = gb[gain : gain + 1, at] * hn + gb[gain + 1 : gain + 2, at]
            grad = source(at) * pack[:, 0:1] * slope(n)
            act[lane(at), 0:rows, :] = grad
            slots[me, 0:4, at] = by_batch(grad)
            slots[me, 4:8, at] = by_batch(grad * hn)

        return body

    def through(gain, stat_at, row, hidden, out):
        def body(at):
            offset = spread8(sums_out[row : row + 4, at] / valid)
            scale = spread8(sums_out[row + 4 : row + 8, at] / valid)
            inv = spread8(stats[stat_at : stat_at + 4, at])
            g = tile8(act[lane(at), 0:rows, :])
            value = inv * gb[gain : gain + 1, at][None] * (g - (offset + tile8(hidden[:, at]) * scale))
            value = (pack[:, 0:1] * value.reshape(rows, value.shape[2])).astype(BF16)
            out[:, at] = value
            act[lane(at), 0:rows, :] = value.astype(F32)

        return body

    over(narrow, 128, into(2, lambda at: act[lane(at), 0:rows, :], h2n, b2))
    sums_out[0:8, :] = exchange(count, b2, send2, recv2)
    between()
    over(narrow, 128, through(2, 12, 0, h2n, dh2))
    acc[...] = jnp.zeros((rows, narrow), F32)
    for t, (vertical, lateral) in enumerate(OFFSETS):
        shift = -4 * (7 * vertical + lateral)
        other = 8 - t

        def place_back(j, carry, t=t, shift=shift, other=other):
            at = pl.ds(pl.multiple_of(j * 128, 128), 128)
            moved = unrolled_shift(act[j, 0:rows, :], shift)
            hold[:, at] = (pack[:, 1 + other : 2 + other] * moved).astype(BF16)
            return carry

        lax.fori_loop(0, narrow // 128, place_back, 0)

        def gather(at, t=t):
            row = pl.ds(pl.multiple_of(t * narrow + at.start, TILE), TILE)
            acc[:, at] += dot_t(hold[...], k[row, :])

        over(narrow, TILE, gather)
        taps_term(t)
    over(narrow, 128, into(0, lambda at: acc[:, at], h1n, b1))
    sums_out[8:16, :] = exchange(count, b1, send1, recv1)
    over(narrow, 128, through(0, 4, 8, h1n, dh1))


def back_kernel(
    sections,
    count,
    dy,
    res,
    h3n,
    mask,
    gains,
    stats3,
    w1,
    k_far,
    gb,
    pack,
    h1n_far,
    h2n_far,
    stats,
    counts,
    k2,
    y2,
    a2,
    a1_in,
    x_in,
    dh1,
    sums3,
    sums12,
    k2_out,
    dz_all,
    map_two,
    map_three,
    p1_out,
    k0_out,
    p0_out,
    sh_out,
    piece_out,
    dz,
    dh3,
    dh2,
    dzq_out,
    a1,
    x,
    k,
    h1n,
    h2n,
    stage,
    stage_sem,
    x_sem,
    da2,
    da2_all,
    dzq,
    act,
    acc,
    hold,
    *rest,
):
    sync, rest = rest[:9], list(rest[9:])
    half, theirs, pieces, whole = rest[:4]
    load_sem, swap_send, swap_recv, piece_send, piece_recv, out_sem = rest[4:10]
    sh_half, sh_other, sh_theirs, sh_pieces, sh_sum = rest[10:15]
    sh_swap_send, sh_swap_recv, sh_send, sh_recv, sh_sem = rest[15:20]
    rest = rest[20:]
    a_send, a_recv, q_send, q_recv = rest[:4]
    maps = [rest[4:7], rest[7:10], rest[10:13]]
    me, place = lax.axis_index("segment"), lax.axis_index("dp")
    quarter, narrow = dzq.shape[2], da2.shape[1]
    greet(count, sections)
    send_dz, wait_dz = map_sender(sections, dz, dz_all, 0, *maps[0])
    send_two, wait_two = map_sender(sections, dy, map_two, 2, *maps[1])
    send_three, wait_three = map_sender(sections, y2, map_three, 3, *maps[2])

    def q_copy(k_):
        other = jnp.bitwise_xor(me, k_)
        at = pl.ds(pl.multiple_of(other * quarter, 128), quarter)
        return mesh_copy(dz.at[:, at], dzq.at[me], q_send.at[k_], q_recv.at[k_], other, place)

    greeted(count, sections)
    core, z = lax.rem(place, 2), lax.div(place, 2)
    depth = count // 2
    x_loads = [
        pltpu.make_async_copy(src, dst, x_sem.at[i])
        for i, (src, dst) in enumerate(
            ((h2n_far, h2n), (k_far, k), (h1n_far, h1n), (a1_in, a1), (x_in, x))
        )
    ]
    for copy in x_loads:
        copy.start()
    load = pltpu.make_async_copy(k2.at[core], half, load_sem)
    swap = mesh_copy(k2.at[1 - core], theirs, swap_send, swap_recv, me, place + 1 - 2 * core)
    swap.start()
    load.start()

    def to_chip(k_):
        to = lax.rem(z + k_, depth)
        return mesh_copy(
            half.at[:, to],
            pieces.at[k_],
            piece_send.at[k_],
            piece_recv.at[k_],
            me,
            2 * to + core,
        )

    def add_cores():
        load.wait()
        swap.wait_recv()

        def add(n):
            q, y = lax.div(n, depth), lax.rem(n, depth)
            half[q, y] = (half[q, y].astype(F32) + theirs[q, y].astype(F32)).astype(BF16)

        loop(0, sections * depth, add)

    send_three()

    def after():
        return

    image_back_part(
        count,
        after,
        dy,
        res,
        h3n,
        mask,
        gains.at[1],
        stats3,
        batch_valid(counts, 0),
        w1,
        dz,
        dh3,
        da2,
        sums3,
        *sync[:3],
    )

    def a_copy(k_):
        return mesh_copy(da2, da2_all.at[me], a_send, a_recv.at[k_], 0, place)

    for k_ in range(1, sections):

        @pl.when(me == k_)
        def _(k_=k_):
            a_copy(k_).start()

    for k_ in range(1, sections):
        q_copy(k_).start()
    send_dz()
    send_two()
    add_cores()

    def to_chips():
        loop(1, depth, lambda k_: to_chip(k_).start())

    pl.when(me != 0)(to_chips)

    @pl.when(me == 0)
    def _():
        for k_ in range(1, sections):
            a_copy(k_).wait_recv()
        da2_all[0] = da2[...]
        for copy in x_loads:
            copy.wait()
        writer = Writer(stage, stage_sem)

        def taps_term(t):
            tall = narrow
            writer.put(dot_0(a1[...], hold[...]), k0_out.at[pl.ds(t * tall, tall)])

        last_part(
            count,
            to_chips,
            taps_term,
            da2_all,
            k,
            gb,
            pack,
            h1n,
            h2n,
            stats,
            counts,
            dh2,
            dh1,
            sums12,
            act,
            acc,
            hold,
            *sync[3:],
        )
        writer.rows_of_dot(x, dh1, p0_out)
        writer.drain()

    @pl.when(me != 0)
    def _():
        for copy in x_loads:
            copy.wait()
        a_copy(0).wait_send()
        sums12[...] = jnp.zeros(sums12.shape, F32)

    for k_ in range(1, sections):
        q_copy(k_).wait_recv()
    dzq[me] = dz[:, pl.ds(pl.multiple_of(me * quarter, 128), quarter)]
    rows, full = dzq_out.shape[0], act.shape[1]
    for m in range(4):

        def put(j, carry, m=m):
            at = pl.ds(pl.multiple_of(j * 128, 128), 128)
            act[j, pl.ds(m, full // 4, stride=4), :] = dzq[m, :, at].astype(F32)
            return carry

        lax.fori_loop(0, quarter // 128, put, 0)

    def weave(j, carry):
        at = pl.ds(pl.multiple_of(j * 128, 128), 128)
        dzq_out[:, at] = act[j, 0:rows, :].astype(BF16)
        return carry

    lax.fori_loop(0, quarter // 128, weave, 0)
    tall = stage.shape[1]
    sh_rows = sh_half.shape[0]
    fine = sh_rows // depth
    sh_swap = mesh_copy(
        sh_other, sh_theirs, sh_swap_send, sh_swap_recv, me, place + 1 - 2 * core
    )

    def sh_to_chip(k_):
        to = lax.rem(z + k_, depth)
        return mesh_copy(
            sh_half.at[pl.ds(pl.multiple_of(to * fine, 16), fine)],
            sh_pieces.at[k_],
            sh_send.at[k_],
            sh_recv.at[k_],
            me,
            2 * to + core,
        )

    @pl.when(me != 0)
    def _():
        for half_of, target in ((1 - core, sh_other), (core, sh_half)):
            for j in range(sh_rows // tall):
                at = pl.ds(pl.multiple_of(half_of * sh_rows + j * tall, 128), tall)
                target[j * tall : j * tall + tall, :] = dot_0(x[:, at], dzq_out[...]).astype(BF16)
            if target is sh_other:
                sh_swap.start()
        sh_swap.wait_recv()

        def add(n):
            at = pl.ds(pl.multiple_of(n * 32, 32), 32)
            sh_half[at, :] = (sh_half[at, :].astype(F32) + sh_theirs[at, :].astype(F32)).astype(BF16)

        loop(0, sh_rows // 32, add)
        loop(1, depth, lambda k_: sh_to_chip(k_).start())

    writer = Writer(stage, stage_sem)
    writer.rows_of_dot(dh3, a2, p1_out)
    writer.drain()
    loop(1, depth, lambda k_: to_chip(k_).wait_recv())

    def k2_sum(q):
        total = half[q, z].astype(F32)
        for k_ in range(1, depth):
            total = total + pieces[k_, q].astype(F32)
        whole[q] = total.astype(BF16)

    loop(0, sections, k2_sum)
    out = pltpu.make_async_copy(whole, k2_out, out_sem)
    out.start()

    @pl.when(me == 0)
    def _():
        writer = Writer(stage, stage_sem)
        writer.rows_of_dot(x, dzq_out, sh_out)
        writer.drain()

    @pl.when(me != 0)
    def _():
        loop(1, depth, lambda k_: sh_to_chip(k_).wait_recv())
        acc = sh_half[pl.ds(pl.multiple_of(z * fine, 16), fine), :].astype(F32)
        for k_ in range(1, depth):
            acc = acc + sh_pieces[k_].astype(F32)
        sh_sum[...] = acc.astype(BF16)
        written = pltpu.make_async_copy(sh_sum, piece_out, sh_sem)
        written.start()
        sh_swap.wait_send()
        loop(1, depth, lambda k_: sh_to_chip(k_).wait_send())
        written.wait()

    for k_ in range(1, sections):
        q_copy(k_).wait_send()
    loop(1, depth, lambda k_: to_chip(k_).wait_send())
    swap.wait_send()
    out.wait()
    wait_dz()
    wait_two()
    wait_three()


SUMS = (
    ("k0", 0, "owner"),
    ("p0", 0, "owner"),
    ("p1", 1, "each"),
    ("p2", 2, "each"),
    ("p3", 3, "each"),
    ("k2", 2, "chips"),
)


def gradient_kernel(
    sections,
    count,
    sh,
    sh_piece,
    k0,
    p0,
    p1,
    p2,
    p3,
    k2,
    vec,
    dh1,
    w,
    short,
    map_zero,
    map_one,
    map_two,
    map_three,
    sh_out,
    p_out,
    k_out,
    vec_out,
    maps,
    *scratch,
):
    names = [name for name, _, _ in SUMS]
    terms = dict(zip(names, (k0, p0, p1, p2, p3, k2)))
    owner = {name: section for name, section, _ in SUMS}
    held = {name: kind for name, _, kind in SUMS}
    fresh = [name for name in names if held[name] in ("owner", "each")]
    depth = count // 2
    me, place = lax.axis_index("segment"), lax.axis_index("dp")
    core, z = lax.rem(place, 2), lax.div(place, 2)
    sibling = place + 1 - 2 * core
    scratch = list(scratch)
    take = lambda: scratch.pop(0)
    half, theirs, planes, total, others, whole = {}, {}, {}, {}, {}, {}
    for name in names:
        if name in fresh:
            half[name], theirs[name] = take(), take()
        if held[name] in ("each", "chips"):
            planes[name] = take()
        if name in fresh:
            total[name], others[name] = take(), take()
        whole[name] = terms[name] if held[name] == "done" else take()
    relay = {name: take() for name in names if owner[name] == 0}
    relay["sh"] = take()
    sh_half, sh_theirs, sh_others, sh_whole, vec_slots = take(), take(), take(), take(), take()
    load_sem, a_send, a_recv, b_send, b_recv, c_send, c_recv, d_send, d_recv = (take() for _ in range(9))
    e_send, e_recv, e_own, f_send, f_recv, v_send, v_recv = (take() for _ in range(7))
    r_send, r_recv = take(), take()
    pages, s_rows, w_rows, hold, stage, page_sem, s_sem, w_sem, stage_sem = (take() for _ in range(9))
    slot = {name: i for i, name in enumerate(names)}
    last = len(names)

    page_loads = [
        pltpu.make_async_copy(source, pages, page_sem)
        for source in (map_zero, map_one, map_two, map_three)
    ]
    for i, copy in enumerate(page_loads):
        pl.when(me == i)(copy.start)
    wide = pages.shape[2]
    full_rows, map_rows = hold.shape[1], maps.shape[0] * maps.shape[1]

    def tile_loads(j):
        at = pl.ds(pl.multiple_of(j * TILE, TILE), TILE)
        at_slot = lax.rem(j, 2)
        return (
            pltpu.make_async_copy(short.at[at], s_rows.at[at_slot], s_sem.at[at_slot]),
            pltpu.make_async_copy(w.at[at], w_rows.at[at_slot], w_sem.at[at_slot]),
        )

    def tile_store(j):
        at = pl.ds(pl.multiple_of(j * TILE, TILE), TILE)
        at_slot = lax.rem(j, 2)
        return pltpu.make_async_copy(stage.at[at_slot], maps.at[:, :, at], stage_sem.at[at_slot])

    @pl.when(me == 0)
    def _():
        for copy in tile_loads(0):
            copy.start()

    def map_tile(j):
        at = pl.ds(pl.multiple_of(j * TILE, TILE), TILE)
        at_slot = lax.rem(j, 2)

        def weave(m, value):
            for part in range(TILE // 128):
                hold[part, pl.ds(m, full_rows // 4, stride=4), :] = value[
                    :, part * 128 : part * 128 + 128
                ]

        @pl.when(j >= 2)
        def _():
            tile_store(j - 2).wait()

        @pl.when(me == 0)
        def _():
            @pl.when(j + 1 < wide // TILE)
            def _():
                for copy in tile_loads(j + 1):
                    copy.start()

            for copy in tile_loads(j):
                copy.wait()
            for m in range(4):
                weave(m, dot_t(pages[m], s_rows[at_slot]))
            extra = dot_t(dh1[...], w_rows[at_slot])
            for part in range(TILE // 128):
                cols = slice(part * 128, part * 128 + 128)
                value = (hold[part, 0:map_rows, :] + extra[:, cols]).astype(BF16)
                stage[at_slot, :, :, cols] = value.reshape(map_rows // 4, 4, 128)

        @pl.when(me != 0)
        def _():
            for m in range(4):
                weave(m, pages[m, :, at].astype(F32))
            for part in range(TILE // 128):
                cols = slice(part * 128, part * 128 + 128)
                value = hold[part, 0:map_rows, :].astype(BF16)
                stage[at_slot, :, :, cols] = value.reshape(map_rows // 4, 4, 128)

        tile_store(j).start()

    def chip(k):
        return 2 * lax.rem(z + k, depth) + core

    barrier = pltpu.get_barrier_semaphore()
    pl.semaphore_signal(barrier, inc=1, device_id=(me, sibling), device_id_type=MESH)
    for k in range(1, sections):
        pl.semaphore_signal(
            barrier, inc=1, device_id=(jnp.bitwise_xor(me, k), place), device_id_type=MESH
        )
    loop(
        1,
        depth,
        lambda k: pl.semaphore_signal(
            barrier, inc=1, device_id=(me, chip(k)), device_id_type=MESH
        ),
    )
    pl.semaphore_wait(barrier, 1 + sections - 1 + depth - 1)

    def swap(name):
        return mesh_copy(
            terms[name].at[1 - core],
            theirs[name],
            a_send.at[slot[name]],
            a_recv.at[slot[name]],
            me,
            sibling,
        )

    def load(name):
        return pltpu.make_async_copy(terms[name].at[core], half[name], load_sem.at[slot[name]])

    def when_held(name, body):
        if held[name] == "each":
            body()
        else:
            pl.when(me == owner[name])(body)

    sh_rows = sh_half.shape[0]
    sh_swap = mesh_copy(
        sh.at[1 - core], sh_theirs, a_send.at[last], a_recv.at[last], me, sibling
    )
    sh_load = pltpu.make_async_copy(sh.at[core], sh_half, load_sem.at[last])
    piece = sh_rows // depth

    def sh_at(i):
        return pl.ds(pl.multiple_of(i * piece, 16), piece)

    mine = sh_at(z)
    piece_load = pltpu.make_async_copy(sh_piece, sh_whole.at[mine], load_sem.at[last])

    def sh_share(k):
        return mesh_copy(
            sh_whole.at[mine],
            sh_whole.at[mine],
            d_send.at[last, k],
            d_recv.at[last, k],
            me,
            chip(k),
        )

    @pl.when(me == 0)
    def _():
        sh_swap.start()
        sh_load.start()

    @pl.when(me != 0)
    def _():
        piece_load.start()
        piece_load.wait()
        loop(1, depth, lambda k: sh_share(k).start())


    def vec_copy(k):
        other = jnp.bitwise_xor(me, k)
        return mesh_copy(
            vec.at[other], vec_slots.at[k], v_send.at[k], v_recv.at[k], other, place
        )

    for k in range(1, sections):
        vec_copy(k).start()
    for name in fresh:

        def begin(name=name):
            swap(name).start()
            load(name).start()

        when_held(name, begin)

    def final(name):
        return k_out if name[0] == "k" else p_out

    def deliver(name, k):
        return mesh_copy(
            whole[name],
            final(name).at[core, me],
            e_send.at[slot[name]],
            e_recv.at[slot[name], k],
            owner[name],
            place,
        )

    def keep_own(name):
        return pltpu.make_async_copy(whole[name], final(name).at[core, me], e_own.at[slot[name]])

    def to_plane(name, k):
        other = jnp.bitwise_xor(me, k)
        return mesh_copy(
            terms[name].at[other],
            planes[name].at[k],
            b_send.at[slot[name], k],
            b_recv.at[slot[name], k],
            other,
            place,
        )

    def load_plane(name):
        return pltpu.make_async_copy(terms[name].at[me], planes[name].at[0], load_sem.at[slot[name]])

    for name in names:
        if held[name] == "chips":
            for k in range(1, sections):
                to_plane(name, k).start()
            load_plane(name).start()
        if held[name] == "done":

            @pl.when(me == owner[name])
            def _(name=name):
                keep_own(name).start()

            for k in range(1, sections):

                @pl.when(me == owner[name] ^ k)
                def _(name=name, k=k):
                    deliver(name, k).start()

    step = 32

    def sh_send(k):
        to = lax.rem(z + k, depth)
        return mesh_copy(
            sh_half.at[sh_at(to)],
            sh_others.at[k],
            c_send.at[last, k],
            c_recv.at[last, k],
            me,
            2 * to + core,
        )

    @pl.when(me == 0)
    def _():
        sh_load.wait()
        sh_swap.wait_recv()

        def sh_add(i):
            at = pl.ds(pl.multiple_of(i * step, step), step)
            sh_half[at, :] = (sh_half[at, :].astype(F32) + sh_theirs[at, :].astype(F32)).astype(BF16)

        loop(0, sh_rows // step, sh_add)
        loop(1, depth, lambda k: sh_send(k).start())

    def to_section(name, k):
        other = jnp.bitwise_xor(me, k)
        target = planes[name].at[k] if held[name] == "each" else total[name]
        return mesh_copy(
            half[name].at[other],
            target,
            b_send.at[slot[name], k],
            b_recv.at[slot[name], k],
            other,
            place,
        )

    def scattered(name, onward):
        if onward:
            return mesh_copy(
                relay[name], total[name], r_send.at[slot[name]], b_recv.at[slot[name], 3], 3, place
            )
        return mesh_copy(
            half[name].at[3], relay[name], b_send.at[slot[name], 3], r_recv.at[slot[name]], 2, place
        )

    for name in fresh:

        def combine(name=name):
            load(name).wait()
            swap(name).wait_recv()

            def add(i):
                q, y = lax.div(i, depth), lax.rem(i, depth)
                half[name][q, y] = (
                    half[name][q, y].astype(F32) + theirs[name][q, y].astype(F32)
                ).astype(BF16)

            loop(0, sections * depth, add)
            for k in range(1, sections):
                if held[name] == "owner" and k == 3:
                    pl.when(core == 0)(to_section(name, k).start)
                    pl.when(core == 1)(scattered(name, False).start)
                else:
                    to_section(name, k).start()

        when_held(name, combine)

    def share(name, k):
        return mesh_copy(
            whole[name].at[z],
            whole[name].at[z],
            d_send.at[slot[name], k],
            d_recv.at[slot[name], k],
            me,
            chip(k),
        )

    def planes_end(name):
        load_plane(name).wait()
        acc = planes[name][0].astype(F32)
        for k in range(1, sections):
            to_plane(name, k).wait_recv()
            acc = acc + planes[name][k].astype(F32)
        whole[name][z] = acc.astype(BF16)
        loop(1, depth, lambda k: share(name, k).start())

    planes_end("k2")
    for i, copy in enumerate(page_loads):
        pl.when(me == i)(copy.wait)
    loop(0, 2, map_tile)

    @pl.when((me == 2) & (core == 1))
    def _():
        for name in ("k0", "p0"):
            scattered(name, False).wait_recv()
            scattered(name, True).start()


    @pl.when(me == 0)
    def _():
        loop(1, depth, lambda k: sh_send(k).wait_recv())
        acc = sh_half[mine, :].astype(F32)
        for k in range(1, depth):
            acc = acc + sh_others[k].astype(F32)
        sh_whole[mine, :] = acc.astype(BF16)
        loop(1, depth, lambda k: sh_share(k).start())

    loop(2, wide // TILE, map_tile)

    def to_chip(name, k):
        to = lax.rem(z + k, depth)
        return mesh_copy(
            total[name].at[to],
            others[name].at[k],
            c_send.at[slot[name], k],
            c_recv.at[slot[name], k],
            me,
            2 * to + core,
        )

    def b_end(name):
        if held[name] == "each":
            for k in range(1, sections):
                to_section(name, k).wait_recv()

            def plane_add(y, name=name):
                acc = half[name][me, y].astype(F32)
                for k in range(1, sections):
                    acc = acc + planes[name][k, y].astype(F32)
                total[name][y] = acc.astype(BF16)

            loop(0, depth, plane_add)
        else:

            @pl.when(me == owner[name])
            def _(name=name):
                def keep(y):
                    total[name][y] = half[name][owner[name], y]

                loop(0, depth, keep)

            for k in range(1, sections):

                @pl.when(me == owner[name] ^ k)
                def _(name=name, k=k):
                    to_section(name, k).wait_recv()

        loop(1, depth, lambda k, name=name: to_chip(name, k).start())

    for name in ("k0", "p0"):
        b_end(name)

    def sh_deliver(k):
        at = pl.ds(pl.multiple_of(me * sh_whole.shape[1], 128), sh_whole.shape[1])
        return mesh_copy(
            sh_whole,
            sh_out.at[core, :, at],
            e_send.at[last],
            e_recv.at[last, k],
            0,
            place,
        )

    loop(1, depth, lambda k: sh_share(k).wait_recv())
    at_zero = pl.ds(0, sh_whole.shape[1])
    sh_keep = pltpu.make_async_copy(sh_whole, sh_out.at[core, :, at_zero], e_own.at[last])

    @pl.when(me == 0)
    def _():
        sh_keep.start()

    def relayed(name, onward):
        index = last if name == "sh" else slot[name]
        at = pl.ds(3 * sh_whole.shape[1], sh_whole.shape[1])
        src, dst = (sh_whole, sh_out.at[core, :, at]) if name == "sh" else (whole[name], final(name).at[core, 3])
        if onward:
            return mesh_copy(relay[name], dst, r_send.at[index], e_recv.at[index, 3], 0, place)
        return mesh_copy(src, relay[name], e_send.at[index], r_recv.at[index], 1, place)

    def start_delivery(name):
        index = last if name == "sh" else slot[name]
        section = 0 if name == "sh" else owner[name]
        copy = sh_deliver if name == "sh" else functools.partial(deliver, name)
        for k in range(1, sections):
            direct = me == section ^ k
            if section == 0 and k == 3:
                direct = direct & (core == 0)

                @pl.when((me == 3) & (core == 1))
                def _():
                    relayed(name, False).start()

            @pl.when(direct)
            def _(k=k):
                copy(k).start()

    def pass_on(name):
        @pl.when((me == 1) & (core == 1))
        def _():
            relayed(name, False).wait_recv()
            relayed(name, True).start()

    start_delivery("sh")

    def c_end(name):
        loop(1, depth, lambda k: to_chip(name, k).wait_recv())
        acc = total[name][z].astype(F32)
        for k in range(1, depth):
            acc = acc + others[name][k].astype(F32)
        whole[name][z] = acc.astype(BF16)
        loop(1, depth, lambda k: share(name, k).start())

    def d_end(name):
        loop(1, depth, lambda k: share(name, k).wait_recv())

        @pl.when(me == owner[name])
        def _():
            keep_own(name).start()

        start_delivery(name)

    later = ("p1", "p2", "p3")
    for name in ("k0", "p0"):
        c_end(name)
    for name in later:
        b_end(name)
    pass_on("sh")
    for name in ("k0", "p0", "k2"):
        d_end(name)
    for name in later:
        c_end(name)
    for name in ("k0", "p0"):
        pass_on(name)
    for name in later:
        d_end(name)

    def cross(name):
        return mesh_copy(
            final(name).at[core],
            final(name).at[core],
            f_send.at[slot[name]],
            f_recv.at[slot[name]],
            me,
            sibling,
        )

    sh_cross = mesh_copy(
        sh_out.at[core], sh_out.at[core], f_send.at[last], f_recv.at[last], me, sibling
    )

    @pl.when(me == 0)
    def _():
        sh_keep.wait()
        for k in range(1, sections):
            sh_deliver(k).wait_recv()
        sh_cross.start()

    for name in names:

        @pl.when(me == owner[name])
        def _(name=name):
            keep_own(name).wait()
            for k in range(1, sections):
                deliver(name, k).wait_recv()
            cross(name).start()

    for k in range(1, sections):
        vec_copy(k).wait_recv()
    sums = vec[me]
    for k in range(1, sections):
        sums = sums + vec_slots[k]
    vec_out[...] = sums

    tile_store(wide // TILE - 2).wait()
    tile_store(wide // TILE - 1).wait()
    for k in range(1, sections):
        vec_copy(k).wait_send()

    @pl.when(me == 0)
    def _():
        sh_swap.wait_send()
        loop(1, depth, lambda k: sh_send(k).wait_send())

    loop(1, depth, lambda k: sh_share(k).wait_send())

    @pl.when(me == 0)
    def _():
        sh_cross.wait()

    @pl.when(me != 0)
    def _():
        sh_deliver(0).wait_send()

    @pl.when((me == 1) & (core == 1))
    def _():
        for name in relay:
            relayed(name, True).wait_send()

    @pl.when((me == 2) & (core == 1))
    def _():
        for name in ("k0", "p0"):
            scattered(name, True).wait_send()

    for name in names:

        def sent(name=name):
            swap(name).wait_send()
            for k in range(1, sections):
                to_section(name, k).wait_send()

        if name in fresh:
            when_held(name, sent)
            loop(1, depth, lambda k, name=name: to_chip(name, k).wait_send())
        if held[name] == "chips":
            for k in range(1, sections):
                to_plane(name, k).wait_send()
        if held[name] != "done":
            loop(1, depth, lambda k, name=name: share(name, k).wait_send())

        @pl.when(me == owner[name])
        def _(name=name):
            cross(name).wait()

        @pl.when(me != owner[name])
        def _(name=name):
            deliver(name, 0).wait_send()


def sum_gradients(sections, count, short, piece, terms, vectors, dh1, w, weights, map_sources, real):
    narrow = short.shape[1]
    depth = count // 2
    args, scratch = [], []
    relays = []
    for name, section, kind in SUMS:
        args.append(terms[name])
        full = (sections, depth) + terms[name].shape[-2:]
        shapes = []
        if kind in ("owner", "each"):
            shapes += [full, full]
        if kind == "each":
            shapes.append(full)
        if kind == "chips":
            shapes.append((sections,) + full[2:])
        if kind in ("owner", "each"):
            shapes += [full[1:]] * 2
        if kind != "done":
            shapes.append(full[1:])
        if section == 0:
            relays.append(pltpu.VMEM(full[1:], BF16))
        scratch += [pltpu.VMEM(a, BF16) for a in shapes]
    scratch += relays + [pltpu.VMEM((short.shape[0] // 2, narrow), BF16)]
    sh_rows = short.shape[0] // 2
    scratch += [
        pltpu.VMEM((sh_rows, narrow), BF16),
        pltpu.VMEM((sh_rows, narrow), BF16),
        pltpu.VMEM((depth, sh_rows // depth, narrow), BF16),
        pltpu.VMEM((sh_rows, narrow), BF16),
        pltpu.VMEM((sections,) + vectors.shape[1:], F32),
    ]
    kinds = len(SUMS) + 1
    for shape in [(kinds,)] * 3 + [(kinds, sections)] * 2 + [(kinds, depth)] * 4:
        scratch.append(pltpu.SemaphoreType.DMA(shape))
    for shape in [(kinds,), (kinds, sections), (kinds,), (kinds,), (kinds,), (sections,), (sections,), (kinds,), (kinds,)]:
        scratch.append(pltpu.SemaphoreType.DMA(shape))
    wide = w.shape[0]
    padded = map_sources[0].shape[1]
    scratch += [
        pltpu.VMEM(map_sources[0].shape, BF16),
        pltpu.VMEM((2, TILE, wide), BF16),
        pltpu.VMEM((2, TILE, narrow), BF16),
        pltpu.VMEM((TILE // 128, 4 * padded, 128), F32),
        pltpu.VMEM((2, real, 4, TILE), BF16),
        pltpu.SemaphoreType.DMA,
        pltpu.SemaphoreType.DMA((2,)),
        pltpu.SemaphoreType.DMA((2,)),
        pltpu.SemaphoreType.DMA((2,)),
    ]
    hbm = pl.BlockSpec(memory_space=pl.ANY)
    vmem = pl.BlockSpec(memory_space=pltpu.VMEM)
    taps_shape, proj_shape = args[0].shape, args[1].shape
    return pl.pallas_call(
        functools.partial(gradient_kernel, sections, count),
        out_shape=[
            shape_of((2, sh_rows, narrow * sections), BF16),
            shape_of(proj_shape, BF16),
            shape_of(taps_shape, BF16),
            shape_of(vectors.shape[1:], F32),
            shape_of((real, 4, wide), BF16),
        ],
        in_specs=[hbm] * 8 + [vmem, vmem] + [hbm] * 6,
        out_specs=[hbm, hbm, hbm, vmem, hbm],
        scratch_shapes=scratch,
        compiler_params=pltpu.CompilerParams(
            has_side_effects=True, vmem_limit_bytes=VMEM_BYTES, collective_id=5
        ),
        cost_estimate=pl.CostEstimate(flops=0, bytes_accessed=400 * 2**20, transcendentals=0),
    )(short.reshape(2, sh_rows, narrow), piece, *args, vectors, dh1, w, weights, *map_sources)


def cast_kernel(proj, taps, short, maps, proj_out, taps_out, short_out, maps_out):
    me = lax.axis_index("segment")
    maps_out[...] = maps[...]
    proj_out[...] = proj[...].astype(F32)
    for held, src, out in (
        ((me == 0) | (me == 2), taps, taps_out),
        (me == 0, short, short_out),
    ):

        @pl.when(held)
        def _(src=src, out=out):
            out[...] = src[...].astype(F32)

        @pl.when(jnp.logical_not(held))
        def _(out=out):
            out[...] = jnp.zeros(out.shape, F32)


def cast_sums(maps, *sums):
    steps = 8
    blocks = [pl.BlockSpec((a.shape[0] // steps, a.shape[1]), lambda i: (i, 0)) for a in sums]
    blocks.append(pl.BlockSpec(maps.shape[:2] + (maps.shape[2] // steps,), lambda i: (0, 0, i)))
    return pl.pallas_call(
        cast_kernel,
        grid=(steps,),
        out_shape=[shape_of(a.shape, F32) for a in sums] + [shape_of(maps.shape, BF16)],
        in_specs=blocks,
        out_specs=blocks,
        compiler_params=pltpu.CompilerParams(vmem_limit_bytes=VMEM_BYTES),
        cost_estimate=pl.CostEstimate(flops=0, bytes_accessed=54 * 2**20, transcendentals=0),
    )(*sums, maps)


def layouts(resolution_ids, order_ids):
    pixels = jnp.arange(MAP * MAP, dtype=jnp.int32)
    row_of = pixels // MAP
    column_of = pixels % MAP
    extent = 5 + resolution_ids[:, None]
    image_mask = ((row_of[None, :] < extent) & (column_of[None, :] < extent)).astype(F32)
    inside = (row_of < 6) & (column_of < 6)
    position = jnp.where(inside, row_of // 2 * 3 + column_of // 2, 0)
    onehot_tile = (position[:, None] == jnp.arange(9)[None, :]).astype(jnp.int32)
    picked = jnp.sum(onehot_tile[None] * order_ids[:, None, :], axis=2)
    row_to = 2 * (picked // 3) + row_of % 2
    column_to = 2 * (picked % 3) + column_of % 2
    target = row_to * MAP + column_to
    tile_mask = (inside & (row_to < extent) & (column_to < extent)).astype(F32)
    return image_mask, tile_mask, jnp.where(inside, target, -1)


def tap_tables(tiled):
    lattice = np.arange(MAP)
    tables = []
    for vertical, lateral in OFFSETS:
        row, column = lattice + vertical, lattice + lateral
        in_row = (row >= 0) & (row < MAP)
        in_column = (column >= 0) & (column < MAP)
        if tiled:
            in_row &= row // 2 == lattice // 2
            in_column &= column // 2 == lattice // 2
        tables.append((in_row[:, None] & in_column[None, :]).reshape(-1))
    return np.stack(tables, axis=1).astype(np.float32)


def body(
    layer_input,
    output_grad,
    resolution,
    tile_order,
    proj_weight,
    spatial_weight,
    shortcut_weight,
    bn_gain,
    bn_bias,
):
    micro, images, pixels, wide = layer_input.shape
    narrow = proj_weight.shape[2]
    rows = images * pixels
    padded = -(-rows // 16) * 16
    sections = lax.axis_size("segment")
    count = lax.axis_size("dp")
    section = lax.axis_index("segment")
    first = section == 0
    proj, spatial, shortcut = proj_weight[0], spatial_weight[0], shortcut_weight[0]
    pick = lambda a: lax.dynamic_index_in_dim(a, section, 0, keepdims=False)

    image_masks, tile_masks, targets = layouts(
        resolution.reshape(-1), tile_order.reshape(micro * images, -1)
    )
    interleave = lambda a: jnp.transpose(a.reshape(micro, rows), (1, 0)).reshape(rows * micro, 1)
    taps_image = np.tile(np.repeat(tap_tables(False), micro, axis=0), (images, 1))
    pack_all = jnp.concatenate(
        [interleave(image_masks), jnp.asarray(taps_image), jnp.zeros((rows * micro, 6), F32)], axis=1
    )
    tiles_all = interleave(tile_masks)
    pad_rows = lambda a: jnp.pad(a, ((0, padded - rows), (0, 0)))
    image_mask = pad_rows(pick(image_masks.reshape(micro, rows, 1)))
    tile_mask = pad_rows(pick(tile_masks.reshape(micro, rows, 1)))
    taps_tile = np.pad(np.tile(tap_tables(True), (images, 1)), ((0, padded - rows), (0, 6)))
    pack_tile = jnp.concatenate([tile_mask, jnp.asarray(taps_tile)], axis=1)
    target = pick(targets.reshape(micro, images, pixels))
    base = (jnp.arange(images) * pixels)[:, None]
    target = jnp.where(target >= 0, target + base, -1).reshape(rows)
    target = jnp.pad(target, (0, padded - rows), constant_values=-1)
    index = jnp.arange(padded)
    moves = (target[:, None] == index[None, :]).astype(BF16)
    moves_back = (target[None, :] == index[:, None]).astype(BF16)

    x_in = jnp.transpose(layer_input, (1, 2, 0, 3)).reshape(rows, micro, wide)
    og_in = jnp.transpose(output_grad, (1, 2, 0, 3)).reshape(rows, micro, wide)
    gb_first = jnp.stack(
        [bn_gain[0, :narrow], bn_bias[0, :narrow]]
        + [bn_gain[0, narrow : 2 * narrow], bn_bias[0, narrow : 2 * narrow]]
    )
    gains_here = jnp.concatenate([bn_gain, bn_bias])
    total = rows * micro
    quarter = wide // sections
    dma = pltpu.SemaphoreType.DMA
    stats_all, counts, gains, y1, u, h3n, stats3, *far = kernel_call(
        functools.partial(head_kernel, sections, count),
        [
            shape_of((16, narrow), F32),
            shape_of((8, 128), F32),
            shape_of((sections, 2, wide), F32),
            shape_of((padded, wide), BF16),
            shape_of((padded, wide), BF16),
            shape_of((padded, wide), F32),
            shape_of((2, wide), F32),
            shape_of((padded, narrow), BF16),
            shape_of((wide, narrow), BF16),
            shape_of((sections, padded, quarter), BF16),
            shape_of((total, wide), BF16),
            shape_of((total, narrow), BF16),
            shape_of((total, narrow), F32),
            shape_of((total, narrow), F32),
            shape_of((wide, narrow), BF16),
            shape_of((wide, narrow), BF16),
            shape_of((9 * narrow, narrow), BF16),
        ],
        [x_in, proj, shortcut, spatial, gb_first, gains_here, pack_all, tiles_all, image_mask, moves],
        [
            pltpu.VMEM((total, wide), BF16),
            pltpu.VMEM((total, 9 * narrow), BF16),
            pltpu.VMEM((total, narrow), F32),
            pltpu.VMEM((total, narrow), F32),
            pltpu.VMEM((narrow // 128, 4 * padded, 128), F32),
            pltpu.VMEM((micro, padded, narrow), BF16),
            pltpu.VMEM((padded, narrow), BF16),
            pltpu.VMEM((wide, quarter), BF16),
            pltpu.VMEM((wide, narrow), BF16),
            pltpu.VMEM((micro, padded, quarter), BF16),
            pltpu.VMEM((sections, padded, quarter), BF16),
            pltpu.VMEM((sections, 2, wide), F32),
        ]
        + sync_scratch(count, [(8, narrow + 128), (8, narrow), (2, wide)])
        + [dma((sections,)), dma, dma, dma]
        + [dma((sections,)), dma, dma, dma]
        + [dma((sections,)), dma((sections,)), dma((sections,)), dma]
        + [dma((sections,)), dma((sections,)), dma((2,)), dma((7,))]
        + [dma((5, sections)), dma((5,)), dma((5,)), dma((5,))]
        + [dma((5, 2)), dma((5, 2)), dma((3,))]
        + [dma((5,)), pltpu.VMEM((9 * narrow, narrow), BF16), dma],
        0,
        2 * total * (narrow * (wide + 9 * narrow) + wide * quarter),
        60 * 2**20,
        far_in=(2, 3),
        far_out=tuple(range(7, 17)),
    )
    a2, w1, res, x_all, a1_all, h1n_all, h2n_all, w3, w2, k2 = far
    paged = shape_of((sections, padded, wide), BF16)
    y2, dy1, t_sums, map_one, p3_term, p2_term, k2_term = kernel_call(
        functools.partial(tile_kernel, sections, count),
        [
            shape_of((padded, wide), BF16),
            shape_of((padded, wide), BF16),
            shape_of((6, wide), F32),
            paged,
            shape_of((wide, narrow), BF16),
            shape_of((wide, narrow), BF16),
            shape_of((9 * narrow, narrow), BF16),
        ],
        [u, w2, k2, w3, og_in, pack_tile, gains, counts, moves_back, y1],
        [
            pltpu.VMEM((padded, narrow), BF16),
            pltpu.VMEM((padded, 9 * narrow), BF16),
            pltpu.VMEM((padded, wide), BF16),
            pltpu.VMEM((padded, narrow), BF16),
            pltpu.VMEM((padded, narrow), BF16),
            pltpu.VMEM((2, 512, narrow), BF16),
            dma((2,)),
            pltpu.VMEM((9 * narrow, narrow), BF16),
            pltpu.VMEM((wide, narrow), BF16),
            pltpu.VMEM((rows, micro, wide), BF16),
            dma((3,)),
            pltpu.VMEM((padded, narrow), F32),
            pltpu.VMEM((padded, narrow), F32),
            pltpu.VMEM((padded, wide), F32),
            pltpu.VMEM((padded, narrow), F32),
            pltpu.VMEM((padded, wide), BF16),
            pltpu.VMEM((6, wide), F32),
            pltpu.VMEM((padded, wide), F32),
        ]
        + [dma, dma((sections,)), dma]
        + sync_scratch(
            count, [(2, narrow), (2, narrow), (2, wide), (2, wide), (2, narrow), (2, narrow)]
        ),
        1,
        4 * padded * narrow * (2 * wide + 9 * narrow),
        30 * 2**20,
        far_in=(2, 3, 4, 9),
        far_out=(3, 4, 5, 6),
    )
    depth = count // 2

    def split(term):
        return term.reshape(2, sections, depth, term.shape[0] // (2 * sections * depth), narrow)

    p3_term, p2_term, k2_term = split(p3_term), split(p2_term), split(k2_term)
    taps_piece = k2_term.shape[3]
    dh1_all, i_sums, f_sums, k2_part, *far = kernel_call(
        functools.partial(back_kernel, sections, count),
        [
            shape_of((total, narrow), BF16),
            shape_of((2, wide), F32),
            shape_of((16, narrow), F32),
            shape_of((sections, taps_piece, narrow), BF16),
            paged,
            paged,
            paged,
            shape_of((wide, narrow), BF16),
            shape_of((9 * narrow, narrow), BF16),
            shape_of((wide, narrow), BF16),
            shape_of((wide, narrow), BF16),
            shape_of((wide // count, narrow), BF16),
        ],
        [dy1, res, h3n, image_mask, gains, stats3, w1, spatial, gb_first, pack_all]
        + [h1n_all, h2n_all, stats_all, counts, k2_term, y2, a2, a1_all, x_all],
        [
            pltpu.VMEM((padded, wide), BF16),
            pltpu.VMEM((padded, wide), BF16),
            pltpu.VMEM((total, narrow), BF16),
            pltpu.VMEM((total, quarter), BF16),
            pltpu.VMEM((total, narrow), BF16),
            pltpu.VMEM((total, wide), BF16),
            pltpu.VMEM((9 * narrow, narrow), BF16),
            pltpu.VMEM((total, narrow), F32),
            pltpu.VMEM((total, narrow), F32),
            pltpu.VMEM((2, 512, narrow), BF16),
            dma((2,)),
            dma((5,)),
            pltpu.VMEM((padded, narrow), BF16),
            pltpu.VMEM((micro, padded, narrow), BF16),
            pltpu.VMEM((micro, padded, quarter), BF16),
            pltpu.VMEM((narrow // 128, 4 * padded, 128), F32),
            pltpu.VMEM((total, narrow), F32),
            pltpu.VMEM((total, narrow), BF16),
        ]
        + sync_scratch(count, [(2, wide), (8, narrow), (8, narrow)])
        + [pltpu.VMEM(k2_term.shape[1:], BF16)] * 2
        + [pltpu.VMEM((depth, sections, taps_piece, narrow), BF16)]
        + [pltpu.VMEM((sections, taps_piece, narrow), BF16)]
        + [dma, dma, dma, dma((depth,)), dma((depth,)), dma]
        + [pltpu.VMEM((wide // 2, narrow), BF16)] * 3
        + [pltpu.VMEM((depth, wide // count, narrow), BF16), pltpu.VMEM((wide // count, narrow), BF16)]
        + [dma, dma, dma((depth,)), dma((depth,)), dma]
        + [dma, dma((sections,)), dma((sections,)), dma((sections,))]
        + [dma, dma((sections,)), dma] * 3,
        2,
        2 * total * narrow * 9 * narrow,
        40 * 2**20,
        far_in=(7, 10, 11, 14, 15, 17, 18),
        far_out=tuple(range(3, 12)),
    )
    map_zero, map_two, map_three, p1_term, k0_term, p0_term, short_term, short_piece = far

    terms = {
        "p3": p3_term,
        "k2": k2_part,
        "p2": p2_term,
        "p1": split(p1_term),
        "k0": split(k0_term),
        "p0": split(p0_term),
    }

    blank = jnp.zeros((wide,), F32)
    pad = jnp.zeros((wide - 2 * narrow,), F32)
    of_batches = lambda at: jnp.sum(f_sums[at : at + 4], axis=0)
    zero_gain = jnp.where(first, jnp.concatenate([of_batches(12), of_batches(4), pad]), blank)
    zero_bias = jnp.where(first, jnp.concatenate([of_batches(8), of_batches(0), pad]), blank)
    vectors = jnp.stack(
        [
            zero_gain,
            zero_bias,
            i_sums[1],
            i_sums[0],
            jnp.concatenate([t_sums[5, :narrow], t_sums[3, :narrow], pad]),
            jnp.concatenate([t_sums[4, :narrow], t_sums[2, :narrow], pad]),
            t_sums[1],
            t_sums[0],
        ]
    )
    short_sum, proj_sum, taps_sum, vectors, maps = sum_gradients(
        sections,
        count,
        short_term,
        short_piece,
        terms,
        vectors.reshape(sections, 2, wide),
        dh1_all,
        proj,
        shortcut,
        (map_zero, map_one, map_two, map_three),
        rows,
    )
    proj_grad, spatial_grad, short_grad, maps = cast_sums(
        maps,
        proj_sum.reshape(wide, narrow),
        taps_sum.reshape(9 * narrow, narrow),
        short_sum.reshape(wide, wide),
    )
    maps = jnp.transpose(maps.reshape(images, pixels, micro, wide), (2, 0, 1, 3))
    return (
        maps[None],
        proj_grad[None],
        spatial_grad[None],
        short_grad[None],
        vectors[:1],
        vectors[1:],
    )


def solution(mesh):
    return jax.shard_map(
        body,
        mesh=mesh,
        in_specs=(
            P(None, "dp", None, None),
            P(None, "dp", None, None),
            P(None, "dp"),
            P(None, "dp", None),
            P("segment", None, None),
            P("segment", None, None),
            P("segment", None, None),
            P("segment", None),
            P("segment", None),
        ),
        out_specs=(
            P("segment", None, "dp", None, None),
            P("segment", None, None),
            P("segment", None, None),
            P("segment", None, None),
            P("segment", None),
            P("segment", None),
        ),
        check_vma=False,
    )
```

```python
import functools

import jax
import jax.numpy as jnp
import numpy as np
from jax import lax
from jax.experimental import pallas as pl
from jax.experimental.pallas import tpu as pltpu
from jax.sharding import PartitionSpec as P

MAP = 7
EPSILON = 1e-05
OFFSETS = ((-1, -1), (-1, 0), (-1, 1), (0, -1), (0, 0), (0, 1), (1, -1), (1, 0), (1, 1))
MESH = pl.DeviceIdType.MESH
F32 = jnp.float32
BF16 = jnp.bfloat16
VMEM_BYTES = 60 * 2**20
TILE = 256


def greet(count, sections=0):
    segment, me = lax.axis_index("segment"), lax.axis_index("dp")
    barrier = pltpu.get_barrier_semaphore()

    def one(k, carry):
        pl.semaphore_signal(
            barrier, inc=1, device_id=(segment, lax.rem(me + k, count)), device_id_type=MESH
        )
        return carry

    lax.fori_loop(1, count, one, 0)
    for k in range(1, sections):
        pl.semaphore_signal(
            barrier, inc=1, device_id=(jnp.bitwise_xor(segment, k), me), device_id_type=MESH
        )


def greeted(count, sections=1):
    pl.semaphore_wait(pltpu.get_barrier_semaphore(), count - 1 + sections - 1)


def exchange(count, slots, send_sem, recv_sem):
    segment, me = lax.axis_index("segment"), lax.axis_index("dp")

    def copy(k):
        return pltpu.make_async_remote_copy(
            src_ref=slots.at[me],
            dst_ref=slots.at[me],
            send_sem=send_sem.at[k],
            recv_sem=recv_sem.at[k],
            device_id=(segment, lax.rem(me + k, count)),
            device_id_type=MESH,
        )

    def start(k, carry):
        copy(k).start()
        return carry

    def finish(k, carry):
        copy(k).wait_recv()
        copy(k).wait_send()
        return carry

    lax.fori_loop(1, count, start, 0)
    lax.fori_loop(1, count, finish, 0)
    total = slots[0]
    for k in range(1, count):
        total = total + slots[k]
    return total


def mesh_copy(src, dst, send_sem, recv_sem, segment, place):
    return pltpu.make_async_remote_copy(
        src_ref=src,
        dst_ref=dst,
        send_sem=send_sem,
        recv_sem=recv_sem,
        device_id=(segment, place),
        device_id_type=MESH,
    )


def loop(low, high, body):
    def one(k, carry):
        body(k)
        return carry

    lax.fori_loop(low, high, one, 0)


def sync_scratch(count, shapes):
    out = []
    for shape in shapes:
        out += [
            pltpu.VMEM((count,) + shape, F32),
            pltpu.SemaphoreType.DMA((count,)),
            pltpu.SemaphoreType.DMA((count,)),
        ]
    return out


def kernel_call(kernel, outs, args, scratch, ident, flops, moved, far_in=(), far_out=()):
    params = dict(has_side_effects=True, vmem_limit_bytes=VMEM_BYTES)
    if ident is not None:
        params["collective_id"] = ident
    return pl.pallas_call(
        kernel,
        out_shape=outs,
        in_specs=[
            pl.BlockSpec(memory_space=pl.ANY if i in far_in else pltpu.VMEM) for i in range(len(args))
        ],
        out_specs=[
            pl.BlockSpec(memory_space=pl.ANY if i in far_out else pltpu.VMEM) for i in range(len(outs))
        ],
        scratch_shapes=scratch,
        compiler_params=pltpu.CompilerParams(**params),
        cost_estimate=pl.CostEstimate(flops=flops, bytes_accessed=moved, transcendentals=0),
    )(*args)


def shape_of(shape, dtype):
    return jax.ShapeDtypeStruct(shape, dtype)


def dot(a, b):
    return jnp.dot(a, b, preferred_element_type=F32)


def dot_t(a, b):
    return lax.dot_general(a, b, (((1,), (1,)), ((), ())), preferred_element_type=F32)


def dot_0(a, b):
    return lax.dot_general(a, b, (((0,), (0,)), ((), ())), preferred_element_type=F32)


class Writer:
    def __init__(self, stage, sems):
        self.stage, self.sems, self.open, self.turn = stage, sems, [None, None], 0

    def put(self, value, dst):
        at = self.turn % 2
        self.turn += 1
        if self.open[at] is not None:
            self.open[at].wait()
        self.stage[at] = value.astype(BF16)
        self.open[at] = pltpu.make_async_copy(self.stage.at[at], dst, self.sems.at[at])
        self.open[at].start()

    def rows_of_dot(self, left, right, out):
        tall = self.stage.shape[1]
        for j in range(out.shape[0] // tall):
            at = pl.ds(j * tall, tall)
            self.put(dot_0(left[:, at], right[...]), out.at[at])

    def drain(self):
        for at in range(2):
            if self.open[at] is not None:
                self.open[at].wait()
        self.open = [None, None]


def sigmoid(v):
    return 1.0 / (1.0 + jnp.exp(-v))


def slope(v):
    s = sigmoid(v)
    return s * (1.0 + v * (1.0 - s))


def over(width, step, body):
    def one(j, carry):
        body(pl.ds(pl.multiple_of(j * step, step), step))
        return carry

    lax.fori_loop(0, width // step, one, 0)


def lane(at):
    return lax.div(at.start, 128)


def unrolled_shift(ref_value, shift):
    rows = ref_value.shape[0]
    return ref_value if shift % rows == 0 else pltpu.roll(ref_value, (-shift) % rows, 0)


def by_batch(values):
    rows, width = values.shape
    part = jnp.sum(values.reshape(rows // 8, 8, width), axis=0)
    return part[:4] + part[4:]


def spread8(values):
    return jnp.concatenate([values, values], axis=0)[None]


def first_part(
    count, hooks, writes, x, w, k, gb, pack, tiles, a2_out, cols, h1n, h2n, stats_out, count_out, act, *sync
):
    s1, send1, recv1, s2, send2, recv2 = sync
    rows, narrow = h1n.shape
    me = lax.axis_index("dp")
    full = act.shape[1]

    def tile8(v):
        return v.reshape(rows // 8, 8, v.shape[1])

    def project(at):
        h = dot(x[...], w[:, at])
        h1n[:, at] = h
        m = pack[:, 0:1] * h
        s1[me, 0:4, at] = by_batch(m)
        s1[me, 4:8, at] = by_batch(m * h)

    over(narrow, TILE, project)
    s1[me, 0:4, narrow:] = jnp.broadcast_to(by_batch(pack[:, 0:1]), (4, 128))
    s1[me, 4:8, narrow:] = jnp.broadcast_to(by_batch(tiles[:, 0:1]), (4, 128))
    total = exchange(count, s1, send1, recv1)
    counts = total[:, narrow:]
    count_out[...] = counts
    valid = counts[0:4, 0:1]
    average = total[0:4, :narrow] / valid
    inverse = lax.rsqrt(total[4:8, :narrow] / valid - average * average + EPSILON)
    stats_out[0:4, :] = average
    stats_out[4:8, :] = inverse
    hooks[0]()

    def activate(stat_at, gain_at, source):
        def body(at):
            mean = spread8(stats_out[stat_at : stat_at + 4, at])
            inv = spread8(stats_out[stat_at + 4 : stat_at + 8, at])
            hn = (tile8(source[:, at]) - mean) * inv
            source[:, at] = hn.reshape(rows, hn.shape[2])
            n = gb[gain_at : gain_at + 1, at][None] * hn + gb[gain_at + 1 : gain_at + 2, at][None]
            n = n.reshape(rows, n.shape[2])
            act[lane(at), 0:rows, :] = pack[:, 0:1] * (n * sigmoid(n))

        return body

    over(narrow, 128, activate(0, 0, h1n))

    for t, (vertical, lateral) in enumerate(OFFSETS):
        shift = 4 * (7 * vertical + lateral)

        def place(j, carry, t=t, shift=shift):
            at = pl.ds(pl.multiple_of(j * 128, 128), 128)
            to = pl.ds(pl.multiple_of(t * narrow + j * 128, 128), 128)
            moved = unrolled_shift(act[j, 0:rows, :], shift)
            cols[:, to] = (pack[:, 1 + t : 2 + t] * moved).astype(BF16)
            return carry

        lax.fori_loop(0, narrow // 128, place, 0)

    def convolve(at):
        h = dot(cols[...], k[:, at])
        h2n[:, at] = h
        m = pack[:, 0:1] * h
        s2[me, 0:4, at] = by_batch(m)
        s2[me, 4:8, at] = by_batch(m * h)

    for write in writes:
        write.start()
    hooks[1]()
    over(narrow, TILE, convolve)
    total = exchange(count, s2, send2, recv2)
    average = total[0:4] / valid
    hooks[2]()
    stats_out[8:12, :] = average
    stats_out[12:16, :] = lax.rsqrt(total[4:8] / valid - average * average + EPSILON)
    over(narrow, 128, activate(8, 2, h2n))
    act[:, rows:, :] = jnp.zeros((narrow // 128, full - rows, 128), F32)
    for m in range(4):

        def pick(j, carry, m=m):
            at = pl.ds(pl.multiple_of(j * 128, 128), 128)
            a2_out[m, :, at] = act[j, pl.ds(m, full // 4, stride=4), :].astype(BF16)
            return carry

        lax.fori_loop(0, narrow // 128, pick, 0)


def residual_part(x, w, out, hold):
    rows, full, quarter = x.shape[0], hold.shape[1], out.shape[2]
    hold[:, rows:, :] = jnp.zeros((quarter // 128, full - rows, 128), F32)

    def body(at):
        value = dot(x[...], w[:, at])
        for part in range(TILE // 128):
            hold[lane(at) + part, 0:rows, :] = value[:, part * 128 : part * 128 + 128]

    over(quarter, TILE, body)
    for m in range(4):

        def pick(j, carry, m=m):
            at = pl.ds(pl.multiple_of(j * 128, 128), 128)
            out[m, :, at] = hold[j, pl.ds(m, full // 4, stride=4), :].astype(BF16)
            return carry

        lax.fori_loop(0, quarter // 128, pick, 0)


def norm_sums(slots, me, at, masked, h):
    slots[me, 0:1, at] = jnp.sum(masked, axis=0, keepdims=True)
    slots[me, 1:2, at] = jnp.sum(masked * h, axis=0, keepdims=True)


def finish_stats(total, valid, stats_out, at_row):
    average = total[0:1] / valid
    width = average.shape[1]
    stats_out[at_row : at_row + 1, 0:width] = average
    stats_out[at_row + 1 : at_row + 2, 0:width] = lax.rsqrt(
        total[1:2] / valid - average * average + EPSILON
    )


def second_part(
    count, before, a2, w1, res, mask, gb, valid, moves, y_out, u_out, h3n, stats_out, s1, send1, recv1
):
    wide = h3n.shape[1]
    quarter = res.shape[2]
    me = lax.axis_index("dp")

    def project(at):
        h = dot_t(a2[...], w1[at, :])
        h3n[:, at] = h
        norm_sums(s1, me, at, mask[:, 0:1] * h, h)

    over(wide, TILE, project)
    finish_stats(exchange(count, s1, send1, recv1), valid, stats_out, 0)
    before()
    for q in range(wide // quarter):

        def body(j, carry, q=q):
            at = pl.ds(pl.multiple_of(q * quarter + j * 128, 128), 128)
            own = pl.ds(pl.multiple_of(j * 128, 128), 128)
            hn = (h3n[:, at] - stats_out[0:1, at]) * stats_out[1:2, at]
            h3n[:, at] = hn
            z = gb[1, 0:1, at] * hn + gb[1, 1:2, at] + res[q, :, own].astype(F32)
            y_out[:, at] = (mask[:, 0:1] * (z * sigmoid(z))).astype(BF16)
            return carry

        lax.fori_loop(0, quarter // 128, body, 0)

    def permute(at):
        u_out[:, at] = dot(moves[...], y_out[:, at]).astype(BF16)

    over(wide, TILE, permute)


def batch_valid(counts, row):
    me = lax.axis_index("segment")
    value = counts[row : row + 1, 0:1]
    for m in range(1, 4):
        value = jnp.where(me == m, counts[row + m : row + m + 1, 0:1], value)
    return value


def head_kernel(
    sections,
    count,
    x3,
    w,
    short,
    k,
    gb,
    vec,
    pack,
    tiles,
    mask,
    moves,
    stats_out,
    count_out,
    g_out,
    y_out,
    u_out,
    h3n,
    stats3,
    a2_out,
    w1_out,
    res_out,
    x_out,
    a1_out,
    h1n_out,
    h2n_out,
    w3_out,
    w2_out,
    k2_out,
    x,
    cols,
    h1n,
    h2n,
    act,
    a2_all,
    a2,
    wsc,
    w1,
    rq,
    res,
    gslots,
    *rest,
):
    sync, rest = rest[:9], list(rest[9:])
    short_send, short_recv, short_relay_send, short_relay_recv = rest[:4]
    w1_send, w1_recv, w1_relay_send, w1_relay_recv = rest[4:8]
    g_send, g_recv, a2_send, a2_recv, res_send, res_recv, own_sem, out_sem = rest[8:16]
    spread_send, spread_recv, far_send, far_recv, near_send, near_recv, keep_sem = rest[16:23]
    pass_send, kv, kv_sem = rest[23:]
    me, place = lax.axis_index("segment"), lax.axis_index("dp")
    core = lax.rem(place, 2)
    sibling = place + 1 - 2 * core
    wide = x.shape[1]
    quarter = wide // sections
    half_rows = wide // 2
    mine = pl.ds(pl.multiple_of(core * half_rows, 16), half_rows)
    greet(count, sections)
    k_load = pltpu.make_async_copy(k, kv, kv_sem)
    k_load.start()

    odd = lax.rem(lax.div(place, 2), 2)
    beside = place + 2 - 4 * odd
    parts = [("w3", w, w3_out, 3, 0, 1), ("w2", w, w2_out, 2, 0, 1)]
    parts += [("k2", k, k2_out, 2, i, 3) for i in range(3)]

    def part_rows(i, at_odd):
        _, src, _, _, piece, pieces = parts[i]
        fine = src.shape[0] // (4 * pieces)
        start = ((2 * at_odd + core) * pieces + piece) * fine
        return pl.ds(pl.multiple_of(start, 16), fine)

    def spread_copy(i, t):
        _, src, dst, _, _, _ = parts[i]
        at = part_rows(i, odd)
        return mesh_copy(src.at[at], dst.at[at], spread_send.at[i, t], spread_recv.at[i], t, place)

    def far_copy(i):
        dst, at = parts[i][2], part_rows(i, odd)
        return mesh_copy(dst.at[at], dst.at[at], far_send.at[i], far_recv.at[i], me, beside)

    def near_copy(i, second):
        dst = parts[i][2]
        at = part_rows(i, 1 - odd if second else odd)
        sems = near_send.at[i, second], near_recv.at[i, second]
        return mesh_copy(dst.at[at], dst.at[at], *sems, me, sibling)

    keeps = [
        (3, pltpu.make_async_copy(w, w3_out, keep_sem.at[0])),
        (2, pltpu.make_async_copy(w, w2_out, keep_sem.at[1])),
        (2, pltpu.make_async_copy(kv, k2_out, keep_sem.at[2])),
    ]

    def spread_start(i):
        owner = parts[i][3]

        @pl.when(me == owner)
        def _():
            for d in (1, 2):
                spread_copy(i, owner ^ d).start()

    def spread_sent(i):
        for d in (1, 2):
            spread_copy(i, parts[i][3] ^ d).wait_send()

    def pass_copy(i):
        dst, at = parts[i][2], part_rows(i, odd)
        return mesh_copy(
            dst.at[at], dst.at[at], pass_send.at[i], spread_recv.at[i], parts[i][3] ^ 3, place
        )

    def spread_on(i):
        owner = parts[i][3]

        @pl.when(me == owner ^ 1)
        def _():
            spread_copy(i, 0).wait_recv()
            pass_copy(i).start()

        @pl.when((me != owner) & (me != owner ^ 1))
        def _():
            spread_copy(i, 0).wait_recv()

        @pl.when(me != owner)
        def _():
            far_copy(i).start()
            near_copy(i, 0).start()

    def far_on(i):
        @pl.when(me != parts[i][3])
        def _():
            far_copy(i).wait_recv()
            near_copy(i, 1).start()

    def short_copy(t):
        src = short.at[mine, pl.ds(t * quarter, quarter)]
        return mesh_copy(src, wsc.at[mine], short_send.at[t], short_recv, t, place)

    def w1_copy(t):
        return mesh_copy(w.at[mine], w1.at[mine], w1_send.at[t], w1_recv, t, place)

    short_own = pltpu.make_async_copy(short.at[:, pl.ds(0, quarter)], wsc, own_sem.at[0])
    w1_own = pltpu.make_async_copy(w, w1, own_sem.at[1])
    short_relay = mesh_copy(
        wsc.at[mine], wsc.at[mine], short_relay_send, short_relay_recv, me, sibling
    )
    w1_relay = mesh_copy(w1.at[mine], w1.at[mine], w1_relay_send, w1_relay_recv, me, sibling)

    def g_copy(k_):
        return mesh_copy(
            gslots.at[me],
            gslots.at[me],
            g_send.at[k_],
            g_recv.at[k_],
            jnp.bitwise_xor(me, k_),
            place,
        )

    gslots[me] = vec[...]
    greeted(count, sections)

    @pl.when(me == 0)
    def _():
        for t in (3, 1, 2):
            short_copy(t).start()
        short_own.start()

    @pl.when(me == 1)
    def _():
        for t in (2, 0, 3):
            w1_copy(t).start()
        w1_own.start()

    for k_ in range(1, sections):
        g_copy(k_).start()
    for i in range(3):
        spread_start(i)
    for owner, copy in keeps[:2]:
        pl.when(me == owner)(copy.start)

    def relayout(j, carry):
        at = pl.ds(pl.multiple_of(j * 128, 128), 128)
        x[:, at] = x3[:, :, at].reshape(x.shape[0], 128)
        return carry

    lax.fori_loop(0, wide // 128, relayout, 0)
    writes = [
        pltpu.make_async_copy(src, dst, out_sem.at[i])
        for i, (src, dst) in enumerate(
            ((x, x_out), (h1n, h1n_out), (cols.at[:, pl.ds(4 * h1n.shape[1], h1n.shape[1])], a1_out), (h2n, h2n_out))
            + ((a2, a2_out), (w1, w1_out), (res, res_out))
        )
    ]
    writes[0].start()

    def a2_copy(t):
        return mesh_copy(a2_all.at[t], a2, a2_send.at[t], a2_recv, t, place)

    @pl.when(me == 0)
    def _():
        def between():
            spread_on(0)
            spread_on(1)

        first_part(
            count,
            (lambda: spread_on(1), k_load.wait, lambda: spread_on(0)),
            writes[1:3],
            x,
            w,
            kv,
            gb,
            pack,
            tiles,
            a2_all,
            cols,
            h1n,
            h2n,
            stats_out,
            count_out,
            act,
            *sync[:6],
        )
        writes[3].start()
        for t in range(1, sections):
            a2_copy(t).start()
        a2[...] = a2_all[0]
        short_own.wait()
        for i in (2, 3, 4):
            spread_on(i)

    @pl.when(me != 0)
    def _():
        k_load.wait()
        pl.when(me == keeps[2][0])(keeps[2][1].start)
        slots, send1, recv1 = sync[:3]
        narrow = h1n.shape[1]
        stats_out[...] = jnp.zeros(stats_out.shape, F32)
        slots[place, :, 0:narrow] = jnp.zeros((8, narrow), F32)
        slots[place, 0:4, narrow:] = jnp.broadcast_to(by_batch(pack[:, 0:1]), (4, 128))
        slots[place, 4:8, narrow:] = jnp.broadcast_to(by_batch(tiles[:, 0:1]), (4, 128))
        count_out[...] = exchange(count, slots, send1, recv1)[:, narrow:]

    def spread_paced(i, after):
        @pl.when(me == parts[i][3])
        def _():
            spread_sent(after)
            for d in (1, 2):
                spread_copy(i, parts[i][3] ^ d).start()

    def unless_zero(i):
        pl.when(me != 0)(lambda: spread_on(i))

    unless_zero(0)
    spread_paced(3, 1)
    unless_zero(1)
    spread_paced(4, 2)
    unless_zero(2)
    unless_zero(3)
    pl.when(me == parts[4][3] ^ 1)(lambda: spread_on(4))

    @pl.when(me != 0)
    def _():
        short_copy(0).wait_recv()
        short_relay.start()

    @pl.when(me == 1)
    def _():
        w1_own.wait()

    @pl.when(me != 1)
    def _():
        w1_copy(0).wait_recv()
        w1_relay.start()

    @pl.when(me != 0)
    def _():
        short_relay.wait_recv()

    residual_part(x, wsc, rq, act)

    def res_copy(k_):
        other = jnp.bitwise_xor(me, k_)
        return mesh_copy(
            rq.at[other], res.at[me], res_send.at[k_], res_recv.at[k_], other, place
        )

    for k_ in range(1, sections):
        res_copy(k_).start()
    res[me] = rq[me]
    pl.when((me != 0) & (me != parts[4][3] ^ 1))(lambda: spread_on(4))

    @pl.when(me != 0)
    def _():
        a2_copy(0).wait_recv()

    @pl.when(me != 1)
    def _():
        w1_relay.wait_recv()

    for k_ in range(1, sections):
        g_copy(k_).wait_recv()
    g_out[...] = gslots[...]

    def before():
        far_on(0)
        far_on(1)
        for k_ in range(1, sections):
            res_copy(k_).wait_recv()

    second_part(
        count,
        before,
        a2,
        w1,
        res,
        mask,
        gslots,
        batch_valid(count_out, 0),
        moves,
        y_out,
        u_out,
        h3n,
        stats3,
        *sync[6:],
    )
    for copy in writes[4:]:
        copy.start()
    for i in range(2, len(parts)):
        far_on(i)
    for k_ in range(1, sections):
        g_copy(k_).wait_send()
        res_copy(k_).wait_send()

    @pl.when(me == 0)
    def _():
        for t in range(1, sections):
            short_copy(t).wait_send()
            a2_copy(t).wait_send()

    @pl.when(me != 0)
    def _():
        short_relay.wait_send()

    @pl.when(me == 1)
    def _():
        for t in (0, 2, 3):
            w1_copy(t).wait_send()

    @pl.when(me != 1)
    def _():
        w1_relay.wait_send()

    for i in range(len(parts)):
        owner = parts[i][3]

        if i not in (1, 2):
            pl.when(me == owner)(functools.partial(spread_sent, i))
        pl.when(me == owner ^ 1)(lambda i=i: pass_copy(i).wait_send())

        @pl.when(me != owner)
        def _(i=i):
            far_copy(i).wait_send()
            near_copy(i, 0).wait()
            near_copy(i, 1).wait()

    for owner, copy in keeps:
        pl.when(me == owner)(copy.wait)
    for i, copy in enumerate(writes):
        if i in (1, 2, 3):
            pl.when(me == 0)(copy.wait)
        else:
            copy.wait()


def back_sums(slots, me, at, grad, hn):
    slots[me, 0:1, at] = jnp.sum(grad, axis=0, keepdims=True)
    slots[me, 1:2, at] = jnp.sum(grad * hn, axis=0, keepdims=True)


def map_sender(sections, src, dst, owner, send_sem, recv_sem, own_sem):
    me, place = lax.axis_index("segment"), lax.axis_index("dp")
    own = pltpu.make_async_copy(src, dst.at[me], own_sem)

    def copy(k):
        return mesh_copy(src, dst.at[me], send_sem, recv_sem.at[k], owner, place)

    def start():
        @pl.when(me == owner)
        def _():
            own.start()

        for k in range(1, sections):

            @pl.when(me == owner ^ k)
            def _(k=k):
                copy(k).start()

    def finish():
        @pl.when(me == owner)
        def _():
            own.wait()
            for k in range(1, sections):
                copy(k).wait_recv()

        @pl.when(me != owner)
        def _():
            copy(0).wait_send()

    return start, finish


def tile_kernel(
    sections,
    count,
    u,
    w2,
    k2_far,
    w3_far,
    og_far,
    pack,
    gains,
    counts,
    back,
    y1,
    y_out,
    dy,
    sums_out,
    map_one,
    p3_out,
    p2_out,
    k2_out,
    a2,
    cols,
    dh3,
    dh2,
    dh1,
    stage,
    stage_sem,
    k2,
    w3,
    og3,
    load_sem,
    h1n,
    h2n,
    h3n,
    act,
    dz,
    stats,
    og,
    map_send,
    map_recv,
    map_own,
    *sync,
):
    s1, send1, recv1, s2, send2, recv2, s3, send3, recv3 = sync[:9]
    b3, bsend3, brecv3, b2, bsend2, brecv2, b1, bsend1, brecv1 = sync[9:]
    rows, wide = u.shape
    narrow = h1n.shape[1]
    me = lax.axis_index("dp")
    section = lax.axis_index("segment")
    valid = batch_valid(counts, 4)
    gb3 = gains.at[3]
    loads = [
        pltpu.make_async_copy(src, dst, load_sem.at[i])
        for i, (src, dst) in enumerate(((og_far, og3), (k2_far, k2), (w3_far, w3)))
    ]
    for load in loads:
        load.start()

    def gb2(row, at):
        return gains[2, row % 2 : row % 2 + 1, pl.ds(at.start + row // 2 * narrow, at.size)]

    greet(count, sections)

    def project(at):
        h = dot(u[...], w2[:, at])
        h1n[:, at] = h
        norm_sums(s1, me, at, pack[:, 0:1] * h, h)

    over(narrow, TILE, project)
    greeted(count, sections)
    send_map, wait_map = map_sender(sections, y1, map_one, 1, map_send, map_recv, map_own)
    send_map()
    loads[0].wait()
    real = og3.shape[0]
    for m in range(sections):

        @pl.when(section == m)
        def _(m=m):
            def one(j, carry):
                at = pl.ds(pl.multiple_of(j * 128, 128), 128)
                og[0:real, at] = og3[:, m, at].astype(F32)
                return carry

            lax.fori_loop(0, wide // 128, one, 0)

    og[real:, :] = jnp.zeros((rows - real, wide), F32)
    finish_stats(exchange(count, s1, send1, recv1), valid, stats, 0)

    def activate(row, gain, source, store):
        def body(at):
            hn = (source[:, at] - stats[row : row + 1, at]) * stats[row + 1 : row + 2, at]
            source[:, at] = hn
            n = gb2(gain, at) * hn + gb2(gain + 1, at)
            store(at, pack[:, 0:1] * (n * sigmoid(n)))

        return body

    def to_act(at, value):
        act[:, at] = value

    def to_a2(at, value):
        a2[:, at] = value.astype(BF16)

    over(narrow, 128, activate(0, 0, h1n, to_act))
    for t, (vertical, lateral) in enumerate(OFFSETS):
        shift = 7 * vertical + lateral

        def place(j, carry, t=t, shift=shift):
            at = pl.ds(pl.multiple_of(j * 128, 128), 128)
            to = pl.ds(pl.multiple_of(t * narrow + j * 128, 128), 128)
            moved = unrolled_shift(act[:, at], shift)
            cols[:, to] = (pack[:, 1 + t : 2 + t] * moved).astype(BF16)
            return carry

        lax.fori_loop(0, narrow // 128, place, 0)

    def convolve(at):
        h = dot(cols[...], k2[:, at])
        h2n[:, at] = h
        norm_sums(s2, me, at, pack[:, 0:1] * h, h)

    loads[1].wait()
    over(narrow, TILE, convolve)
    finish_stats(exchange(count, s2, send2, recv2), valid, stats, 2)
    over(narrow, 128, activate(2, 2, h2n, to_a2))

    def expand(at):
        h = dot_t(a2[...], w3[at, :])
        h3n[:, at] = h
        norm_sums(s3, me, at, pack[:, 0:1] * h, h)

    loads[2].wait()
    over(wide, TILE, expand)
    finish_stats(exchange(count, s3, send3, recv3), valid, stats, 4)

    def result(at):
        hn = (h3n[:, at] - stats[4:5, at]) * stats[5:6, at]
        h3n[:, at] = hn
        z = gb3[0:1, at] * hn + gb3[1:2, at] + u[:, at].astype(F32)
        s = sigmoid(z)
        m = pack[:, 0:1]
        y_out[:, at] = (m * (z * s)).astype(BF16)
        grad = (og[:, at] * m * (s * (1.0 + z * (1.0 - s)))).astype(BF16)
        dz[:, at] = grad
        grad = grad.astype(F32)
        back_sums(b3, me, at, grad, hn)

    over(wide, 128, result)
    total = exchange(count, b3, bsend3, brecv3)
    sums_out[0:2, :] = total

    def through(at):
        offset, scale = sums_out[0:1, at], sums_out[1:2, at]
        dh3[:, at] = (
            pack[:, 0:1]
            * gb3[0:1, at]
            * stats[5:6, at]
            * (dz[:, at].astype(F32) - (offset + h3n[:, at] * scale) / valid)
        ).astype(BF16)

    over(wide, 128, through)

    def into_two(at):
        grad = dot(dh3[...], w3[:, at]).astype(BF16).astype(F32)
        hn = h2n[:, at]
        n = gb2(2, at) * hn + gb2(3, at)
        grad = grad * pack[:, 0:1] * slope(n)
        act[:, at] = grad
        back_sums(b2, me, at, grad, hn)

    over(narrow, TILE, into_two)
    total = exchange(count, b2, bsend2, brecv2)
    sums_out[2:4, 0:narrow] = total

    def through_two(at):
        offset, scale = sums_out[2:3, at], sums_out[3:4, at]
        grad = (
            pack[:, 0:1]
            * gb2(2, at)
            * stats[3:4, at]
            * (act[:, at] - (offset + h2n[:, at] * scale) / valid)
        )
        dh2[:, at] = grad.astype(BF16)
        act[:, at] = dh2[:, at].astype(F32)

    over(narrow, 128, through_two)
    h2n[...] = jnp.zeros((rows, narrow), F32)
    for t, (vertical, lateral) in enumerate(OFFSETS):
        shift = -(7 * vertical + lateral)
        other = 8 - t

        def place_back(j, carry, t=t, shift=shift, other=other):
            at = pl.ds(pl.multiple_of(j * 128, 128), 128)
            moved = unrolled_shift(act[:, at], shift)
            dy[:, at] = (pack[:, 1 + other : 2 + other] * moved).astype(BF16)
            return carry

        lax.fori_loop(0, narrow // 128, place_back, 0)

        def gather(at, t=t):
            row = pl.ds(pl.multiple_of(t * narrow + at.start, TILE), TILE)
            h2n[:, at] += dot_t(dy[:, 0:narrow], k2[row, :])

        over(narrow, TILE, gather)

    def into_one(at):
        hn = h1n[:, at]
        n = gb2(0, at) * hn + gb2(1, at)
        grad = h2n[:, at] * pack[:, 0:1] * slope(n)
        act[:, at] = grad
        back_sums(b1, me, at, grad, hn)

    over(narrow, 128, into_one)
    total = exchange(count, b1, bsend1, brecv1)
    sums_out[4:6, 0:narrow] = total

    def through_one(at):
        offset, scale = sums_out[4:5, at], sums_out[5:6, at]
        dh1[:, at] = (
            pack[:, 0:1]
            * gb2(0, at)
            * stats[1:2, at]
            * (act[:, at] - (offset + h1n[:, at] * scale) / valid)
        ).astype(BF16)

    over(narrow, 128, through_one)

    def into_input(at):
        grad = dot_t(dh1[...], w2[at, :]) + dz[:, at].astype(F32)
        dy[:, at] = dot(back[...], grad.astype(BF16)).astype(BF16)

    over(wide, TILE, into_input)
    writer = Writer(stage, stage_sem)
    writer.rows_of_dot(dh3, a2, p3_out)
    writer.rows_of_dot(cols, dh2, k2_out)
    writer.rows_of_dot(u, dh1, p2_out)
    writer.drain()
    wait_map()


def image_back_part(
    count, after, dy, res, h3n, mask, gb, stats, valid, w1, dz, dh3, da2, sums_out, b3, send3, recv3
):
    wide = dy.shape[1]
    quarter = res.shape[2]
    narrow = da2.shape[1]
    me = lax.axis_index("dp")
    for q in range(wide // quarter):

        def body(j, carry, q=q):
            at = pl.ds(pl.multiple_of(q * quarter + j * 128, 128), 128)
            own = pl.ds(pl.multiple_of(j * 128, 128), 128)
            hn = h3n[:, at]
            z = gb[0:1, at] * hn + gb[1:2, at] + res[q, :, own].astype(F32)
            grad = (dy[:, at].astype(F32) * mask[:, 0:1] * slope(z)).astype(BF16)
            dz[:, at] = grad
            back_sums(b3, me, at, grad.astype(F32), hn)
            return carry

        lax.fori_loop(0, quarter // 128, body, 0)
    after()
    total = exchange(count, b3, send3, recv3)
    sums_out[...] = total

    def through(at):
        offset, scale = sums_out[0:1, at], sums_out[1:2, at]
        dh3[:, at] = (
            mask[:, 0:1]
            * gb[0:1, at]
            * stats[1:2, at]
            * (dz[:, at].astype(F32) - (offset + h3n[:, at] * scale) / valid)
        ).astype(BF16)

    over(wide, 128, through)

    def into(at):
        da2[:, at] = dot(dh3[...], w1[:, at]).astype(BF16)

    over(narrow, TILE, into)


def last_part(
    count, between, taps_term, da2, k, gb, pack, h1n, h2n, stats, counts, dh2, dh1, sums_out, act, acc, hold, *sync
):
    b2, send2, recv2, b1, send1, recv1 = sync
    rows, narrow = h1n.shape
    full = act.shape[1]
    me = lax.axis_index("dp")
    valid = counts[0:4, 0:1]

    def tile8(v):
        return v.reshape(rows // 8, 8, v.shape[1])

    for m in range(4):

        def put(j, carry, m=m):
            at = pl.ds(pl.multiple_of(j * 128, 128), 128)
            act[j, pl.ds(m, full // 4, stride=4), :] = da2[m, :, at].astype(F32)
            return carry

        lax.fori_loop(0, narrow // 128, put, 0)

    def into(gain, source, hidden, slots):
        def body(at):
            hn = hidden[:, at]
            n = gb[gain : gain + 1, at] * hn + gb[gain + 1 : gain + 2, at]
            grad = source(at) * pack[:, 0:1] * slope(n)
            act[lane(at), 0:rows, :] = grad
            slots[me, 0:4, at] = by_batch(grad)
            slots[me, 4:8, at] = by_batch(grad * hn)

        return body

    def through(gain, stat_at, row, hidden, out):
        def body(at):
            offset = spread8(sums_out[row : row + 4, at] / valid)
            scale = spread8(sums_out[row + 4 : row + 8, at] / valid)
            inv = spread8(stats[stat_at : stat_at + 4, at])
            g = tile8(act[lane(at), 0:rows, :])
            value = inv * gb[gain : gain + 1, at][None] * (g - (offset + tile8(hidden[:, at]) * scale))
            value = (pack[:, 0:1] * value.reshape(rows, value.shape[2])).astype(BF16)
            out[:, at] = value
            act[lane(at), 0:rows, :] = value.astype(F32)

        return body

    over(narrow, 128, into(2, lambda at: act[lane(at), 0:rows, :], h2n, b2))
    sums_out[0:8, :] = exchange(count, b2, send2, recv2)
    between()
    over(narrow, 128, through(2, 12, 0, h2n, dh2))
    acc[...] = jnp.zeros((rows, narrow), F32)
    for t, (vertical, lateral) in enumerate(OFFSETS):
        shift = -4 * (7 * vertical + lateral)
        other = 8 - t

        def place_back(j, carry, t=t, shift=shift, other=other):
            at = pl.ds(pl.multiple_of(j * 128, 128), 128)
            moved = unrolled_shift(act[j, 0:rows, :], shift)
            hold[:, at] = (pack[:, 1 + other : 2 + other] * moved).astype(BF16)
            return carry

        lax.fori_loop(0, narrow // 128, place_back, 0)

        def gather(at, t=t):
            row = pl.ds(pl.multiple_of(t * narrow + at.start, TILE), TILE)
            acc[:, at] += dot_t(hold[...], k[row, :])

        over(narrow, TILE, gather)
        taps_term(t)
    over(narrow, 128, into(0, lambda at: acc[:, at], h1n, b1))
    sums_out[8:16, :] = exchange(count, b1, send1, recv1)
    over(narrow, 128, through(0, 4, 8, h1n, dh1))


def back_kernel(
    sections,
    count,
    dy,
    res,
    h3n,
    mask,
    gains,
    stats3,
    w1,
    k_far,
    gb,
    pack,
    h1n_far,
    h2n_far,
    stats,
    counts,
    k2,
    y2,
    a2,
    a1_in,
    x_in,
    dh1,
    sums3,
    sums12,
    k2_out,
    dz_all,
    map_two,
    map_three,
    p1_out,
    k0_out,
    p0_out,
    sh_out,
    piece_out,
    dz,
    dh3,
    dh2,
    dzq_out,
    a1,
    x,
    k,
    h1n,
    h2n,
    stage,
    stage_sem,
    x_sem,
    da2,
    da2_all,
    dzq,
    act,
    acc,
    hold,
    *rest,
):
    sync, rest = rest[:9], list(rest[9:])
    half, theirs, pieces, whole = rest[:4]
    load_sem, swap_send, swap_recv, piece_send, piece_recv, out_sem = rest[4:10]
    sh_half, sh_other, sh_theirs, sh_pieces, sh_sum = rest[10:15]
    sh_swap_send, sh_swap_recv, sh_send, sh_recv, sh_sem = rest[15:20]
    rest = rest[20:]
    a_send, a_recv, q_send, q_recv = rest[:4]
    maps = [rest[4:7], rest[7:10], rest[10:13]]
    me, place = lax.axis_index("segment"), lax.axis_index("dp")
    quarter, narrow = dzq.shape[2], da2.shape[1]
    greet(count, sections)
    send_dz, wait_dz = map_sender(sections, dz, dz_all, 0, *maps[0])
    send_two, wait_two = map_sender(sections, dy, map_two, 2, *maps[1])
    send_three, wait_three = map_sender(sections, y2, map_three, 3, *maps[2])

    def q_copy(k_):
        other = jnp.bitwise_xor(me, k_)
        at = pl.ds(pl.multiple_of(other * quarter, 128), quarter)
        return mesh_copy(dz.at[:, at], dzq.at[me], q_send.at[k_], q_recv.at[k_], other, place)

    greeted(count, sections)
    core, z = lax.rem(place, 2), lax.div(place, 2)
    depth = count // 2
    x_loads = [
        pltpu.make_async_copy(src, dst, x_sem.at[i])
        for i, (src, dst) in enumerate(
            ((h2n_far, h2n), (k_far, k), (h1n_far, h1n), (a1_in, a1), (x_in, x))
        )
    ]
    for copy in x_loads:
        copy.start()
    load = pltpu.make_async_copy(k2.at[core], half, load_sem)
    swap = mesh_copy(k2.at[1 - core], theirs, swap_send, swap_recv, me, place + 1 - 2 * core)
    swap.start()
    load.start()

    def to_chip(k_):
        to = lax.rem(z + k_, depth)
        return mesh_copy(
            half.at[:, to],
            pieces.at[k_],
            piece_send.at[k_],
            piece_recv.at[k_],
            me,
            2 * to + core,
        )

    def add_cores():
        load.wait()
        swap.wait_recv()

        def add(n):
            q, y = lax.div(n, depth), lax.rem(n, depth)
            half[q, y] = (half[q, y].astype(F32) + theirs[q, y].astype(F32)).astype(BF16)

        loop(0, sections * depth, add)

    send_three()

    def after():
        return

    image_back_part(
        count,
        after,
        dy,
        res,
        h3n,
        mask,
        gains.at[1],
        stats3,
        batch_valid(counts, 0),
        w1,
        dz,
        dh3,
        da2,
        sums3,
        *sync[:3],
    )

    def a_copy(k_):
        return mesh_copy(da2, da2_all.at[me], a_send, a_recv.at[k_], 0, place)

    for k_ in range(1, sections):

        @pl.when(me == k_)
        def _(k_=k_):
            a_copy(k_).start()

    for k_ in range(1, sections):
        q_copy(k_).start()
    send_dz()
    send_two()
    add_cores()
    writer = Writer(stage, stage_sem)
    writer.rows_of_dot(dh3, a2, p1_out)
    writer.drain()

    def to_chips():
        loop(1, depth, lambda k_: to_chip(k_).start())

    pl.when(me != 0)(to_chips)

    @pl.when(me == 0)
    def _():
        for k_ in range(1, sections):
            a_copy(k_).wait_recv()
        da2_all[0] = da2[...]
        for copy in x_loads:
            copy.wait()
        writer = Writer(stage, stage_sem)

        def taps_term(t):
            tall = narrow
            writer.put(dot_0(a1[...], hold[...]), k0_out.at[pl.ds(t * tall, tall)])

        last_part(
            count,
            to_chips,
            taps_term,
            da2_all,
            k,
            gb,
            pack,
            h1n,
            h2n,
            stats,
            counts,
            dh2,
            dh1,
            sums12,
            act,
            acc,
            hold,
            *sync[3:],
        )
        writer.rows_of_dot(x, dh1, p0_out)
        writer.drain()

    @pl.when(me != 0)
    def _():
        for copy in x_loads:
            copy.wait()
        a_copy(0).wait_send()
        sums12[...] = jnp.zeros(sums12.shape, F32)

    for k_ in range(1, sections):
        q_copy(k_).wait_recv()
    dzq[me] = dz[:, pl.ds(pl.multiple_of(me * quarter, 128), quarter)]
    rows, full = dzq_out.shape[0], act.shape[1]
    for m in range(4):

        def put(j, carry, m=m):
            at = pl.ds(pl.multiple_of(j * 128, 128), 128)
            act[j, pl.ds(m, full // 4, stride=4), :] = dzq[m, :, at].astype(F32)
            return carry

        lax.fori_loop(0, quarter // 128, put, 0)

    def weave(j, carry):
        at = pl.ds(pl.multiple_of(j * 128, 128), 128)
        dzq_out[:, at] = act[j, 0:rows, :].astype(BF16)
        return carry

    lax.fori_loop(0, quarter // 128, weave, 0)
    tall = stage.shape[1]
    sh_rows = sh_half.shape[0]
    fine = sh_rows // depth
    sh_swap = mesh_copy(
        sh_other, sh_theirs, sh_swap_send, sh_swap_recv, me, place + 1 - 2 * core
    )

    def sh_to_chip(k_):
        to = lax.rem(z + k_, depth)
        return mesh_copy(
            sh_half.at[pl.ds(pl.multiple_of(to * fine, 16), fine)],
            sh_pieces.at[k_],
            sh_send.at[k_],
            sh_recv.at[k_],
            me,
            2 * to + core,
        )

    @pl.when(me != 0)
    def _():
        for half_of, target in ((1 - core, sh_other), (core, sh_half)):
            for j in range(sh_rows // tall):
                at = pl.ds(pl.multiple_of(half_of * sh_rows + j * tall, 128), tall)
                target[j * tall : j * tall + tall, :] = dot_0(x[:, at], dzq_out[...]).astype(BF16)
            if target is sh_other:
                sh_swap.start()
        sh_swap.wait_recv()

        def add(n):
            at = pl.ds(pl.multiple_of(n * 32, 32), 32)
            sh_half[at, :] = (sh_half[at, :].astype(F32) + sh_theirs[at, :].astype(F32)).astype(BF16)

        loop(0, sh_rows // 32, add)
        loop(1, depth, lambda k_: sh_to_chip(k_).start())

    loop(1, depth, lambda k_: to_chip(k_).wait_recv())

    def k2_sum(q):
        total = half[q, z].astype(F32)
        for k_ in range(1, depth):
            total = total + pieces[k_, q].astype(F32)
        whole[q] = total.astype(BF16)

    loop(0, sections, k2_sum)
    out = pltpu.make_async_copy(whole, k2_out, out_sem)
    out.start()

    @pl.when(me == 0)
    def _():
        writer = Writer(stage, stage_sem)
        writer.rows_of_dot(x, dzq_out, sh_out)
        writer.drain()

    @pl.when(me != 0)
    def _():
        loop(1, depth, lambda k_: sh_to_chip(k_).wait_recv())
        acc = sh_half[pl.ds(pl.multiple_of(z * fine, 16), fine), :].astype(F32)
        for k_ in range(1, depth):
            acc = acc + sh_pieces[k_].astype(F32)
        sh_sum[...] = acc.astype(BF16)
        written = pltpu.make_async_copy(sh_sum, piece_out, sh_sem)
        written.start()
        sh_swap.wait_send()
        loop(1, depth, lambda k_: sh_to_chip(k_).wait_send())
        written.wait()

    for k_ in range(1, sections):
        q_copy(k_).wait_send()
    loop(1, depth, lambda k_: to_chip(k_).wait_send())
    swap.wait_send()
    out.wait()
    wait_dz()
    wait_two()
    wait_three()


SUMS = (
    ("k0", 0, "owner"),
    ("p0", 0, "owner"),
    ("p1", 1, "each"),
    ("p2", 2, "each"),
    ("p3", 3, "each"),
    ("k2", 2, "chips"),
)


def gradient_kernel(
    sections,
    count,
    sh,
    sh_piece,
    k0,
    p0,
    p1,
    p2,
    p3,
    k2,
    vec,
    dh1,
    w,
    short,
    map_zero,
    map_one,
    map_two,
    map_three,
    sh_out,
    p_out,
    k_out,
    vec_out,
    maps,
    *scratch,
):
    names = [name for name, _, _ in SUMS]
    terms = dict(zip(names, (k0, p0, p1, p2, p3, k2)))
    owner = {name: section for name, section, _ in SUMS}
    held = {name: kind for name, _, kind in SUMS}
    fresh = [name for name in names if held[name] in ("owner", "each")]
    depth = count // 2
    me, place = lax.axis_index("segment"), lax.axis_index("dp")
    core, z = lax.rem(place, 2), lax.div(place, 2)
    sibling = place + 1 - 2 * core
    scratch = list(scratch)
    take = lambda: scratch.pop(0)
    half, theirs, planes, total, others, whole = {}, {}, {}, {}, {}, {}
    for name in names:
        if name in fresh:
            half[name], theirs[name] = take(), take()
        if held[name] in ("each", "chips"):
            planes[name] = take()
        if name in fresh:
            total[name], others[name] = take(), take()
        whole[name] = terms[name] if held[name] == "done" else take()
    relay = {name: take() for name in names if owner[name] == 0}
    relay["sh"] = take()
    sh_half, sh_theirs, sh_others, sh_whole, vec_slots = take(), take(), take(), take(), take()
    load_sem, a_send, a_recv, b_send, b_recv, c_send, c_recv, d_send, d_recv = (take() for _ in range(9))
    e_send, e_recv, e_own, f_send, f_recv, v_send, v_recv = (take() for _ in range(7))
    r_send, r_recv = take(), take()
    pages, s_rows, w_rows, hold, stage, page_sem, s_sem, w_sem, stage_sem = (take() for _ in range(9))
    slot = {name: i for i, name in enumerate(names)}
    last = len(names)

    page_loads = [
        pltpu.make_async_copy(source, pages, page_sem)
        for source in (map_zero, map_one, map_two, map_three)
    ]
    for i, copy in enumerate(page_loads):
        pl.when(me == i)(copy.start)
    wide = pages.shape[2]
    full_rows, map_rows = hold.shape[1], maps.shape[0] * maps.shape[1]

    def tile_loads(j):
        at = pl.ds(pl.multiple_of(j * TILE, TILE), TILE)
        at_slot = lax.rem(j, 2)
        return (
            pltpu.make_async_copy(short.at[at], s_rows.at[at_slot], s_sem.at[at_slot]),
            pltpu.make_async_copy(w.at[at], w_rows.at[at_slot], w_sem.at[at_slot]),
        )

    def tile_store(j):
        at = pl.ds(pl.multiple_of(j * TILE, TILE), TILE)
        at_slot = lax.rem(j, 2)
        return pltpu.make_async_copy(stage.at[at_slot], maps.at[:, :, at], stage_sem.at[at_slot])

    @pl.when(me == 0)
    def _():
        for copy in tile_loads(0):
            copy.start()

    def map_tile(j):
        at = pl.ds(pl.multiple_of(j * TILE, TILE), TILE)
        at_slot = lax.rem(j, 2)

        def weave(m, value):
            for part in range(TILE // 128):
                hold[part, pl.ds(m, full_rows // 4, stride=4), :] = value[
                    :, part * 128 : part * 128 + 128
                ]

        @pl.when(j >= 2)
        def _():
            tile_store(j - 2).wait()

        @pl.when(me == 0)
        def _():
            @pl.when(j + 1 < wide // TILE)
            def _():
                for copy in tile_loads(j + 1):
                    copy.start()

            for copy in tile_loads(j):
                copy.wait()
            for m in range(4):
                weave(m, dot_t(pages[m], s_rows[at_slot]))
            extra = dot_t(dh1[...], w_rows[at_slot])
            for part in range(TILE // 128):
                cols = slice(part * 128, part * 128 + 128)
                value = (hold[part, 0:map_rows, :] + extra[:, cols]).astype(BF16)
                stage[at_slot, :, :, cols] = value.reshape(map_rows // 4, 4, 128)

        @pl.when(me != 0)
        def _():
            for m in range(4):
                weave(m, pages[m, :, at].astype(F32))
            for part in range(TILE // 128):
                cols = slice(part * 128, part * 128 + 128)
                value = hold[part, 0:map_rows, :].astype(BF16)
                stage[at_slot, :, :, cols] = value.reshape(map_rows // 4, 4, 128)

        tile_store(j).start()

    def chip(k):
        return 2 * lax.rem(z + k, depth) + core

    barrier = pltpu.get_barrier_semaphore()
    pl.semaphore_signal(barrier, inc=1, device_id=(me, sibling), device_id_type=MESH)
    for k in range(1, sections):
        pl.semaphore_signal(
            barrier, inc=1, device_id=(jnp.bitwise_xor(me, k), place), device_id_type=MESH
        )
    loop(
        1,
        depth,
        lambda k: pl.semaphore_signal(
            barrier, inc=1, device_id=(me, chip(k)), device_id_type=MESH
        ),
    )
    pl.semaphore_wait(barrier, 1 + sections - 1 + depth - 1)

    def swap(name):
        return mesh_copy(
            terms[name].at[1 - core],
            theirs[name],
            a_send.at[slot[name]],
            a_recv.at[slot[name]],
            me,
            sibling,
        )

    def load(name):
        return pltpu.make_async_copy(terms[name].at[core], half[name], load_sem.at[slot[name]])

    def when_held(name, body):
        if held[name] == "each":
            body()
        else:
            pl.when(me == owner[name])(body)

    sh_rows = sh_half.shape[0]
    sh_swap = mesh_copy(
        sh.at[1 - core], sh_theirs, a_send.at[last], a_recv.at[last], me, sibling
    )
    sh_load = pltpu.make_async_copy(sh.at[core], sh_half, load_sem.at[last])
    piece = sh_rows // depth

    def sh_at(i):
        return pl.ds(pl.multiple_of(i * piece, 16), piece)

    mine = sh_at(z)
    piece_load = pltpu.make_async_copy(sh_piece, sh_whole.at[mine], load_sem.at[last])

    def sh_share(k):
        return mesh_copy(
            sh_whole.at[mine],
            sh_whole.at[mine],
            d_send.at[last, k],
            d_recv.at[last, k],
            me,
            chip(k),
        )

    @pl.when(me == 0)
    def _():
        sh_swap.start()
        sh_load.start()

    @pl.when(me != 0)
    def _():
        piece_load.start()
        piece_load.wait()
        loop(1, depth, lambda k: sh_share(k).start())


    def vec_copy(k):
        other = jnp.bitwise_xor(me, k)
        return mesh_copy(
            vec.at[other], vec_slots.at[k], v_send.at[k], v_recv.at[k], other, place
        )

    for k in range(1, sections):
        vec_copy(k).start()
    for name in fresh:

        def begin(name=name):
            swap(name).start()
            load(name).start()

        when_held(name, begin)

    def final(name):
        return k_out if name[0] == "k" else p_out

    def deliver(name, k):
        return mesh_copy(
            whole[name],
            final(name).at[core, me],
            e_send.at[slot[name]],
            e_recv.at[slot[name], k],
            owner[name],
            place,
        )

    def keep_own(name):
        return pltpu.make_async_copy(whole[name], final(name).at[core, me], e_own.at[slot[name]])

    def to_plane(name, k):
        other = jnp.bitwise_xor(me, k)
        return mesh_copy(
            terms[name].at[other],
            planes[name].at[k],
            b_send.at[slot[name], k],
            b_recv.at[slot[name], k],
            other,
            place,
        )

    def load_plane(name):
        return pltpu.make_async_copy(terms[name].at[me], planes[name].at[0], load_sem.at[slot[name]])

    for name in names:
        if held[name] == "chips":
            for k in range(1, sections):
                to_plane(name, k).start()
            load_plane(name).start()
        if held[name] == "done":

            @pl.when(me == owner[name])
            def _(name=name):
                keep_own(name).start()

            for k in range(1, sections):

                @pl.when(me == owner[name] ^ k)
                def _(name=name, k=k):
                    deliver(name, k).start()

    step = 32

    def sh_send(k):
        to = lax.rem(z + k, depth)
        return mesh_copy(
            sh_half.at[sh_at(to)],
            sh_others.at[k],
            c_send.at[last, k],
            c_recv.at[last, k],
            me,
            2 * to + core,
        )

    @pl.when(me == 0)
    def _():
        sh_load.wait()
        sh_swap.wait_recv()

        def sh_add(i):
            at = pl.ds(pl.multiple_of(i * step, step), step)
            sh_half[at, :] = (sh_half[at, :].astype(F32) + sh_theirs[at, :].astype(F32)).astype(BF16)

        loop(0, sh_rows // step, sh_add)
        loop(1, depth, lambda k: sh_send(k).start())

    def to_section(name, k):
        other = jnp.bitwise_xor(me, k)
        target = planes[name].at[k] if held[name] == "each" else total[name]
        return mesh_copy(
            half[name].at[other],
            target,
            b_send.at[slot[name], k],
            b_recv.at[slot[name], k],
            other,
            place,
        )

    def scattered(name, onward):
        if onward:
            return mesh_copy(
                relay[name], total[name], r_send.at[slot[name]], b_recv.at[slot[name], 3], 3, place
            )
        return mesh_copy(
            half[name].at[3], relay[name], b_send.at[slot[name], 3], r_recv.at[slot[name]], 2, place
        )

    for name in fresh:

        def combine(name=name):
            load(name).wait()
            swap(name).wait_recv()

            def add(i):
                q, y = lax.div(i, depth), lax.rem(i, depth)
                half[name][q, y] = (
                    half[name][q, y].astype(F32) + theirs[name][q, y].astype(F32)
                ).astype(BF16)

            loop(0, sections * depth, add)
            for k in range(1, sections):
                if held[name] == "owner" and k == 3:
                    pl.when(core == 0)(to_section(name, k).start)
                    pl.when(core == 1)(scattered(name, False).start)
                else:
                    to_section(name, k).start()

        when_held(name, combine)

    def share(name, k):
        return mesh_copy(
            whole[name].at[z],
            whole[name].at[z],
            d_send.at[slot[name], k],
            d_recv.at[slot[name], k],
            me,
            chip(k),
        )

    def planes_end(name):
        load_plane(name).wait()
        acc = planes[name][0].astype(F32)
        for k in range(1, sections):
            to_plane(name, k).wait_recv()
            acc = acc + planes[name][k].astype(F32)
        whole[name][z] = acc.astype(BF16)
        loop(1, depth, lambda k: share(name, k).start())

    planes_end("k2")
    for i, copy in enumerate(page_loads):
        pl.when(me == i)(copy.wait)
    loop(0, 2, map_tile)

    @pl.when((me == 2) & (core == 1))
    def _():
        for name in ("k0", "p0"):
            scattered(name, False).wait_recv()
            scattered(name, True).start()


    @pl.when(me == 0)
    def _():
        loop(1, depth, lambda k: sh_send(k).wait_recv())
        acc = sh_half[mine, :].astype(F32)
        for k in range(1, depth):
            acc = acc + sh_others[k].astype(F32)
        sh_whole[mine, :] = acc.astype(BF16)
        loop(1, depth, lambda k: sh_share(k).start())

    loop(2, wide // TILE, map_tile)

    def to_chip(name, k):
        to = lax.rem(z + k, depth)
        return mesh_copy(
            total[name].at[to],
            others[name].at[k],
            c_send.at[slot[name], k],
            c_recv.at[slot[name], k],
            me,
            2 * to + core,
        )

    def b_end(name):
        if held[name] == "each":
            for k in range(1, sections):
                to_section(name, k).wait_recv()

            def plane_add(y, name=name):
                acc = half[name][me, y].astype(F32)
                for k in range(1, sections):
                    acc = acc + planes[name][k, y].astype(F32)
                total[name][y] = acc.astype(BF16)

            loop(0, depth, plane_add)
        else:

            @pl.when(me == owner[name])
            def _(name=name):
                def keep(y):
                    total[name][y] = half[name][owner[name], y]

                loop(0, depth, keep)

            for k in range(1, sections):

                @pl.when(me == owner[name] ^ k)
                def _(name=name, k=k):
                    to_section(name, k).wait_recv()

        loop(1, depth, lambda k, name=name: to_chip(name, k).start())

    for name in ("k0", "p0"):
        b_end(name)

    def sh_deliver(k):
        at = pl.ds(pl.multiple_of(me * sh_whole.shape[1], 128), sh_whole.shape[1])
        return mesh_copy(
            sh_whole,
            sh_out.at[core, :, at],
            e_send.at[last],
            e_recv.at[last, k],
            0,
            place,
        )

    loop(1, depth, lambda k: sh_share(k).wait_recv())
    at_zero = pl.ds(0, sh_whole.shape[1])
    sh_keep = pltpu.make_async_copy(sh_whole, sh_out.at[core, :, at_zero], e_own.at[last])

    @pl.when(me == 0)
    def _():
        sh_keep.start()

    def relayed(name, onward):
        index = last if name == "sh" else slot[name]
        at = pl.ds(3 * sh_whole.shape[1], sh_whole.shape[1])
        src, dst = (sh_whole, sh_out.at[core, :, at]) if name == "sh" else (whole[name], final(name).at[core, 3])
        if onward:
            return mesh_copy(relay[name], dst, r_send.at[index], e_recv.at[index, 3], 0, place)
        return mesh_copy(src, relay[name], e_send.at[index], r_recv.at[index], 1, place)

    def start_delivery(name):
        index = last if name == "sh" else slot[name]
        section = 0 if name == "sh" else owner[name]
        copy = sh_deliver if name == "sh" else functools.partial(deliver, name)
        for k in range(1, sections):
            direct = me == section ^ k
            if section == 0 and k == 3:
                direct = direct & (core == 0)

                @pl.when((me == 3) & (core == 1))
                def _():
                    relayed(name, False).start()

            @pl.when(direct)
            def _(k=k):
                copy(k).start()

    def pass_on(name):
        @pl.when((me == 1) & (core == 1))
        def _():
            relayed(name, False).wait_recv()
            relayed(name, True).start()

    start_delivery("sh")

    def c_end(name):
        loop(1, depth, lambda k: to_chip(name, k).wait_recv())
        acc = total[name][z].astype(F32)
        for k in range(1, depth):
            acc = acc + others[name][k].astype(F32)
        whole[name][z] = acc.astype(BF16)
        loop(1, depth, lambda k: share(name, k).start())

    def d_end(name):
        loop(1, depth, lambda k: share(name, k).wait_recv())

        @pl.when(me == owner[name])
        def _():
            keep_own(name).start()

        start_delivery(name)

    later = ("p1", "p2", "p3")
    for name in ("k0", "p0"):
        c_end(name)
    for name in later:
        b_end(name)
    pass_on("sh")
    for name in ("k0", "p0", "k2"):
        d_end(name)
    for name in later:
        c_end(name)
    for name in ("k0", "p0"):
        pass_on(name)
    for name in later:
        d_end(name)

    def cross(name):
        return mesh_copy(
            final(name).at[core],
            final(name).at[core],
            f_send.at[slot[name]],
            f_recv.at[slot[name]],
            me,
            sibling,
        )

    sh_cross = mesh_copy(
        sh_out.at[core], sh_out.at[core], f_send.at[last], f_recv.at[last], me, sibling
    )

    @pl.when(me == 0)
    def _():
        sh_keep.wait()
        for k in range(1, sections):
            sh_deliver(k).wait_recv()
        sh_cross.start()

    for name in names:

        @pl.when(me == owner[name])
        def _(name=name):
            keep_own(name).wait()
            for k in range(1, sections):
                deliver(name, k).wait_recv()
            cross(name).start()

    for k in range(1, sections):
        vec_copy(k).wait_recv()
    sums = vec[me]
    for k in range(1, sections):
        sums = sums + vec_slots[k]
    vec_out[...] = sums

    tile_store(wide // TILE - 2).wait()
    tile_store(wide // TILE - 1).wait()
    for k in range(1, sections):
        vec_copy(k).wait_send()

    @pl.when(me == 0)
    def _():
        sh_swap.wait_send()
        loop(1, depth, lambda k: sh_send(k).wait_send())

    loop(1, depth, lambda k: sh_share(k).wait_send())

    @pl.when(me == 0)
    def _():
        sh_cross.wait()

    @pl.when(me != 0)
    def _():
        sh_deliver(0).wait_send()

    @pl.when((me == 1) & (core == 1))
    def _():
        for name in relay:
            relayed(name, True).wait_send()

    @pl.when((me == 2) & (core == 1))
    def _():
        for name in ("k0", "p0"):
            scattered(name, True).wait_send()

    for name in names:

        def sent(name=name):
            swap(name).wait_send()
            for k in range(1, sections):
                to_section(name, k).wait_send()

        if name in fresh:
            when_held(name, sent)
            loop(1, depth, lambda k, name=name: to_chip(name, k).wait_send())
        if held[name] == "chips":
            for k in range(1, sections):
                to_plane(name, k).wait_send()
        if held[name] != "done":
            loop(1, depth, lambda k, name=name: share(name, k).wait_send())

        @pl.when(me == owner[name])
        def _(name=name):
            cross(name).wait()

        @pl.when(me != owner[name])
        def _(name=name):
            deliver(name, 0).wait_send()


def sum_gradients(sections, count, short, piece, terms, vectors, dh1, w, weights, map_sources, real):
    narrow = short.shape[1]
    depth = count // 2
    args, scratch = [], []
    relays = []
    for name, section, kind in SUMS:
        args.append(terms[name])
        full = (sections, depth) + terms[name].shape[-2:]
        shapes = []
        if kind in ("owner", "each"):
            shapes += [full, full]
        if kind == "each":
            shapes.append(full)
        if kind == "chips":
            shapes.append((sections,) + full[2:])
        if kind in ("owner", "each"):
            shapes += [full[1:]] * 2
        if kind != "done":
            shapes.append(full[1:])
        if section == 0:
            relays.append(pltpu.VMEM(full[1:], BF16))
        scratch += [pltpu.VMEM(a, BF16) for a in shapes]
    scratch += relays + [pltpu.VMEM((short.shape[0] // 2, narrow), BF16)]
    sh_rows = short.shape[0] // 2
    scratch += [
        pltpu.VMEM((sh_rows, narrow), BF16),
        pltpu.VMEM((sh_rows, narrow), BF16),
        pltpu.VMEM((depth, sh_rows // depth, narrow), BF16),
        pltpu.VMEM((sh_rows, narrow), BF16),
        pltpu.VMEM((sections,) + vectors.shape[1:], F32),
    ]
    kinds = len(SUMS) + 1
    for shape in [(kinds,)] * 3 + [(kinds, sections)] * 2 + [(kinds, depth)] * 4:
        scratch.append(pltpu.SemaphoreType.DMA(shape))
    for shape in [(kinds,), (kinds, sections), (kinds,), (kinds,), (kinds,), (sections,), (sections,), (kinds,), (kinds,)]:
        scratch.append(pltpu.SemaphoreType.DMA(shape))
    wide = w.shape[0]
    padded = map_sources[0].shape[1]
    scratch += [
        pltpu.VMEM(map_sources[0].shape, BF16),
        pltpu.VMEM((2, TILE, wide), BF16),
        pltpu.VMEM((2, TILE, narrow), BF16),
        pltpu.VMEM((TILE // 128, 4 * padded, 128), F32),
        pltpu.VMEM((2, real, 4, TILE), BF16),
        pltpu.SemaphoreType.DMA,
        pltpu.SemaphoreType.DMA((2,)),
        pltpu.SemaphoreType.DMA((2,)),
        pltpu.SemaphoreType.DMA((2,)),
    ]
    hbm = pl.BlockSpec(memory_space=pl.ANY)
    vmem = pl.BlockSpec(memory_space=pltpu.VMEM)
    taps_shape, proj_shape = args[0].shape, args[1].shape
    return pl.pallas_call(
        functools.partial(gradient_kernel, sections, count),
        out_shape=[
            shape_of((2, sh_rows, narrow * sections), BF16),
            shape_of(proj_shape, BF16),
            shape_of(taps_shape, BF16),
            shape_of(vectors.shape[1:], F32),
            shape_of((real, 4, wide), BF16),
        ],
        in_specs=[hbm] * 8 + [vmem, vmem] + [hbm] * 6,
        out_specs=[hbm, hbm, hbm, vmem, hbm],
        scratch_shapes=scratch,
        compiler_params=pltpu.CompilerParams(
            has_side_effects=True, vmem_limit_bytes=VMEM_BYTES, collective_id=5
        ),
        cost_estimate=pl.CostEstimate(flops=0, bytes_accessed=400 * 2**20, transcendentals=0),
    )(short.reshape(2, sh_rows, narrow), piece, *args, vectors, dh1, w, weights, *map_sources)


def cast_kernel(proj, taps, short, maps, proj_out, taps_out, short_out, maps_out):
    me = lax.axis_index("segment")
    maps_out[...] = maps[...]
    proj_out[...] = proj[...].astype(F32)
    for held, src, out in (
        ((me == 0) | (me == 2), taps, taps_out),
        (me == 0, short, short_out),
    ):

        @pl.when(held)
        def _(src=src, out=out):
            out[...] = src[...].astype(F32)

        @pl.when(jnp.logical_not(held))
        def _(out=out):
            out[...] = jnp.zeros(out.shape, F32)


def cast_sums(maps, *sums):
    steps = 8
    blocks = [pl.BlockSpec((a.shape[0] // steps, a.shape[1]), lambda i: (i, 0)) for a in sums]
    blocks.append(pl.BlockSpec(maps.shape[:2] + (maps.shape[2] // steps,), lambda i: (0, 0, i)))
    return pl.pallas_call(
        cast_kernel,
        grid=(steps,),
        out_shape=[shape_of(a.shape, F32) for a in sums] + [shape_of(maps.shape, BF16)],
        in_specs=blocks,
        out_specs=blocks,
        compiler_params=pltpu.CompilerParams(vmem_limit_bytes=VMEM_BYTES),
        cost_estimate=pl.CostEstimate(flops=0, bytes_accessed=54 * 2**20, transcendentals=0),
    )(*sums, maps)


def layouts(resolution_ids, order_ids):
    pixels = jnp.arange(MAP * MAP, dtype=jnp.int32)
    row_of = pixels // MAP
    column_of = pixels % MAP
    extent = 5 + resolution_ids[:, None]
    image_mask = ((row_of[None, :] < extent) & (column_of[None, :] < extent)).astype(F32)
    inside = (row_of < 6) & (column_of < 6)
    position = jnp.where(inside, row_of // 2 * 3 + column_of // 2, 0)
    onehot_tile = (position[:, None] == jnp.arange(9)[None, :]).astype(jnp.int32)
    picked = jnp.sum(onehot_tile[None] * order_ids[:, None, :], axis=2)
    row_to = 2 * (picked // 3) + row_of % 2
    column_to = 2 * (picked % 3) + column_of % 2
    target = row_to * MAP + column_to
    tile_mask = (inside & (row_to < extent) & (column_to < extent)).astype(F32)
    return image_mask, tile_mask, jnp.where(inside, target, -1)


def tap_tables(tiled):
    lattice = np.arange(MAP)
    tables = []
    for vertical, lateral in OFFSETS:
        row, column = lattice + vertical, lattice + lateral
        in_row = (row >= 0) & (row < MAP)
        in_column = (column >= 0) & (column < MAP)
        if tiled:
            in_row &= row // 2 == lattice // 2
            in_column &= column // 2 == lattice // 2
        tables.append((in_row[:, None] & in_column[None, :]).reshape(-1))
    return np.stack(tables, axis=1).astype(np.float32)


def body(
    layer_input,
    output_grad,
    resolution,
    tile_order,
    proj_weight,
    spatial_weight,
    shortcut_weight,
    bn_gain,
    bn_bias,
):
    micro, images, pixels, wide = layer_input.shape
    narrow = proj_weight.shape[2]
    rows = images * pixels
    padded = -(-rows // 16) * 16
    sections = lax.axis_size("segment")
    count = lax.axis_size("dp")
    section = lax.axis_index("segment")
    first = section == 0
    proj, spatial, shortcut = proj_weight[0], spatial_weight[0], shortcut_weight[0]
    pick = lambda a: lax.dynamic_index_in_dim(a, section, 0, keepdims=False)

    image_masks, tile_masks, targets = layouts(
        resolution.reshape(-1), tile_order.reshape(micro * images, -1)
    )
    interleave = lambda a: jnp.transpose(a.reshape(micro, rows), (1, 0)).reshape(rows * micro, 1)
    taps_image = np.tile(np.repeat(tap_tables(False), micro, axis=0), (images, 1))
    pack_all = jnp.concatenate(
        [interleave(image_masks), jnp.asarray(taps_image), jnp.zeros((rows * micro, 6), F32)], axis=1
    )
    tiles_all = interleave(tile_masks)
    pad_rows = lambda a: jnp.pad(a, ((0, padded - rows), (0, 0)))
    image_mask = pad_rows(pick(image_masks.reshape(micro, rows, 1)))
    tile_mask = pad_rows(pick(tile_masks.reshape(micro, rows, 1)))
    taps_tile = np.pad(np.tile(tap_tables(True), (images, 1)), ((0, padded - rows), (0, 6)))
    pack_tile = jnp.concatenate([tile_mask, jnp.asarray(taps_tile)], axis=1)
    target = pick(targets.reshape(micro, images, pixels))
    base = (jnp.arange(images) * pixels)[:, None]
    target = jnp.where(target >= 0, target + base, -1).reshape(rows)
    target = jnp.pad(target, (0, padded - rows), constant_values=-1)
    index = jnp.arange(padded)
    moves = (target[:, None] == index[None, :]).astype(BF16)
    moves_back = (target[None, :] == index[:, None]).astype(BF16)

    x_in = jnp.transpose(layer_input, (1, 2, 0, 3)).reshape(rows, micro, wide)
    og_in = jnp.transpose(output_grad, (1, 2, 0, 3)).reshape(rows, micro, wide)
    gb_first = jnp.stack(
        [bn_gain[0, :narrow], bn_bias[0, :narrow]]
        + [bn_gain[0, narrow : 2 * narrow], bn_bias[0, narrow : 2 * narrow]]
    )
    gains_here = jnp.concatenate([bn_gain, bn_bias])
    total = rows * micro
    quarter = wide // sections
    dma = pltpu.SemaphoreType.DMA
    stats_all, counts, gains, y1, u, h3n, stats3, *far = kernel_call(
        functools.partial(head_kernel, sections, count),
        [
            shape_of((16, narrow), F32),
            shape_of((8, 128), F32),
            shape_of((sections, 2, wide), F32),
            shape_of((padded, wide), BF16),
            shape_of((padded, wide), BF16),
            shape_of((padded, wide), F32),
            shape_of((2, wide), F32),
            shape_of((padded, narrow), BF16),
            shape_of((wide, narrow), BF16),
            shape_of((sections, padded, quarter), BF16),
            shape_of((total, wide), BF16),
            shape_of((total, narrow), BF16),
            shape_of((total, narrow), F32),
            shape_of((total, narrow), F32),
            shape_of((wide, narrow), BF16),
            shape_of((wide, narrow), BF16),
            shape_of((9 * narrow, narrow), BF16),
        ],
        [x_in, proj, shortcut, spatial, gb_first, gains_here, pack_all, tiles_all, image_mask, moves],
        [
            pltpu.VMEM((total, wide), BF16),
            pltpu.VMEM((total, 9 * narrow), BF16),
            pltpu.VMEM((total, narrow), F32),
            pltpu.VMEM((total, narrow), F32),
            pltpu.VMEM((narrow // 128, 4 * padded, 128), F32),
            pltpu.VMEM((micro, padded, narrow), BF16),
            pltpu.VMEM((padded, narrow), BF16),
            pltpu.VMEM((wide, quarter), BF16),
            pltpu.VMEM((wide, narrow), BF16),
            pltpu.VMEM((micro, padded, quarter), BF16),
            pltpu.VMEM((sections, padded, quarter), BF16),
            pltpu.VMEM((sections, 2, wide), F32),
        ]
        + sync_scratch(count, [(8, narrow + 128), (8, narrow), (2, wide)])
        + [dma((sections,)), dma, dma, dma]
        + [dma((sections,)), dma, dma, dma]
        + [dma((sections,)), dma((sections,)), dma((sections,)), dma]
        + [dma((sections,)), dma((sections,)), dma((2,)), dma((7,))]
        + [dma((5, sections)), dma((5,)), dma((5,)), dma((5,))]
        + [dma((5, 2)), dma((5, 2)), dma((3,))]
        + [dma((5,)), pltpu.VMEM((9 * narrow, narrow), BF16), dma],
        0,
        2 * total * (narrow * (wide + 9 * narrow) + wide * quarter),
        60 * 2**20,
        far_in=(2, 3),
        far_out=tuple(range(7, 17)),
    )
    a2, w1, res, x_all, a1_all, h1n_all, h2n_all, w3, w2, k2 = far
    paged = shape_of((sections, padded, wide), BF16)
    y2, dy1, t_sums, map_one, p3_term, p2_term, k2_term = kernel_call(
        functools.partial(tile_kernel, sections, count),
        [
            shape_of((padded, wide), BF16),
            shape_of((padded, wide), BF16),
            shape_of((6, wide), F32),
            paged,
            shape_of((wide, narrow), BF16),
            shape_of((wide, narrow), BF16),
            shape_of((9 * narrow, narrow), BF16),
        ],
        [u, w2, k2, w3, og_in, pack_tile, gains, counts, moves_back, y1],
        [
            pltpu.VMEM((padded, narrow), BF16),
            pltpu.VMEM((padded, 9 * narrow), BF16),
            pltpu.VMEM((padded, wide), BF16),
            pltpu.VMEM((padded, narrow), BF16),
            pltpu.VMEM((padded, narrow), BF16),
            pltpu.VMEM((2, 512, narrow), BF16),
            dma((2,)),
            pltpu.VMEM((9 * narrow, narrow), BF16),
            pltpu.VMEM((wide, narrow), BF16),
            pltpu.VMEM((rows, micro, wide), BF16),
            dma((3,)),
            pltpu.VMEM((padded, narrow), F32),
            pltpu.VMEM((padded, narrow), F32),
            pltpu.VMEM((padded, wide), F32),
            pltpu.VMEM((padded, narrow), F32),
            pltpu.VMEM((padded, wide), BF16),
            pltpu.VMEM((6, wide), F32),
            pltpu.VMEM((padded, wide), F32),
        ]
        + [dma, dma((sections,)), dma]
        + sync_scratch(
            count, [(2, narrow), (2, narrow), (2, wide), (2, wide), (2, narrow), (2, narrow)]
        ),
        1,
        4 * padded * narrow * (2 * wide + 9 * narrow),
        30 * 2**20,
        far_in=(2, 3, 4, 9),
        far_out=(3, 4, 5, 6),
    )
    depth = count // 2

    def split(term):
        return term.reshape(2, sections, depth, term.shape[0] // (2 * sections * depth), narrow)

    p3_term, p2_term, k2_term = split(p3_term), split(p2_term), split(k2_term)
    taps_piece = k2_term.shape[3]
    dh1_all, i_sums, f_sums, k2_part, *far = kernel_call(
        functools.partial(back_kernel, sections, count),
        [
            shape_of((total, narrow), BF16),
            shape_of((2, wide), F32),
            shape_of((16, narrow), F32),
            shape_of((sections, taps_piece, narrow), BF16),
            paged,
            paged,
            paged,
            shape_of((wide, narrow), BF16),
            shape_of((9 * narrow, narrow), BF16),
            shape_of((wide, narrow), BF16),
            shape_of((wide, narrow), BF16),
            shape_of((wide // count, narrow), BF16),
        ],
        [dy1, res, h3n, image_mask, gains, stats3, w1, spatial, gb_first, pack_all]
        + [h1n_all, h2n_all, stats_all, counts, k2_term, y2, a2, a1_all, x_all],
        [
            pltpu.VMEM((padded, wide), BF16),
            pltpu.VMEM((padded, wide), BF16),
            pltpu.VMEM((total, narrow), BF16),
            pltpu.VMEM((total, quarter), BF16),
            pltpu.VMEM((total, narrow), BF16),
            pltpu.VMEM((total, wide), BF16),
            pltpu.VMEM((9 * narrow, narrow), BF16),
            pltpu.VMEM((total, narrow), F32),
            pltpu.VMEM((total, narrow), F32),
            pltpu.VMEM((2, 512, narrow), BF16),
            dma((2,)),
            dma((5,)),
            pltpu.VMEM((padded, narrow), BF16),
            pltpu.VMEM((micro, padded, narrow), BF16),
            pltpu.VMEM((micro, padded, quarter), BF16),
            pltpu.VMEM((narrow // 128, 4 * padded, 128), F32),
            pltpu.VMEM((total, narrow), F32),
            pltpu.VMEM((total, narrow), BF16),
        ]
        + sync_scratch(count, [(2, wide), (8, narrow), (8, narrow)])
        + [pltpu.VMEM(k2_term.shape[1:], BF16)] * 2
        + [pltpu.VMEM((depth, sections, taps_piece, narrow), BF16)]
        + [pltpu.VMEM((sections, taps_piece, narrow), BF16)]
        + [dma, dma, dma, dma((depth,)), dma((depth,)), dma]
        + [pltpu.VMEM((wide // 2, narrow), BF16)] * 3
        + [pltpu.VMEM((depth, wide // count, narrow), BF16), pltpu.VMEM((wide // count, narrow), BF16)]
        + [dma, dma, dma((depth,)), dma((depth,)), dma]
        + [dma, dma((sections,)), dma((sections,)), dma((sections,))]
        + [dma, dma((sections,)), dma] * 3,
        2,
        2 * total * narrow * 9 * narrow,
        40 * 2**20,
        far_in=(7, 10, 11, 14, 15, 17, 18),
        far_out=tuple(range(3, 12)),
    )
    map_zero, map_two, map_three, p1_term, k0_term, p0_term, short_term, short_piece = far

    terms = {
        "p3": p3_term,
        "k2": k2_part,
        "p2": p2_term,
        "p1": split(p1_term),
        "k0": split(k0_term),
        "p0": split(p0_term),
    }

    blank = jnp.zeros((wide,), F32)
    pad = jnp.zeros((wide - 2 * narrow,), F32)
    of_batches = lambda at: jnp.sum(f_sums[at : at + 4], axis=0)
    zero_gain = jnp.where(first, jnp.concatenate([of_batches(12), of_batches(4), pad]), blank)
    zero_bias = jnp.where(first, jnp.concatenate([of_batches(8), of_batches(0), pad]), blank)
    vectors = jnp.stack(
        [
            zero_gain,
            zero_bias,
            i_sums[1],
            i_sums[0],
            jnp.concatenate([t_sums[5, :narrow], t_sums[3, :narrow], pad]),
            jnp.concatenate([t_sums[4, :narrow], t_sums[2, :narrow], pad]),
            t_sums[1],
            t_sums[0],
        ]
    )
    short_sum, proj_sum, taps_sum, vectors, maps = sum_gradients(
        sections,
        count,
        short_term,
        short_piece,
        terms,
        vectors.reshape(sections, 2, wide),
        dh1_all,
        proj,
        shortcut,
        (map_zero, map_one, map_two, map_three),
        rows,
    )
    proj_grad, spatial_grad, short_grad, maps = cast_sums(
        maps,
        proj_sum.reshape(wide, narrow),
        taps_sum.reshape(9 * narrow, narrow),
        short_sum.reshape(wide, wide),
    )
    maps = jnp.transpose(maps.reshape(images, pixels, micro, wide), (2, 0, 1, 3))
    return (
        maps[None],
        proj_grad[None],
        spatial_grad[None],
        short_grad[None],
        vectors[:1],
        vectors[1:],
    )


def solution(mesh):
    return jax.shard_map(
        body,
        mesh=mesh,
        in_specs=(
            P(None, "dp", None, None),
            P(None, "dp", None, None),
            P(None, "dp"),
            P(None, "dp", None),
            P("segment", None, None),
            P("segment", None, None),
            P("segment", None, None),
            P("segment", None),
            P("segment", None),
        ),
        out_specs=(
            P("segment", None, "dp", None, None),
            P("segment", None, None),
            P("segment", None, None),
            P("segment", None, None),
            P("segment", None),
            P("segment", None),
        ),
        check_vma=False,
    )
```
